32 devices in a mesh: section: 2 (over x), dp: 2 (over core), ctx: 8 (over z, y).
Axes of the slice: x: 2, y: 2, z: 4, core: 2. Of those that a mesh axis runs over, the one named last changes fastest.
Arguments:
- inputs: bfloat16 [2, 2, 1024, 1600], P(None, 'dp', 'ctx'), may hold values from -6 to 6
- cotangent: bfloat16 [2, 2, 1024, 1600], P(None, 'dp', 'ctx'), may hold values from -6 to 6
- positions: int32 [2, 1024], P(None, 'ctx'), may hold values from 0 to 1023, each once within a row
- w_qkv: bfloat16 [2, 1600, 4800], P('section', ('dp', 'ctx')), may hold values from -0.15625 to 0.15625
- w_attn_out: bfloat16 [2, 1600, 1600], P('section', ('dp', 'ctx')), may hold values from -0.625 to 0.625
- w_fc: bfloat16 [2, 1600, 6400], P('section', ('dp', 'ctx')), may hold values from -0.15625 to 0.15625
- w_proj: bfloat16 [2, 6400, 1600], P('section', ('dp', 'ctx')), may hold values from -0.078125 to 0.078125
- norm_gains: bfloat16 [2, 1600, 2], P('section', ('dp', 'ctx')), may hold values from 0.5 to 1.5
- biases: bfloat16 [2, 1600, 6], P('section', ('dp', 'ctx')), may hold values from -3 to 3
- fc_bias: bfloat16 [2, 6400], P('section', ('dp', 'ctx')), may hold values from -3 to 3
Outputs:
- section_out: bfloat16 [2, 2, 2, 1024, 1600], P('section', None, 'dp', 'ctx')
- section_grad: bfloat16 [2, 2, 2, 1024, 1600], P('section', None, 'dp', 'ctx')
- grad_qkv: float32 [2, 1600, 4800], P('section', ('dp', 'ctx'))
- grad_attn_out: float32 [2, 1600, 1600], P('section', ('dp', 'ctx'))
- grad_fc: float32 [2, 1600, 6400], P('section', ('dp', 'ctx'))
- grad_proj: float32 [2, 6400, 1600], P('section', ('dp', 'ctx'))
- grad_gains: float32 [2, 1600, 2], P('section', ('dp', 'ctx'))
- grad_biases: float32 [2, 1600, 6], P('section', ('dp', 'ctx'))
- grad_fc_bias: float32 [2, 6400], P('section', ('dp', 'ctx'))
The draws below stay inside these ranges and needn't reach their ends.
Inputs may be any that keep to these rules, and one draw needn't show every extreme that they name: `positions`: each row of a micro-batch holds every position from 0 to 1023 once, in any order over the slots.
All inputs are finite; a program needn't handle non-finite values.
Results may differ from the reference program's by a relative error of at most 0.02.
Values may be sent and summed in bfloat16 or wider, within the bound.
A program may use at most 576 MiB of HBM per device.

```python
import jax
import jax.numpy as jnp
from jax import lax

D = 1600
HEADS = 25
FF = 6400
SEQ = 1024
SEQS = 2
MICRO = 2


def block_scale(rng, shape, split, least, top_value):
    level, own = 1.0, jax.random.fold_in(rng, 6)
    for position, blocks in split:
        heights = jnp.exp(jax.random.uniform(jax.random.fold_in(own, position), (blocks,), jnp.float32, least / len(split), top_value / len(split)))
        level = level * jnp.repeat(heights, shape[position] // blocks).reshape([-1 if axis == position else 1 for axis in range(len(shape))])
    return level


def noise(stream_key, dims, deviation, limit, cuts=(), dtype=jnp.bfloat16):
    factor_of = block_scale(stream_key, dims, cuts, -0.22, 0.18) if cuts else 1.0
    entries = jax.random.normal(stream_key, dims, jnp.float32) * deviation * factor_of
    return jnp.minimum(jnp.maximum(entries, -limit), limit).astype(dtype)


def setup_inputs(seed: int = 0) -> dict:
    streams_of = jax.random.split(jax.random.key(seed), 11)
    inputs = noise(streams_of[0], (MICRO, SEQS, SEQ, D), 1.0, 6.0, ((1, 2), (2, 8)))
    cotangent = noise(streams_of[1], (MICRO, SEQS, SEQ, D), 1.0, 6.0, ((1, 2), (2, 8)))
    positions = jax.vmap(lambda own: jax.random.permutation(own, SEQ))(jax.random.split(streams_of[2], MICRO)).reshape((MICRO, SEQ)).astype(jnp.int32)
    w_qkv = noise(streams_of[3], (2, D, 3 * D), D ** -0.5, 0.15625, ((0, 2), (1, 16)))
    w_attn_out = noise(streams_of[4], (2, D, D), (D // 16) ** -0.5, 0.625, ((0, 2), (1, 16)))
    w_fc = noise(streams_of[5], (2, D, FF), D ** -0.5, 0.15625, ((0, 2), (1, 16)))
    w_proj = noise(streams_of[6], (2, FF, D), FF ** -0.5, 0.078125, ((0, 2), (1, 16)))
    norm_gains = jnp.clip(1.0 + 0.1 * jax.random.normal(streams_of[7], (2, D, 2), jnp.float32), 0.5, 1.5).astype(jnp.bfloat16)
    biases = noise(streams_of[8], (2, D, 6), 0.5, 3.0, ((0, 2), (1, 16)))
    fc_bias = noise(streams_of[9], (2, FF), 0.5, 3.0, ((0, 2), (1, 16)))
    return {"inputs": inputs, "cotangent": cotangent, "positions": positions, "w_qkv": w_qkv, "w_attn_out": w_attn_out, "w_fc": w_fc, "w_proj": w_proj, "norm_gains": norm_gains, "biases": biases, "fc_bias": fc_bias}


EPSILON = 1e-05
HIGHEST = lax.Precision.HIGHEST

@jax.custom_vjp
def low(v):
    return lax.optimization_barrier(v.astype(jnp.bfloat16)).astype(jnp.float32)

@jax.custom_vjp
def low_back(v):
    return v

def low_keep(v):
    return (low(v), None)

def low_pass(kept, grad):
    return (grad,)

def back_keep(v):
    return (v, None)

def back_low(kept, grad):
    return (low(grad),)
low.defvjp(low_keep, low_pass)
low_back.defvjp(back_keep, back_low)

def normalize(rows_in, gain_col, shift_col):
    centred = rows_in - lax.optimization_barrier(jnp.mean(rows_in, axis=-1, keepdims=True))
    spread = lax.optimization_barrier(jnp.mean(centred * centred, axis=-1, keepdims=True))
    return centred * lax.rsqrt(spread + EPSILON) * gain_col + shift_col

def attention(queries, key_rows, value_rows, position_row):
    token_count, model_width = queries.shape
    head_size = model_width // HEADS
    score_scale = head_size ** (-0.5)
    block_rows = min(512, token_count)
    query_blocks = queries.reshape(token_count // block_rows, block_rows, HEADS, head_size)
    place_blocks = position_row.reshape(token_count // block_rows, block_rows)
    key_heads = key_rows.reshape(token_count, HEADS, head_size)
    value_heads = value_rows.reshape(token_count, HEADS, head_size)

    def one_block(element):
        query_part, place_part = element
        scores = low_back(jnp.einsum('qhd,nhd->hqn', query_part, key_heads, precision=HIGHEST) * score_scale)
        allowed = place_part[:, None] >= position_row[None, :]
        scores = jnp.where(allowed[None], scores, -1e+30)
        probs = low(jax.nn.softmax(scores, axis=-1))
        return jnp.einsum('hqn,nhd->qhd', probs, value_heads, precision=HIGHEST)
    attended = lax.map(jax.checkpoint(one_block), (query_blocks, place_blocks))
    return attended.reshape(token_count, model_width)

def layer(rows_in, params, position_row):
    w_joint, w_output, w_hidden, w_back, gain_cols, shift_cols, unit_shift = params
    model_width = rows_in.shape[1]
    source = low_back(rows_in)
    normed = low(normalize(source, gain_cols[:, 0], shift_cols[:, 0]))
    projected = jnp.dot(normed, w_joint, precision=HIGHEST)
    queries = low_back(low(projected[:, :model_width] + shift_cols[:, 1]))
    key_rows = low_back(low(projected[:, model_width:2 * model_width]))
    value_rows = low_back(low(projected[:, 2 * model_width:] + shift_cols[:, 2]))
    attended = low_back(low(attention(queries, key_rows, value_rows, position_row)))
    residual_mid = source + low_back(jnp.dot(attended, w_output, precision=HIGHEST) + shift_cols[:, 3])
    normed_two = low(normalize(residual_mid, gain_cols[:, 1], shift_cols[:, 4]))
    hidden = low_back(jnp.dot(normed_two, w_hidden, precision=HIGHEST) + unit_shift)
    activated = low(jax.nn.gelu(hidden, approximate=True))
    result = residual_mid + low_back(jnp.dot(activated, w_back, precision=HIGHEST) + shift_cols[:, 5])
    return low(result)

def reference(inputs, cotangent, positions, w_qkv, w_attn_out, w_fc, w_proj, norm_gains, biases, fc_bias):
    micro_count, seq_count, token_count, model_width = inputs.shape
    stacked = (w_qkv.astype(jnp.float32), w_attn_out.astype(jnp.float32), w_fc.astype(jnp.float32), w_proj.astype(jnp.float32), norm_gains.astype(jnp.float32), biases.astype(jnp.float32), fc_bias.astype(jnp.float32))
    first_params = tuple((weight[0] for weight in stacked))
    second_params = tuple((weight[1] for weight in stacked))
    flat_inputs = inputs.reshape(micro_count * seq_count, token_count, model_width)
    flat_cotangent = cotangent.reshape(micro_count * seq_count, token_count, model_width)
    flat_positions = jnp.repeat(positions, seq_count, axis=0)
    zero_grads = jax.tree.map(jnp.zeros_like, (first_params, second_params))

    def one_sequence(carried, element):
        source, seed_grad, position_row = element

        def apply_layer(rows_in, params):
            return layer(rows_in, params, position_row)
        middle_out, first_back = jax.vjp(apply_layer, source.astype(jnp.float32), first_params)
        final_out, second_back = jax.vjp(apply_layer, middle_out, second_params)
        grad_middle, grad_second = second_back(seed_grad.astype(jnp.float32))
        grad_source, grad_first = first_back(grad_middle)
        carried = jax.tree.map(jnp.add, carried, (grad_first, grad_second))
        return (carried, (middle_out.astype(jnp.bfloat16), final_out.astype(jnp.bfloat16), grad_source.astype(jnp.bfloat16), grad_middle.astype(jnp.bfloat16)))
    totals, (middles, finals, grad_sources, grad_middles) = lax.scan(one_sequence, zero_grads, (flat_inputs, flat_cotangent, flat_positions))
    full_shape = (micro_count, seq_count, token_count, model_width)
    section_out = jnp.stack([middles.reshape(full_shape), finals.reshape(full_shape)])
    section_grad = jnp.stack([grad_sources.reshape(full_shape), grad_middles.reshape(full_shape)])
    first_totals, second_totals = totals
    paired = [jnp.stack([first_part, second_part]) for first_part, second_part in zip(first_totals, second_totals)]
    return (section_out, section_grad, paired[0], paired[1], paired[2], paired[3], paired[4], paired[5], paired[6])
```

```python
import jax
import jax.numpy as jnp
from jax import lax
from jax.sharding import Mesh
from jax.sharding import PartitionSpec as P

HEADS = 25
EPSILON = 1e-05

SLAB = ("section", "dp", "r")
ALL = ("section", "dp", "z", "r")


def normalize(rows_in, gain_col, shift_col):
    centred = rows_in - jnp.mean(rows_in, axis=-1, keepdims=True)
    spread = jnp.mean(centred * centred, axis=-1, keepdims=True)
    return centred * lax.rsqrt(spread + EPSILON) * gain_col + shift_col


def smooth(values_in):
    return jax.nn.gelu(values_in, approximate=True)


def dot(a, b, ca, cb):
    return lax.dot_general(a, b, (((ca,), (cb,)), ((), ())), preferred_element_type=jnp.float32)


class Layout:
    def __init__(self, inputs, w_fc):
        self.micros, _, self.rows, self.width = inputs.shape
        self.sections = lax.axis_size("section")
        self.cores = lax.axis_size("dp")
        self.zs = lax.axis_size("z")
        self.rest = lax.axis_size("r")
        self.slab = self.sections * self.cores * self.rest
        self.shards = self.cores * self.zs * self.rest
        self.units = w_fc.shape[2]
        self.tokens = self.rows * self.slab
        self.seqs = self.cores
        self.head = self.width // HEADS
        self.slots = -(-HEADS // self.slab)
        self.block = self.width // self.shards
        self.unit_block = self.units // self.shards
        self.half = self.unit_block // self.sections
        self.cols = self.width // self.slab
        self.x = lax.axis_index("section")
        self.c = lax.axis_index("dp")
        self.z = lax.axis_index("z")
        self.r = lax.axis_index("r")
        self.t = (self.x * self.cores + self.c) * self.rest + self.r

    def number(self, x, c, z, r):
        return ((x * self.cores + c) * self.zs + z) * self.rest + r

    def order(self, a):
        lead = a.shape[:-1]
        a = a.reshape(*lead, self.cores, self.zs, self.rest * self.block)
        return jnp.swapaxes(a, -3, -2).reshape(*lead, self.width)

    def restore(self, a):
        lead = a.shape[:-1]
        a = a.reshape(*lead, self.zs, self.cores, self.rest * self.block)
        return jnp.swapaxes(a, -3, -2).reshape(*lead, self.width)

    def routes(self, micro):
        pairs = []
        for x in range(self.sections):
            for c in range(self.cores):
                for s in range(self.seqs):
                    for r in range(self.rest):
                        place = x * self.cores + c
                        pairs.append(((x, s, place, r), (x, c, micro * self.seqs + s, r)))
        return pairs

    def tokens_in(self, a):
        got = []
        for micro in range(self.micros):
            route = [(self.number(*f), self.number(*g)) for f, g in self.routes(micro)]
            got.append(lax.ppermute(a[micro, 0], ALL, route))
        out = got[0]
        for micro in range(1, self.micros):
            out = jnp.where(self.z // self.seqs == micro, got[micro], out)
        return out

    def tokens_out(self, parts):
        result = []
        for micro in range(self.micros):
            got = []
            for layer, part in enumerate(parts):
                route = [
                    (self.number(*g), self.number(layer, *f[1:])) for f, g in self.routes(micro)
                ]
                got.append(lax.ppermute(part, ALL, route))
            out = got[0]
            for layer in range(1, len(parts)):
                out = jnp.where(self.x == layer, got[layer], out)
            result.append(out)
        return jnp.stack(result)[None, :, None]


def slab_gather(a):
    return lax.all_gather(a, SLAB, axis=0, tiled=True)


def slab_sum(a, lay):
    parts = a.astype(jnp.bfloat16).reshape(lay.slab, lay.rows, a.shape[1])
    got = lax.all_to_all(parts, SLAB, 0, 0, tiled=True)
    return jnp.sum(got.astype(jnp.float32), axis=0)


def ring_sum(part, lay):
    ring = [(i, (i + 1) % lay.zs) for i in range(lay.zs)]

    def own(step):
        return lax.dynamic_index_in_dim(part, (lay.z - 1 - step) % lay.zs, 0, keepdims=False)

    acc = own(0).astype(jnp.bfloat16)
    for step in range(1, lay.zs):
        acc = lax.ppermute(acc, "z", ring)
        acc = (acc.astype(jnp.float32) + own(step).astype(jnp.float32)).astype(jnp.bfloat16)
    return acc


def spread_weights(lay, w_qkv, w_attn_out, w_fc, w_proj):
    n = lay.slab
    width, block = lay.width, lay.block
    slot_cols = lay.slots * lay.head
    qkv = w_qkv[0].reshape(block, 3, width)
    qkv = jnp.pad(qkv, ((0, 0), (0, 0), (0, n * slot_cols - width)))
    qkv = qkv.reshape(block, 3, n, slot_cols).transpose(2, 0, 1, 3).reshape(n, block, 3 * slot_cols)
    out = lay.order(w_attn_out[0]).reshape(block, n, lay.cols).transpose(1, 0, 2)
    fc = w_fc[0].reshape(block, lay.cores, lay.zs, lay.rest, lay.sections, lay.half)
    fc = fc.transpose(4, 1, 3, 0, 2, 5).reshape(n, block, lay.zs * lay.half)
    proj = lay.order(w_proj[0]).reshape(lay.sections, lay.half, width)

    def move(a):
        got = lax.all_to_all(a, SLAB, 0, 0, tiled=True)
        got = got.reshape(lay.sections, lay.cores * lay.rest * block, a.shape[2])
        return [got[layer] for layer in range(lay.sections)]

    qkv, out, fc = move(qkv), move(out), move(fc)
    proj = lax.all_to_all(proj, ("section",), 0, 0, tiled=True)
    params = []
    for layer in range(lay.sections):
        full = [
            lax.all_gather(a, "z", axis=0, tiled=True)
            for a in (qkv[layer], out[layer], fc[layer], proj[layer])
        ]
        wo = full[1].reshape(lay.zs, lay.cores, lay.rest * block, lay.cols)
        wo = jnp.swapaxes(wo, 0, 1).reshape(width, lay.cols)
        wo = jnp.pad(wo, ((0, n * slot_cols - width), (0, 0))).reshape(n, slot_cols, lay.cols)
        wo = lax.all_to_all(wo, SLAB, 0, 0, tiled=True)
        wo = wo.transpose(1, 0, 2).reshape(slot_cols, width)
        params.append((full[0], wo, full[2], full[3]))
    return params


def attend(q, k, v, places, lay):
    tokens = q.shape[0]
    scale = lay.head ** (-0.5)
    qh = q.reshape(tokens, lay.slots, lay.head)
    kh = k.reshape(tokens, lay.slots, lay.head)
    vh = v.reshape(tokens, lay.slots, lay.head)
    scores = jnp.einsum("qhd,nhd->hqn", qh, kh, preferred_element_type=jnp.float32) * scale
    allowed = (places[:, None] >= places[None, :])[None]
    scores = jnp.where(allowed, scores, -1e30)
    top = jnp.max(scores, axis=-1)
    weights = jnp.exp(scores - top[..., None])
    total = jnp.sum(weights, axis=-1)
    mixed = jnp.einsum(
        "hqn,nhd->hqd", weights.astype(jnp.bfloat16), vh, preferred_element_type=jnp.float32
    )
    mixed = (mixed / total[..., None]).transpose(1, 0, 2).reshape(tokens, -1)
    return mixed.astype(jnp.bfloat16), top + jnp.log(total)


def attend_back(q, k, v, g, logs, places, lay):
    tokens = q.shape[0]
    scale = lay.head ** (-0.5)
    qh = q.reshape(tokens, lay.slots, lay.head)
    kh = k.reshape(tokens, lay.slots, lay.head)
    vh = v.reshape(tokens, lay.slots, lay.head)
    gh = g.reshape(tokens, lay.slots, lay.head)
    scores = jnp.einsum("qhd,nhd->hqn", qh, kh, preferred_element_type=jnp.float32) * scale
    allowed = (places[:, None] >= places[None, :])[None]
    probs = jnp.where(allowed, jnp.exp(scores - logs[..., None]), 0.0)
    g_probs = jnp.einsum("qhd,nhd->hqn", gh, vh, preferred_element_type=jnp.float32)
    centre = jnp.sum(probs * g_probs, axis=-1, keepdims=True)
    g_scores = (probs * (g_probs - centre)).astype(jnp.bfloat16)
    gq = jnp.einsum("hqn,nhd->qhd", g_scores, kh, preferred_element_type=jnp.float32) * scale
    gk = jnp.einsum("hqn,qhd->nhd", g_scores, qh, preferred_element_type=jnp.float32) * scale
    gv = jnp.einsum(
        "hqn,qhd->nhd", probs.astype(jnp.bfloat16), gh, preferred_element_type=jnp.float32
    )
    return [a.reshape(tokens, -1).astype(jnp.bfloat16) for a in (gq, gk, gv)]


def forward(h, params, small, places, lay):
    w_qkv, w_out, w_fc, w_proj = params
    gains, shifts, q_bias, v_bias, unit_bias = small
    span = lay.slots * lay.head
    normed = slab_gather(normalize(h, gains[0], shifts[0]).astype(jnp.bfloat16))
    qkv = dot(normed, w_qkv, 1, 0)
    q = (qkv[:, :span] + q_bias).astype(jnp.bfloat16)
    k = qkv[:, span : 2 * span].astype(jnp.bfloat16)
    v = (qkv[:, 2 * span :] + v_bias).astype(jnp.bfloat16)
    attended, logs = attend(q, k, v, places, lay)
    mid = h + (slab_sum(dot(attended, w_out, 1, 0), lay) + shifts[3])
    normed_two = slab_gather(normalize(mid, gains[1], shifts[4]).astype(jnp.bfloat16))
    hidden = dot(normed_two, w_fc, 1, 0) + unit_bias
    activated = smooth(hidden).astype(jnp.bfloat16)
    result = mid + (slab_sum(dot(activated, w_proj, 1, 0), lay) + shifts[5])
    kept = (h, mid, normed, q, k, v, attended, logs, normed_two, hidden, activated)
    return result.astype(jnp.bfloat16), kept


def backward(g_rows, kept, params, small, places, lay):
    w_qkv, w_out, w_fc, w_proj = params
    gains, shifts, q_bias, v_bias, unit_bias = small
    h, mid, normed, q, k, v, attended, logs, normed_two, hidden, activated = kept
    branch_rows = g_rows.astype(jnp.bfloat16)
    branch = slab_gather(branch_rows)
    g_activated = dot(branch, w_proj, 1, 1)
    _, smooth_back = jax.vjp(smooth, hidden)
    g_hidden = smooth_back(g_activated)[0].astype(jnp.bfloat16)
    grad_proj = dot(activated, branch, 0, 0)
    g_normed_two = slab_sum(dot(g_hidden, w_fc, 1, 1), lay)
    grad_fc = dot(normed_two, g_hidden, 0, 0)
    _, second_back = jax.vjp(normalize, mid, gains[1], shifts[4])
    mid_part, gain_two, shift_two = second_back(g_normed_two)
    g_mid = g_rows + mid_part
    g_attn_rows = g_mid.astype(jnp.bfloat16)
    g_attn = slab_gather(g_attn_rows)
    g_attended = dot(g_attn, w_out, 1, 1).astype(jnp.bfloat16)
    grad_out = dot(attended, g_attn, 0, 0)
    gq, gk, gv = attend_back(q, k, v, g_attended, logs, places, lay)
    joint = jnp.concatenate([gq, gk, gv], axis=1)
    g_normed = slab_sum(dot(joint, w_qkv, 1, 1), lay)
    grad_qkv = dot(normed, joint, 0, 0)
    _, first_back = jax.vjp(normalize, h, gains[0], shifts[0])
    in_part, gain_one, shift_one = first_back(g_normed)
    g_in = g_mid + in_part

    def total(a):
        return jnp.sum(a.astype(jnp.float32), axis=0)

    local = (gain_one, gain_two, shift_one, total(g_attn_rows), shift_two, total(branch_rows))
    shard = (total(gq), total(gv), total(g_hidden))
    return g_in, (grad_qkv, grad_out, grad_fc, grad_proj), local, shard


def on_device(
    inputs, cotangent, positions, w_qkv, w_attn_out, w_fc, w_proj, norm_gains, biases, fc_bias
):
    lay = Layout(inputs, w_fc)
    n, block, width = lay.slab, lay.block, lay.width
    span = lay.slots * lay.head
    micro = lay.z // lay.seqs

    params = spread_weights(lay, w_qkv, w_attn_out, w_fc, w_proj)

    per_row = lay.unit_block // block
    thin = jnp.concatenate([norm_gains[0], biases[0], fc_bias[0].reshape(block, per_row)], axis=1)
    thin = lax.all_gather(thin, ALL, axis=0, tiled=True).astype(jnp.float32)
    thin = thin.reshape(lay.sections, width, 8 + per_row)
    smalls = []
    for layer in range(lay.sections):
        gains = [lay.order(thin[layer, :, i]) for i in range(2)]
        shifts = [lay.order(thin[layer, :, 2 + i]) for i in range(6)]
        heads = [
            lax.dynamic_slice_in_dim(
                jnp.pad(thin[layer, :, 2 + i], (0, n * span - width)), lay.t * span, span
            )
            for i in (1, 2)
        ]
        unit = thin[layer, :, 8:].reshape(lay.cores, lay.zs, lay.rest, lay.sections, lay.half)
        unit = unit.transpose(3, 0, 2, 1, 4).reshape(n, lay.zs * lay.half)
        unit = lax.dynamic_index_in_dim(unit, lay.t, 0, keepdims=False)
        smalls.append((gains, shifts, heads[0], heads[1], unit))

    places = lax.all_gather(positions, ("z", "r"), axis=1, tiled=True)
    places = lax.dynamic_index_in_dim(places, micro, 0, keepdims=False)

    h = lay.order(lay.tokens_in(inputs))
    g = lay.order(lay.tokens_in(cotangent))

    outs, keeps = [], []
    for layer in range(lay.sections):
        h, kept = forward(h.astype(jnp.float32), params[layer], smalls[layer], places, lay)
        outs.append(h)
        keeps.append(kept)

    grads = [None] * lay.sections
    grad_rows = [None] * lay.sections
    locals_, shards = [None] * lay.sections, [None] * lay.sections
    for layer in reversed(range(lay.sections)):
        g, grads[layer], locals_[layer], shards[layer] = backward(
            g.astype(jnp.float32), keeps[layer], params[layer], smalls[layer], places, lay
        )
        g = g.astype(jnp.bfloat16)
        grad_rows[layer] = g

    section_out = lay.tokens_out([lay.restore(a) for a in outs])
    section_grad = lay.tokens_out([lay.restore(a) for a in grad_rows])

    def by_z(a):
        return a.reshape(lay.zs, a.shape[0] // lay.zs, a.shape[1])

    sums = []
    for layer in range(lay.sections):
        grad_qkv, grad_out, grad_fc, grad_proj = grads[layer]
        wo = grad_out.astype(jnp.bfloat16).reshape(span, n, lay.cols).transpose(1, 0, 2)
        wo = lax.all_to_all(wo, SLAB, 0, 0, tiled=True).reshape(n * span, lay.cols)[:width]
        wo = wo.reshape(lay.cores, lay.zs, lay.rest * block, lay.cols)
        wo = jnp.swapaxes(wo, 0, 1).reshape(width, lay.cols)
        sums.append([ring_sum(by_z(a), lay) for a in (grad_qkv, wo, grad_fc, grad_proj)])

    def back(i):
        both = jnp.stack([sums[layer][i] for layer in range(lay.sections)])
        return lax.all_to_all(
            both.reshape(n, block, both.shape[2]), SLAB, 0, 0, tiled=True
        )

    got = back(0).reshape(n, block, 3, span).transpose(1, 2, 0, 3).reshape(block, 3, n * span)
    out_qkv = got[:, :, :width].reshape(block, 3 * width).astype(jnp.float32)
    got = back(1).transpose(1, 0, 2).reshape(block, width)
    out_attn = lay.restore(got).astype(jnp.float32)
    got = back(2).reshape(lay.sections, lay.cores, lay.rest, block, lay.zs, lay.half)
    out_fc = got.transpose(3, 1, 4, 2, 0, 5).reshape(block, lay.units).astype(jnp.float32)
    both = jnp.stack([sums[layer][3] for layer in range(lay.sections)])
    got = lax.all_to_all(both, ("section",), 0, 0, tiled=True)
    out_proj = lay.restore(got.reshape(lay.unit_block, width)).astype(jnp.float32)

    rows = []
    for layer in range(lay.sections):
        gain_one, gain_two, shift_one, s_attn, shift_two, s_branch = [
            lay.restore(a) for a in locals_[layer]
        ]
        gq, gv, units = shards[layer]
        zero = jnp.zeros((n * span,), jnp.float32)
        s_q = lax.dynamic_update_slice_in_dim(zero, gq, lay.t * span, 0)[:width]
        s_v = lax.dynamic_update_slice_in_dim(zero, gv, lay.t * span, 0)[:width]
        cols = [gain_one, gain_two, shift_one, s_q, s_v, s_attn, shift_two, s_branch]
        cols = jnp.stack(cols, axis=1).reshape(lay.shards, block * 8)
        spots = jnp.zeros((n, lay.zs, lay.half), jnp.float32)
        spots = lax.dynamic_update_index_in_dim(
            spots, units.reshape(lay.zs, lay.half), lay.t, 0
        )
        spots = spots.reshape(lay.sections, lay.cores, lay.rest, lay.zs, lay.half)
        spots = spots.transpose(1, 3, 2, 0, 4).reshape(lay.shards, lay.unit_block)
        rows.append(jnp.concatenate([cols, spots], axis=1))
    rows = jnp.concatenate(rows, axis=0)
    rows = jnp.sum(lax.all_to_all(rows, ALL, 0, 0, tiled=True), axis=0)
    cols = rows[: block * 8].reshape(block, 8)
    return (
        section_out,
        section_grad,
        out_qkv[None],
        out_attn[None],
        out_fc[None],
        out_proj[None],
        cols[None, :, :2],
        cols[None, :, 2:],
        rows[None, block * 8 :],
    )


def solution(mesh):
    sections, cores, contexts = (mesh.shape[a] for a in ("section", "dp", "ctx"))
    zs = sections * cores
    shape = (sections, cores, zs, contexts // zs)
    inner = Mesh(mesh.devices.reshape(shape), ALL)
    tokens = P(None, "dp", ("z", "r"), None)
    rows = P("section", ("dp", "z", "r"), None)
    units = P("section", ("dp", "z", "r"))
    out_tokens = P("section", None, "dp", ("z", "r"), None)
    return jax.shard_map(
        on_device,
        mesh=inner,
        in_specs=(tokens, tokens, P(None, ("z", "r"))) + (rows,) * 6 + (units,),
        out_specs=(out_tokens, out_tokens) + (rows,) * 6 + (units,),
        check_vma=False,
    )
```

```python
import jax
import jax.numpy as jnp
from jax import lax
from jax.experimental import pallas as pl
from jax.experimental.pallas import tpu as pltpu
from jax.sharding import Mesh
from jax.sharding import PartitionSpec as P

HEADS = 25
EPSILON = 1e-05

SLAB = ("section", "dp", "r")
ALL = ("section", "dp", "z", "r")
MESH = pl.DeviceIdType.MESH


def normalize(rows_in, gain_col, shift_col):
    centred = rows_in - jnp.mean(rows_in, axis=-1, keepdims=True)
    spread = jnp.mean(centred * centred, axis=-1, keepdims=True)
    return centred * lax.rsqrt(spread + EPSILON) * gain_col + shift_col


def smooth(values_in):
    return jax.nn.gelu(values_in, approximate=True)


def dot(a, b, ca, cb):
    return lax.dot_general(a, b, (((ca,), (cb,)), ((), ())), preferred_element_type=jnp.float32)


class Layout:
    def __init__(self, inputs, w_fc):
        self.micros, _, self.rows, self.width = inputs.shape
        self.sections = lax.axis_size("section")
        self.cores = lax.axis_size("dp")
        self.zs = lax.axis_size("z")
        self.rest = lax.axis_size("r")
        self.slab = self.sections * self.cores * self.rest
        self.shards = self.cores * self.zs * self.rest
        self.units = w_fc.shape[2]
        self.tokens = self.rows * self.slab
        self.seqs = self.cores
        self.head = self.width // HEADS
        self.slots = -(-HEADS // self.slab)
        self.block = self.width // self.shards
        self.unit_block = self.units // self.shards
        self.half = self.unit_block // self.sections
        self.cols = self.width // self.slab
        self.x = lax.axis_index("section")
        self.c = lax.axis_index("dp")
        self.z = lax.axis_index("z")
        self.r = lax.axis_index("r")
        self.t = (self.x * self.cores + self.c) * self.rest + self.r

    def number(self, x, c, z, r):
        return ((x * self.cores + c) * self.zs + z) * self.rest + r

    def order(self, a):
        lead = a.shape[:-1]
        a = a.reshape(*lead, self.cores, self.zs, self.rest * self.block)
        return jnp.swapaxes(a, -3, -2).reshape(*lead, self.width)

    def restore(self, a):
        lead = a.shape[:-1]
        a = a.reshape(*lead, self.zs, self.cores, self.rest * self.block)
        return jnp.swapaxes(a, -3, -2).reshape(*lead, self.width)

    def routes(self, micro):
        pairs = []
        for x in range(self.sections):
            for c in range(self.cores):
                for s in range(self.seqs):
                    for r in range(self.rest):
                        place = x * self.cores + c
                        pairs.append(((x, s, place, r), (x, c, micro * self.seqs + s, r)))
        return pairs

    def tokens_in(self, a):
        got = []
        for micro in range(self.micros):
            route = [(self.number(*f), self.number(*g)) for f, g in self.routes(micro)]
            got.append(lax.ppermute(a[micro, 0], ALL, route))
        out = got[0]
        for micro in range(1, self.micros):
            out = jnp.where(self.z // self.seqs == micro, got[micro], out)
        return out

    def tokens_out(self, parts):
        result = []
        for micro in range(self.micros):
            got = []
            for layer, part in enumerate(parts):
                route = [
                    (self.number(*g), self.number(layer, *f[1:])) for f, g in self.routes(micro)
                ]
                got.append(lax.ppermute(part, ALL, route))
            out = got[0]
            for layer in range(1, len(parts)):
                out = jnp.where(self.x == layer, got[layer], out)
            result.append(out)
        return jnp.stack(result)[None, :, None]


class Peers:
    def __init__(self):
        self.sections, self.rest = lax.axis_size("section"), lax.axis_size("r")
        self.chips = self.sections * self.rest
        self.x, self.c, self.r = (lax.axis_index(a) for a in ("section", "dp", "r"))
        self.chip = self.x * self.rest + self.r

    def ahead(self, k):
        return lax.rem(self.chip + k, self.chips)

    def behind(self, k):
        return lax.rem(self.chip + self.chips - k, self.chips)

    def device(self, chip, core):
        return {"section": chip // self.rest, "dp": core, "r": lax.rem(chip, self.rest)}

    def slot(self, chip, core):
        return (chip // self.rest * 2 + core) * self.rest + lax.rem(chip, self.rest)

    def greet(self):
        barrier = pltpu.get_barrier_semaphore()
        for k in range(1, self.chips):
            pl.semaphore_signal(barrier, inc=1, device_id=self.device(self.ahead(k), self.c), device_id_type=MESH)
        pl.semaphore_signal(barrier, inc=1, device_id=self.device(self.chip, 1 - self.c), device_id_type=MESH)
        pl.semaphore_wait(barrier, self.chips)


def remote(src, dst, send, recv, device):
    return pltpu.make_async_remote_copy(src_ref=src, dst_ref=dst, send_sem=send, recv_sem=recv, device_id=device, device_id_type=MESH)


def gather_steps(peers, src, out, local, chip_send, chip_recv, core_send, core_recv):
    me, c = peers.slot(peers.chip, peers.c), peers.c
    sibling = peers.device(peers.chip, 1 - c)
    sent = []
    for k in range(1, peers.chips):
        copy = remote(src, out.at[me], chip_send.at[k], chip_recv.at[k], peers.device(peers.ahead(k), c))
        copy.start()
        sent.append(copy)
    copy = remote(src, out.at[me], core_send.at[0], core_recv.at[0], sibling)
    copy.start()
    sent.append(copy)
    own = pltpu.make_async_copy(src, out.at[me], local)
    own.start()
    for k in range(1, peers.chips):
        block = out.at[peers.slot(peers.behind(k), c)]
        remote(block, block, chip_send.at[k], chip_recv.at[k], sibling).wait_recv()
        copy = remote(block, block, core_send.at[k], core_recv.at[k], sibling)
        copy.start()
        sent.append(copy)
    for k in range(peers.chips):
        block = out.at[peers.slot(peers.behind(k), 1 - c)]
        remote(block, block, core_send.at[k], core_recv.at[k], sibling).wait_recv()
    for copy in sent:
        copy.wait_send()
    own.wait()


def gather_kernel(src, out, local, chip_send, chip_recv, core_send, core_recv):
    peers = Peers()
    peers.greet()
    gather_steps(peers, src, out, local, chip_send, chip_recv, core_send, core_recv)


def slab_gather(a, name=1):
    chips = lax.axis_size("section") * lax.axis_size("r")
    sems = pltpu.SemaphoreType.DMA((chips,))
    out = pl.pallas_call(
        gather_kernel,
        out_shape=jax.ShapeDtypeStruct((2 * chips, *a.shape), a.dtype),
        in_specs=[pl.BlockSpec(memory_space=pl.ANY)],
        out_specs=pl.BlockSpec(memory_space=pl.ANY),
        scratch_shapes=[pltpu.SemaphoreType.DMA] + [sems] * 4,
        compiler_params=pltpu.CompilerParams(collective_id=name, has_side_effects=True),
    )(a)
    return out.reshape(2 * chips * a.shape[0], a.shape[1])


def sum_steps(peers, part, mine, other, out, going, coming, local, chip_send, chip_recv, core_send, core_recv):
    c = peers.c
    sibling = peers.device(peers.chip, 1 - c)
    sent = []
    order = [k for k in range(1, peers.chips)] + [0]
    for k in order:
        chip = peers.ahead(k)
        copy = remote(part.at[peers.slot(chip, 1 - c)], other.at[k], core_send.at[k], core_recv.at[k], sibling)
        copy.start()
        sent.append(copy)
        pltpu.make_async_copy(part.at[peers.slot(chip, c)], mine.at[k], local.at[k]).start()
    for k in order:
        chip = peers.ahead(k)
        remote(mine.at[k], other.at[k], core_send.at[k], core_recv.at[k], sibling).wait_recv()
        pltpu.make_async_copy(part.at[peers.slot(chip, c)], mine.at[k], local.at[k]).wait()
        if k:
            going[k - 1] = (mine[k].astype(jnp.float32) + other[k].astype(jnp.float32)).astype(going.dtype)
            copy = remote(going.at[k - 1], coming.at[k - 1], chip_send.at[k], chip_recv.at[k], peers.device(chip, c))
            copy.start()
            sent.append(copy)
    out[...] = mine[0].astype(jnp.float32) + other[0].astype(jnp.float32)
    for k in range(1, peers.chips):
        remote(going.at[k - 1], coming.at[k - 1], chip_send.at[k], chip_recv.at[k], sibling).wait_recv()
        out[...] += coming[k - 1].astype(jnp.float32)
    for copy in sent:
        copy.wait_send()


def sum_scratch(chips, rows, width):
    return [
        pltpu.VMEM((chips, rows, width), jnp.bfloat16),
        pltpu.VMEM((chips, rows, width), jnp.bfloat16),
        pltpu.VMEM((chips - 1, rows, width), jnp.bfloat16),
        pltpu.VMEM((chips - 1, rows, width), jnp.bfloat16),
    ] + [pltpu.SemaphoreType.DMA((chips,))] * 5


def sum_kernel(part, out, mine, other, going, coming, local, chip_send, chip_recv, core_send, core_recv):
    peers = Peers()
    peers.greet()
    sum_steps(peers, part, mine, other, out, going, coming, local, chip_send, chip_recv, core_send, core_recv)


def slab_sum(a, name=2):
    chips = lax.axis_size("section") * lax.axis_size("r")
    rows, width = a.shape[0] // (2 * chips), a.shape[1]
    return pl.pallas_call(
        sum_kernel,
        out_shape=jax.ShapeDtypeStruct((rows, width), jnp.float32),
        in_specs=[pl.BlockSpec(memory_space=pl.ANY)],
        out_specs=pl.BlockSpec(memory_space=pltpu.VMEM),
        scratch_shapes=sum_scratch(chips, rows, width),
        compiler_params=pltpu.CompilerParams(collective_id=name, has_side_effects=True, vmem_limit_bytes=40 * 2**20),
    )(a.astype(jnp.bfloat16).reshape(2 * chips, rows, width))


def ring_sum(part, lay):
    ring = [(i, (i + 1) % lay.zs) for i in range(lay.zs)]

    def own(step):
        return lax.dynamic_index_in_dim(part, (lay.z - 1 - step) % lay.zs, 0, keepdims=False)

    acc = own(0).astype(jnp.bfloat16)
    for step in range(1, lay.zs):
        acc = lax.ppermute(acc, "z", ring)
        acc = (acc.astype(jnp.float32) + own(step).astype(jnp.float32)).astype(jnp.bfloat16)
    return acc


def spread_weights(lay, w_qkv, w_attn_out, w_fc, w_proj):
    n = lay.slab
    width, block = lay.width, lay.block
    slot_cols = lay.slots * lay.head
    qkv = w_qkv[0].reshape(block, 3, width)
    qkv = jnp.pad(qkv, ((0, 0), (0, 0), (0, n * slot_cols - width)))
    qkv = qkv.reshape(block, 3, n, slot_cols).transpose(2, 0, 1, 3).reshape(n, block, 3 * slot_cols)
    out = lay.order(w_attn_out[0]).reshape(block, n, lay.cols).transpose(1, 0, 2)
    fc = w_fc[0].reshape(block, lay.cores, lay.zs, lay.rest, lay.sections, lay.half)
    fc = fc.transpose(4, 1, 3, 0, 2, 5).reshape(n, block, lay.zs * lay.half)
    proj = lay.order(w_proj[0]).reshape(lay.sections, lay.half, width)

    def move(a):
        got = lax.all_to_all(a, SLAB, 0, 0, tiled=True)
        got = got.reshape(lay.sections, lay.cores * lay.rest * block, a.shape[2])
        return [got[layer] for layer in range(lay.sections)]

    qkv, out, fc = move(qkv), move(out), move(fc)
    proj = lax.all_to_all(proj, ("section",), 0, 0, tiled=True)
    params = []
    for layer in range(lay.sections):
        full = [
            lax.all_gather(a, "z", axis=0, tiled=True)
            for a in (qkv[layer], out[layer], fc[layer], proj[layer])
        ]
        wo = full[1].reshape(lay.zs, lay.cores, lay.rest * block, lay.cols)
        wo = jnp.swapaxes(wo, 0, 1).reshape(width, lay.cols)
        wo = jnp.pad(wo, ((0, n * slot_cols - width), (0, 0))).reshape(n, slot_cols, lay.cols)
        wo = lax.all_to_all(wo, SLAB, 0, 0, tiled=True)
        wo = wo.transpose(1, 0, 2).reshape(slot_cols, width)
        params.append((full[0], wo, full[2], full[3]))
    return params


def attend(q, k, v, places, lay):
    tokens = q.shape[0]
    scale = lay.head ** (-0.5)
    qh = q.reshape(tokens, lay.slots, lay.head)
    kh = k.reshape(tokens, lay.slots, lay.head)
    vh = v.reshape(tokens, lay.slots, lay.head)
    scores = jnp.einsum("qhd,nhd->hqn", qh, kh, preferred_element_type=jnp.float32) * scale
    allowed = (places[:, None] >= places[None, :])[None]
    scores = jnp.where(allowed, scores, -1e30)
    top = jnp.max(scores, axis=-1)
    weights = jnp.exp(scores - top[..., None])
    total = jnp.sum(weights, axis=-1)
    mixed = jnp.einsum(
        "hqn,nhd->hqd", weights.astype(jnp.bfloat16), vh, preferred_element_type=jnp.float32
    )
    mixed = (mixed / total[..., None]).transpose(1, 0, 2).reshape(tokens, -1)
    return mixed.astype(jnp.bfloat16), top + jnp.log(total)


def attend_back(q, k, v, g, logs, places, lay):
    tokens = q.shape[0]
    scale = lay.head ** (-0.5)
    qh = q.reshape(tokens, lay.slots, lay.head)
    kh = k.reshape(tokens, lay.slots, lay.head)
    vh = v.reshape(tokens, lay.slots, lay.head)
    gh = g.reshape(tokens, lay.slots, lay.head)
    scores = jnp.einsum("qhd,nhd->hqn", qh, kh, preferred_element_type=jnp.float32) * scale
    allowed = (places[:, None] >= places[None, :])[None]
    probs = jnp.where(allowed, jnp.exp(scores - logs[..., None]), 0.0)
    g_probs = jnp.einsum("qhd,nhd->hqn", gh, vh, preferred_element_type=jnp.float32)
    centre = jnp.sum(probs * g_probs, axis=-1, keepdims=True)
    g_scores = (probs * (g_probs - centre)).astype(jnp.bfloat16)
    gq = jnp.einsum("hqn,nhd->qhd", g_scores, kh, preferred_element_type=jnp.float32) * scale
    gk = jnp.einsum("hqn,qhd->nhd", g_scores, qh, preferred_element_type=jnp.float32) * scale
    gv = jnp.einsum(
        "hqn,qhd->nhd", probs.astype(jnp.bfloat16), gh, preferred_element_type=jnp.float32
    )
    return [a.reshape(tokens, -1).astype(jnp.bfloat16) for a in (gq, gk, gv)]


def forward(h, params, small, places, lay):
    w_qkv, w_out, w_fc, w_proj = params
    gains, shifts, q_bias, v_bias, unit_bias = small
    span = lay.slots * lay.head
    normed = slab_gather(normalize(h, gains[0], shifts[0]).astype(jnp.bfloat16))
    qkv = dot(normed, w_qkv, 1, 0)
    q = (qkv[:, :span] + q_bias).astype(jnp.bfloat16)
    k = qkv[:, span : 2 * span].astype(jnp.bfloat16)
    v = (qkv[:, 2 * span :] + v_bias).astype(jnp.bfloat16)
    attended, logs = attend(q, k, v, places, lay)
    mid = h + (slab_sum(dot(attended, w_out, 1, 0)) + shifts[3])
    normed_two = slab_gather(normalize(mid, gains[1], shifts[4]).astype(jnp.bfloat16))
    hidden = dot(normed_two, w_fc, 1, 0) + unit_bias
    activated = smooth(hidden).astype(jnp.bfloat16)
    result = mid + (slab_sum(dot(activated, w_proj, 1, 0)) + shifts[5])
    kept = (h, mid, normed, q, k, v, attended, logs, normed_two, hidden, activated)
    return result.astype(jnp.bfloat16), kept


def backward(g_rows, kept, params, small, places, lay):
    w_qkv, w_out, w_fc, w_proj = params
    gains, shifts, q_bias, v_bias, unit_bias = small
    h, mid, normed, q, k, v, attended, logs, normed_two, hidden, activated = kept
    branch_rows = g_rows.astype(jnp.bfloat16)
    branch = slab_gather(branch_rows)
    g_activated = dot(branch, w_proj, 1, 1)
    _, smooth_back = jax.vjp(smooth, hidden)
    g_hidden = smooth_back(g_activated)[0].astype(jnp.bfloat16)
    grad_proj = dot(activated, branch, 0, 0)
    g_normed_two = slab_sum(dot(g_hidden, w_fc, 1, 1))
    grad_fc = dot(normed_two, g_hidden, 0, 0)
    _, second_back = jax.vjp(normalize, mid, gains[1], shifts[4])
    mid_part, gain_two, shift_two = second_back(g_normed_two)
    g_mid = g_rows + mid_part
    g_attn_rows = g_mid.astype(jnp.bfloat16)
    g_attn = slab_gather(g_attn_rows)
    g_attended = dot(g_attn, w_out, 1, 1).astype(jnp.bfloat16)
    grad_out = dot(attended, g_attn, 0, 0)
    gq, gk, gv = attend_back(q, k, v, g_attended, logs, places, lay)
    joint = jnp.concatenate([gq, gk, gv], axis=1)
    g_normed = slab_sum(dot(joint, w_qkv, 1, 1))
    grad_qkv = dot(normed, joint, 0, 0)
    _, first_back = jax.vjp(normalize, h, gains[0], shifts[0])
    in_part, gain_one, shift_one = first_back(g_normed)
    g_in = g_mid + in_part

    def total(a):
        return jnp.sum(a.astype(jnp.float32), axis=0)

    local = (gain_one, gain_two, shift_one, total(g_attn_rows), shift_two, total(branch_rows))
    shard = (total(gq), total(gv), total(g_hidden))
    return g_in, (grad_qkv, grad_out, grad_fc, grad_proj), local, shard


def on_device(
    inputs, cotangent, positions, w_qkv, w_attn_out, w_fc, w_proj, norm_gains, biases, fc_bias
):
    lay = Layout(inputs, w_fc)
    n, block, width = lay.slab, lay.block, lay.width
    span = lay.slots * lay.head
    micro = lay.z // lay.seqs

    params = spread_weights(lay, w_qkv, w_attn_out, w_fc, w_proj)

    per_row = lay.unit_block // block
    thin = jnp.concatenate([norm_gains[0], biases[0], fc_bias[0].reshape(block, per_row)], axis=1)
    thin = lax.all_gather(thin, ALL, axis=0, tiled=True).astype(jnp.float32)
    thin = thin.reshape(lay.sections, width, 8 + per_row)
    smalls = []
    for layer in range(lay.sections):
        gains = [lay.order(thin[layer, :, i]) for i in range(2)]
        shifts = [lay.order(thin[layer, :, 2 + i]) for i in range(6)]
        heads = [
            lax.dynamic_slice_in_dim(
                jnp.pad(thin[layer, :, 2 + i], (0, n * span - width)), lay.t * span, span
            )
            for i in (1, 2)
        ]
        unit = thin[layer, :, 8:].reshape(lay.cores, lay.zs, lay.rest, lay.sections, lay.half)
        unit = unit.transpose(3, 0, 2, 1, 4).reshape(n, lay.zs * lay.half)
        unit = lax.dynamic_index_in_dim(unit, lay.t, 0, keepdims=False)
        smalls.append((gains, shifts, heads[0], heads[1], unit))

    places = lax.all_gather(positions, ("z", "r"), axis=1, tiled=True)
    places = lax.dynamic_index_in_dim(places, micro, 0, keepdims=False)

    h = lay.order(lay.tokens_in(inputs))
    g = lay.order(lay.tokens_in(cotangent))

    outs, keeps = [], []
    for layer in range(lay.sections):
        h, kept = forward(h.astype(jnp.float32), params[layer], smalls[layer], places, lay)
        outs.append(h)
        keeps.append(kept)

    grads = [None] * lay.sections
    grad_rows = [None] * lay.sections
    locals_, shards = [None] * lay.sections, [None] * lay.sections
    for layer in reversed(range(lay.sections)):
        g, grads[layer], locals_[layer], shards[layer] = backward(
            g.astype(jnp.float32), keeps[layer], params[layer], smalls[layer], places, lay
        )
        g = g.astype(jnp.bfloat16)
        grad_rows[layer] = g

    section_out = lay.tokens_out([lay.restore(a) for a in outs])
    section_grad = lay.tokens_out([lay.restore(a) for a in grad_rows])

    def by_z(a):
        return a.reshape(lay.zs, a.shape[0] // lay.zs, a.shape[1])

    sums = []
    for layer in range(lay.sections):
        grad_qkv, grad_out, grad_fc, grad_proj = grads[layer]
        wo = grad_out.astype(jnp.bfloat16).reshape(span, n, lay.cols).transpose(1, 0, 2)
        wo = lax.all_to_all(wo, SLAB, 0, 0, tiled=True).reshape(n * span, lay.cols)[:width]
        wo = wo.reshape(lay.cores, lay.zs, lay.rest * block, lay.cols)
        wo = jnp.swapaxes(wo, 0, 1).reshape(width, lay.cols)
        sums.append([ring_sum(by_z(a), lay) for a in (grad_qkv, wo, grad_fc, grad_proj)])

    def back(i):
        both = jnp.stack([sums[layer][i] for layer in range(lay.sections)])
        return lax.all_to_all(
            both.reshape(n, block, both.shape[2]), SLAB, 0, 0, tiled=True
        )

    got = back(0).reshape(n, block, 3, span).transpose(1, 2, 0, 3).reshape(block, 3, n * span)
    out_qkv = got[:, :, :width].reshape(block, 3 * width).astype(jnp.float32)
    got = back(1).transpose(1, 0, 2).reshape(block, width)
    out_attn = lay.restore(got).astype(jnp.float32)
    got = back(2).reshape(lay.sections, lay.cores, lay.rest, block, lay.zs, lay.half)
    out_fc = got.transpose(3, 1, 4, 2, 0, 5).reshape(block, lay.units).astype(jnp.float32)
    both = jnp.stack([sums[layer][3] for layer in range(lay.sections)])
    got = lax.all_to_all(both, ("section",), 0, 0, tiled=True)
    out_proj = lay.restore(got.reshape(lay.unit_block, width)).astype(jnp.float32)

    rows = []
    for layer in range(lay.sections):
        gain_one, gain_two, shift_one, s_attn, shift_two, s_branch = [
            lay.restore(a) for a in locals_[layer]
        ]
        gq, gv, units = shards[layer]
        zero = jnp.zeros((n * span,), jnp.float32)
        s_q = lax.dynamic_update_slice_in_dim(zero, gq, lay.t * span, 0)[:width]
        s_v = lax.dynamic_update_slice_in_dim(zero, gv, lay.t * span, 0)[:width]
        cols = [gain_one, gain_two, shift_one, s_q, s_v, s_attn, shift_two, s_branch]
        cols = jnp.stack(cols, axis=1).reshape(lay.shards, block * 8)
        spots = jnp.zeros((n, lay.zs, lay.half), jnp.float32)
        spots = lax.dynamic_update_index_in_dim(
            spots, units.reshape(lay.zs, lay.half), lay.t, 0
        )
        spots = spots.reshape(lay.sections, lay.cores, lay.rest, lay.zs, lay.half)
        spots = spots.transpose(1, 3, 2, 0, 4).reshape(lay.shards, lay.unit_block)
        rows.append(jnp.concatenate([cols, spots], axis=1))
    rows = jnp.concatenate(rows, axis=0)
    rows = jnp.sum(lax.all_to_all(rows, ALL, 0, 0, tiled=True), axis=0)
    cols = rows[: block * 8].reshape(block, 8)
    return (
        section_out,
        section_grad,
        out_qkv[None],
        out_attn[None],
        out_fc[None],
        out_proj[None],
        cols[None, :, :2],
        cols[None, :, 2:],
        rows[None, block * 8 :],
    )


def solution(mesh):
    sections, cores, contexts = (mesh.shape[a] for a in ("section", "dp", "ctx"))
    zs = sections * cores
    shape = (sections, cores, zs, contexts // zs)
    inner = Mesh(mesh.devices.reshape(shape), ALL)
    tokens = P(None, "dp", ("z", "r"), None)
    rows = P("section", ("dp", "z", "r"), None)
    units = P("section", ("dp", "z", "r"))
    out_tokens = P("section", None, "dp", ("z", "r"), None)
    return jax.shard_map(
        on_device,
        mesh=inner,
        in_specs=(tokens, tokens, P(None, ("z", "r"))) + (rows,) * 6 + (units,),
        out_specs=(out_tokens, out_tokens) + (rows,) * 6 + (units,),
        check_vma=False,
    )
```

```python
import functools

import jax
import jax.numpy as jnp
from jax import lax
from jax.experimental import pallas as pl
from jax.experimental.pallas import tpu as pltpu
from jax.sharding import Mesh
from jax.sharding import PartitionSpec as P

HEADS = 25
EPSILON = 1e-05

SLAB = ("section", "dp", "r")
ALL = ("section", "dp", "z", "r")
MESH = pl.DeviceIdType.MESH


def normalize(rows_in, gain_col, shift_col):
    centred = rows_in - jnp.mean(rows_in, axis=-1, keepdims=True)
    spread = jnp.mean(centred * centred, axis=-1, keepdims=True)
    return centred * lax.rsqrt(spread + EPSILON) * gain_col + shift_col


def smooth(values_in):
    return jax.nn.gelu(values_in, approximate=True)


def dot(a, b, ca, cb):
    return lax.dot_general(a, b, (((ca,), (cb,)), ((), ())), preferred_element_type=jnp.float32)


class Layout:
    def __init__(self, inputs, w_fc):
        self.micros, _, self.rows, self.width = inputs.shape
        self.sections = lax.axis_size("section")
        self.cores = lax.axis_size("dp")
        self.zs = lax.axis_size("z")
        self.rest = lax.axis_size("r")
        self.slab = self.sections * self.cores * self.rest
        self.shards = self.cores * self.zs * self.rest
        self.units = w_fc.shape[2]
        self.tokens = self.rows * self.slab
        self.seqs = self.cores
        self.head = self.width // HEADS
        self.slots = -(-HEADS // self.slab)
        self.block = self.width // self.shards
        self.unit_block = self.units // self.shards
        self.half = self.unit_block // self.sections
        self.cols = self.width // self.slab
        self.x = lax.axis_index("section")
        self.c = lax.axis_index("dp")
        self.z = lax.axis_index("z")
        self.r = lax.axis_index("r")
        self.t = (self.x * self.cores + self.c) * self.rest + self.r

    def number(self, x, c, z, r):
        return ((x * self.cores + c) * self.zs + z) * self.rest + r

    def order(self, a):
        lead = a.shape[:-1]
        a = a.reshape(*lead, self.cores, self.zs, self.rest * self.block)
        return jnp.swapaxes(a, -3, -2).reshape(*lead, self.width)

    def restore(self, a):
        lead = a.shape[:-1]
        a = a.reshape(*lead, self.zs, self.cores, self.rest * self.block)
        return jnp.swapaxes(a, -3, -2).reshape(*lead, self.width)

    def routes(self, micro):
        pairs = []
        for x in range(self.sections):
            for c in range(self.cores):
                for s in range(self.seqs):
                    for r in range(self.rest):
                        place = x * self.cores + c
                        pairs.append(((x, s, place, r), (x, c, micro * self.seqs + s, r)))
        return pairs

    def tokens_in(self, a):
        got = []
        for micro in range(self.micros):
            route = [(self.number(*f), self.number(*g)) for f, g in self.routes(micro)]
            got.append(lax.ppermute(a[micro, 0], ALL, route))
        out = got[0]
        for micro in range(1, self.micros):
            out = jnp.where(self.z // self.seqs == micro, got[micro], out)
        return out

    def tokens_out(self, parts):
        result = []
        for micro in range(self.micros):
            got = []
            for layer, part in enumerate(parts):
                route = [
                    (self.number(*g), self.number(layer, *f[1:])) for f, g in self.routes(micro)
                ]
                got.append(lax.ppermute(part, ALL, route))
            out = got[0]
            for layer in range(1, len(parts)):
                out = jnp.where(self.x == layer, got[layer], out)
            result.append(out)
        return jnp.stack(result)[None, :, None]


class Peers:
    def __init__(self):
        self.sections, self.rest = lax.axis_size("section"), lax.axis_size("r")
        self.chips = self.sections * self.rest
        self.x, self.c, self.r = (lax.axis_index(a) for a in ("section", "dp", "r"))
        self.chip = self.x * self.rest + self.r

    def ahead(self, k):
        return lax.rem(self.chip + k, self.chips)

    def behind(self, k):
        return lax.rem(self.chip + self.chips - k, self.chips)

    def device(self, chip, core):
        return {"section": chip // self.rest, "dp": core, "r": lax.rem(chip, self.rest)}

    def slot(self, chip, core):
        return (chip // self.rest * 2 + core) * self.rest + lax.rem(chip, self.rest)

    def greet(self, zs=1):
        barrier = pltpu.get_barrier_semaphore()
        z = lax.axis_index("z")
        for k in range(1, zs):
            pl.semaphore_signal(barrier, inc=1, device_id={"z": lax.rem(z + k, zs)}, device_id_type=MESH)
        for k in range(1, self.chips):
            pl.semaphore_signal(barrier, inc=1, device_id=self.device(self.ahead(k), self.c), device_id_type=MESH)
        pl.semaphore_signal(barrier, inc=1, device_id=self.device(self.chip, 1 - self.c), device_id_type=MESH)
        pl.semaphore_wait(barrier, self.chips + zs - 1)


def remote(src, dst, send, recv, device):
    return pltpu.make_async_remote_copy(src_ref=src, dst_ref=dst, send_sem=send, recv_sem=recv, device_id=device, device_id_type=MESH)


def gather_steps(peers, src, out, local, chip_send, chip_recv, core_send, core_recv):
    me, c = peers.slot(peers.chip, peers.c), peers.c
    sibling = peers.device(peers.chip, 1 - c)
    sent = []
    for k in range(1, peers.chips):
        copy = remote(src, out.at[me], chip_send.at[k], chip_recv.at[k], peers.device(peers.ahead(k), c))
        copy.start()
        sent.append(copy)
    copy = remote(src, out.at[me], core_send.at[0], core_recv.at[0], sibling)
    copy.start()
    sent.append(copy)
    own = pltpu.make_async_copy(src, out.at[me], local)
    own.start()
    for k in range(1, peers.chips):
        block = out.at[peers.slot(peers.behind(k), c)]
        remote(block, block, chip_send.at[k], chip_recv.at[k], sibling).wait_recv()
        copy = remote(block, block, core_send.at[k], core_recv.at[k], sibling)
        copy.start()
        sent.append(copy)
    for k in range(peers.chips):
        block = out.at[peers.slot(peers.behind(k), 1 - c)]
        remote(block, block, core_send.at[k], core_recv.at[k], sibling).wait_recv()
    for copy in sent:
        copy.wait_send()
    own.wait()


def gather_kernel(ties, src, *rest):
    out, local, chip_send, chip_recv, core_send, core_recv = rest[ties:]
    peers = Peers()
    peers.greet()
    gather_steps(peers, src, out, local, chip_send, chip_recv, core_send, core_recv)


def slab_gather(a, ties, name):
    chips = lax.axis_size("section") * lax.axis_size("r")
    sems = pltpu.SemaphoreType.DMA((chips,))
    out = pl.pallas_call(
        functools.partial(gather_kernel, len(ties)),
        out_shape=jax.ShapeDtypeStruct((2 * chips, *a.shape), a.dtype),
        in_specs=[pl.BlockSpec(memory_space=pl.ANY)] * (1 + len(ties)),
        out_specs=pl.BlockSpec(memory_space=pl.ANY),
        scratch_shapes=[pltpu.SemaphoreType.DMA] + [sems] * 4,
        compiler_params=pltpu.CompilerParams(collective_id=name, has_side_effects=True),
    )(a, *ties)
    return out.reshape(2 * chips * a.shape[0], a.shape[1])


def tiny_kernel(src, out, stage, local, z_send, z_recv, chip_send, chip_recv, core_send, core_recv):
    peers = Peers()
    zs, z = lax.axis_size("z"), lax.axis_index("z")
    peers.greet(zs)
    sent = []
    for k in range(1, zs):
        copy = remote(src, stage.at[z], z_send.at[k], z_recv.at[k], {"z": lax.rem(z + k, zs)})
        copy.start()
        sent.append(copy)
    stage[z] = src[...]
    for k in range(1, zs):
        block = stage.at[lax.rem(z + zs - k, zs)]
        remote(block, block, z_send.at[k], z_recv.at[k], {"z": lax.rem(z + k, zs)}).wait_recv()
    gather_steps(peers, stage, out, local, chip_send, chip_recv, core_send, core_recv)
    for copy in sent:
        copy.wait_send()


def tiny_gather(a, name=0):
    sections, rest, zs = (lax.axis_size(i) for i in ("section", "r", "z"))
    chips = sections * rest
    sems = pltpu.SemaphoreType.DMA((chips,))
    vmem = pl.BlockSpec(memory_space=pltpu.VMEM)
    out = pl.pallas_call(
        tiny_kernel,
        out_shape=jax.ShapeDtypeStruct((2 * chips, zs, *a.shape), a.dtype),
        in_specs=[vmem],
        out_specs=vmem,
        scratch_shapes=[pltpu.VMEM((zs, *a.shape), a.dtype), pltpu.SemaphoreType.DMA]
        + [pltpu.SemaphoreType.DMA((zs,))] * 2
        + [sems] * 4,
        compiler_params=pltpu.CompilerParams(collective_id=name, has_side_effects=True),
    )(a)
    return out.reshape(sections, 2, rest, zs, *a.shape)


def sum_steps(peers, part, mine, other, out, going, coming, local, chip_send, chip_recv, core_send, core_recv):
    c = peers.c
    sibling = peers.device(peers.chip, 1 - c)
    sent = []
    order = [k for k in range(1, peers.chips)] + [0]
    for k in order:
        chip = peers.ahead(k)
        copy = remote(part.at[peers.slot(chip, 1 - c)], other.at[k], core_send.at[k], core_recv.at[k], sibling)
        copy.start()
        sent.append(copy)
        pltpu.make_async_copy(part.at[peers.slot(chip, c)], mine.at[k], local.at[k]).start()
    for k in order:
        chip = peers.ahead(k)
        remote(mine.at[k], other.at[k], core_send.at[k], core_recv.at[k], sibling).wait_recv()
        pltpu.make_async_copy(part.at[peers.slot(chip, c)], mine.at[k], local.at[k]).wait()
        if k:
            going[k - 1] = (mine[k].astype(jnp.float32) + other[k].astype(jnp.float32)).astype(going.dtype)
            copy = remote(going.at[k - 1], coming.at[k - 1], chip_send.at[k], chip_recv.at[k], peers.device(chip, c))
            copy.start()
            sent.append(copy)
    out[...] = mine[0].astype(jnp.float32) + other[0].astype(jnp.float32)
    for k in range(1, peers.chips):
        remote(going.at[k - 1], coming.at[k - 1], chip_send.at[k], chip_recv.at[k], sibling).wait_recv()
        out[...] += coming[k - 1].astype(jnp.float32)
    for copy in sent:
        copy.wait_send()


def sum_scratch(chips, rows, width):
    return [
        pltpu.VMEM((chips, rows, width), jnp.bfloat16),
        pltpu.VMEM((chips, rows, width), jnp.bfloat16),
        pltpu.VMEM((chips - 1, rows, width), jnp.bfloat16),
        pltpu.VMEM((chips - 1, rows, width), jnp.bfloat16),
    ] + [pltpu.SemaphoreType.DMA((chips,))] * 5


def sum_kernel(ties, part, *rest):
    out, mine, other, going, coming, local, chip_send, chip_recv, core_send, core_recv = rest[ties:]
    peers = Peers()
    peers.greet()
    sum_steps(peers, part, mine, other, out, going, coming, local, chip_send, chip_recv, core_send, core_recv)


def slab_sum(a, ties, name):
    chips = lax.axis_size("section") * lax.axis_size("r")
    rows, width = a.shape[0] // (2 * chips), a.shape[1]
    return pl.pallas_call(
        functools.partial(sum_kernel, len(ties)),
        out_shape=jax.ShapeDtypeStruct((rows, width), jnp.float32),
        in_specs=[pl.BlockSpec(memory_space=pl.ANY)] * (1 + len(ties)),
        out_specs=pl.BlockSpec(memory_space=pltpu.VMEM),
        scratch_shapes=sum_scratch(chips, rows, width),
        compiler_params=pltpu.CompilerParams(collective_id=name, has_side_effects=True, vmem_limit_bytes=40 * 2**20),
    )(a.astype(jnp.bfloat16).reshape(2 * chips, rows, width), *ties)


class Rings:
    def __init__(self, lay):
        self.lay = lay
        self.live = []

    def own(self, part, step):
        lay = self.lay
        block = lax.dynamic_index_in_dim(part, (lay.z - 1 - step) % lay.zs, 0, keepdims=False)
        return block.astype(jnp.float32)

    def add(self, term):
        zs = self.lay.zs
        part = term.reshape(zs, term.shape[0] // zs, term.shape[1])
        ring = [self.own(part, 0).astype(jnp.bfloat16), part, 0]
        self.live.append(ring)
        return ring

    def step(self):
        zs = self.lay.zs
        self.live = [ring for ring in self.live if ring[2] < zs - 1]
        route = [(i, (i + 1) % zs) for i in range(zs)]
        for ring in self.live:
            got = lax.ppermute(ring[0], "z", route).astype(jnp.float32)
            ring[2] += 1
            ring[0] = (got + self.own(ring[1], ring[2])).astype(jnp.bfloat16)

    def ties(self):
        now = [ring[0] for ring in self.live]
        self.step()
        return now

    def finish(self):
        while any(ring[2] < self.lay.zs - 1 for ring in self.live):
            self.step()


def spread_weights(lay, w_qkv, w_attn_out, w_fc, w_proj):
    n = lay.slab
    width, block = lay.width, lay.block
    slot_cols = lay.slots * lay.head
    qkv = w_qkv[0].reshape(block, 3, width)
    qkv = jnp.pad(qkv, ((0, 0), (0, 0), (0, n * slot_cols - width)))
    qkv = qkv.reshape(block, 3, n, slot_cols).transpose(2, 0, 1, 3).reshape(n, block, 3 * slot_cols)
    out = lay.order(w_attn_out[0]).reshape(block, n, lay.cols).transpose(1, 0, 2)
    fc = w_fc[0].reshape(block, lay.cores, lay.zs, lay.rest, lay.sections, lay.half)
    fc = fc.transpose(4, 1, 3, 0, 2, 5).reshape(n, block, lay.zs * lay.half)
    proj = lay.order(w_proj[0]).reshape(lay.sections, lay.half, width)

    def move(a):
        got = lax.all_to_all(a, SLAB, 0, 0, tiled=True)
        got = got.reshape(lay.sections, lay.cores * lay.rest * block, a.shape[2])
        return [got[layer] for layer in range(lay.sections)]

    first = move(jnp.concatenate([qkv, out], axis=2))
    fc = move(fc)
    proj = lax.all_to_all(proj, ("section",), 0, 0, tiled=True)
    params = []
    for layer in range(lay.sections):
        full = [
            lax.all_gather(a, "z", axis=0, tiled=True) for a in (first[layer], fc[layer], proj[layer])
        ]
        wo = full[0][:, 3 * slot_cols :]
        wo = wo.reshape(lay.zs, lay.cores, lay.rest * block, lay.cols)
        wo = jnp.swapaxes(wo, 0, 1).reshape(width, lay.cols)
        wo = jnp.pad(wo, ((0, n * slot_cols - width), (0, 0))).reshape(n, slot_cols, lay.cols)
        wo = lax.all_to_all(wo, SLAB, 0, 0, tiled=True)
        wo = wo.transpose(1, 0, 2).reshape(slot_cols, width)
        params.append((full[0][:, : 3 * slot_cols], wo, full[1], full[2]))
    return params


def attend(q, k, v, places, lay):
    tokens = q.shape[0]
    scale = lay.head ** (-0.5)
    qh = q.reshape(tokens, lay.slots, lay.head)
    kh = k.reshape(tokens, lay.slots, lay.head)
    vh = v.reshape(tokens, lay.slots, lay.head)
    scores = jnp.einsum("qhd,nhd->hqn", qh, kh, preferred_element_type=jnp.float32) * scale
    allowed = (places[:, None] >= places[None, :])[None]
    scores = jnp.where(allowed, scores, -1e30)
    top = jnp.max(scores, axis=-1)
    weights = jnp.exp(scores - top[..., None])
    total = jnp.sum(weights, axis=-1)
    mixed = jnp.einsum(
        "hqn,nhd->hqd", weights.astype(jnp.bfloat16), vh, preferred_element_type=jnp.float32
    )
    mixed = (mixed / total[..., None]).transpose(1, 0, 2).reshape(tokens, -1)
    return mixed.astype(jnp.bfloat16), top + jnp.log(total)


def attend_back(q, k, v, g, logs, places, lay):
    tokens = q.shape[0]
    scale = lay.head ** (-0.5)
    qh = q.reshape(tokens, lay.slots, lay.head)
    kh = k.reshape(tokens, lay.slots, lay.head)
    vh = v.reshape(tokens, lay.slots, lay.head)
    gh = g.reshape(tokens, lay.slots, lay.head)
    scores = jnp.einsum("qhd,nhd->hqn", qh, kh, preferred_element_type=jnp.float32) * scale
    allowed = (places[:, None] >= places[None, :])[None]
    probs = jnp.where(allowed, jnp.exp(scores - logs[..., None]), 0.0)
    g_probs = jnp.einsum("qhd,nhd->hqn", gh, vh, preferred_element_type=jnp.float32)
    centre = jnp.sum(probs * g_probs, axis=-1, keepdims=True)
    g_scores = (probs * (g_probs - centre)).astype(jnp.bfloat16)
    gq = jnp.einsum("hqn,nhd->qhd", g_scores, kh, preferred_element_type=jnp.float32) * scale
    gk = jnp.einsum("hqn,qhd->nhd", g_scores, qh, preferred_element_type=jnp.float32) * scale
    gv = jnp.einsum(
        "hqn,qhd->nhd", probs.astype(jnp.bfloat16), gh, preferred_element_type=jnp.float32
    )
    return [a.reshape(tokens, -1).astype(jnp.bfloat16) for a in (gq, gk, gv)]


def forward(h, params, small, places, lay, name):
    w_qkv, w_out, w_fc, w_proj = params
    gains, shifts, q_bias, v_bias, unit_bias = small
    span = lay.slots * lay.head
    normed = slab_gather(normalize(h, gains[0], shifts[0]).astype(jnp.bfloat16), (), name)
    qkv = dot(normed, w_qkv, 1, 0)
    q = (qkv[:, :span] + q_bias).astype(jnp.bfloat16)
    k = qkv[:, span : 2 * span].astype(jnp.bfloat16)
    v = (qkv[:, 2 * span :] + v_bias).astype(jnp.bfloat16)
    attended, logs = attend(q, k, v, places, lay)
    mid = h + (slab_sum(dot(attended, w_out, 1, 0), (), name + 1) + shifts[3])
    normed_two = slab_gather(normalize(mid, gains[1], shifts[4]).astype(jnp.bfloat16), (), name + 2)
    hidden = dot(normed_two, w_fc, 1, 0) + unit_bias
    activated = smooth(hidden).astype(jnp.bfloat16)
    result = mid + (slab_sum(dot(activated, w_proj, 1, 0), (), name + 3) + shifts[5])
    kept = (h, mid, normed, q, k, v, attended, logs, normed_two, hidden, activated)
    return result.astype(jnp.bfloat16), kept


def backward(g_rows, branch, kept, params, small, places, lay, rings, name):
    w_qkv, w_out, w_fc, w_proj = params
    gains, shifts, q_bias, v_bias, unit_bias = small
    h, mid, normed, q, k, v, attended, logs, normed_two, hidden, activated = kept
    branch_rows = g_rows.astype(jnp.bfloat16)
    if branch is None:
        branch = slab_gather(branch_rows, rings.ties(), name)
    g_activated = dot(branch, w_proj, 1, 1)
    _, smooth_back = jax.vjp(smooth, hidden)
    g_hidden = smooth_back(g_activated)[0].astype(jnp.bfloat16)
    grad_proj = rings.add(dot(activated, branch, 0, 0))
    g_normed_two = slab_sum(dot(g_hidden, w_fc, 1, 1), rings.ties(), name + 1)
    grad_fc = rings.add(dot(normed_two, g_hidden, 0, 0))
    _, second_back = jax.vjp(normalize, mid, gains[1], shifts[4])
    mid_part, gain_two, shift_two = second_back(g_normed_two)
    g_mid = g_rows + mid_part
    g_attn_rows = g_mid.astype(jnp.bfloat16)
    g_attn = slab_gather(g_attn_rows, rings.ties(), name + 2)
    g_attended = dot(g_attn, w_out, 1, 1).astype(jnp.bfloat16)
    n, span, block, width = lay.slab, lay.slots * lay.head, lay.block, lay.width
    wo = dot(attended, g_attn, 0, 0).astype(jnp.bfloat16).reshape(span, n, lay.cols)
    wo = lax.all_to_all(wo.transpose(1, 0, 2), SLAB, 0, 0, tiled=True)
    wo = wo.reshape(n * span, lay.cols)[:width].reshape(lay.cores, lay.zs, lay.rest * block, lay.cols)
    wo = jnp.swapaxes(wo, 0, 1).reshape(width, lay.cols)
    gq, gk, gv = attend_back(q, k, v, g_attended, logs, places, lay)
    joint = jnp.concatenate([gq, gk, gv], axis=1)
    g_normed = slab_sum(dot(joint, w_qkv, 1, 1), rings.ties(), name + 3)
    grad_qkv = rings.add(jnp.concatenate([dot(normed, joint, 0, 0), wo.astype(jnp.float32)], axis=1))
    _, first_back = jax.vjp(normalize, h, gains[0], shifts[0])
    in_part, gain_one, shift_one = first_back(g_normed)
    g_in = g_mid + in_part

    def total(a):
        return jnp.sum(a.astype(jnp.float32), axis=0)

    local = (gain_one, gain_two, shift_one, total(g_attn_rows), shift_two, total(branch_rows))
    shard = (total(gq), total(gv), total(g_hidden))
    return g_in, (grad_qkv, grad_fc, grad_proj), local, shard


def on_device(
    inputs, cotangent, positions, w_qkv, w_attn_out, w_fc, w_proj, norm_gains, biases, fc_bias
):
    lay = Layout(inputs, w_fc)
    n, block, width = lay.slab, lay.block, lay.width
    span = lay.slots * lay.head
    micro = lay.z // lay.seqs

    params = spread_weights(lay, w_qkv, w_attn_out, w_fc, w_proj)

    per_row = lay.unit_block // block
    thin = jnp.concatenate([norm_gains[0], biases[0], fc_bias[0].reshape(block, per_row)], axis=1)
    thin = jnp.concatenate([thin.reshape(-1).astype(jnp.float32), positions.reshape(-1).astype(jnp.float32)])
    used, spots = block * (8 + per_row), positions.size
    thin = jnp.pad(thin, (0, -thin.size % 1024)).reshape(-1, 128)
    thin = tiny_gather(thin).reshape(lay.sections, lay.cores, lay.rest, lay.zs, -1)
    places = thin[0, 0, :, :, used : used + spots].astype(jnp.int32)
    places = places.reshape(lay.rest, lay.zs, lay.micros, lay.rows).transpose(2, 1, 0, 3)
    places = places.reshape(lay.micros, lay.tokens)
    places = lax.dynamic_index_in_dim(places, micro, 0, keepdims=False)
    thin = jnp.swapaxes(thin[..., :used], 2, 3).reshape(lay.sections, width, 8 + per_row)
    smalls = []
    for layer in range(lay.sections):
        gains = [lay.order(thin[layer, :, i]) for i in range(2)]
        shifts = [lay.order(thin[layer, :, 2 + i]) for i in range(6)]
        heads = [
            lax.dynamic_slice_in_dim(
                jnp.pad(thin[layer, :, 2 + i], (0, n * span - width)), lay.t * span, span
            )
            for i in (1, 2)
        ]
        unit = thin[layer, :, 8:].reshape(lay.cores, lay.zs, lay.rest, lay.sections, lay.half)
        unit = unit.transpose(3, 0, 2, 1, 4).reshape(n, lay.zs * lay.half)
        unit = lax.dynamic_index_in_dim(unit, lay.t, 0, keepdims=False)
        smalls.append((gains, shifts, heads[0], heads[1], unit))

    h = lay.order(lay.tokens_in(inputs))
    g = lay.order(lay.tokens_in(cotangent))

    outs, keeps = [], []
    for layer in range(lay.sections):
        h, kept = forward(h.astype(jnp.float32), params[layer], smalls[layer], places, lay, 1 + 4 * layer)
        outs.append(h)
        keeps.append(kept)

    grads = [None] * lay.sections
    grad_rows = [None] * lay.sections
    locals_, shards = [None] * lay.sections, [None] * lay.sections
    rings = Rings(lay)
    first_name = 1 + 4 * lay.sections
    branch = slab_gather(g, (), first_name)
    for layer in reversed(range(lay.sections)):
        g, grads[layer], locals_[layer], shards[layer] = backward(
            g.astype(jnp.float32),
            branch,
            keeps[layer],
            params[layer],
            smalls[layer],
            places,
            lay,
            rings,
            first_name + 1 + 4 * layer,
        )
        g, branch = g.astype(jnp.bfloat16), None
        grad_rows[layer] = g
    rings.finish()

    section_out = lay.tokens_out([lay.restore(a) for a in outs])
    section_grad = lay.tokens_out([lay.restore(a) for a in grad_rows])

    def back(i):
        both = jnp.stack([grads[layer][i][0] for layer in range(lay.sections)])
        return lax.all_to_all(both.reshape(n, block, both.shape[2]), SLAB, 0, 0, tiled=True)

    first = back(0)
    got = first[:, :, : 3 * span].reshape(n, block, 3, span).transpose(1, 2, 0, 3)
    out_qkv = got.reshape(block, 3, n * span)[:, :, :width].reshape(block, 3 * width).astype(jnp.float32)
    got = first[:, :, 3 * span :].transpose(1, 0, 2).reshape(block, width)
    out_attn = lay.restore(got).astype(jnp.float32)
    got = back(1).reshape(lay.sections, lay.cores, lay.rest, block, lay.zs, lay.half)
    out_fc = got.transpose(3, 1, 4, 2, 0, 5).reshape(block, lay.units).astype(jnp.float32)
    both = jnp.stack([grads[layer][2][0] for layer in range(lay.sections)])
    got = lax.all_to_all(both, ("section",), 0, 0, tiled=True)
    out_proj = lay.restore(got.reshape(lay.unit_block, width)).astype(jnp.float32)

    rows = []
    for layer in range(lay.sections):
        gain_one, gain_two, shift_one, s_attn, shift_two, s_branch = [
            lay.restore(a) for a in locals_[layer]
        ]
        gq, gv, units = shards[layer]
        zero = jnp.zeros((n * span,), jnp.float32)
        s_q = lax.dynamic_update_slice_in_dim(zero, gq, lay.t * span, 0)[:width]
        s_v = lax.dynamic_update_slice_in_dim(zero, gv, lay.t * span, 0)[:width]
        cols = [gain_one, gain_two, shift_one, s_q, s_v, s_attn, shift_two, s_branch]
        cols = jnp.stack(cols, axis=1).reshape(lay.shards, block * 8)
        spots = jnp.zeros((n, lay.zs, lay.half), jnp.float32)
        spots = lax.dynamic_update_index_in_dim(
            spots, units.reshape(lay.zs, lay.half), lay.t, 0
        )
        spots = spots.reshape(lay.sections, lay.cores, lay.rest, lay.zs, lay.half)
        spots = spots.transpose(1, 3, 2, 0, 4).reshape(lay.shards, lay.unit_block)
        rows.append(jnp.concatenate([cols, spots], axis=1))
    rows = jnp.concatenate(rows, axis=0)
    rows = jnp.sum(lax.all_to_all(rows, ALL, 0, 0, tiled=True), axis=0)
    cols = rows[: block * 8].reshape(block, 8)
    return (
        section_out,
        section_grad,
        out_qkv[None],
        out_attn[None],
        out_fc[None],
        out_proj[None],
        cols[None, :, :2],
        cols[None, :, 2:],
        rows[None, block * 8 :],
    )


def solution(mesh):
    sections, cores, contexts = (mesh.shape[a] for a in ("section", "dp", "ctx"))
    zs = sections * cores
    shape = (sections, cores, zs, contexts // zs)
    inner = Mesh(mesh.devices.reshape(shape), ALL)
    tokens = P(None, "dp", ("z", "r"), None)
    rows = P("section", ("dp", "z", "r"), None)
    units = P("section", ("dp", "z", "r"))
    out_tokens = P("section", None, "dp", ("z", "r"), None)
    return jax.shard_map(
        on_device,
        mesh=inner,
        in_specs=(tokens, tokens, P(None, ("z", "r"))) + (rows,) * 6 + (units,),
        out_specs=(out_tokens, out_tokens) + (rows,) * 6 + (units,),
        check_vma=False,
    )
```

```python
import functools

import jax
import jax.numpy as jnp
from jax import lax
from jax.experimental import pallas as pl
from jax.experimental.pallas import tpu as pltpu
from jax.sharding import Mesh
from jax.sharding import PartitionSpec as P

HEADS = 25
EPSILON = 1e-05

SLAB = ("section", "dp", "r")
ALL = ("section", "dp", "z", "r")
MESH = pl.DeviceIdType.MESH


class Layout:
    def __init__(self, inputs, w_fc):
        self.micros, _, self.rows, self.width = inputs.shape
        self.sections = lax.axis_size("section")
        self.cores = lax.axis_size("dp")
        self.zs = lax.axis_size("z")
        self.rest = lax.axis_size("r")
        self.slab = self.sections * self.cores * self.rest
        self.shards = self.cores * self.zs * self.rest
        self.units = w_fc.shape[2]
        self.tokens = self.rows * self.slab
        self.seqs = self.cores
        self.head = self.width // HEADS
        self.slots = -(-HEADS // self.slab)
        self.block = self.width // self.shards
        self.unit_block = self.units // self.shards
        self.half = self.unit_block // self.sections
        self.cols = self.width // self.slab
        self.x = lax.axis_index("section")
        self.c = lax.axis_index("dp")
        self.z = lax.axis_index("z")
        self.r = lax.axis_index("r")
        self.t = (self.x * self.cores + self.c) * self.rest + self.r

    def number(self, x, c, z, r):
        return ((x * self.cores + c) * self.zs + z) * self.rest + r

    def order(self, a):
        lead = a.shape[:-1]
        a = a.reshape(*lead, self.cores, self.zs, self.rest * self.block)
        return jnp.swapaxes(a, -3, -2).reshape(*lead, self.width)

    def restore(self, a):
        lead = a.shape[:-1]
        a = a.reshape(*lead, self.zs, self.cores, self.rest * self.block)
        return jnp.swapaxes(a, -3, -2).reshape(*lead, self.width)

    def routes(self, micro):
        pairs = []
        for x in range(self.sections):
            for c in range(self.cores):
                for s in range(self.seqs):
                    for r in range(self.rest):
                        place = x * self.cores + c
                        pairs.append(((x, s, place, r), (x, c, micro * self.seqs + s, r)))
        return pairs

    def tokens_in(self, a):
        got = []
        for micro in range(self.micros):
            route = [(self.number(*f), self.number(*g)) for f, g in self.routes(micro)]
            got.append(lax.ppermute(a[micro, 0], ALL, route))
        out = got[0]
        for micro in range(1, self.micros):
            out = jnp.where(self.z // self.seqs == micro, got[micro], out)
        return out

    def tokens_out(self, parts):
        result = []
        for micro in range(self.micros):
            got = []
            for layer, part in enumerate(parts):
                route = [
                    (self.number(*g), self.number(layer, *f[1:])) for f, g in self.routes(micro)
                ]
                got.append(lax.ppermute(part, ALL, route))
            out = got[0]
            for layer in range(1, len(parts)):
                out = jnp.where(self.x == layer, got[layer], out)
            result.append(out)
        return jnp.stack(result)[None, :, None]


LOW = -1e30
BF = jnp.bfloat16
F32 = jnp.float32


class Peers:
    def __init__(self):
        self.sections, self.rest = lax.axis_size("section"), lax.axis_size("r")
        self.chips = self.sections * self.rest
        self.x, self.c, self.r = (lax.axis_index(a) for a in ("section", "dp", "r"))
        self.chip = self.x * self.rest + self.r

    def away(self, k, sign):
        x = lax.rem(self.x + self.sections + sign * (k // self.rest), self.sections)
        r = lax.rem(self.r + self.rest + sign * (k % self.rest), self.rest)
        return x, r

    def ahead(self, k):
        x, r = self.away(k, 1)
        return {"section": x, "dp": self.c, "r": r}

    def behind(self, k):
        x, r = self.away(k, -1)
        return {"section": x, "dp": self.c, "r": r}

    def sibling(self):
        return {"section": self.x, "dp": 1 - self.c, "r": self.r}

    def behind_chip(self, k):
        x, r = self.away(k, -1)
        return x * self.rest + r

    def greet(self, zs=1):
        barrier = pltpu.get_barrier_semaphore()
        z = lax.axis_index("z")
        for k in range(1, zs):
            pl.semaphore_signal(barrier, inc=1, device_id={"z": lax.rem(z + k, zs)}, device_id_type=MESH)
        for k in range(1, self.chips):
            pl.semaphore_signal(barrier, inc=1, device_id=self.ahead(k), device_id_type=MESH)
        pl.semaphore_signal(barrier, inc=1, device_id=self.sibling(), device_id_type=MESH)
        pl.semaphore_wait(barrier, self.chips + zs - 1)


def remote(src, dst, send, recv, device):
    return pltpu.make_async_remote_copy(
        src_ref=src, dst_ref=dst, send_sem=send, recv_sem=recv, device_id=device, device_id_type=MESH
    )


class Gather:
    def __init__(self, peers, full, sems):
        self.peers, self.full = peers, full
        self.chip_send, self.chip_recv, self.core_send, self.core_recv = sems
        self.sent = []

    def start(self, src):
        p = self.peers
        mine = self.full.at[p.chip, p.c]
        mine[...] = src[...]
        for k in range(1, p.chips):
            self.send(remote(mine, mine, self.chip_send.at[k], self.chip_recv.at[k], p.ahead(k)))
        self.send(remote(mine, mine, self.core_send.at[0], self.core_recv.at[0], p.sibling()))

    def send(self, copy):
        copy.start()
        self.sent.append(copy)

    def forward(self, k):
        p = self.peers
        block = self.full.at[p.behind_chip(k), p.c]
        remote(block, block, self.chip_send.at[k], self.chip_recv.at[k], p.sibling()).wait_recv()
        self.send(remote(block, block, self.core_send.at[k], self.core_recv.at[k], p.sibling()))

    def chip(self, k):
        p = self.peers
        block = self.full.at[p.behind_chip(k), 1 - p.c]
        remote(block, block, self.core_send.at[k], self.core_recv.at[k], p.sibling()).wait_recv()
        return p.behind_chip(k)

    def arrivals(self):
        yield 0, self.chip(0)
        chips = self.peers.chips
        for k in range(1, chips):
            for later in (1, 2) if k == 1 else (k + 1,):
                if later < chips:
                    self.forward(later)
            yield k, self.chip(k)

    def finish(self):
        for copy in self.sent:
            copy.wait_send()


class Reduce:
    def __init__(self, peers, mine, stage, other, going, coming, sems):
        self.peers = peers
        self.mine, self.stage, self.other, self.going, self.coming = mine, stage, other, going, coming
        self.chip_send, self.chip_recv, self.core_send, self.core_recv = sems
        self.sent = []

    def send(self, copy):
        copy.start()
        self.sent.append(copy)

    def put(self, k, both):
        p = self.peers
        rows = both.shape[0] // 2
        low, high = both[:rows], both[rows:]
        first = p.c == 0
        self.mine[k] = jnp.where(first, low, high)
        self.stage[k] = jnp.where(first, high, low).astype(BF)
        self.send(remote(self.stage.at[k], self.other.at[k], self.core_send.at[k], self.core_recv.at[k], p.sibling()))

    def arrived(self, k):
        p = self.peers
        remote(self.stage.at[k], self.other.at[k], self.core_send.at[k], self.core_recv.at[k], p.sibling()).wait_recv()
        return self.mine[k] + self.other[k].astype(F32)

    def push(self, k):
        p = self.peers
        if k:
            self.going[k - 1] = self.arrived(k).astype(BF)
            self.send(remote(self.going.at[k - 1], self.coming.at[k - 1], self.chip_send.at[k], self.chip_recv.at[k], p.behind(k)))

    def total(self):
        p = self.peers
        out = self.arrived(0)
        for k in range(1, p.chips):
            remote(self.going.at[k - 1], self.coming.at[k - 1], self.chip_send.at[k], self.chip_recv.at[k], p.sibling()).wait_recv()
            out = out + self.coming[k - 1].astype(F32)
        return out

    def finish(self):
        for copy in self.sent:
            copy.wait_send()


def gather_scratch(chips, rows, width):
    return [pltpu.VMEM((chips, 2, rows, width), BF)] + [pltpu.SemaphoreType.DMA((chips,))] * 4


def reduce_scratch(chips, rows, width):
    return [
        pltpu.VMEM((chips, rows, width), F32),
        pltpu.VMEM((chips, rows, width), BF),
        pltpu.VMEM((chips, rows, width), BF),
        pltpu.VMEM((chips - 1, rows, width), BF),
        pltpu.VMEM((chips - 1, rows, width), BF),
    ] + [pltpu.SemaphoreType.DMA((chips,))] * 4


def norm_parts(v):
    centred = v - jnp.mean(v, axis=-1, keepdims=True)
    spread = jnp.mean(centred * centred, axis=-1, keepdims=True)
    scale = lax.rsqrt(spread + EPSILON)
    return centred * scale, scale


def norm_back(v, gain, grad):
    unit, scale = norm_parts(v)
    scaled = grad * gain
    part = scaled - jnp.mean(scaled, axis=-1, keepdims=True)
    part = part - unit * jnp.mean(scaled * unit, axis=-1, keepdims=True)
    return part * scale, jnp.sum(grad * unit, axis=0, keepdims=True), jnp.sum(grad, axis=0, keepdims=True)


def dot(a, b, ca=1, cb=0):
    return lax.dot_general(a, b, (((ca,), (cb,)), ((), ())), preferred_element_type=F32)


def chip_rows(chip, rows):
    return pl.ds(pl.multiple_of(chip * (2 * rows), 2 * rows), 2 * rows)


def groups(span, head):
    wide = 128 if span % 128 == 0 else span
    for g in range(span // wide):
        yield slice(g * wide, (g + 1) * wide), [(g * wide // head + i, i * head) for i in range(wide // head)]


def only(a, start, head):
    lane = lax.broadcasted_iota(jnp.int32, a.shape, 1)
    return jnp.where((lane >= start) & (lane < start + head), a, jnp.zeros_like(a))


def attention_forward(head, ties, *refs):
    (src, h, w_qkv, w_out, bias, col, row, vec) = refs[:8]
    refs = refs[8 + ties :]
    (normed, qkv, attended, logs, mid, normed_two), refs = refs[:6], refs[6:]
    gather_refs, reduce_refs = refs[:5], refs[5:]
    rows, width = src.shape
    span = w_out.shape[0]
    peers = Peers()
    gather = Gather(peers, gather_refs[0], gather_refs[1:])
    reduce = Reduce(peers, *reduce_refs[:5], reduce_refs[5:9])
    kept_sem = reduce_refs[9]
    full = gather.full
    peers.greet()
    gather.start(src)
    for k, chip in gather.arrivals():
        part = dot(full[chip].reshape(2 * rows, width), w_qkv[...]) + bias[...]
        qkv[chip_rows(chip, rows), :] = part.astype(BF)
    kept = pltpu.make_async_copy(full, normed, kept_sem)
    kept.start()
    scale = head ** (-0.5)
    order = list(range(1, peers.chips)) + [0]
    before = None
    for k in order:
        chip = peers.behind_chip(k)
        here = chip_rows(chip, rows)
        block = jnp.where(col[...] <= row[:, here], 0.0, LOW).astype(F32)
        for lanes, heads in groups(span, head):
            q = qkv[here, lanes]
            keys = qkv[:, slice(span + lanes.start, span + lanes.stop)]
            values = qkv[:, slice(2 * span + lanes.start, 2 * span + lanes.stop)]
            merged = None
            for slot, start in heads:
                scores = dot(keys, only(q, start, head) * scale, 1, 1) + block
                top = jnp.max(scores, axis=0, keepdims=True)
                weights = jnp.exp(scores - top)
                total = jnp.sum(weights, axis=0, keepdims=True)
                logs[slot : slot + 1, here] = top + jnp.log(total)
                mixed = dot(values, weights.astype(BF), 0, 0) / total
                lane = lax.broadcasted_iota(jnp.int32, mixed.shape, 0)
                merged = mixed if merged is None else jnp.where(lane >= start, mixed, merged)
            attended[here, lanes] = merged.T.astype(BF)
        reduce.put(k, dot(attended[here, :], w_out[...]))
        if before is not None:
            reduce.push(before)
        before = k
    reduce.push(before)
    out = h[...].astype(F32) + (reduce.total() + vec[4:5, :])
    mid[...] = out
    normed_two[...] = (norm_parts(out)[0] * vec[1:2, :] + vec[3:4, :]).astype(BF)
    gather.finish()
    reduce.finish()
    kept.wait()


ROOT = 0.7978845608028654


def feed_forward(ties, *refs):
    (src, mid, w_fc, w_proj, bias, vec, next_vec) = refs[:7]
    refs = refs[7 + ties :]
    (normed_two, slope, activated, result, normed), refs = refs[:5], refs[5:]
    gather_refs, reduce_refs = refs[:5], refs[5:]
    rows, width = src.shape
    peers = Peers()
    gather = Gather(peers, gather_refs[0], gather_refs[1:])
    reduce = Reduce(peers, *reduce_refs[:5], reduce_refs[5:9])
    kept_sem = reduce_refs[9]
    full = gather.full
    peers.greet()
    gather.start(src)
    before = None
    for k, chip in gather.arrivals():
        here = chip_rows(chip, rows)
        u = dot(full[chip].reshape(2 * rows, width), w_fc[...]) + bias[...]
        bend = jnp.tanh(ROOT * (u + 0.044715 * (u * u * u)))
        slope[here, :] = (0.5 * (1.0 + bend) + 0.5 * u * (1.0 - bend * bend) * (ROOT * (1.0 + 3 * 0.044715 * (u * u)))).astype(BF)
        act = (0.5 * u * (1.0 + bend)).astype(BF)
        activated[here, :] = act
        reduce.put(k, dot(act, w_proj[...]))
        if before is not None:
            reduce.push(before)
        before = k
    kept = pltpu.make_async_copy(full, normed_two, kept_sem)
    kept.start()
    reduce.push(before)
    out = (mid[...] + (reduce.total() + vec[5:6, :])).astype(BF)
    result[...] = out
    normed[...] = (norm_parts(out.astype(F32))[0] * next_vec[0:1, :] + next_vec[2:3, :]).astype(BF)
    gather.finish()
    reduce.finish()
    kept.wait()


def chunks(size, step):
    return [(a, min(a + step, size)) for a in range(0, size, step)]


def feed_backward(ties, *refs):
    (src, mid, w_fc, w_proj, slope, activated, normed_two, vec) = refs[:8]
    refs = refs[8 + ties :]
    (grad_mid, attn_rows, grad_proj, grad_fc, sums, unit_sums), refs = refs[:6], refs[6:]
    gather_refs, reduce_refs = refs[:5], refs[5:]
    hidden, = reduce_refs[9:10]
    rows, width = src.shape
    tokens = slope.shape[0]
    peers = Peers()
    gather = Gather(peers, gather_refs[0], gather_refs[1:])
    reduce = Reduce(peers, *reduce_refs[:5], reduce_refs[5:9])
    full = gather.full
    peers.greet()
    gather.start(src)
    before = None
    for k, chip in gather.arrivals():
        here = chip_rows(chip, rows)
        back = dot(full[chip].reshape(2 * rows, width), w_proj[...], 1, 1) * slope[here, :].astype(F32)
        back = back.astype(BF)
        hidden[here, :] = back
        reduce.put(k, dot(back, w_fc[...], 1, 1))
        if before is not None:
            reduce.push(before)
        before = k
    reduce.push(before)
    branch = full[...].reshape(tokens, width)
    for a, b in chunks(activated.shape[1], 256):
        grad_proj[a:b, :] = dot(activated[:, a:b], branch, 0, 0).astype(BF)
    back = hidden[...]
    for a, b in chunks(width, 512):
        grad_fc[a:b, :] = dot(normed_two[:, a:b], back, 0, 0).astype(BF)
    unit_sums[...] = jnp.sum(back.astype(F32), axis=0, keepdims=True)
    own = src[...].astype(F32)
    part, gain, shift = norm_back(mid[...], vec[1:2, :], reduce.total())
    out = own + part
    grad_mid[...] = out
    low = out.astype(BF)
    attn_rows[...] = low
    sums[0:1, :] = gain
    sums[1:2, :] = shift
    sums[2:3, :] = jnp.sum(own, axis=0, keepdims=True)
    sums[3:4, :] = jnp.sum(low.astype(F32), axis=0, keepdims=True)
    sums[4:8, :] = jnp.zeros((4, width), F32)
    gather.finish()
    reduce.finish()


def attention_backward(head, ties, *refs):
    (src, grad_mid, h, w_qkv, w_out, qkv, attended, logs, normed, col, row, vec) = refs[:12]
    refs = refs[12 + ties :]
    (grad_in, grad_qkv, grad_out, sums, head_sums), refs = refs[:5], refs[5:]
    gather_refs, reduce_refs = refs[:5], refs[5:]
    joint, key_sum, value_sum = reduce_refs[9:12]
    rows, width = src.shape
    tokens, span = attended.shape
    scale = head ** (-0.5)
    peers = Peers()
    gather = Gather(peers, gather_refs[0], gather_refs[1:])
    reduce = Reduce(peers, *reduce_refs[:5], reduce_refs[5:9])
    full = gather.full
    peers.greet()
    gather.start(src)
    for k, chip in gather.arrivals():
        here = chip_rows(chip, rows)
        g_all = dot(full[chip].reshape(2 * rows, width), w_out[...], 1, 1).astype(BF)
        block = jnp.where(col[...] <= row[:, here], 0.0, LOW).astype(F32)
        for lanes, heads in groups(span, head):
            q = qkv[here, lanes]
            g = g_all[:, lanes]
            keys = qkv[:, slice(span + lanes.start, span + lanes.stop)]
            values = qkv[:, slice(2 * span + lanes.start, 2 * span + lanes.stop)]
            merged = None
            key_term, value_term = 0.0, 0.0
            for slot, start in heads:
                q_one, g_one = only(q, start, head) * scale, only(g, start, head)
                probs = jnp.exp(dot(keys, q_one, 1, 1) + block - logs[slot : slot + 1, here])
                g_probs = dot(values, g_one, 1, 1)
                both = probs * g_probs
                centre = jnp.sum(both, axis=0, keepdims=True)
                g_scores = (both - probs * centre).astype(BF)
                value_term += dot(probs.astype(BF), g_one)
                key_term += dot(g_scores, q_one)
                g_query = dot(keys, g_scores, 0, 0)
                lane = lax.broadcasted_iota(jnp.int32, g_query.shape, 0)
                merged = g_query if merged is None else jnp.where(lane >= start, g_query, merged)
            joint[here, lanes] = (merged.T * scale).astype(BF)
            if k == 0:
                key_sum[:, lanes] = key_term
                value_sum[:, lanes] = value_term
            else:
                key_sum[:, lanes] += key_term
                value_sum[:, lanes] += value_term
    joint[:, span : 2 * span] = key_sum[...].astype(BF)
    joint[:, 2 * span :] = value_sum[...].astype(BF)
    order = list(range(1, peers.chips)) + [0]
    before = None
    for k in order:
        reduce.put(k, dot(joint[chip_rows(peers.behind_chip(k), rows), :], w_qkv[...], 1, 1))
        if before is not None:
            reduce.push(before)
        before = k
    grads = joint[...]
    for a, b in chunks(width, 512):
        grad_qkv[a:b, :] = dot(normed[:, a:b], grads, 0, 0).astype(BF)
    grad_out[...] = dot(attended[...], full[...].reshape(tokens, width), 0, 0).astype(BF)
    head_sums[...] = jnp.sum(grads.astype(F32), axis=0, keepdims=True)
    part, gain, shift = norm_back(h[...].astype(F32), vec[0:1, :], reduce.total())
    grad_in[...] = (grad_mid[...] + part).astype(BF)
    sums[0:1, :] = gain
    sums[1:2, :] = shift
    sums[2:8, :] = jnp.zeros((6, width), F32)
    gather.finish()
    reduce.finish()


def call(kernel, name, outs, operands, ties, kept, scratch):
    chips = lax.axis_size("section") * lax.axis_size("r")
    rows, width = operands[0].shape
    vmem, hbm = pl.BlockSpec(memory_space=pltpu.VMEM), pl.BlockSpec(memory_space=pl.ANY)
    return pl.pallas_call(
        kernel,
        out_shape=[jax.ShapeDtypeStruct(*o) for o in outs],
        in_specs=[vmem] * len(operands) + [hbm] * len(ties),
        out_specs=[hbm if i in kept else vmem for i in range(len(outs))],
        scratch_shapes=gather_scratch(chips, rows, width) + reduce_scratch(chips, rows, width) + scratch,
        compiler_params=pltpu.CompilerParams(collective_id=name, has_side_effects=True, vmem_limit_bytes=60 * 2**20),
    )(*operands, *ties)


def run_attention_forward(name, head, ties, *operands):
    src, h, w_qkv, w_out, bias, col, row, vec = operands
    rows, width = src.shape
    tokens, span = col.shape[0], w_out.shape[0]
    slots = -(-(span // head) // 8) * 8
    chips = tokens // (2 * rows)
    outs = [
        ((chips, 2, rows, width), BF),
        ((tokens, 3 * span), BF),
        ((tokens, span), BF),
        ((slots, tokens), F32),
        ((rows, width), F32),
        ((rows, width), BF),
    ]
    return call(functools.partial(attention_forward, head, len(ties)), name, outs, operands, ties, (0,), [pltpu.SemaphoreType.DMA])


def run_feed_forward(name, ties, *operands):
    src, mid, w_fc, w_proj, bias, vec, next_vec = operands
    rows, width = src.shape
    units = w_fc.shape[1]
    chips = lax.axis_size("section") * lax.axis_size("r")
    tokens = 2 * chips * rows
    outs = [
        ((chips, 2, rows, width), BF),
        ((tokens, units), BF),
        ((tokens, units), BF),
        ((rows, width), BF),
        ((rows, width), BF),
    ]
    return call(functools.partial(feed_forward, len(ties)), name, outs, operands, ties, (0,), [pltpu.SemaphoreType.DMA])


def run_feed_backward(name, ties, *operands):
    src, mid, w_fc, w_proj, slope, activated, normed_two, vec = operands
    rows, width = src.shape
    tokens, units = slope.shape
    outs = [
        ((rows, width), F32),
        ((rows, width), BF),
        ((units, width), BF),
        ((width, units), BF),
        ((8, width), F32),
        ((1, units), F32),
    ]
    return call(functools.partial(feed_backward, len(ties)), name, outs, operands, ties, (), [pltpu.VMEM((tokens, units), BF)])


def run_attention_backward(name, head, ties, *operands):
    src, grad_mid, h, w_qkv, w_out, qkv, attended, logs, normed, col, row, vec = operands
    rows, width = src.shape
    tokens, span = attended.shape
    outs = [
        ((rows, width), BF),
        ((width, 3 * span), BF),
        ((span, width), BF),
        ((8, width), F32),
        ((1, 3 * span), F32),
    ]
    scratch = [pltpu.VMEM((tokens, 3 * span), BF), pltpu.VMEM((tokens, span), F32), pltpu.VMEM((tokens, span), F32)]
    return call(functools.partial(attention_backward, head, len(ties)), name, outs, operands, ties, (), scratch)


def tiny_kernel(src, out, stage, z_send, z_recv, *sems):
    peers = Peers()
    zs, z = lax.axis_size("z"), lax.axis_index("z")
    peers.greet(zs)
    sent = []
    for k in range(1, zs):
        copy = remote(src, stage.at[z], z_send.at[k], z_recv.at[k], {"z": lax.rem(z + k, zs)})
        copy.start()
        sent.append(copy)
    stage[z] = src[...]
    for k in range(1, zs):
        block = stage.at[lax.rem(z + zs - k, zs)]
        remote(block, block, z_send.at[k], z_recv.at[k], {"z": lax.rem(z + k, zs)}).wait_recv()
    gather = Gather(peers, out, sems)
    gather.start(stage)
    for _ in gather.arrivals():
        pass
    gather.finish()
    for copy in sent:
        copy.wait_send()


def tiny_gather(a, name):
    sections, rest, zs = (lax.axis_size(i) for i in ("section", "r", "z"))
    chips = sections * rest
    vmem = pl.BlockSpec(memory_space=pltpu.VMEM)
    out = pl.pallas_call(
        tiny_kernel,
        out_shape=jax.ShapeDtypeStruct((chips, 2, zs, *a.shape), a.dtype),
        in_specs=[vmem],
        out_specs=vmem,
        scratch_shapes=[pltpu.VMEM((zs, *a.shape), a.dtype)]
        + [pltpu.SemaphoreType.DMA((zs,))] * 2
        + [pltpu.SemaphoreType.DMA((chips,))] * 4,
        compiler_params=pltpu.CompilerParams(collective_id=name, has_side_effects=True),
    )(a)
    return out.reshape(sections, rest, 2, zs, *a.shape)


class Rings:
    def __init__(self, lay):
        self.lay = lay
        self.live = []

    def own(self, part, step):
        lay = self.lay
        block = lax.dynamic_index_in_dim(part, (lay.z - 1 - step) % lay.zs, 0, keepdims=False)
        return block.astype(jnp.float32)

    def add(self, term):
        zs = self.lay.zs
        part = term.reshape(zs, term.shape[0] // zs, term.shape[1])
        ring = [self.own(part, 0).astype(jnp.bfloat16), part, 0]
        self.live.append(ring)
        return ring

    def step(self):
        zs = self.lay.zs
        self.live = [ring for ring in self.live if ring[2] < zs - 1]
        route = [(i, (i + 1) % zs) for i in range(zs)]
        for ring in self.live:
            got = lax.ppermute(ring[0], "z", route).astype(jnp.float32)
            ring[2] += 1
            ring[0] = (got + self.own(ring[1], ring[2])).astype(jnp.bfloat16)

    def ties(self):
        now = [ring[0] for ring in self.live]
        self.step()
        return now

    def finish(self):
        while any(ring[2] < self.lay.zs - 1 for ring in self.live):
            self.step()


def spread_weights(lay, w_qkv, w_attn_out, w_fc, w_proj):
    n = lay.slab
    width, block = lay.width, lay.block
    slot_cols = lay.slots * lay.head
    qkv = w_qkv[0].reshape(block, 3, width)
    qkv = jnp.pad(qkv, ((0, 0), (0, 0), (0, n * slot_cols - width)))
    qkv = qkv.reshape(block, 3, n, slot_cols).transpose(2, 0, 1, 3).reshape(n, block, 3 * slot_cols)
    out = lay.order(w_attn_out[0]).reshape(block, n, lay.cols).transpose(1, 0, 2)
    fc = w_fc[0].reshape(block, lay.cores, lay.zs, lay.rest, lay.sections, lay.half)
    fc = fc.transpose(4, 1, 3, 0, 2, 5).reshape(n, block, lay.zs * lay.half)
    proj = lay.order(w_proj[0]).reshape(lay.sections, lay.half, width)

    def move(a):
        got = lax.all_to_all(a, SLAB, 0, 0, tiled=True)
        got = got.reshape(lay.sections, lay.cores * lay.rest * block, a.shape[2])
        return [got[layer] for layer in range(lay.sections)]

    first = move(jnp.concatenate([qkv, out], axis=2))
    fc = move(fc)
    proj = lax.all_to_all(proj, ("section",), 0, 0, tiled=True)
    params = []
    for layer in range(lay.sections):
        full = [
            lax.all_gather(a, "z", axis=0, tiled=True) for a in (first[layer], fc[layer], proj[layer])
        ]
        wo = full[0][:, 3 * slot_cols :]
        wo = wo.reshape(lay.zs, lay.cores, lay.rest * block, lay.cols)
        wo = jnp.swapaxes(wo, 0, 1).reshape(width, lay.cols)
        wo = jnp.pad(wo, ((0, n * slot_cols - width), (0, 0))).reshape(n, slot_cols, lay.cols)
        wo = lax.all_to_all(wo, SLAB, 0, 0, tiled=True)
        wo = wo.transpose(1, 0, 2).reshape(slot_cols, width)
        params.append((full[0][:, : 3 * slot_cols], wo, full[1], full[2]))
    return params


def on_device(
    inputs, cotangent, positions, w_qkv, w_attn_out, w_fc, w_proj, norm_gains, biases, fc_bias
):
    lay = Layout(inputs, w_fc)
    n, block, width = lay.slab, lay.block, lay.width
    span = lay.slots * lay.head
    micro = lay.z // lay.seqs

    params = spread_weights(lay, w_qkv, w_attn_out, w_fc, w_proj)

    per_row = lay.unit_block // block
    thin = jnp.concatenate([norm_gains[0], biases[0], fc_bias[0].reshape(block, per_row)], axis=1)
    thin = jnp.concatenate([thin.reshape(-1).astype(jnp.float32), positions.reshape(-1).astype(jnp.float32)])
    used, spots = block * (8 + per_row), positions.size
    thin = jnp.pad(thin, (0, -thin.size % 1024)).reshape(-1, 128)
    thin = tiny_gather(thin, 0).reshape(lay.sections, lay.rest, lay.cores, lay.zs, -1)
    places = thin[0, :, 0, :, used : used + spots].astype(jnp.int32)
    places = places.reshape(lay.rest, lay.sections, lay.cores, lay.micros, lay.rows)
    places = places.transpose(3, 1, 0, 2, 4).reshape(lay.micros, lay.tokens)
    places = lax.dynamic_slice_in_dim(places, micro, 1, 0)
    col, row = places.reshape(lay.tokens, 1), places
    thin = thin[..., :used].transpose(0, 2, 3, 1, 4).reshape(lay.sections, width, 8 + per_row)
    smalls = []
    for layer in range(lay.sections):
        vec = jnp.stack([thin[layer, :, i] for i in (0, 1, 2, 6, 5, 7)] + [thin[layer, :, 0]] * 2)
        vec = lay.order(vec)
        heads = [
            lax.dynamic_slice_in_dim(
                jnp.pad(thin[layer, :, 2 + i], (0, n * span - width)), lay.t * span, span
            )
            for i in (1, 2)
        ]
        bias = jnp.concatenate([heads[0], jnp.zeros_like(heads[0]), heads[1]])[None]
        unit = thin[layer, :, 8:].reshape(lay.cores, lay.zs, lay.rest, lay.sections, lay.half)
        unit = unit.transpose(3, 0, 2, 1, 4).reshape(n, lay.zs * lay.half)
        unit = lax.dynamic_slice_in_dim(unit, lay.t, 1, 0)
        smalls.append((vec, bias, unit))

    h = lay.order(lay.tokens_in(inputs))
    g = lay.order(lay.tokens_in(cotangent))

    vec = smalls[0][0]
    normed = (norm_parts(h.astype(F32))[0] * vec[0:1] + vec[2:3]).astype(BF)
    outs, keeps = [], []
    for layer in range(lay.sections):
        w_qkv, w_out, w_fc, w_proj = params[layer]
        vec, bias, unit = smalls[layer]
        full, qkv, attended, logs, mid, normed_two = run_attention_forward(
            1, lay.head, (), normed, h, w_qkv, w_out, bias, col, row, vec
        )
        next_vec = smalls[min(layer + 1, lay.sections - 1)][0]
        full_two, slope, activated, result, normed = run_feed_forward(
            2, (), normed_two, mid, w_fc, w_proj, unit, vec, next_vec
        )
        keeps.append((h, full, qkv, attended, logs, mid, full_two, slope, activated))
        h = result
        outs.append(h)

    grads, grad_rows, sums = [None] * lay.sections, [None] * lay.sections, [None] * lay.sections
    rings = Rings(lay)
    for layer in reversed(range(lay.sections)):
        w_qkv, w_out, w_fc, w_proj = params[layer]
        vec = smalls[layer][0]
        h, full, qkv, attended, logs, mid, full_two, slope, activated = keeps[layer]
        full, full_two = (a.reshape(lay.tokens, width) for a in (full, full_two))
        grad_mid, attn_rows, grad_proj, grad_fc, feed_sums, unit_sums = run_feed_backward(
            3 + 2 * layer, rings.ties(), g, mid, w_fc, w_proj, slope, activated, full_two, vec
        )
        grad_proj, grad_fc = rings.add(grad_proj), rings.add(grad_fc)
        g, grad_qkv, grad_out, attn_sums, head_sums = run_attention_backward(
            4 + 2 * layer, lay.head, rings.ties(), attn_rows, grad_mid, h, w_qkv, w_out, qkv, attended, logs, full, col, row, vec
        )
        wo = grad_out.reshape(span, n, lay.cols).transpose(1, 0, 2)
        wo = lax.all_to_all(wo, SLAB, 0, 0, tiled=True)
        wo = wo.reshape(n * span, lay.cols)[:width].reshape(lay.cores, lay.zs, lay.rest * block, lay.cols)
        wo = jnp.swapaxes(wo, 0, 1).reshape(width, lay.cols)
        first = rings.add(jnp.concatenate([grad_qkv, wo], axis=1))
        grads[layer] = (first, grad_fc, grad_proj)
        grad_rows[layer] = g
        sums[layer] = (feed_sums, unit_sums, attn_sums, head_sums)
    rings.finish()

    section_out = lay.tokens_out([lay.restore(a) for a in outs])
    section_grad = lay.tokens_out([lay.restore(a) for a in grad_rows])

    def back(i):
        both = jnp.stack([grads[layer][i][0] for layer in range(lay.sections)])
        return lax.all_to_all(both.reshape(n, block, both.shape[2]), SLAB, 0, 0, tiled=True)

    first = back(0)
    got = first[:, :, : 3 * span].reshape(n, block, 3, span).transpose(1, 2, 0, 3)
    out_qkv = got.reshape(block, 3, n * span)[:, :, :width].reshape(block, 3 * width).astype(jnp.float32)
    got = first[:, :, 3 * span :].transpose(1, 0, 2).reshape(block, width)
    out_attn = lay.restore(got).astype(jnp.float32)
    got = back(1).reshape(lay.sections, lay.cores, lay.rest, block, lay.zs, lay.half)
    out_fc = got.transpose(3, 1, 4, 2, 0, 5).reshape(block, lay.units).astype(jnp.float32)
    both = jnp.stack([grads[layer][2][0] for layer in range(lay.sections)])
    got = lax.all_to_all(both, ("section",), 0, 0, tiled=True)
    out_proj = lay.restore(got.reshape(lay.unit_block, width)).astype(jnp.float32)

    rows = []
    for layer in range(lay.sections):
        feed_sums, unit_sums, attn_sums, head_sums = sums[layer]
        feed_sums, attn_sums = lay.restore(feed_sums), lay.restore(attn_sums)
        zero = jnp.zeros((n * span,), jnp.float32)
        s_q = lax.dynamic_update_slice_in_dim(zero, head_sums[0, :span], lay.t * span, 0)[:width]
        s_v = lax.dynamic_update_slice_in_dim(zero, head_sums[0, 2 * span :], lay.t * span, 0)[:width]
        cols = [attn_sums[0], feed_sums[0], attn_sums[1], s_q, s_v, feed_sums[3], feed_sums[1], feed_sums[2]]
        cols = jnp.stack(cols, axis=1).reshape(lay.shards, block * 8)
        spots = jnp.zeros((n, lay.zs, lay.half), jnp.float32)
        spots = lax.dynamic_update_index_in_dim(
            spots, unit_sums.reshape(lay.zs, lay.half), lay.t, 0
        )
        spots = spots.reshape(lay.sections, lay.cores, lay.rest, lay.zs, lay.half)
        spots = spots.transpose(1, 3, 2, 0, 4).reshape(lay.shards, lay.unit_block)
        rows.append(jnp.concatenate([cols, spots], axis=1))
    rows = jnp.concatenate(rows, axis=0)
    rows = jnp.sum(lax.all_to_all(rows, ALL, 0, 0, tiled=True), axis=0)
    cols = rows[: block * 8].reshape(block, 8)
    return (
        section_out,
        section_grad,
        out_qkv[None],
        out_attn[None],
        out_fc[None],
        out_proj[None],
        cols[None, :, :2],
        cols[None, :, 2:],
        rows[None, block * 8 :],
    )


def solution(mesh):
    sections, cores, contexts = (mesh.shape[a] for a in ("section", "dp", "ctx"))
    zs = sections * cores
    shape = (sections, cores, zs, contexts // zs)
    inner = Mesh(mesh.devices.reshape(shape), ALL)
    tokens = P(None, "dp", ("z", "r"), None)
    rows = P("section", ("dp", "z", "r"), None)
    units = P("section", ("dp", "z", "r"))
    out_tokens = P("section", None, "dp", ("z", "r"), None)
    return jax.shard_map(
        on_device,
        mesh=inner,
        in_specs=(tokens, tokens, P(None, ("z", "r"))) + (rows,) * 6 + (units,),
        out_specs=(out_tokens, out_tokens) + (rows,) * 6 + (units,),
        check_vma=False,
    )
```

```python
import functools

import jax
import jax.numpy as jnp
from jax import lax
from jax.experimental import pallas as pl
from jax.experimental.pallas import tpu as pltpu
from jax.sharding import Mesh
from jax.sharding import PartitionSpec as P

HEADS = 25
EPSILON = 1e-05

SLAB = ("section", "dp", "r")
ALL = ("section", "dp", "z", "r")
MESH = pl.DeviceIdType.MESH


class Layout:
    def __init__(self, inputs, w_fc):
        self.micros, _, self.rows, self.width = inputs.shape
        self.sections = lax.axis_size("section")
        self.cores = lax.axis_size("dp")
        self.zs = lax.axis_size("z")
        self.rest = lax.axis_size("r")
        self.slab = self.sections * self.cores * self.rest
        self.shards = self.cores * self.zs * self.rest
        self.units = w_fc.shape[2]
        self.tokens = self.rows * self.slab
        self.seqs = self.cores
        self.head = self.width // HEADS
        self.slots = -(-HEADS // self.slab)
        self.block = self.width // self.shards
        self.unit_block = self.units // self.shards
        self.half = self.unit_block // self.sections
        self.cols = self.width // self.slab
        self.x = lax.axis_index("section")
        self.c = lax.axis_index("dp")
        self.z = lax.axis_index("z")
        self.r = lax.axis_index("r")
        self.t = (self.x * self.cores + self.c) * self.rest + self.r

    def number(self, x, c, z, r):
        return ((x * self.cores + c) * self.zs + z) * self.rest + r

    def order(self, a):
        lead = a.shape[:-1]
        a = a.reshape(*lead, self.cores, self.zs, self.rest * self.block)
        return jnp.swapaxes(a, -3, -2).reshape(*lead, self.width)

    def restore(self, a):
        lead = a.shape[:-1]
        a = a.reshape(*lead, self.zs, self.cores, self.rest * self.block)
        return jnp.swapaxes(a, -3, -2).reshape(*lead, self.width)

    def routes(self, micro):
        pairs = []
        for x in range(self.sections):
            for c in range(self.cores):
                for s in range(self.seqs):
                    for r in range(self.rest):
                        place = x * self.cores + c
                        pairs.append(((x, s, place, r), (x, c, micro * self.seqs + s, r)))
        return pairs

    def tokens_in(self, a):
        got = []
        for micro in range(self.micros):
            route = [(self.number(*f), self.number(*g)) for f, g in self.routes(micro)]
            got.append(lax.ppermute(a[micro, 0], ALL, route))
        out = got[0]
        for micro in range(1, self.micros):
            out = jnp.where(self.z // self.seqs == micro, got[micro], out)
        return out

    def tokens_out(self, parts):
        result = []
        for micro in range(self.micros):
            got = []
            for layer, part in enumerate(parts):
                route = [
                    (self.number(*g), self.number(layer, *f[1:])) for f, g in self.routes(micro)
                ]
                got.append(lax.ppermute(part, ALL, route))
            out = got[0]
            for layer in range(1, len(parts)):
                out = jnp.where(self.x == layer, got[layer], out)
            result.append(out)
        return jnp.stack(result)[None, :, None]


LOW = -1e30
BF = jnp.bfloat16
F32 = jnp.float32


class Peers:
    def __init__(self):
        self.sections, self.rest = lax.axis_size("section"), lax.axis_size("r")
        self.chips = self.sections * self.rest
        self.x, self.c, self.r = (lax.axis_index(a) for a in ("section", "dp", "r"))
        self.chip = self.x * self.rest + self.r

    def away(self, k, sign):
        x = lax.rem(self.x + self.sections + sign * (k // self.rest), self.sections)
        r = lax.rem(self.r + self.rest + sign * (k % self.rest), self.rest)
        return x, r

    def ahead(self, k):
        x, r = self.away(k, 1)
        return {"section": x, "dp": self.c, "r": r}

    def behind(self, k):
        x, r = self.away(k, -1)
        return {"section": x, "dp": self.c, "r": r}

    def sibling(self):
        return {"section": self.x, "dp": 1 - self.c, "r": self.r}

    def behind_chip(self, k):
        x, r = self.away(k, -1)
        return x * self.rest + r

    def other(self, dx, dc, dr):
        x = lax.rem(self.x + self.sections + dx, self.sections)
        c = lax.rem(self.c + 2 + dc, 2)
        r = lax.rem(self.r + self.rest + dr, self.rest)
        return {"section": x, "dp": c, "r": r}, (x * 2 + c) * self.rest + r

    def offsets(self):
        every = [(x, c, r) for x in range(self.sections) for c in range(2) for r in range(self.rest)]
        return list(enumerate(every))[1:]

    def greet(self, zs=1):
        barrier = pltpu.get_barrier_semaphore()
        z = lax.axis_index("z")
        size = lax.axis_size("z")
        for k in range(1, zs):
            pl.semaphore_signal(barrier, inc=1, device_id={"z": lax.rem(z + size - k, size)}, device_id_type=MESH)
        others = self.offsets()
        for _, place in others:
            pl.semaphore_signal(barrier, inc=1, device_id=self.other(*place)[0], device_id_type=MESH)
        pl.semaphore_wait(barrier, len(others) + zs - 1)


def remote(src, dst, send, recv, device):
    return pltpu.make_async_remote_copy(
        src_ref=src, dst_ref=dst, send_sem=send, recv_sem=recv, device_id=device, device_id_type=MESH
    )


class Gather:
    def __init__(self, peers, full, sems):
        self.peers, self.full = peers, full
        self.chip_send, self.chip_recv, self.core_send, self.core_recv = sems
        self.sent = []

    def start(self, src):
        p = self.peers
        mine = self.full.at[p.chip, p.c]
        mine[...] = src[...]
        for k in range(1, p.chips):
            self.send(remote(mine, mine, self.chip_send.at[k], self.chip_recv.at[k], p.ahead(k)))
        self.send(remote(mine, mine, self.core_send.at[0], self.core_recv.at[0], p.sibling()))

    def send(self, copy):
        copy.start()
        self.sent.append(copy)

    def forward(self, k):
        p = self.peers
        block = self.full.at[p.behind_chip(k), p.c]
        remote(block, block, self.chip_send.at[k], self.chip_recv.at[k], p.sibling()).wait_recv()
        self.send(remote(block, block, self.core_send.at[k], self.core_recv.at[k], p.sibling()))

    def chip(self, k):
        p = self.peers
        block = self.full.at[p.behind_chip(k), 1 - p.c]
        remote(block, block, self.core_send.at[k], self.core_recv.at[k], p.sibling()).wait_recv()
        return p.behind_chip(k)

    def arrivals(self):
        yield 0, self.chip(0)
        chips = self.peers.chips
        for k in range(1, chips):
            for later in (1, 2) if k == 1 else (k + 1,):
                if later < chips:
                    self.forward(later)
            yield k, self.chip(k)

    def finish(self):
        for copy in self.sent:
            copy.wait_send()


class Reduce:
    def __init__(self, peers, mine, stage, other, going, coming, sems):
        self.peers = peers
        self.mine, self.stage, self.other, self.going, self.coming = mine, stage, other, going, coming
        self.chip_send, self.chip_recv, self.core_send, self.core_recv = sems
        self.sent = []

    def send(self, copy):
        copy.start()
        self.sent.append(copy)

    def put(self, k, both):
        p = self.peers
        rows = both.shape[0] // 2
        low, high = both[:rows], both[rows:]
        first = p.c == 0
        self.mine[k] = jnp.where(first, low, high)
        self.stage[k] = jnp.where(first, high, low).astype(BF)
        self.send(remote(self.stage.at[k], self.other.at[k], self.core_send.at[k], self.core_recv.at[k], p.sibling()))

    def arrived(self, k):
        p = self.peers
        remote(self.stage.at[k], self.other.at[k], self.core_send.at[k], self.core_recv.at[k], p.sibling()).wait_recv()
        return self.mine[k] + self.other[k].astype(F32)

    def push(self, k):
        p = self.peers
        if k:
            self.going[k - 1] = self.arrived(k).astype(BF)
            self.send(remote(self.going.at[k - 1], self.coming.at[k - 1], self.chip_send.at[k], self.chip_recv.at[k], p.behind(k)))

    def total(self):
        p = self.peers
        out = self.arrived(0)
        for k in range(1, p.chips):
            remote(self.going.at[k - 1], self.coming.at[k - 1], self.chip_send.at[k], self.chip_recv.at[k], p.sibling()).wait_recv()
            out = out + self.coming[k - 1].astype(F32)
        return out

    def finish(self):
        for copy in self.sent:
            copy.wait_send()


class RingGather:
    def __init__(self, pairs, local, send, recv):
        self.pairs, self.local, self.send_sem, self.recv_sem = pairs, local, send, recv
        self.zs, self.z = lax.axis_size("z"), lax.axis_index("z")
        self.steps = [(p, s) for s in range(self.zs - 1) for p in range(len(pairs))]
        self.sent = []

    def block(self, step):
        return lax.rem(self.z + self.zs - step, self.zs)

    def send(self, p, step, src):
        dst = self.pairs[p][1].at[self.block(step)]
        copy = remote(src, dst, self.send_sem.at[p, step], self.recv_sem.at[p, step], {"z": lax.rem(self.z + 1, self.zs)})
        copy.start()
        self.sent.append(copy)

    def start(self):
        for p, (shard, full) in enumerate(self.pairs):
            self.send(p, 0, shard)
            pltpu.make_async_copy(shard, full.at[self.z], self.local.at[p]).start()

    def tick(self):
        if not self.steps:
            return None
        p, step = self.steps.pop(0)
        block = self.pairs[p][1].at[self.block(step + 1)]
        remote(block, block, self.send_sem.at[p, step], self.recv_sem.at[p, step], {"z": lax.rem(self.z + 1, self.zs)}).wait_recv()
        if step < self.zs - 2:
            self.send(p, step + 1, block)
            return None
        shard, full = self.pairs[p]
        pltpu.make_async_copy(shard, full.at[self.z], self.local.at[p]).wait()
        return p

    def finish(self):
        while self.steps:
            self.tick()
        for copy in self.sent:
            copy.wait_send()


class RingSum:
    def __init__(self, triples, send, recv):
        self.triples, self.send_sem, self.recv_sem = triples, send, recv
        self.zs, self.z = lax.axis_size("z"), lax.axis_index("z")
        self.steps = [(p, s) for s in range(self.zs - 1) for p in range(len(triples))]
        self.sent = []

    def copy(self, p, step, src):
        dst = self.triples[p][1].at[step]
        return remote(src, dst, self.send_sem.at[p, step], self.recv_sem.at[p, step], {"z": lax.rem(self.z + 1, self.zs)})

    def send(self, p, step, src):
        copy = self.copy(p, step, src)
        copy.start()
        self.sent.append(copy)

    def start(self):
        for p, (part, came, out) in enumerate(self.triples):
            self.send(p, 0, part.at[lax.rem(self.z + self.zs - 1, self.zs)])

    def tick(self):
        if not self.steps:
            return
        p, step = self.steps.pop(0)
        part, came, out = self.triples[p]
        self.copy(p, step, came.at[step]).wait_recv()
        own = part[lax.rem(self.z + 2 * self.zs - 2 - step, self.zs)]
        total = (came[step].astype(F32) + own.astype(F32)).astype(BF)
        if step < self.zs - 2:
            came[step] = total
            self.send(p, step + 1, came.at[step])
        else:
            out[...] = total

    def finish(self):
        while self.steps:
            self.tick()
        for copy in self.sent:
            copy.wait_send()


class Turn:
    def __init__(self, peers, full, nat, land, w_out, send, recv):
        self.peers, self.full, self.nat, self.land, self.w_out = peers, full, nat, land, w_out
        self.send_sem, self.recv_sem = send, recv
        self.sent = []

    def start(self):
        zs, rows, cols = self.full.shape
        part, span = rows // 2, self.w_out.shape[0]
        for c in range(2):
            for z in range(zs):
                at = (c * zs + z) * part
                self.nat[at : at + part, :] = self.full[z, c * part : (c + 1) * part, :]
        used = zs * rows
        if used < self.nat.shape[0]:
            self.nat[used:, :] = jnp.zeros((self.nat.shape[0] - used, cols), BF)
        _, me = self.peers.other(0, 0, 0)
        for i, place in self.peers.offsets():
            device, t = self.peers.other(*place)
            src = self.nat.at[pl.ds(pl.multiple_of(t * span, span), span)]
            copy = remote(src, self.land.at[me], self.send_sem.at[i], self.recv_sem.at[i], device)
            copy.start()
            self.sent.append(copy)
        self.land[me] = self.nat[pl.ds(pl.multiple_of(me * span, span), span), :]

    def finish(self):
        for i, place in self.peers.offsets():
            device, t = self.peers.other(*(-d for d in place))
            block = self.land.at[t]
            remote(block, block, self.send_sem.at[i], self.recv_sem.at[i], device).wait_recv()
        slab, _, cols = self.land.shape
        for t in range(slab):
            self.w_out[:, t * cols : (t + 1) * cols] = self.land[t]
        for copy in self.sent:
            copy.wait_send()


class NoSide:
    def start(self):
        pass

    def tick(self):
        pass

    def finish(self):
        pass


class Both:
    def __init__(self, ring, turn):
        self.ring, self.turn, self.turned = ring, turn, False

    def start(self):
        self.ring.start()

    def tick(self):
        if self.ring.tick() == 0:
            self.turn.start()

    def finish(self):
        while self.ring.steps:
            self.tick()
        self.ring.finish()
        self.turn.finish()


class SideWork:
    def __init__(self, operands=(), in_hbm=(), outs=(), out_hbm=(), scratch=(), build=None):
        self.operands, self.in_hbm, self.outs, self.out_hbm = operands, in_hbm, outs, out_hbm
        self.scratch, self.build = scratch, build
        self.zs = 1 if build is None else 2

    def make(self, peers, ins, outs, scratch):
        return NoSide() if self.build is None else self.build(peers, ins, outs, scratch)


def gather_side(shards, turn=None):
    zs = lax.axis_size("z")
    n = len(shards)
    outs = [((zs, *a.shape), BF) for a in shards]
    sems = [pltpu.SemaphoreType.DMA((n,))] + [pltpu.SemaphoreType.DMA((n, zs - 1))] * 2
    if turn is None:

        def build(peers, ins, outs, scratch):
            return RingGather(list(zip(ins, outs)), *scratch)

        return SideWork(shards, (True,) * n, outs, (True,) * n, sems, build)
    slab = 2 * lax.axis_size("section") * lax.axis_size("r")
    cols = shards[0].shape[1]
    outs[0] = ((turn, slab * cols), BF)
    more = [
        pltpu.VMEM((zs, *shards[0].shape), BF),
        pltpu.VMEM((slab * turn, cols), BF),
        pltpu.VMEM((slab, turn, cols), BF),
    ] + [pltpu.SemaphoreType.DMA((slab,))] * 2

    def build_turn(peers, ins, outs, scratch):
        pairs = [(ins[0], scratch[3])] + list(zip(ins[1:], outs[1:]))
        return Both(RingGather(pairs, *scratch[:3]), Turn(peers, scratch[3], scratch[4], scratch[5], outs[0], *scratch[6:8]))

    return SideWork(shards, (True,) * n, outs, (False,) + (True,) * (n - 1), sems + more, build_turn)


def sum_side(parts):
    zs = lax.axis_size("z")
    parts = [a.reshape(zs, a.shape[0] // zs, a.shape[1]) for a in parts]
    n = len(parts)
    outs = [(a.shape[1:], BF) for a in parts]
    scratch = [pltpu.VMEM((zs - 1, *a.shape[1:]), BF) for a in parts]
    scratch += [pltpu.SemaphoreType.DMA((n, zs - 1))] * 2

    def build(peers, ins, outs, scratch):
        return RingSum(list(zip(ins, scratch[:n], outs)), *scratch[n:])

    return SideWork(parts, (False,) * n, outs, (False,) * n, scratch, build)


def gather_scratch(chips, rows, width):
    return [pltpu.VMEM((chips, 2, rows, width), BF)] + [pltpu.SemaphoreType.DMA((chips,))] * 4


def reduce_scratch(chips, rows, width):
    return [
        pltpu.VMEM((chips, rows, width), F32),
        pltpu.VMEM((chips, rows, width), BF),
        pltpu.VMEM((chips, rows, width), BF),
        pltpu.VMEM((chips - 1, rows, width), BF),
        pltpu.VMEM((chips - 1, rows, width), BF),
    ] + [pltpu.SemaphoreType.DMA((chips,))] * 4


def norm_parts(v):
    centred = v - jnp.mean(v, axis=-1, keepdims=True)
    spread = jnp.mean(centred * centred, axis=-1, keepdims=True)
    scale = lax.rsqrt(spread + EPSILON)
    return centred * scale, scale


def norm_back(v, gain, grad):
    unit, scale = norm_parts(v)
    scaled = grad * gain
    part = scaled - jnp.mean(scaled, axis=-1, keepdims=True)
    part = part - unit * jnp.mean(scaled * unit, axis=-1, keepdims=True)
    return part * scale, jnp.sum(grad * unit, axis=0, keepdims=True), jnp.sum(grad, axis=0, keepdims=True)


def dot(a, b, ca=1, cb=0):
    return lax.dot_general(a, b, (((ca,), (cb,)), ((), ())), preferred_element_type=F32)


def chip_rows(chip, rows):
    return pl.ds(pl.multiple_of(chip * (2 * rows), 2 * rows), 2 * rows)


def groups(span, head):
    wide = 128 if span % 128 == 0 else span
    for g in range(span // wide):
        yield slice(g * wide, (g + 1) * wide), [(g * wide // head + i, i * head) for i in range(wide // head)]


def only(a, start, head):
    lane = lax.broadcasted_iota(jnp.int32, a.shape, 1)
    return jnp.where((lane >= start) & (lane < start + head), a, jnp.zeros_like(a))


def attention_forward(head, side, *refs):
    (src, h, w_qkv, w_out, bias, col, row, vec) = refs[:8]
    ins, refs = refs[8 : 8 + len(side.operands)], refs[8 + len(side.operands) :]
    (normed, qkv, attended, logs, mid, normed_two), refs = refs[:6], refs[6:]
    side_outs, refs = refs[: len(side.outs)], refs[len(side.outs) :]
    gather_refs, reduce_refs, side_refs = refs[:5], refs[5 : 14 + 1], refs[14 + 1 :]
    rows, width = src.shape
    span = w_out.shape[0]
    peers = Peers()
    gather = Gather(peers, gather_refs[0], gather_refs[1:])
    reduce = Reduce(peers, *reduce_refs[:5], reduce_refs[5:9])
    kept_sem = reduce_refs[9]
    full = gather.full
    work = side.make(peers, ins, side_outs, side_refs)
    peers.greet(side.zs)
    gather.start(src)
    work.start()
    for k, chip in gather.arrivals():
        part = dot(full[chip].reshape(2 * rows, width), w_qkv[...]) + bias[...]
        qkv[chip_rows(chip, rows), :] = part.astype(BF)
    work.tick()
    kept = pltpu.make_async_copy(full, normed, kept_sem)
    kept.start()
    scale = head ** (-0.5)
    order = list(range(1, peers.chips)) + [0]
    before = None
    for k in order:
        chip = peers.behind_chip(k)
        here = chip_rows(chip, rows)
        block = jnp.where(col[...] <= row[:, here], 0.0, LOW).astype(F32)
        for lanes, heads in groups(span, head):
            q = qkv[here, lanes]
            keys = qkv[:, slice(span + lanes.start, span + lanes.stop)]
            values = qkv[:, slice(2 * span + lanes.start, 2 * span + lanes.stop)]
            merged = None
            for slot, start in heads:
                scores = dot(keys, only(q, start, head) * scale, 1, 1) + block
                top = jnp.max(scores, axis=0, keepdims=True)
                weights = jnp.exp(scores - top)
                total = jnp.sum(weights, axis=0, keepdims=True)
                logs[slot : slot + 1, here] = top + jnp.log(total)
                mixed = dot(values, weights.astype(BF), 0, 0) / total
                lane = lax.broadcasted_iota(jnp.int32, mixed.shape, 0)
                merged = mixed if merged is None else jnp.where(lane >= start, mixed, merged)
            attended[here, lanes] = merged.T.astype(BF)
        reduce.put(k, dot(attended[here, :], w_out[...]))
        if before is not None:
            reduce.push(before)
        work.tick()
        before = k
    reduce.push(before)
    out = h[...].astype(F32) + (reduce.total() + vec[4:5, :])
    mid[...] = out
    normed_two[...] = (norm_parts(out)[0] * vec[1:2, :] + vec[3:4, :]).astype(BF)
    work.finish()
    gather.finish()
    reduce.finish()
    kept.wait()


ROOT = 0.7978845608028654


def feed_forward(side, *refs):
    (src, mid, w_fc, w_proj, bias, vec, next_vec) = refs[:7]
    ins, refs = refs[7 : 7 + len(side.operands)], refs[7 + len(side.operands) :]
    (normed_two, slope, activated, result, normed), refs = refs[:5], refs[5:]
    side_outs, refs = refs[: len(side.outs)], refs[len(side.outs) :]
    gather_refs, reduce_refs, side_refs = refs[:5], refs[5 : 14 + 1], refs[14 + 1 :]
    rows, width = src.shape
    peers = Peers()
    gather = Gather(peers, gather_refs[0], gather_refs[1:])
    reduce = Reduce(peers, *reduce_refs[:5], reduce_refs[5:9])
    kept_sem = reduce_refs[9]
    full = gather.full
    work = side.make(peers, ins, side_outs, side_refs)
    peers.greet(side.zs)
    gather.start(src)
    work.start()
    before = None
    for k, chip in gather.arrivals():
        here = chip_rows(chip, rows)
        u = dot(full[chip].reshape(2 * rows, width), w_fc[...]) + bias[...]
        bend = jnp.tanh(ROOT * (u + 0.044715 * (u * u * u)))
        slope[here, :] = (0.5 * (1.0 + bend) + 0.5 * u * (1.0 - bend * bend) * (ROOT * (1.0 + 3 * 0.044715 * (u * u)))).astype(BF)
        act = (0.5 * u * (1.0 + bend)).astype(BF)
        activated[here, :] = act
        reduce.put(k, dot(act, w_proj[...]))
        if before is not None:
            reduce.push(before)
        if k:
            work.tick()
        before = k
    kept = pltpu.make_async_copy(full, normed_two, kept_sem)
    kept.start()
    reduce.push(before)
    out = (mid[...] + (reduce.total() + vec[5:6, :])).astype(BF)
    result[...] = out
    normed[...] = (norm_parts(out.astype(F32))[0] * next_vec[0:1, :] + next_vec[2:3, :]).astype(BF)
    work.finish()
    gather.finish()
    reduce.finish()
    kept.wait()


def chunks(size, step):
    return [(a, min(a + step, size)) for a in range(0, size, step)]


def feed_backward(side, *refs):
    (src, mid, w_fc, w_proj, slope, activated, normed_two, vec) = refs[:8]
    ins, refs = refs[8 : 8 + len(side.operands)], refs[8 + len(side.operands) :]
    (grad_mid, attn_rows, grad_proj, grad_fc, sums, unit_sums), refs = refs[:6], refs[6:]
    side_outs, refs = refs[: len(side.outs)], refs[len(side.outs) :]
    gather_refs, reduce_refs, side_refs = refs[:5], refs[5 : 14 + 1], refs[14 + 1 :]
    hidden, = reduce_refs[9:10]
    rows, width = src.shape
    tokens = slope.shape[0]
    peers = Peers()
    gather = Gather(peers, gather_refs[0], gather_refs[1:])
    reduce = Reduce(peers, *reduce_refs[:5], reduce_refs[5:9])
    full = gather.full
    work = side.make(peers, ins, side_outs, side_refs)
    peers.greet(side.zs)
    gather.start(src)
    work.start()
    before = None
    for k, chip in gather.arrivals():
        here = chip_rows(chip, rows)
        back = dot(full[chip].reshape(2 * rows, width), w_proj[...], 1, 1) * slope[here, :].astype(F32)
        back = back.astype(BF)
        hidden[here, :] = back
        reduce.put(k, dot(back, w_fc[...], 1, 1))
        if before is not None:
            reduce.push(before)
        if k > 1:
            work.tick()
        before = k
    reduce.push(before)
    branch = full[...].reshape(tokens, width)
    for a, b in chunks(activated.shape[1], 256):
        grad_proj[a:b, :] = dot(activated[:, a:b], branch, 0, 0).astype(BF)
    work.tick()
    back = hidden[...]
    for a, b in chunks(width, 512):
        grad_fc[a:b, :] = dot(normed_two[:, a:b], back, 0, 0).astype(BF)
    unit_sums[...] = jnp.sum(back.astype(F32), axis=0, keepdims=True)
    own = src[...].astype(F32)
    part, gain, shift = norm_back(mid[...], vec[1:2, :], reduce.total())
    out = own + part
    grad_mid[...] = out
    low = out.astype(BF)
    attn_rows[...] = low
    sums[0:1, :] = gain
    sums[1:2, :] = shift
    sums[2:3, :] = jnp.sum(own, axis=0, keepdims=True)
    sums[3:4, :] = jnp.sum(low.astype(F32), axis=0, keepdims=True)
    sums[4:8, :] = jnp.zeros((4, width), F32)
    work.finish()
    gather.finish()
    reduce.finish()


def attention_backward(head, side, *refs):
    (src, grad_mid, h, w_qkv, w_out, qkv, attended, logs, normed, col, row, vec) = refs[:12]
    ins, refs = refs[12 : 12 + len(side.operands)], refs[12 + len(side.operands) :]
    (grad_in, grad_qkv, grad_out, sums, head_sums), refs = refs[:5], refs[5:]
    side_outs, refs = refs[: len(side.outs)], refs[len(side.outs) :]
    gather_refs, reduce_refs, side_refs = refs[:5], refs[5 : 14 + 3], refs[14 + 3 :]
    joint, key_sum, value_sum = reduce_refs[9:12]
    rows, width = src.shape
    tokens, span = attended.shape
    scale = head ** (-0.5)
    peers = Peers()
    gather = Gather(peers, gather_refs[0], gather_refs[1:])
    reduce = Reduce(peers, *reduce_refs[:5], reduce_refs[5:9])
    full = gather.full
    work = side.make(peers, ins, side_outs, side_refs)
    peers.greet(side.zs)
    gather.start(src)
    work.start()
    for k, chip in gather.arrivals():
        here = chip_rows(chip, rows)
        g_all = dot(full[chip].reshape(2 * rows, width), w_out[...], 1, 1).astype(BF)
        block = jnp.where(col[...] <= row[:, here], 0.0, LOW).astype(F32)
        for lanes, heads in groups(span, head):
            q = qkv[here, lanes]
            g = g_all[:, lanes]
            keys = qkv[:, slice(span + lanes.start, span + lanes.stop)]
            values = qkv[:, slice(2 * span + lanes.start, 2 * span + lanes.stop)]
            merged = None
            key_term, value_term = 0.0, 0.0
            for slot, start in heads:
                q_one, g_one = only(q, start, head) * scale, only(g, start, head)
                probs = jnp.exp(dot(keys, q_one, 1, 1) + block - logs[slot : slot + 1, here])
                g_probs = dot(values, g_one, 1, 1)
                both = probs * g_probs
                centre = jnp.sum(both, axis=0, keepdims=True)
                g_scores = (both - probs * centre).astype(BF)
                value_term += dot(probs.astype(BF), g_one)
                key_term += dot(g_scores, q_one)
                g_query = dot(keys, g_scores, 0, 0)
                lane = lax.broadcasted_iota(jnp.int32, g_query.shape, 0)
                merged = g_query if merged is None else jnp.where(lane >= start, g_query, merged)
            joint[here, lanes] = (merged.T * scale).astype(BF)
            if k == 0:
                key_sum[:, lanes] = key_term
                value_sum[:, lanes] = value_term
            else:
                key_sum[:, lanes] += key_term
                value_sum[:, lanes] += value_term
        if k:
            work.tick()
    joint[:, span : 2 * span] = key_sum[...].astype(BF)
    joint[:, 2 * span :] = value_sum[...].astype(BF)
    order = list(range(1, peers.chips)) + [0]
    before = None
    for k in order:
        reduce.put(k, dot(joint[chip_rows(peers.behind_chip(k), rows), :], w_qkv[...], 1, 1))
        if before is not None:
            reduce.push(before)
        before = k
    work.tick()
    grads = joint[...]
    for a, b in chunks(width, 512):
        grad_qkv[a:b, :] = dot(normed[:, a:b], grads, 0, 0).astype(BF)
    grad_out[...] = dot(attended[...], full[...].reshape(tokens, width), 0, 0).astype(BF)
    head_sums[...] = jnp.sum(grads.astype(F32), axis=0, keepdims=True)
    part, gain, shift = norm_back(h[...].astype(F32), vec[0:1, :], reduce.total())
    grad_in[...] = (grad_mid[...] + part).astype(BF)
    sums[0:1, :] = gain
    sums[1:2, :] = shift
    sums[2:8, :] = jnp.zeros((6, width), F32)
    work.finish()
    gather.finish()
    reduce.finish()


def call(kernel, name, outs, operands, side, kept, scratch):
    chips = lax.axis_size("section") * lax.axis_size("r")
    rows, width = operands[0].shape
    vmem, hbm = pl.BlockSpec(memory_space=pltpu.VMEM), pl.BlockSpec(memory_space=pl.ANY)
    out = pl.pallas_call(
        kernel,
        out_shape=[jax.ShapeDtypeStruct(*o) for o in (*outs, *side.outs)],
        in_specs=[vmem] * len(operands) + [hbm if i else vmem for i in side.in_hbm],
        out_specs=[hbm if i in kept else vmem for i in range(len(outs))] + [hbm if i else vmem for i in side.out_hbm],
        scratch_shapes=gather_scratch(chips, rows, width) + reduce_scratch(chips, rows, width) + scratch + list(side.scratch),
        compiler_params=pltpu.CompilerParams(collective_id=name, has_side_effects=True, vmem_limit_bytes=60 * 2**20),
    )(*operands, *side.operands)
    return out[: len(outs)], out[len(outs) :]


def run_attention_forward(name, head, side, *operands):
    src, h, w_qkv, w_out, bias, col, row, vec = operands
    rows, width = src.shape
    tokens, span = col.shape[0], w_out.shape[0]
    slots = -(-(span // head) // 8) * 8
    chips = tokens // (2 * rows)
    outs = [
        ((chips, 2, rows, width), BF),
        ((tokens, 3 * span), BF),
        ((tokens, span), BF),
        ((slots, tokens), F32),
        ((rows, width), F32),
        ((rows, width), BF),
    ]
    return call(functools.partial(attention_forward, head, side), name, outs, operands, side, (0,), [pltpu.SemaphoreType.DMA])


def run_feed_forward(name, side, *operands):
    src, mid, w_fc, w_proj, bias, vec, next_vec = operands
    rows, width = src.shape
    units = w_fc.shape[1]
    chips = lax.axis_size("section") * lax.axis_size("r")
    tokens = 2 * chips * rows
    outs = [
        ((chips, 2, rows, width), BF),
        ((tokens, units), BF),
        ((tokens, units), BF),
        ((rows, width), BF),
        ((rows, width), BF),
    ]
    return call(functools.partial(feed_forward, side), name, outs, operands, side, (0,), [pltpu.SemaphoreType.DMA])


def run_feed_backward(name, side, *operands):
    src, mid, w_fc, w_proj, slope, activated, normed_two, vec = operands
    rows, width = src.shape
    tokens, units = slope.shape
    outs = [
        ((rows, width), F32),
        ((rows, width), BF),
        ((units, width), BF),
        ((width, units), BF),
        ((8, width), F32),
        ((1, units), F32),
    ]
    return call(functools.partial(feed_backward, side), name, outs, operands, side, (), [pltpu.VMEM((tokens, units), BF)])


def run_attention_backward(name, head, side, *operands):
    src, grad_mid, h, w_qkv, w_out, qkv, attended, logs, normed, col, row, vec = operands
    rows, width = src.shape
    tokens, span = attended.shape
    outs = [
        ((rows, width), BF),
        ((width, 3 * span), BF),
        ((span, width), BF),
        ((8, width), F32),
        ((1, 3 * span), F32),
    ]
    scratch = [pltpu.VMEM((tokens, 3 * span), BF), pltpu.VMEM((tokens, span), F32), pltpu.VMEM((tokens, span), F32)]
    return call(functools.partial(attention_backward, head, side), name, outs, operands, side, (), scratch)


def start_kernel(ties, block, *refs):
    (tiny, qkv_src, wo_src, fc_src, proj_src), refs = refs[:5], refs[5 + ties :]
    (tiny_out, qkv, wo, fc, proj, qkv_full, w_out), refs = refs[:7], refs[7:]
    stage, qkv_land, wo_land, fc_land, wo_full, nat, land = refs[:7]
    z_send, z_recv, *sems = refs[7:13]
    all_send, all_recv, far_send, far_recv, turn_send, turn_recv, ring_local, ring_send, ring_recv = refs[13:]
    peers = Peers()
    zs, z = lax.axis_size("z"), lax.axis_index("z")
    x, rest = peers.x, peers.rest
    spot = peers.c * rest + peers.r
    peers.greet(zs)
    sent = []

    def send(copy):
        copy.start()
        sent.append(copy)

    for k in range(1, zs):
        send(remote(tiny, stage.at[z], z_send.at[k], z_recv.at[k], {"z": lax.rem(z + k, zs)}))
    stage[z] = tiny[...]
    moves = [(wo_src, wo_land), (qkv_src, qkv_land), (fc_src, fc_land)]
    for a, (src, dst) in enumerate(moves):
        for i, place in peers.offsets():
            device, t = peers.other(*place)
            send(remote(src.at[t], dst.at[x, spot], all_send.at[a, i], all_recv.at[a, i], device))
        if a == 1:
            for k in range(1, zs):
                came = stage.at[lax.rem(z + zs - k, zs)]
                remote(came, came, z_send.at[k], z_recv.at[k], {"z": lax.rem(z + k, zs)}).wait_recv()
            gather = Gather(peers, tiny_out, sems)
            gather.start(stage)
    for d in range(1, peers.sections):
        device, _ = peers.other(d, 0, 0)
        there = lax.rem(x + d, peers.sections)
        send(remote(proj_src.at[there], proj.at[x], far_send.at[d], far_recv.at[d], device))
    _, me = peers.other(0, 0, 0)
    own = []
    for a, (src, dst) in enumerate(moves):
        own.append(pltpu.make_async_copy(src.at[me], dst.at[x, spot], all_recv.at[a, 0]))
    own.append(pltpu.make_async_copy(proj_src.at[x], proj.at[x], far_recv.at[0]))
    for copy in own:
        copy.start()

    def settle(a, shard):
        dst = moves[a][1]
        for i, place in peers.offsets():
            device, _ = peers.other(*(-d for d in place))
            came = dst.at[device["section"], device["dp"] * rest + device["r"]]
            remote(came, came, all_send.at[a, i], all_recv.at[a, i], device).wait_recv()
        own[a].wait()
        for layer in range(peers.sections):
            for i in range(2 * rest):
                shard[layer, i * block : (i + 1) * block, :] = dst[layer, i, :block, :]

    settle(0, wo)
    settle(1, qkv)
    turn = Turn(peers, wo_full, nat, land, w_out, turn_send, turn_recv)
    ring = RingGather([(wo.at[0], wo_full), (qkv.at[0], qkv_full)], ring_local, ring_send, ring_recv)
    work = Both(ring, turn)
    work.start()
    for _ in gather.arrivals():
        pass
    settle(2, fc)
    for d in range(1, peers.sections):
        device, _ = peers.other(-d, 0, 0)
        came = proj.at[device["section"]]
        remote(came, came, far_send.at[d], far_recv.at[d], device).wait_recv()
    own[3].wait()
    work.finish()
    gather.finish()
    for copy in sent:
        copy.wait_send()


def run_start(name, lay, ties, tiny, qkv, wo, fc, proj):
    zs, n, chips = lay.zs, lay.slab, lay.slab // 2
    span = lay.slots * lay.head
    spots = lay.cores * lay.rest
    rows = spots * lay.block
    vmem, hbm = pl.BlockSpec(memory_space=pltpu.VMEM), pl.BlockSpec(memory_space=pl.ANY)
    widths = [a.shape[2] for a in (qkv, wo, fc)]
    outs = [((chips, 2, zs, *tiny.shape), F32)]
    outs += [((lay.sections, rows, m), BF) for m in widths]
    outs += [(proj.shape, BF), ((zs, rows, widths[0]), BF), ((span, lay.width), BF)]
    dma = pltpu.SemaphoreType.DMA
    return pl.pallas_call(
        functools.partial(start_kernel, len(ties), lay.block),
        out_shape=[jax.ShapeDtypeStruct(*o) for o in outs],
        in_specs=[vmem] + [hbm] * (4 + len(ties)),
        out_specs=[vmem] * 5 + [hbm, vmem],
        scratch_shapes=[pltpu.VMEM((zs, *tiny.shape), F32)]
        + [pltpu.VMEM((lay.sections, spots, qkv.shape[1], m), BF) for m in widths]
        + [pltpu.VMEM((zs, rows, widths[1]), BF), pltpu.VMEM((n * span, widths[1]), BF), pltpu.VMEM((n, span, widths[1]), BF)]
        + [dma((zs,))] * 2
        + [dma((chips,))] * 4
        + [dma((3, n))] * 2
        + [dma((lay.sections,))] * 2
        + [dma((n,))] * 2
        + [dma((2,))]
        + [dma((2, zs - 1))] * 2,
        compiler_params=pltpu.CompilerParams(collective_id=name, has_side_effects=True, vmem_limit_bytes=60 * 2**20),
    )(tiny, qkv, wo, fc, proj, *ties)


def end_kernel(sizes, *refs):
    block, width, units, heads = sizes
    (part, turned, qkv_one, wo_one, fc_zero, fc_one, proj_zero, proj_one, small), refs = refs[:9], refs[9:]
    (out_qkv, out_wo, out_fc, out_proj, out_small), refs = refs[:5], refs[5:]
    (qkv_total, wo_part, wo_total, wo_cut, wo_back, proj_both, proj_land), refs = refs[:7], refs[7:]
    stages, lands, refs = refs[:3], refs[3:6], refs[6:]
    (small_land, small_sum, z_land, came_qkv, came_wo), refs = refs[:5], refs[5:]
    all_send, all_recv, far_send, far_recv, z_send, z_recv, turn_send, turn_recv, ring_send, ring_recv, late_send, late_recv = refs
    peers = Peers()
    zs, z = lax.axis_size("z"), lax.axis_index("z")
    x, rest, slab = peers.x, peers.rest, 2 * peers.chips
    spot = peers.c * rest + peers.r
    span, cols = turned.shape[0], wo_total.shape[1]
    half, wide = proj_zero.shape[0], rest * block
    _, me = peers.other(0, 0, 0)
    offsets = peers.offsets()
    peers.greet(zs)
    sent = []

    def send(copy):
        copy.start()
        sent.append(copy)

    ring = RingSum([(part, came_qkv, qkv_total)], ring_send, ring_recv)
    ring.start()
    for t in range(slab):
        wo_cut[t] = turned[:, t * cols : (t + 1) * cols]
    for i, place in offsets:
        device, t = peers.other(*place)
        send(remote(wo_cut.at[t], wo_back.at[me], turn_send.at[i], turn_recv.at[i], device))
    wo_back[me] = wo_cut[me]
    for i, place in offsets:
        device, t = peers.other(*place)
        send(remote(small.at[t], small_land.at[me], all_send.at[3, i], all_recv.at[3, i], device))
    small_land[me] = small[me]

    def cut(a, totals):
        for layer, total in enumerate(totals):
            for i in range(2 * rest):
                stages[a][layer, i, :block, :] = total[i * block : (i + 1) * block, :]
        for i, place in offsets:
            device, t = peers.other(*place)
            src = stages[a].at[device["section"], device["dp"] * rest + device["r"]]
            send(remote(src, lands[a].at[me], all_send.at[a, i], all_recv.at[a, i], device))
        lands[a][me] = stages[a][x, spot]

    def settle(a, land):
        for i, place in offsets:
            device, t = peers.other(*(-d for d in place))
            came = land.at[t]
            remote(came, came, all_send.at[a, i], all_recv.at[a, i], device).wait_recv()

    cut(0, (fc_zero, fc_one))
    proj_both[0] = proj_zero[...]
    proj_both[1] = proj_one[...]
    device, _ = peers.other(1, 0, 0)
    send(remote(proj_both.at[1 - x], proj_land.at[x], far_send, far_recv, device))
    proj_land[x] = proj_both[x]

    for i, place in offsets:
        device, t = peers.other(*(-d for d in place))
        came = wo_back.at[t]
        remote(came, came, turn_send.at[i], turn_recv.at[i], device).wait_recv()
    for c in range(2):
        for k in range(zs):
            at, done = (c * zs + k) * wide, 0
            while done < wide:
                t, row = divmod(at + done, span)
                count = min(wide - done, span - row)
                wo_part[k, c * wide + done : c * wide + done + count, :] = wo_back[t, row : row + count, :]
                done += count
    wo_ring = RingSum([(wo_part, came_wo, wo_total)], late_send, late_recv)
    wo_ring.start()
    settle(3, small_land)
    total = small_land[0]
    for t in range(1, slab):
        total = total + small_land[t]
    small_sum[...] = total
    for k in range(1, zs):
        there = lax.rem(z + k, zs)
        send(remote(small_sum.at[there], z_land.at[z], z_send.at[k], z_recv.at[k], {"z": there}))
    z_land[z] = small_sum[z]
    ring.tick()
    wo_ring.tick()
    settle(0, lands[0])
    for t in range(slab):
        h, c, r = t // (2 * rest), t // rest % 2, t % rest
        for k in range(zs):
            at = ((c * zs + k) * rest + r) * (units // (2 * zs * rest)) + h * half
            out_fc[:, at : at + half] = lands[0][t, :block, k * half : (k + 1) * half].astype(F32)
    ring.tick()
    wo_ring.tick()
    came = proj_land.at[1 - x]
    remote(came, came, far_send, far_recv, device).wait_recv()
    for h in range(2):
        for c in range(2):
            for k in range(zs):
                at, of = (c * zs + k) * wide, (k * 2 + c) * wide
                out_proj[h * half : (h + 1) * half, at : at + wide] = proj_land[h, :, of : of + wide].astype(F32)
    for k in range(1, zs):
        came = z_land.at[lax.rem(z + zs - k, zs)]
        remote(came, came, z_send.at[k], z_recv.at[k], {"z": lax.rem(z + k, zs)}).wait_recv()
    total = z_land[0]
    for k in range(1, zs):
        total = total + z_land[k]
    out_small[...] = total
    wo_ring.finish()
    cut(2, (wo_total, wo_one))
    ring.finish()
    cut(1, (qkv_total, qkv_one))
    settle(2, lands[2])
    for t in range(slab):
        big, off = divmod(t * cols, wide)
        at = (big % 2 * zs + big // 2) * wide + off
        out_wo[:, at : at + cols] = lands[2][t, :block, :].astype(F32)
    settle(1, lands[1])
    for t in range(slab):
        count = min(span, width - t * span)
        for p in range(3):
            if count > 0:
                at = p * width + t * span
                out_qkv[:, at : at + count] = lands[1][t, :block, p * span : p * span + count].astype(F32)
    for copy in sent:
        copy.wait_send()


def run_end(name, lay, part, turned, qkv_one, wo_one, fcs, projs, small):
    zs, n = lay.zs, lay.slab
    span, width, block = lay.slots * lay.head, lay.width, lay.block
    part = part.reshape(zs, part.shape[0] // zs, part.shape[1])
    rows = part.shape[1]
    spots = lay.cores * lay.rest
    tall = -(-block // 16) * 16
    vmem = pl.BlockSpec(memory_space=pltpu.VMEM)
    dma = pltpu.SemaphoreType.DMA
    widths = [fcs[0].shape[1], part.shape[2], lay.cols]
    half = projs[0].shape[0]
    tile = small.shape[2:]
    outs = [(block, 3 * width), (block, width), (block, lay.units), (lay.unit_block, width), tile]
    return pl.pallas_call(
        functools.partial(end_kernel, (block, width, lay.units, lay.slots)),
        out_shape=[jax.ShapeDtypeStruct(o, F32) for o in outs],
        in_specs=[vmem] * 9,
        out_specs=[vmem] * 5,
        scratch_shapes=[
            pltpu.VMEM((rows, part.shape[2]), BF),
            pltpu.VMEM((zs, rows, lay.cols), BF),
            pltpu.VMEM((rows, lay.cols), BF),
            pltpu.VMEM((n, span, lay.cols), BF),
            pltpu.VMEM((n, span, lay.cols), BF),
            pltpu.VMEM((2, half, width), BF),
            pltpu.VMEM((2, half, width), BF),
        ]
        + [pltpu.VMEM((lay.sections, spots, tall, m), BF) for m in widths]
        + [pltpu.VMEM((n, tall, m), BF) for m in widths]
        + [
            pltpu.VMEM((n, zs, *tile), F32),
            pltpu.VMEM((zs, *tile), F32),
            pltpu.VMEM((zs, *tile), F32),
            pltpu.VMEM((zs - 1, rows, part.shape[2]), BF),
            pltpu.VMEM((zs - 1, rows, lay.cols), BF),
        ]
        + [dma((4, n))] * 2
        + [dma] * 2
        + [dma((zs,))] * 2
        + [dma((n,))] * 2
        + [dma((1, zs - 1))] * 4,
        compiler_params=pltpu.CompilerParams(collective_id=name, has_side_effects=True, vmem_limit_bytes=60 * 2**20),
    )(part, turned, qkv_one, wo_one, *fcs, *projs, small)


def weight_parts(lay, w_qkv, w_attn_out, w_fc, w_proj):
    n = lay.slab
    width, block = lay.width, lay.block
    slot_cols = lay.slots * lay.head
    qkv = w_qkv[0].reshape(block, 3, width)
    qkv = jnp.pad(qkv, ((0, 0), (0, 0), (0, n * slot_cols - width)))
    qkv = qkv.reshape(block, 3, n, slot_cols).transpose(2, 0, 1, 3).reshape(n, block, 3 * slot_cols)
    out = lay.order(w_attn_out[0]).reshape(block, n, lay.cols).transpose(1, 0, 2)
    fc = w_fc[0].reshape(block, lay.cores, lay.zs, lay.rest, lay.sections, lay.half)
    fc = fc.transpose(4, 1, 3, 0, 2, 5).reshape(n, block, lay.zs * lay.half)
    proj = lay.order(w_proj[0]).reshape(lay.sections, lay.half, width)

    spare = ((0, 0), (0, -block % 16), (0, 0))
    return jnp.pad(qkv, spare), jnp.pad(out, spare), jnp.pad(fc, spare), proj


def on_device(
    inputs, cotangent, positions, w_qkv, w_attn_out, w_fc, w_proj, norm_gains, biases, fc_bias
):
    lay = Layout(inputs, w_fc)
    n, block, width = lay.slab, lay.block, lay.width
    span = lay.slots * lay.head
    micro = lay.z // lay.seqs

    sources = weight_parts(lay, w_qkv, w_attn_out, w_fc, w_proj)
    h = lay.order(lay.tokens_in(inputs))
    g = lay.order(lay.tokens_in(cotangent))

    per_row = lay.unit_block // block
    thin = jnp.concatenate([norm_gains[0], biases[0], fc_bias[0].reshape(block, per_row)], axis=1)
    thin = jnp.concatenate([thin.reshape(-1).astype(jnp.float32), positions.reshape(-1).astype(jnp.float32)])
    used, spots = block * (8 + per_row), positions.size
    thin = jnp.pad(thin, (0, -thin.size % 1024)).reshape(-1, 128)
    thin, qkv_cut, wo_cut, fc_cut, proj_cut, w_qkv, w_out = run_start(0, lay, (h, g), thin, *sources)
    thin = thin.reshape(lay.sections, lay.rest, lay.cores, lay.zs, -1)
    places = thin[0, :, 0, :, used : used + spots].astype(jnp.int32)
    places = places.reshape(lay.rest, lay.sections, lay.cores, lay.micros, lay.rows)
    places = places.transpose(3, 1, 0, 2, 4).reshape(lay.micros, lay.tokens)
    places = lax.dynamic_slice_in_dim(places, micro, 1, 0)
    col, row = places.reshape(lay.tokens, 1), places
    thin = thin[..., :used].transpose(0, 2, 3, 1, 4).reshape(lay.sections, width, 8 + per_row)
    smalls = []
    for layer in range(lay.sections):
        vec = jnp.stack([thin[layer, :, i] for i in (0, 1, 2, 6, 5, 7)] + [thin[layer, :, 0]] * 2)
        vec = lay.order(vec)
        heads = [
            lax.dynamic_slice_in_dim(
                jnp.pad(thin[layer, :, 2 + i], (0, n * span - width)), lay.t * span, span
            )
            for i in (1, 2)
        ]
        bias = jnp.concatenate([heads[0], jnp.zeros_like(heads[0]), heads[1]])[None]
        unit = thin[layer, :, 8:].reshape(lay.cores, lay.zs, lay.rest, lay.sections, lay.half)
        unit = unit.transpose(3, 0, 2, 1, 4).reshape(n, lay.zs * lay.half)
        unit = lax.dynamic_slice_in_dim(unit, lay.t, 1, 0)
        smalls.append((vec, bias, unit))

    vec = smalls[0][0]
    normed = (norm_parts(h.astype(F32))[0] * vec[0:1] + vec[2:3]).astype(BF)
    outs, keeps, params = [], [], []
    for layer in range(lay.sections):
        last = layer == lay.sections - 1
        vec, bias, unit = smalls[layer]
        w_qkv = w_qkv.reshape(width, 3 * span)
        (full, qkv, attended, logs, mid, normed_two), (w_fc, w_proj) = run_attention_forward(
            1 + 2 * layer,
            lay.head,
            gather_side([fc_cut[layer], proj_cut[layer]]),
            normed,
            h,
            w_qkv,
            w_out,
            bias,
            col,
            row,
            vec,
        )
        w_fc, w_proj = w_fc.reshape(width, -1), w_proj.reshape(-1, width)
        next_vec = smalls[min(layer + 1, lay.sections - 1)][0]
        side = SideWork() if last else gather_side([wo_cut[layer + 1], qkv_cut[layer + 1]], span)
        (full_two, slope, activated, result, normed), later = run_feed_forward(
            2 + 2 * layer, side, normed_two, mid, w_fc, w_proj, unit, vec, next_vec
        )
        params.append((w_qkv, w_out, w_fc, w_proj))
        if not last:
            w_out, w_qkv = later
        keeps.append((h, full, qkv, attended, logs, mid, full_two, slope, activated))
        h = result
        outs.append(h)

    def turned(grad_out):
        wo = grad_out.reshape(span, n, lay.cols).transpose(1, 0, 2)
        wo = lax.all_to_all(wo, SLAB, 0, 0, tiled=True)
        wo = wo.reshape(n * span, lay.cols)[:width].reshape(lay.cores, lay.zs, lay.rest * block, lay.cols)
        return jnp.swapaxes(wo, 0, 1).reshape(width, lay.cols)

    totals = {}
    waiting = []

    def carry(count):
        now = waiting[:count]
        del waiting[:count]
        return [key for key, _ in now], sum_side([part for _, part in now]) if now else SideWork()

    grad_rows, sums = [None] * lay.sections, [None] * lay.sections
    for layer in reversed(range(lay.sections)):
        w_qkv, w_out, w_fc, w_proj = params[layer]
        vec = smalls[layer][0]
        h, full, qkv, attended, logs, mid, full_two, slope, activated = keeps[layer]
        full, full_two = (a.reshape(lay.tokens, width) for a in (full, full_two))
        name = 1 + 4 * lay.sections - 2 * layer
        keys, side = carry(1)
        (grad_mid, attn_rows, grad_proj, grad_fc, feed_sums, unit_sums), done = run_feed_backward(
            name, side, g, mid, w_fc, w_proj, slope, activated, full_two, vec
        )
        totals.update(zip(keys, done))
        waiting = [(("proj", layer), grad_proj), (("fc", layer), grad_fc)] + waiting
        keys, side = carry(3)
        (g, grad_qkv, grad_out, attn_sums, head_sums), done = run_attention_backward(
            name + 1, lay.head, side, attn_rows, grad_mid, h, w_qkv, w_out, qkv, attended, logs, full, col, row, vec
        )
        totals.update(zip(keys, done))
        if layer:
            waiting = waiting + [(("qkv", layer), grad_qkv), (("out", layer), turned(grad_out))]
        grad_rows[layer] = g
        sums[layer] = (feed_sums, unit_sums, attn_sums, head_sums)
    section_out = lay.tokens_out([lay.restore(a) for a in outs])
    section_grad = lay.tokens_out([lay.restore(a) for a in grad_rows])

    rows = []
    for layer in range(lay.sections):
        feed_sums, unit_sums, attn_sums, head_sums = sums[layer]
        feed_sums, attn_sums = lay.restore(feed_sums), lay.restore(attn_sums)
        zero = jnp.zeros((n * span,), jnp.float32)
        s_q = lax.dynamic_update_slice_in_dim(zero, head_sums[0, :span], lay.t * span, 0)[:width]
        s_v = lax.dynamic_update_slice_in_dim(zero, head_sums[0, 2 * span :], lay.t * span, 0)[:width]
        cols = [attn_sums[0], feed_sums[0], attn_sums[1], s_q, s_v, feed_sums[3], feed_sums[1], feed_sums[2]]
        cols = jnp.stack(cols, axis=1).reshape(lay.shards, block * 8)
        spots = jnp.zeros((n, lay.zs, lay.half), jnp.float32)
        spots = lax.dynamic_update_index_in_dim(
            spots, unit_sums.reshape(lay.zs, lay.half), lay.t, 0
        )
        spots = spots.reshape(lay.sections, lay.cores, lay.rest, lay.zs, lay.half)
        spots = spots.transpose(1, 3, 2, 0, 4).reshape(lay.shards, lay.unit_block)
        rows.append(jnp.concatenate([cols, spots], axis=1))
    rows = jnp.stack(rows).reshape(lay.sections, lay.cores, lay.zs, lay.rest, -1)
    used = rows.shape[-1]
    rows = jnp.pad(jnp.swapaxes(rows, 2, 3), ((0, 0),) * 4 + ((0, -used % 1024),))
    rows = rows.reshape(n, lay.zs, -1, 128)
    out_qkv, out_attn, out_fc, out_proj, rows = run_end(
        3 + 4 * lay.sections,
        lay,
        grad_qkv,
        grad_out,
        totals["qkv", 1],
        totals["out", 1],
        [totals["fc", layer] for layer in range(2)],
        [totals["proj", layer] for layer in range(2)],
        rows,
    )
    rows = rows.reshape(-1)[:used]
    cols = rows[: block * 8].reshape(block, 8)
    return (
        section_out,
        section_grad,
        out_qkv[None],
        out_attn[None],
        out_fc[None],
        out_proj[None],
        cols[None, :, :2],
        cols[None, :, 2:],
        rows[None, block * 8 :],
    )


def solution(mesh):
    sections, cores, contexts = (mesh.shape[a] for a in ("section", "dp", "ctx"))
    zs = sections * cores
    shape = (sections, cores, zs, contexts // zs)
    inner = Mesh(mesh.devices.reshape(shape), ALL)
    tokens = P(None, "dp", ("z", "r"), None)
    rows = P("section", ("dp", "z", "r"), None)
    units = P("section", ("dp", "z", "r"))
    out_tokens = P("section", None, "dp", ("z", "r"), None)
    return jax.shard_map(
        on_device,
        mesh=inner,
        in_specs=(tokens, tokens, P(None, ("z", "r"))) + (rows,) * 6 + (units,),
        out_specs=(out_tokens, out_tokens) + (rows,) * 6 + (units,),
        check_vma=False,
    )
```

```python
import functools

import jax
import jax.numpy as jnp
from jax import lax
from jax.experimental import pallas as pl
from jax.experimental.pallas import tpu as pltpu
from jax.sharding import Mesh
from jax.sharding import PartitionSpec as P

HEADS = 25
EPSILON = 1e-05

SLAB = ("section", "dp", "r")
ALL = ("section", "dp", "z", "r")
MESH = pl.DeviceIdType.MESH


class Layout:
    def __init__(self, inputs, w_fc):
        self.micros, _, self.rows, self.width = inputs.shape
        self.sections = lax.axis_size("section")
        self.cores = lax.axis_size("dp")
        self.zs = lax.axis_size("z")
        self.rest = lax.axis_size("r")
        self.slab = self.sections * self.cores * self.rest
        self.shards = self.cores * self.zs * self.rest
        self.units = w_fc.shape[2]
        self.tokens = self.rows * self.slab
        self.seqs = self.cores
        self.head = self.width // HEADS
        self.slots = -(-HEADS // self.slab)
        self.block = self.width // self.shards
        self.unit_block = self.units // self.shards
        self.half = self.unit_block // self.sections
        self.cols = self.width // self.slab
        self.x = lax.axis_index("section")
        self.c = lax.axis_index("dp")
        self.z = lax.axis_index("z")
        self.r = lax.axis_index("r")
        self.t = (self.x * self.cores + self.c) * self.rest + self.r

    def number(self, x, c, z, r):
        return ((x * self.cores + c) * self.zs + z) * self.rest + r

    def order(self, a):
        lead = a.shape[:-1]
        a = a.reshape(*lead, self.cores, self.zs, self.rest * self.block)
        return jnp.swapaxes(a, -3, -2).reshape(*lead, self.width)

    def restore(self, a):
        lead = a.shape[:-1]
        a = a.reshape(*lead, self.zs, self.cores, self.rest * self.block)
        return jnp.swapaxes(a, -3, -2).reshape(*lead, self.width)

    def routes(self, micro):
        pairs = []
        for x in range(self.sections):
            for c in range(self.cores):
                for s in range(self.seqs):
                    for r in range(self.rest):
                        place = x * self.cores + c
                        pairs.append(((x, s, place, r), (x, c, micro * self.seqs + s, r)))
        return pairs

    def tokens_in(self, a):
        got = []
        for micro in range(self.micros):
            route = [(self.number(*f), self.number(*g)) for f, g in self.routes(micro)]
            got.append(lax.ppermute(a[micro, 0], ALL, route))
        out = got[0]
        for micro in range(1, self.micros):
            out = jnp.where(self.z // self.seqs == micro, got[micro], out)
        return out

    def tokens_out(self, parts):
        result = []
        for micro in range(self.micros):
            got = []
            for layer, part in enumerate(parts):
                route = [
                    (self.number(*g), self.number(layer, *f[1:])) for f, g in self.routes(micro)
                ]
                got.append(lax.ppermute(part, ALL, route))
            out = got[0]
            for layer in range(1, len(parts)):
                out = jnp.where(self.x == layer, got[layer], out)
            result.append(out)
        return jnp.stack(result)[None, :, None]


LOW = -1e30
BF = jnp.bfloat16
F32 = jnp.float32


class Peers:
    def __init__(self):
        self.sections, self.rest = lax.axis_size("section"), lax.axis_size("r")
        self.chips = self.sections * self.rest
        self.x, self.c, self.r = (lax.axis_index(a) for a in ("section", "dp", "r"))
        self.chip = self.x * self.rest + self.r

    def away(self, k, sign):
        x = lax.rem(self.x + self.sections + sign * (k // self.rest), self.sections)
        r = lax.rem(self.r + self.rest + sign * (k % self.rest), self.rest)
        return x, r

    def ahead(self, k):
        x, r = self.away(k, 1)
        return {"section": x, "dp": self.c, "r": r}

    def behind(self, k):
        x, r = self.away(k, -1)
        return {"section": x, "dp": self.c, "r": r}

    def sibling(self):
        return {"section": self.x, "dp": 1 - self.c, "r": self.r}

    def behind_chip(self, k):
        x, r = self.away(k, -1)
        return x * self.rest + r

    def other(self, dx, dc, dr):
        x = lax.rem(self.x + self.sections + dx, self.sections)
        c = lax.rem(self.c + 2 + dc, 2)
        r = lax.rem(self.r + self.rest + dr, self.rest)
        return {"section": x, "dp": c, "r": r}, (x * 2 + c) * self.rest + r

    def offsets(self):
        every = [(x, c, r) for x in range(self.sections) for c in range(2) for r in range(self.rest)]
        return list(enumerate(every))[1:]

    def greet(self, zs=1, work=None):
        barrier = pltpu.get_barrier_semaphore()
        z = lax.axis_index("z")
        size = lax.axis_size("z")
        for k in range(1, zs):
            pl.semaphore_signal(barrier, inc=1, device_id={"z": lax.rem(z + size - k, size)}, device_id_type=MESH)
        others = self.offsets()
        for _, place in others:
            pl.semaphore_signal(barrier, inc=1, device_id=self.other(*place)[0], device_id_type=MESH)
        more = 0 if work is None else work.greet()
        pl.semaphore_wait(barrier, len(others) + zs - 1 + more)


def remote(src, dst, send, recv, device):
    return pltpu.make_async_remote_copy(
        src_ref=src, dst_ref=dst, send_sem=send, recv_sem=recv, device_id=device, device_id_type=MESH
    )


class Gather:
    def __init__(self, peers, full, sems):
        self.peers, self.full = peers, full
        self.chip_send, self.chip_recv, self.core_send, self.core_recv = sems
        self.sent = []

    def start(self, src):
        p = self.peers
        mine = self.full.at[p.chip, p.c]
        mine[...] = src if isinstance(src, jax.Array) else src[...]
        for k in range(1, p.chips):
            self.send(remote(mine, mine, self.chip_send.at[k], self.chip_recv.at[k], p.ahead(k)))
        self.send(remote(mine, mine, self.core_send.at[0], self.core_recv.at[0], p.sibling()))

    def send(self, copy):
        copy.start()
        self.sent.append(copy)

    def forward(self, k):
        p = self.peers
        block = self.full.at[p.behind_chip(k), p.c]
        remote(block, block, self.chip_send.at[k], self.chip_recv.at[k], p.sibling()).wait_recv()
        self.send(remote(block, block, self.core_send.at[k], self.core_recv.at[k], p.sibling()))

    def chip(self, k):
        p = self.peers
        block = self.full.at[p.behind_chip(k), 1 - p.c]
        remote(block, block, self.core_send.at[k], self.core_recv.at[k], p.sibling()).wait_recv()
        return p.behind_chip(k)

    def arrivals(self):
        yield 0, self.chip(0)
        chips = self.peers.chips
        for k in range(1, chips):
            for later in (1, 2) if k == 1 else (k + 1,):
                if later < chips:
                    self.forward(later)
            yield k, self.chip(k)

    def finish(self):
        for copy in self.sent:
            copy.wait_send()


class Reduce:
    def __init__(self, peers, mine, stage, other, going, coming, sems):
        self.peers = peers
        self.mine, self.stage, self.other, self.going, self.coming = mine, stage, other, going, coming
        self.chip_send, self.chip_recv, self.core_send, self.core_recv = sems
        self.sent = []

    def send(self, copy):
        copy.start()
        self.sent.append(copy)

    def put(self, k, both):
        p = self.peers
        rows = both.shape[0] // 2
        low, high = both[:rows], both[rows:]
        first = p.c == 0
        self.mine[k] = jnp.where(first, low, high)
        self.stage[k] = jnp.where(first, high, low).astype(BF)
        self.send(remote(self.stage.at[k], self.other.at[k], self.core_send.at[k], self.core_recv.at[k], p.sibling()))

    def arrived(self, k):
        p = self.peers
        remote(self.stage.at[k], self.other.at[k], self.core_send.at[k], self.core_recv.at[k], p.sibling()).wait_recv()
        return self.mine[k] + self.other[k].astype(F32)

    def push(self, k):
        p = self.peers
        if k:
            self.going[k - 1] = self.arrived(k).astype(BF)
            self.send(remote(self.going.at[k - 1], self.coming.at[k - 1], self.chip_send.at[k], self.chip_recv.at[k], p.behind(k)))

    def total(self):
        p = self.peers
        out = self.arrived(0)
        for k in range(1, p.chips):
            remote(self.going.at[k - 1], self.coming.at[k - 1], self.chip_send.at[k], self.chip_recv.at[k], p.sibling()).wait_recv()
            out = out + self.coming[k - 1].astype(F32)
        return out

    def finish(self):
        for copy in self.sent:
            copy.wait_send()


class RingGather:
    def greet(self):
        return 0

    def __init__(self, pieces, local, send, recv):
        self.pieces, self.local, self.send_sem, self.recv_sem = pieces, local, send, recv
        self.zs, self.z = lax.axis_size("z"), lax.axis_index("z")
        self.steps = [(p, s) for s in range(self.zs - 1) for p in range(len(pieces)) if s < pieces[p][2]]
        self.sent = []

    def block(self, step):
        return lax.rem(self.z + self.zs - step, self.zs)

    def send(self, p, step, src):
        dst = self.pieces[p][1].at[self.block(step)]
        copy = remote(src, dst, self.send_sem.at[p, step], self.recv_sem.at[p, step], {"z": lax.rem(self.z + 1, self.zs)})
        copy.start()
        self.sent.append(copy)

    def start(self):
        for p, (shard, full, _) in enumerate(self.pieces):
            self.send(p, 0, shard)
            pltpu.make_async_copy(shard, full.at[self.z], self.local.at[p]).start()

    def tick(self):
        if not self.steps:
            return None
        p, step = self.steps.pop(0)
        shard, full, count = self.pieces[p]
        block = full.at[self.block(step + 1)]
        remote(block, block, self.send_sem.at[p, step], self.recv_sem.at[p, step], {"z": lax.rem(self.z + 1, self.zs)}).wait_recv()
        if step < count - 1:
            self.send(p, step + 1, block)
            return None
        pltpu.make_async_copy(shard, full.at[self.z], self.local.at[p]).wait()
        return p

    def finish(self):
        while self.steps:
            self.tick()
        for copy in self.sent:
            copy.wait_send()


class RingSum:
    def greet(self):
        return 0

    def __init__(self, pieces, send, recv):
        self.pieces, self.send_sem, self.recv_sem = pieces, send, recv
        self.zs, self.z = lax.axis_size("z"), lax.axis_index("z")
        self.steps, self.sent = [], []
        self.late = [p for p, piece in enumerate(pieces) if piece[0] is None]
        ready = [p for p in range(len(pieces)) if p not in self.late]
        self.steps = [(p, i) for i in range(self.zs - 1) for p in ready if i < pieces[p][5] - 1]
        self.steps += [(p, pieces[p][5] - 1) for p in ready]
        self.parts = [piece[0] for piece in pieces]

    def copy(self, p, i, src):
        dst = self.pieces[p][2].at[i]
        return remote(src, dst, self.send_sem.at[p, i], self.recv_sem.at[p, i], {"z": lax.rem(self.z + 1, self.zs)})

    def send(self, p, i, src):
        copy = self.copy(p, i, src)
        copy.start()
        self.sent.append(copy)

    def launch(self, p):
        acc, first = self.pieces[p][1], self.pieces[p][4]
        self.send(p, 0, acc if first else self.parts[p].at[lax.rem(self.z + self.zs - 1, self.zs)])

    def start(self):
        for p in range(len(self.pieces)):
            if p not in self.late:
                self.launch(p)

    def made(self, part):
        if self.late:
            p = self.late.pop(0)
            self.parts[p] = part
            self.launch(p)
            self.steps += [(p, i) for i in range(self.pieces[p][5])]

    def tick(self):
        if not self.steps:
            return
        p, i = self.steps.pop(0)
        part, acc, came, out, first, count = self.pieces[p]
        self.copy(p, i, came.at[i]).wait_recv()
        own = self.parts[p][lax.rem(self.z + 2 * self.zs - 2 - first - i, self.zs)]
        total = (came[i].astype(F32) + own.astype(F32)).astype(BF)
        if i < count - 1:
            came[i] = total
            self.send(p, i + 1, came.at[i])
        else:
            out[...] = total

    def middle(self):
        pass

    def finish(self):
        while self.steps:
            self.tick()
        for copy in self.sent:
            copy.wait_send()


class TurnBack:
    def __init__(self, peers, turned, part, pieces, came, send, recv):
        self.peers, self.turned, self.part, self.pieces, self.came = peers, turned, part, pieces, came
        self.send_sem, self.recv_sem = send, recv
        self.sent = []

    def start(self):
        slab, _, cols = self.pieces.shape
        for t in range(slab):
            self.pieces[t] = self.turned[:, t * cols : (t + 1) * cols]
        _, me = self.peers.other(0, 0, 0)
        for i, place in self.peers.offsets():
            device, t = self.peers.other(*place)
            copy = remote(self.pieces.at[t], self.came.at[me], self.send_sem.at[i], self.recv_sem.at[i], device)
            copy.start()
            self.sent.append(copy)
        self.came[me] = self.pieces[me]

    def finish(self):
        for i, place in self.peers.offsets():
            device, t = self.peers.other(*(-d for d in place))
            block = self.came.at[t]
            remote(block, block, self.send_sem.at[i], self.recv_sem.at[i], device).wait_recv()
        zs, rows, _ = self.part.shape
        wide, span = rows // 2, self.came.shape[1]
        for c in range(2):
            for k in range(zs):
                at, done = (c * zs + k) * wide, 0
                while done < wide:
                    t, row = divmod(at + done, span)
                    count = min(wide - done, span - row)
                    self.part[k, c * wide + done : c * wide + done + count, :] = self.came[t, row : row + count, :]
                    done += count
        for copy in self.sent:
            copy.wait_send()


class SumAndTurn:
    def greet(self):
        return 0

    def __init__(self, ring, turn):
        self.ring, self.turn = ring, turn
        self.start, self.tick, self.made = ring.start, ring.tick, ring.made

    def middle(self):
        self.turn.start()

    def finish(self):
        self.turn.finish()
        self.ring.finish()


class Turn:
    def __init__(self, peers, full, nat, land, w_out, send, recv):
        self.peers, self.full, self.nat, self.land, self.w_out = peers, full, nat, land, w_out
        self.send_sem, self.recv_sem = send, recv
        self.sent = []

    def start(self):
        zs, rows, cols = self.full.shape
        part, span = rows // 2, self.w_out.shape[0]
        for c in range(2):
            for z in range(zs):
                at = (c * zs + z) * part
                self.nat[at : at + part, :] = self.full[z, c * part : (c + 1) * part, :]
        used = zs * rows
        if used < self.nat.shape[0]:
            self.nat[used:, :] = jnp.zeros((self.nat.shape[0] - used, cols), BF)
        _, me = self.peers.other(0, 0, 0)
        for i, place in self.peers.offsets():
            device, t = self.peers.other(*place)
            src = self.nat.at[pl.ds(pl.multiple_of(t * span, span), span)]
            copy = remote(src, self.land.at[me], self.send_sem.at[i], self.recv_sem.at[i], device)
            copy.start()
            self.sent.append(copy)
        self.land[me] = self.nat[pl.ds(pl.multiple_of(me * span, span), span), :]

    def finish(self):
        for i, place in self.peers.offsets():
            device, t = self.peers.other(*(-d for d in place))
            block = self.land.at[t]
            remote(block, block, self.send_sem.at[i], self.recv_sem.at[i], device).wait_recv()
        slab, _, cols = self.land.shape
        for t in range(slab):
            self.w_out[:, t * cols : (t + 1) * cols] = self.land[t]
        for copy in self.sent:
            copy.wait_send()


class Route:
    def __init__(self, layer, seqs, src, out, local, send, recv):
        self.layer, self.seqs, self.src, self.out = layer, seqs, src, out
        self.local, self.send_sem, self.recv_sem = local, send, recv
        x, c, z = (lax.axis_index(a) for a in ("section", "dp", "z"))
        self.here = x == layer
        place = x * 2 + c
        self.to = {"section": layer, "dp": lax.rem(z, seqs), "z": place}
        self.micro = z // seqs
        self.same = (x == layer) & (lax.rem(z, seqs) == c) & (place == z)
        self.sources = []
        for micro in range(out.shape[0]):
            src_x, src_c, src_z = z // 2, lax.rem(z, 2), micro * seqs + c
            same = (src_x == x) & (src_c == c) & (src_z == z)
            self.sources.append(({"section": src_x, "dp": src_c, "z": src_z}, same))

    def greet(self):
        barrier = pltpu.get_barrier_semaphore()
        for device, same in self.sources:

            @pl.when(self.here & jnp.logical_not(same))
            def _(device=device):
                pl.semaphore_signal(barrier, inc=1, device_id=device, device_id_type=MESH)

        return jnp.where(self.same, 0, 1)

    def copy(self):
        return remote(self.src, self.out.at[self.micro], self.send_sem, self.recv_sem.at[self.micro], self.to)

    def own(self):
        return pltpu.make_async_copy(self.src, self.out.at[self.micro], self.local)

    def start(self):
        @pl.when(jnp.logical_not(self.same))
        def _():
            self.copy().start()

        @pl.when(self.same)
        def _():
            self.own().start()

    def tick(self):
        pass

    def made(self, part):
        pass

    def middle(self):
        pass

    def finish(self):
        for micro, (device, same) in enumerate(self.sources):

            @pl.when(self.here & jnp.logical_not(same))
            def _(micro=micro, device=device):
                block = self.out.at[micro]
                remote(block, block, self.send_sem, self.recv_sem.at[micro], device).wait_recv()

        @pl.when(jnp.logical_not(self.same))
        def _():
            self.copy().wait_send()

        @pl.when(self.same)
        def _():
            self.own().wait()


class Several:
    def __init__(self, works):
        self.works = works

    def greet(self):
        return sum(work.greet() for work in self.works)

    def start(self):
        for work in self.works:
            work.start()

    def tick(self):
        for work in self.works:
            work.tick()

    def made(self, part):
        for work in self.works:
            work.made(part)

    def middle(self):
        for work in self.works:
            work.middle()

    def finish(self):
        for work in self.works:
            work.finish()


class NoSide:
    def greet(self):
        return 0

    def start(self):
        pass

    def tick(self):
        pass

    def made(self, part):
        pass

    def middle(self):
        pass

    def finish(self):
        pass


class Both:
    def greet(self):
        return 0

    def __init__(self, ring, turn):
        self.ring, self.turn, self.turned = ring, turn, False

    def start(self):
        self.ring.start()

    def tick(self):
        if self.ring.tick() == 0:
            self.turn.start()

    def finish(self):
        while self.ring.steps:
            self.tick()
        self.ring.finish()
        self.turn.finish()


class SideWork:
    def __init__(self, operands=(), in_hbm=(), outs=(), out_hbm=(), scratch=(), build=None):
        self.operands, self.in_hbm, self.outs, self.out_hbm = operands, in_hbm, outs, out_hbm
        self.scratch, self.build = scratch, build
        self.zs = 1 if build is None else 2

    def make(self, peers, ins, outs, scratch):
        return NoSide() if self.build is None else self.build(peers, ins, outs, scratch)


def route_side(layer, lay, src):
    dma = pltpu.SemaphoreType.DMA
    outs = [((lay.micros, *src.shape), BF)]

    def build(peers, ins, outs, scratch):
        return Route(layer, lay.seqs, ins[0], outs[0], *scratch)

    return SideWork([src], (True,), outs, (True,), [dma, dma, dma((lay.micros,))], build)


def both_sides(*sides):
    sides = [side for side in sides if side.build is not None]
    joined = [[], [], [], [], []]
    for side in sides:
        for into, more in zip(joined, (side.operands, side.in_hbm, side.outs, side.out_hbm, side.scratch)):
            into += list(more)

    def build(peers, ins, outs, scratch):
        works = []
        for side in sides:
            a, b, c = len(side.operands), len(side.outs), len(side.scratch)
            works.append(side.build(peers, ins[:a], outs[:b], scratch[:c]))
            ins, outs, scratch = ins[a:], outs[b:], scratch[c:]
        return Several(works)

    return SideWork(*joined, build)


def gather_side(shards, counts=None, turn=None):
    zs = lax.axis_size("z")
    n = len(shards)
    counts = counts or (zs - 1,) * n
    outs = [((zs, *a.shape), BF) for a in shards]
    sems = [pltpu.SemaphoreType.DMA((n,))] + [pltpu.SemaphoreType.DMA((n, zs - 1))] * 2
    if turn is None:

        def build(peers, ins, outs, scratch):
            return RingGather(list(zip(ins, outs, counts)), *scratch)

        return SideWork(shards, (True,) * n, outs, (True,) * n, sems, build)
    slab = 2 * lax.axis_size("section") * lax.axis_size("r")
    cols = shards[0].shape[1]
    outs[0] = ((turn, slab * cols), BF)
    more = [
        pltpu.VMEM((zs, *shards[0].shape), BF),
        pltpu.VMEM((slab * turn, cols), BF),
        pltpu.VMEM((slab, turn, cols), BF),
    ] + [pltpu.SemaphoreType.DMA((slab,))] * 2

    def build_turn(peers, ins, outs, scratch):
        pieces = list(zip(ins, [scratch[3], *outs[1:]], counts))
        return Both(RingGather(pieces, *scratch[:3]), Turn(peers, scratch[3], scratch[4], scratch[5], outs[0], *scratch[6:8]))

    return SideWork(shards, (True,) * n, outs, (False,) + (True,) * (n - 1), sems + more, build_turn)


def sum_side(pieces, turned=None, cols=0):
    zs = lax.axis_size("z")
    n = len(pieces)
    operands, outs, scratch = [], [], []
    for part, shape, acc, first, count in pieces:
        operands += [a for a in (part, acc) if a is not None]
        outs.append((shape, BF))
        scratch.append(pltpu.VMEM((count, *shape), BF))
    scratch += [pltpu.SemaphoreType.DMA((n, zs - 1))] * 2
    if turned is not None:
        operands.append(turned)
        slab = turned.shape[1] // cols
        rows = turned.shape[1] // zs
        outs.append(((zs, rows, cols), BF))
        scratch += [pltpu.VMEM((slab, turned.shape[0], cols), BF)] * 2 + [pltpu.SemaphoreType.DMA((slab,))] * 2

    def build(peers, ins, outs, scratch):
        ins, made = list(ins), []
        for i, (part, shape, acc, first, count) in enumerate(pieces):
            part_ref = None if part is None else ins.pop(0)
            acc_ref = None if acc is None else ins.pop(0)
            made.append((part_ref, acc_ref, scratch[i], outs[i], first, count))
        ring = RingSum(made, *scratch[n : n + 2])
        if turned is None:
            return ring
        return SumAndTurn(ring, TurnBack(peers, ins.pop(0), outs[n], *scratch[n + 2 :]))

    return SideWork(operands, (False,) * len(operands), outs, (False,) * len(outs), scratch, build)


def gather_scratch(chips, rows, width):
    return [pltpu.VMEM((chips, 2, rows, width), BF)] + [pltpu.SemaphoreType.DMA((chips,))] * 4


def reduce_scratch(chips, rows, width):
    return [
        pltpu.VMEM((chips, rows, width), F32),
        pltpu.VMEM((chips, rows, width), BF),
        pltpu.VMEM((chips, rows, width), BF),
        pltpu.VMEM((chips - 1, rows, width), BF),
        pltpu.VMEM((chips - 1, rows, width), BF),
    ] + [pltpu.SemaphoreType.DMA((chips,))] * 4


def norm_parts(v):
    centred = v - jnp.mean(v, axis=-1, keepdims=True)
    spread = jnp.mean(centred * centred, axis=-1, keepdims=True)
    scale = lax.rsqrt(spread + EPSILON)
    return centred * scale, scale


def norm_back(v, gain, grad):
    unit, scale = norm_parts(v)
    scaled = grad * gain
    part = scaled - jnp.mean(scaled, axis=-1, keepdims=True)
    part = part - unit * jnp.mean(scaled * unit, axis=-1, keepdims=True)
    return part * scale, jnp.sum(grad * unit, axis=0, keepdims=True), jnp.sum(grad, axis=0, keepdims=True)


def dot(a, b, ca=1, cb=0):
    return lax.dot_general(a, b, (((ca,), (cb,)), ((), ())), preferred_element_type=F32)


def chip_rows(chip, rows):
    return pl.ds(pl.multiple_of(chip * (2 * rows), 2 * rows), 2 * rows)


def groups(span, head):
    wide = 128 if span % 128 == 0 else span
    for g in range(span // wide):
        yield slice(g * wide, (g + 1) * wide), [(g * wide // head + i, i * head) for i in range(wide // head)]


def only(a, start, head):
    lane = lax.broadcasted_iota(jnp.int32, a.shape, 1)
    return jnp.where((lane >= start) & (lane < start + head), a, jnp.zeros_like(a))


def attention_forward(head, side, *refs):
    (h, w_qkv, w_out, bias, col, row, vec) = refs[:7]
    ins, refs = refs[7 : 7 + len(side.operands)], refs[7 + len(side.operands) :]
    (normed, qkv, attended, logs, mid, normed_two), refs = refs[:6], refs[6:]
    side_outs, refs = refs[: len(side.outs)], refs[len(side.outs) :]
    gather_refs, reduce_refs, side_refs = refs[:5], refs[5 : 14 + 1], refs[14 + 1 :]
    rows, width = h.shape
    span = w_out.shape[0]
    peers = Peers()
    gather = Gather(peers, gather_refs[0], gather_refs[1:])
    reduce = Reduce(peers, *reduce_refs[:5], reduce_refs[5:9])
    kept_sem = reduce_refs[9]
    full = gather.full
    work = side.make(peers, ins, side_outs, side_refs)
    peers.greet(side.zs, work)
    gather.start((norm_parts(h[...].astype(F32))[0] * vec[0:1, :] + vec[2:3, :]).astype(BF))
    work.start()
    for k, chip in gather.arrivals():
        part = dot(full[chip].reshape(2 * rows, width), w_qkv[...]) + bias[...]
        qkv[chip_rows(chip, rows), :] = part.astype(BF)
    work.tick()
    kept = pltpu.make_async_copy(full, normed, kept_sem)
    kept.start()
    scale = head ** (-0.5)
    order = list(range(1, peers.chips)) + [0]
    before = None
    for k in order:
        chip = peers.behind_chip(k)
        here = chip_rows(chip, rows)
        block = jnp.where(col[...] <= row[:, here], 0.0, LOW).astype(F32)
        for lanes, heads in groups(span, head):
            q = qkv[here, lanes]
            keys = qkv[:, slice(span + lanes.start, span + lanes.stop)]
            values = qkv[:, slice(2 * span + lanes.start, 2 * span + lanes.stop)]
            merged = None
            for slot, start in heads:
                scores = dot(keys, only(q, start, head) * scale, 1, 1) + block
                top = jnp.max(scores, axis=0, keepdims=True)
                weights = jnp.exp(scores - top)
                total = jnp.sum(weights, axis=0, keepdims=True)
                logs[slot : slot + 1, here] = top + jnp.log(total)
                mixed = dot(values, weights.astype(BF), 0, 0) / total
                lane = lax.broadcasted_iota(jnp.int32, mixed.shape, 0)
                merged = mixed if merged is None else jnp.where(lane >= start, mixed, merged)
            attended[here, lanes] = merged.T.astype(BF)
        reduce.put(k, dot(attended[here, :], w_out[...]))
        if before is not None:
            reduce.push(before)
        work.tick()
        before = k
    reduce.push(before)
    out = h[...].astype(F32) + (reduce.total() + vec[4:5, :])
    mid[...] = out
    normed_two[...] = (norm_parts(out)[0] * vec[1:2, :] + vec[3:4, :]).astype(BF)
    work.finish()
    gather.finish()
    reduce.finish()
    kept.wait()


ROOT = 0.7978845608028654


def feed_forward(side, *refs):
    (src, mid, w_fc, w_proj, bias, vec) = refs[:6]
    ins, refs = refs[6 : 6 + len(side.operands)], refs[6 + len(side.operands) :]
    (normed_two, slope, activated, result, proj_out), refs = refs[:5], refs[5:]
    side_outs, refs = refs[: len(side.outs)], refs[len(side.outs) :]
    gather_refs, reduce_refs, side_refs = refs[:5], refs[5 : 14 + 6], refs[14 + 6 :]
    rows, width = src.shape
    peers = Peers()
    gather = Gather(peers, gather_refs[0], gather_refs[1:])
    reduce = Reduce(peers, *reduce_refs[:5], reduce_refs[5:9])
    kept_sem, proj, proj_local, proj_send, proj_recv, proj_sem = reduce_refs[9:15]
    full = gather.full
    work = side.make(peers, ins, side_outs, side_refs)
    zs, z = lax.axis_size("z"), lax.axis_index("z")
    half = proj.shape[1]
    peers.greet(2, work)
    gather.start(src)
    there = lax.rem(z + 2, zs)
    last = remote(w_proj.at[there], proj.at[there], proj_send, proj_recv, {"z": lax.rem(z + 1, zs)})
    last.start()
    here = [lax.rem(z + zs - i, zs) for i in range(zs - 1)]
    placed = [pltpu.make_async_copy(w_proj.at[b], proj.at[b], proj_local.at[i]) for i, b in enumerate(here)]
    for copy in placed:
        copy.start()
    before = None
    for k, chip in gather.arrivals():
        if k == 0:
            last.wait_recv()
            work.start()
            for copy in placed:
                copy.wait()
            proj_kept = pltpu.make_async_copy(proj, proj_out, proj_sem)
            proj_kept.start()
        here = chip_rows(chip, rows)
        u = dot(full[chip].reshape(2 * rows, width), w_fc[...]) + bias[...]
        bend = jnp.tanh(ROOT * (u + 0.044715 * (u * u * u)))
        slope[here, :] = (0.5 * (1.0 + bend) + 0.5 * u * (1.0 - bend * bend) * (ROOT * (1.0 + 3 * 0.044715 * (u * u)))).astype(BF)
        act = (0.5 * u * (1.0 + bend)).astype(BF)
        activated[here, :] = act
        back = dot(act[:, :half], proj[0])
        for b in range(1, zs):
            back = back + dot(act[:, b * half : (b + 1) * half], proj[b])
        reduce.put(k, back)
        if before is not None:
            reduce.push(before)
        if k == peers.chips - 1:
            work.tick()
        before = k
    kept = pltpu.make_async_copy(full, normed_two, kept_sem)
    kept.start()
    reduce.push(before)
    work.tick()
    out = (mid[...] + (reduce.total() + vec[5:6, :])).astype(BF)
    result[...] = out
    last.wait_send()
    proj_kept.wait()
    work.finish()
    gather.finish()
    reduce.finish()
    kept.wait()


def chunks(size, step):
    return [(a, min(a + step, size)) for a in range(0, size, step)]


def feed_backward(side, *refs):
    (src, mid, w_fc, w_proj, slope, activated, normed_two, vec) = refs[:8]
    ins, refs = refs[8 : 8 + len(side.operands)], refs[8 + len(side.operands) :]
    (grad_mid, attn_rows, grad_proj, grad_fc, sums, unit_sums), refs = refs[:6], refs[6:]
    side_outs, refs = refs[: len(side.outs)], refs[len(side.outs) :]
    gather_refs, reduce_refs, side_refs = refs[:5], refs[5 : 14 + 1], refs[14 + 1 :]
    hidden, = reduce_refs[9:10]
    rows, width = src.shape
    tokens = slope.shape[0]
    peers = Peers()
    gather = Gather(peers, gather_refs[0], gather_refs[1:])
    reduce = Reduce(peers, *reduce_refs[:5], reduce_refs[5:9])
    full = gather.full
    work = side.make(peers, ins, side_outs, side_refs)
    peers.greet(side.zs, work)
    gather.start(src)
    work.start()
    before = None
    for k, chip in gather.arrivals():
        here = chip_rows(chip, rows)
        back = dot(full[chip].reshape(2 * rows, width), w_proj[...], 1, 1) * slope[here, :].astype(F32)
        back = back.astype(BF)
        hidden[here, :] = back
        reduce.put(k, dot(back, w_fc[...], 1, 1))
        if before is not None:
            reduce.push(before)
        if k == peers.chips - 1:
            work.tick()
        before = k
    reduce.push(before)
    work.middle()
    branch = full[...].reshape(tokens, width)
    half = grad_proj.shape[1]
    for b in range(grad_proj.shape[0]):
        grad_proj[b] = dot(activated[:, b * half : (b + 1) * half], branch, 0, 0).astype(BF)
    work.made(grad_proj)
    work.tick()
    back = hidden[...]
    for a, b in chunks(width, 512):
        grad_fc[a:b, :] = dot(normed_two[:, a:b], back, 0, 0).astype(BF)
    work.tick()
    unit_sums[...] = jnp.sum(back.astype(F32), axis=0, keepdims=True)
    own = src[...].astype(F32)
    part, gain, shift = norm_back(mid[...], vec[1:2, :], reduce.total())
    out = own + part
    grad_mid[...] = out
    low = out.astype(BF)
    attn_rows[...] = low
    sums[0:1, :] = gain
    sums[1:2, :] = shift
    sums[2:3, :] = jnp.sum(own, axis=0, keepdims=True)
    sums[3:4, :] = jnp.sum(low.astype(F32), axis=0, keepdims=True)
    sums[4:8, :] = jnp.zeros((4, width), F32)
    work.finish()
    gather.finish()
    reduce.finish()


def attention_backward(head, side, *refs):
    (src, grad_mid, h, w_qkv, w_out, qkv, attended, logs, normed, col, row, vec) = refs[:12]
    ins, refs = refs[12 : 12 + len(side.operands)], refs[12 + len(side.operands) :]
    (grad_in, grad_qkv, grad_out, sums, head_sums), refs = refs[:5], refs[5:]
    side_outs, refs = refs[: len(side.outs)], refs[len(side.outs) :]
    gather_refs, reduce_refs, side_refs = refs[:5], refs[5 : 14 + 3], refs[14 + 3 :]
    joint, key_sum, value_sum = reduce_refs[9:12]
    rows, width = src.shape
    tokens, span = attended.shape
    scale = head ** (-0.5)
    peers = Peers()
    gather = Gather(peers, gather_refs[0], gather_refs[1:])
    reduce = Reduce(peers, *reduce_refs[:5], reduce_refs[5:9])
    full = gather.full
    work = side.make(peers, ins, side_outs, side_refs)
    peers.greet(side.zs, work)
    gather.start(src)
    work.start()
    for k, chip in gather.arrivals():
        here = chip_rows(chip, rows)
        g_all = dot(full[chip].reshape(2 * rows, width), w_out[...], 1, 1).astype(BF)
        block = jnp.where(col[...] <= row[:, here], 0.0, LOW).astype(F32)
        for lanes, heads in groups(span, head):
            q = qkv[here, lanes]
            g = g_all[:, lanes]
            keys = qkv[:, slice(span + lanes.start, span + lanes.stop)]
            values = qkv[:, slice(2 * span + lanes.start, 2 * span + lanes.stop)]
            merged = None
            key_term, value_term = 0.0, 0.0
            for slot, start in heads:
                q_one, g_one = only(q, start, head) * scale, only(g, start, head)
                probs = jnp.exp(dot(keys, q_one, 1, 1) + block - logs[slot : slot + 1, here])
                g_probs = dot(values, g_one, 1, 1)
                both = probs * g_probs
                centre = jnp.sum(both, axis=0, keepdims=True)
                g_scores = (both - probs * centre).astype(BF)
                value_term += dot(probs.astype(BF), g_one)
                key_term += dot(g_scores, q_one)
                g_query = dot(keys, g_scores, 0, 0)
                lane = lax.broadcasted_iota(jnp.int32, g_query.shape, 0)
                merged = g_query if merged is None else jnp.where(lane >= start, g_query, merged)
            joint[here, lanes] = (merged.T * scale).astype(BF)
            if k == 0:
                key_sum[:, lanes] = key_term
                value_sum[:, lanes] = value_term
            else:
                key_sum[:, lanes] += key_term
                value_sum[:, lanes] += value_term
        if k == peers.chips - 1:
            work.tick()
    joint[:, span : 2 * span] = key_sum[...].astype(BF)
    joint[:, 2 * span :] = value_sum[...].astype(BF)
    order = list(range(1, peers.chips)) + [0]
    before = None
    for k in order:
        reduce.put(k, dot(joint[chip_rows(peers.behind_chip(k), rows), :], w_qkv[...], 1, 1))
        if before is not None:
            reduce.push(before)
        before = k
    work.tick()
    grads = joint[...]
    for a, b in chunks(width, 512):
        grad_qkv[a:b, :] = dot(normed[:, a:b], grads, 0, 0).astype(BF)
    work.tick()
    grad_out[...] = dot(attended[...], full[...].reshape(tokens, width), 0, 0).astype(BF)
    head_sums[...] = jnp.sum(grads.astype(F32), axis=0, keepdims=True)
    part, gain, shift = norm_back(h[...].astype(F32), vec[0:1, :], reduce.total())
    grad_in[...] = (grad_mid[...] + part).astype(BF)
    sums[0:1, :] = gain
    sums[1:2, :] = shift
    sums[2:8, :] = jnp.zeros((6, width), F32)
    work.finish()
    gather.finish()
    reduce.finish()


def call(kernel, name, outs, operands, side, kept, scratch, far=()):
    chips = lax.axis_size("section") * lax.axis_size("r")
    rows, width = operands[0].shape
    vmem, hbm = pl.BlockSpec(memory_space=pltpu.VMEM), pl.BlockSpec(memory_space=pl.ANY)
    out = pl.pallas_call(
        kernel,
        out_shape=[jax.ShapeDtypeStruct(*o) for o in (*outs, *side.outs)],
        in_specs=[hbm if i in far else vmem for i in range(len(operands))] + [hbm if i else vmem for i in side.in_hbm],
        out_specs=[hbm if i in kept else vmem for i in range(len(outs))] + [hbm if i else vmem for i in side.out_hbm],
        scratch_shapes=gather_scratch(chips, rows, width) + reduce_scratch(chips, rows, width) + scratch + list(side.scratch),
        compiler_params=pltpu.CompilerParams(collective_id=name, has_side_effects=True, vmem_limit_bytes=60 * 2**20),
    )(*operands, *side.operands)
    return out[: len(outs)], out[len(outs) :]


def run_attention_forward(name, head, side, *operands):
    h, w_qkv, w_out, bias, col, row, vec = operands
    rows, width = h.shape
    tokens, span = col.shape[0], w_out.shape[0]
    slots = -(-(span // head) // 8) * 8
    chips = tokens // (2 * rows)
    outs = [
        ((chips, 2, rows, width), BF),
        ((tokens, 3 * span), BF),
        ((tokens, span), BF),
        ((slots, tokens), F32),
        ((rows, width), F32),
        ((rows, width), BF),
    ]
    return call(functools.partial(attention_forward, head, side), name, outs, operands, side, (0,), [pltpu.SemaphoreType.DMA])


def run_feed_forward(name, side, *operands):
    src, mid, w_fc, w_proj, bias, vec = operands
    rows, width = src.shape
    units = w_fc.shape[1]
    chips = lax.axis_size("section") * lax.axis_size("r")
    tokens = 2 * chips * rows
    outs = [
        ((chips, 2, rows, width), BF),
        ((tokens, units), BF),
        ((tokens, units), BF),
        ((rows, width), BF),
        (w_proj.shape, BF),
    ]
    dma = pltpu.SemaphoreType.DMA
    scratch = [dma, pltpu.VMEM(w_proj.shape, BF), dma((w_proj.shape[0],)), dma, dma, dma]
    return call(functools.partial(feed_forward, side), name, outs, operands, side, (0, 4), scratch, (3,))


def run_feed_backward(name, side, *operands):
    src, mid, w_fc, w_proj, slope, activated, normed_two, vec = operands
    rows, width = src.shape
    tokens, units = slope.shape
    zs = lax.axis_size("z")
    outs = [
        ((rows, width), F32),
        ((rows, width), BF),
        ((zs, units // zs, width), BF),
        ((width, units), BF),
        ((8, width), F32),
        ((1, units), F32),
    ]
    return call(functools.partial(feed_backward, side), name, outs, operands, side, (), [pltpu.VMEM((tokens, units), BF)])


def run_attention_backward(name, head, side, *operands):
    src, grad_mid, h, w_qkv, w_out, qkv, attended, logs, normed, col, row, vec = operands
    rows, width = src.shape
    tokens, span = attended.shape
    outs = [
        ((rows, width), BF),
        ((width, 3 * span), BF),
        ((span, width), BF),
        ((8, width), F32),
        ((1, 3 * span), F32),
    ]
    scratch = [pltpu.VMEM((tokens, 3 * span), BF), pltpu.VMEM((tokens, span), F32), pltpu.VMEM((tokens, span), F32)]
    return call(functools.partial(attention_backward, head, side), name, outs, operands, side, (), scratch)


class RouteIn:
    def __init__(self, seqs, pairs, local, send, recv):
        self.pairs, self.local, self.send_sem, self.recv_sem = pairs, local, send, recv
        x, c, z = (lax.axis_index(a) for a in ("section", "dp", "z"))
        self.sends = z // 2 == x
        self.targets = []
        for micro in range(pairs[0][0].shape[0]):
            to_c, to_z = lax.rem(z, 2), micro * seqs + c
            self.targets.append(({"dp": to_c, "z": to_z}, (to_c == c) & (to_z == z)))
        self.micro = z // seqs
        self.source = {"dp": lax.rem(z, seqs), "z": x * 2 + c}
        self.same = (lax.rem(z, seqs) == c) & (x * 2 + c == z)

    def greet(self):
        barrier = pltpu.get_barrier_semaphore()

        @pl.when(jnp.logical_not(self.same))
        def _():
            pl.semaphore_signal(barrier, inc=1, device_id=self.source, device_id_type=MESH)

        return sum(jnp.where(self.sends & jnp.logical_not(same), 1, 0) for _, same in self.targets)

    def far(self, i, micro):
        src, dst = self.pairs[i]
        return remote(src.at[micro], dst, self.send_sem.at[i, micro], self.recv_sem.at[i], self.targets[micro][0])

    def near(self, i, micro):
        src, dst = self.pairs[i]
        return pltpu.make_async_copy(src.at[micro], dst, self.local.at[i])

    def start(self, i):
        for micro, (_, same) in enumerate(self.targets):

            @pl.when(self.sends & jnp.logical_not(same))
            def _(micro=micro):
                self.far(i, micro).start()

            @pl.when(self.sends & same)
            def _(micro=micro):
                self.near(i, micro).start()

    def arrived(self, i):
        dst = self.pairs[i][1]

        @pl.when(jnp.logical_not(self.same))
        def _():
            remote(dst, dst, self.send_sem.at[i, 0], self.recv_sem.at[i], self.source).wait_recv()

        for micro, (_, same) in enumerate(self.targets):

            @pl.when(self.sends & same)
            def _(micro=micro):
                self.near(i, micro).wait()

    def finish(self):
        for i in range(len(self.pairs)):
            for micro, (_, same) in enumerate(self.targets):

                @pl.when(self.sends & jnp.logical_not(same))
                def _(i=i, micro=micro):
                    self.far(i, micro).wait_send()


def start_kernel(sizes, *refs):
    block, span, half, seqs, micros = sizes
    (tiny, w_qkv, w_attn, w_fc, w_proj, inputs, cotangent), refs = refs[:7], refs[7:]
    (qkv, wo, fc, proj, qkv_full, w_out, h, g, row, *smalls), refs = refs[:15], refs[15:]
    tiny_out, stage, h_raw, g_raw, natural, proj_cut = refs[:6]
    cuts, lands, (wo_full, nat, land), refs = refs[6:9], refs[9:12], refs[12:15], refs[15:]
    z_send, z_recv, *sems = refs[:6]
    all_send, all_recv, far_send, far_recv, turn_send, turn_recv = refs[6:12]
    ring_local, ring_send, ring_recv, *route_sems = refs[12:]
    peers = Peers()
    zs, z = lax.axis_size("z"), lax.axis_index("z")
    x, rest, slab = peers.x, peers.rest, 2 * peers.chips
    sections = peers.sections
    spot = peers.c * rest + peers.r
    width, wide = w_attn.shape[1], rest * block
    _, me = peers.other(0, 0, 0)
    route = RouteIn(seqs, [(inputs, h_raw), (cotangent, g_raw)], *route_sems)
    peers.greet(zs, route)
    sent = []

    def send(copy):
        copy.start()
        sent.append(copy)

    for k in range(1, zs):
        send(remote(tiny, stage.at[z], z_send.at[k], z_recv.at[k], {"z": lax.rem(z + k, zs)}))
    stage[z] = tiny[...]
    route.start(0)

    def share(a):
        for i, place in peers.offsets():
            device, t = peers.other(*place)
            send(remote(cuts[a].at[t], lands[a].at[x, spot], all_send.at[a, i], all_recv.at[a, i], device))
        lands[a][x, spot] = cuts[a][me]

    def settle(a, shard):
        for i, place in peers.offsets():
            device, _ = peers.other(*(-d for d in place))
            came = lands[a].at[device["section"], device["dp"] * rest + device["r"]]
            remote(came, came, all_send.at[a, i], all_recv.at[a, i], device).wait_recv()
        for layer in range(sections):
            for i in range(2 * rest):
                shard[layer, i * block : (i + 1) * block, :] = lands[a][layer, i, :block, :]

    cols = width // slab
    for t in range(slab):
        big, off = divmod(t * cols, wide)
        at = (big % 2 * zs + big // 2) * wide + off
        cuts[0][t, :block, :] = w_attn[:, at : at + cols]
    share(0)
    for t in range(slab):
        count = max(0, min(span, width - t * span))
        for p in range(3):
            if count:
                at = p * width + t * span
                cuts[1][t, :block, p * span : p * span + count] = w_qkv[:, at : at + count]
            if count < span:
                cuts[1][t, :block, p * span + count : (p + 1) * span] = jnp.zeros((block, span - count), BF)
    share(1)
    for t in range(slab):
        a, c, r = t // (2 * rest), t // rest % 2, t % rest
        for k in range(zs):
            at = ((c * zs + k) * rest + r) * (sections * half) + a * half
            cuts[2][t, :block, k * half : (k + 1) * half] = w_fc[:, at : at + half]
    for a in range(sections):
        for c in range(2):
            for k in range(zs):
                at, to = (c * zs + k) * wide, (k * 2 + c) * wide
                proj_cut[a, :, to : to + wide] = w_proj[a * half : (a + 1) * half, at : at + wide]
    for k in range(1, zs):
        came = stage.at[lax.rem(z + zs - k, zs)]
        remote(came, came, z_send.at[k], z_recv.at[k], {"z": lax.rem(z + k, zs)}).wait_recv()
    gather = Gather(peers, tiny_out, sems)
    gather.start(stage)
    settle(0, wo)
    settle(1, qkv)
    turn = Turn(peers, wo_full, nat, land, w_out, turn_send, turn_recv)
    ring = RingGather([(wo.at[0], wo_full, zs - 1), (qkv.at[0], qkv_full, zs - 1)], ring_local, ring_send, ring_recv)
    work = Both(ring, turn)
    work.start()
    share(2)
    for d in range(1, sections):
        device, _ = peers.other(d, 0, 0)
        there = lax.rem(x + d, sections)
        send(remote(proj_cut.at[there], proj.at[x], far_send.at[d], far_recv.at[d], device))
    proj[x] = proj_cut[x]
    route.start(1)
    for _ in gather.arrivals():
        pass

    per_row, halves = sections * half // block, half // block
    for layer in range(sections):
        vec, bias, unit = smalls[3 * layer : 3 * layer + 3]
        natural[...] = jnp.zeros_like(natural)
        for c in range(2):
            for k in range(zs):
                for r in range(rest):
                    at = ((k * 2 + c) * rest + r) * block
                    vec[:, at : at + block] = tiny_out[layer * rest + r, c, k, 0:8, :block]
                    at = ((c * zs + k) * rest + r) * block
                    natural[:, at : at + block] = tiny_out[layer * rest + r, c, k, 0:8, :block]
        own = jnp.zeros((8, span), F32)
        for t in range(slab):
            own = jnp.where(me == t, natural[:, t * span : (t + 1) * span], own)
        bias[:, :span] = own[6:7]
        bias[:, span : 2 * span] = jnp.zeros((1, span), F32)
        bias[:, 2 * span :] = own[7:8]
        for k in range(zs):
            for j in range(halves):
                line = tiny_out[layer * rest + peers.r, peers.c, k, pl.ds(8 + x * halves + j, 1), :block]
                unit[:, k * half + j * block : k * half + (j + 1) * block] = line
    rows = h.shape[0]
    for a in range(sections):
        for r in range(rest):
            for c in range(2):
                at = ((a * rest + r) * 2 + c) * rows
                line = tiny_out[r, 0, a * 2 + c, pl.ds(8 + per_row + z // seqs, 1), :rows]
                row[:, at : at + rows] = line.astype(jnp.int32)
    work.tick()
    settle(2, fc)
    work.tick()
    for i, (raw, ordered) in enumerate([(h_raw, h), (g_raw, g)]):
        route.arrived(i)
        for c in range(2):
            for k in range(zs):
                at, to = (c * zs + k) * wide, (k * 2 + c) * wide
                ordered[:, to : to + wide] = raw[:, at : at + wide]
    for d in range(1, sections):
        device, _ = peers.other(-d, 0, 0)
        came = proj.at[device["section"]]
        remote(came, came, far_send.at[d], far_recv.at[d], device).wait_recv()
    work.finish()
    route.finish()
    gather.finish()
    for copy in sent:
        copy.wait_send()


def run_start(name, lay, tiny, w_qkv, w_attn, w_fc, w_proj, inputs, cotangent):
    zs, n, chips, sections = lay.zs, lay.slab, lay.slab // 2, lay.sections
    span, block = lay.slots * lay.head, lay.block
    spots = lay.cores * lay.rest
    rows, tall = spots * block, -(-block // 16) * 16
    vmem, hbm = pl.BlockSpec(memory_space=pltpu.VMEM), pl.BlockSpec(memory_space=pl.ANY)
    units = lay.units // n
    widths = [lay.cols, 3 * span, units]
    flat = inputs.shape[1:]
    outs = [((sections, rows, m), BF) for m in (3 * span, lay.cols, units)]
    outs += [((sections, lay.half, lay.width), BF), ((zs, rows, 3 * span), BF), ((span, lay.width), BF)]
    outs += [(flat, BF), (flat, BF), ((1, lay.tokens), jnp.int32)]
    outs += [((8, lay.width), F32), ((1, 3 * span), F32), ((1, units), F32)] * sections
    dma = pltpu.SemaphoreType.DMA
    return pl.pallas_call(
        functools.partial(start_kernel, (block, span, lay.half, lay.seqs, lay.micros)),
        out_shape=[jax.ShapeDtypeStruct(*o) for o in outs],
        in_specs=[vmem] * 5 + [hbm] * 2,
        out_specs=[vmem] * 4 + [hbm] + [vmem] * (4 + 3 * sections),
        scratch_shapes=[
            pltpu.VMEM((chips, 2, zs, *tiny.shape), F32),
            pltpu.VMEM((zs, *tiny.shape), F32),
            pltpu.VMEM(flat, BF),
            pltpu.VMEM(flat, BF),
            pltpu.VMEM((8, n * span), F32),
            pltpu.VMEM((sections, lay.half, lay.width), BF),
        ]
        + [pltpu.VMEM((n, tall, m), BF) for m in widths]
        + [pltpu.VMEM((sections, spots, tall, m), BF) for m in widths]
        + [pltpu.VMEM((zs, rows, lay.cols), BF), pltpu.VMEM((n * span, lay.cols), BF), pltpu.VMEM((n, span, lay.cols), BF)]
        + [dma((zs,))] * 2
        + [dma((chips,))] * 4
        + [dma((3, n))] * 2
        + [dma((sections,))] * 2
        + [dma((n,))] * 2
        + [dma((2,))]
        + [dma((2, zs - 1))] * 2
        + [dma((2,)), dma((2, lay.micros)), dma((2,))],
        compiler_params=pltpu.CompilerParams(collective_id=name, has_side_effects=True, vmem_limit_bytes=60 * 2**20),
    )(tiny, w_qkv, w_attn, w_fc, w_proj, inputs, cotangent)


def end_kernel(sizes, *refs):
    block, width, units, seqs = sizes
    (part, turned, qkv_one, wo_one, fc_zero, fc_one, proj_zero, proj_one, small, last_rows), refs = refs[:10], refs[10:]
    (out_qkv, out_wo, out_fc, out_proj, out_small, out_rows), refs = refs[:6], refs[6:]
    (qkv_total, wo_part, wo_total, wo_cut, wo_back, proj_both, proj_land), refs = refs[:7], refs[7:]
    stages, lands, refs = refs[:3], refs[3:6], refs[6:]
    (small_land, small_sum, z_land, came_qkv, came_wo), refs = refs[:5], refs[5:]
    all_send, all_recv, far_send, far_recv, z_send, z_recv, turn_send, turn_recv, ring_send, ring_recv, late_send, late_recv, *route_sems = refs
    peers = Peers()
    zs, z = lax.axis_size("z"), lax.axis_index("z")
    x, rest, slab = peers.x, peers.rest, 2 * peers.chips
    spot = peers.c * rest + peers.r
    span, cols = turned.shape[0], wo_total.shape[1]
    half, wide = proj_zero.shape[0], rest * block
    _, me = peers.other(0, 0, 0)
    offsets = peers.offsets()
    route = Route(0, seqs, last_rows, out_rows, *route_sems)
    peers.greet(zs, route)
    sent = []

    def send(copy):
        copy.start()
        sent.append(copy)

    ring = RingSum([(part, None, came_qkv, qkv_total, 0, zs - 1)], ring_send, ring_recv)
    ring.start()
    turn = TurnBack(peers, turned, wo_part, wo_cut, wo_back, turn_send, turn_recv)
    turn.start()
    for i, place in offsets:
        device, t = peers.other(*place)
        send(remote(small.at[t], small_land.at[me], all_send.at[3, i], all_recv.at[3, i], device))
    small_land[me] = small[me]

    def cut(a, totals):
        for layer, total in enumerate(totals):
            for i in range(2 * rest):
                stages[a][layer, i, :block, :] = total[i * block : (i + 1) * block, :]
        for i, place in offsets:
            device, t = peers.other(*place)
            src = stages[a].at[device["section"], device["dp"] * rest + device["r"]]
            send(remote(src, lands[a].at[me], all_send.at[a, i], all_recv.at[a, i], device))
        lands[a][me] = stages[a][x, spot]

    def settle(a, land):
        for i, place in offsets:
            device, t = peers.other(*(-d for d in place))
            came = land.at[t]
            remote(came, came, all_send.at[a, i], all_recv.at[a, i], device).wait_recv()

    route.start()
    cut(0, (fc_zero, fc_one))
    proj_both[0] = proj_zero[...]
    proj_both[1] = proj_one[...]
    device, _ = peers.other(1, 0, 0)
    send(remote(proj_both.at[1 - x], proj_land.at[x], far_send, far_recv, device))
    proj_land[x] = proj_both[x]

    turn.finish()
    wo_ring = RingSum([(wo_part, None, came_wo, wo_total, 0, zs - 1)], late_send, late_recv)
    wo_ring.start()
    settle(3, small_land)
    total = small_land[0]
    for t in range(1, slab):
        total = total + small_land[t]
    small_sum[...] = total
    for k in range(1, zs):
        there = lax.rem(z + k, zs)
        send(remote(small_sum.at[there], z_land.at[z], z_send.at[k], z_recv.at[k], {"z": there}))
    z_land[z] = small_sum[z]
    ring.tick()
    wo_ring.tick()
    settle(0, lands[0])
    for t in range(slab):
        h, c, r = t // (2 * rest), t // rest % 2, t % rest
        for k in range(zs):
            at = ((c * zs + k) * rest + r) * (units // (2 * zs * rest)) + h * half
            out_fc[:, at : at + half] = lands[0][t, :block, k * half : (k + 1) * half].astype(F32)
    ring.tick()
    wo_ring.tick()
    came = proj_land.at[1 - x]
    remote(came, came, far_send, far_recv, device).wait_recv()
    for h in range(2):
        for c in range(2):
            for k in range(zs):
                at, of = (c * zs + k) * wide, (k * 2 + c) * wide
                out_proj[h * half : (h + 1) * half, at : at + wide] = proj_land[h, :, of : of + wide].astype(F32)
    for k in range(1, zs):
        came = z_land.at[lax.rem(z + zs - k, zs)]
        remote(came, came, z_send.at[k], z_recv.at[k], {"z": lax.rem(z + k, zs)}).wait_recv()
    total = z_land[0]
    for k in range(1, zs):
        total = total + z_land[k]
    out_small[...] = total
    wo_ring.finish()
    cut(2, (wo_total, wo_one))
    ring.finish()
    cut(1, (qkv_total, qkv_one))
    settle(2, lands[2])
    for t in range(slab):
        big, off = divmod(t * cols, wide)
        at = (big % 2 * zs + big // 2) * wide + off
        out_wo[:, at : at + cols] = lands[2][t, :block, :].astype(F32)
    settle(1, lands[1])
    for t in range(slab):
        count = min(span, width - t * span)
        for p in range(3):
            if count > 0:
                at = p * width + t * span
                out_qkv[:, at : at + count] = lands[1][t, :block, p * span : p * span + count].astype(F32)
    route.finish()
    for copy in sent:
        copy.wait_send()


def run_end(name, lay, part, turned, qkv_one, wo_one, fcs, projs, small, last_rows):
    zs, n = lay.zs, lay.slab
    span, width, block = lay.slots * lay.head, lay.width, lay.block
    rows = part.shape[1]
    spots = lay.cores * lay.rest
    tall = -(-block // 16) * 16
    vmem = pl.BlockSpec(memory_space=pltpu.VMEM)
    dma = pltpu.SemaphoreType.DMA
    widths = [fcs[0].shape[1], part.shape[2], lay.cols]
    half = projs[0].shape[0]
    tile = small.shape[2:]
    outs = [(block, 3 * width), (block, width), (block, lay.units), (lay.unit_block, width), tile]
    return pl.pallas_call(
        functools.partial(end_kernel, (block, width, lay.units, lay.seqs)),
        out_shape=[jax.ShapeDtypeStruct(o, F32) for o in outs]
        + [jax.ShapeDtypeStruct((lay.micros, *last_rows.shape), BF)],
        in_specs=[vmem] * 9 + [pl.BlockSpec(memory_space=pl.ANY)],
        out_specs=[vmem] * 5 + [pl.BlockSpec(memory_space=pl.ANY)],
        scratch_shapes=[
            pltpu.VMEM((rows, part.shape[2]), BF),
            pltpu.VMEM((zs, rows, lay.cols), BF),
            pltpu.VMEM((rows, lay.cols), BF),
            pltpu.VMEM((n, span, lay.cols), BF),
            pltpu.VMEM((n, span, lay.cols), BF),
            pltpu.VMEM((2, half, width), BF),
            pltpu.VMEM((2, half, width), BF),
        ]
        + [pltpu.VMEM((lay.sections, spots, tall, m), BF) for m in widths]
        + [pltpu.VMEM((n, tall, m), BF) for m in widths]
        + [
            pltpu.VMEM((n, zs, *tile), F32),
            pltpu.VMEM((zs, *tile), F32),
            pltpu.VMEM((zs, *tile), F32),
            pltpu.VMEM((zs - 1, rows, part.shape[2]), BF),
            pltpu.VMEM((zs - 1, rows, lay.cols), BF),
        ]
        + [dma((4, n))] * 2
        + [dma] * 2
        + [dma((zs,))] * 2
        + [dma((n,))] * 2
        + [dma((2, zs - 1))] * 4
        + [dma, dma, dma((lay.micros,))],
        compiler_params=pltpu.CompilerParams(collective_id=name, has_side_effects=True, vmem_limit_bytes=60 * 2**20),
    )(part, turned, qkv_one, wo_one, *fcs, *projs, small, last_rows)


class Rings:
    def __init__(self, lay):
        self.zs = lay.zs
        self.state = {}

    def put(self, kind, layer, part):
        if part.ndim == 2:
            part = part.reshape(self.zs, part.shape[0] // self.zs, part.shape[1])
        _, acc, steps = self.state.get((kind, layer), (None, None, 0))
        self.state[kind, layer] = (part, acc, steps)

    def side(self, plan, makes={}, turned=None, cols=0):
        pieces = []
        for kind, layer, count in plan:
            part, acc, steps = self.state.get((kind, layer), (None, None, 0))
            shape = makes[kind] if part is None else part.shape[1:]
            pieces.append((part, shape, acc, steps, count))
        return sum_side(pieces, turned, cols)

    def done(self, plan, outs):
        for (kind, layer, count), acc in zip(plan, outs):
            part, _, steps = self.state[kind, layer]
            self.state[kind, layer] = (part, acc, steps + count)


def on_device(
    inputs, cotangent, positions, w_qkv, w_attn_out, w_fc, w_proj, norm_gains, biases, fc_bias
):
    lay = Layout(inputs, w_fc)
    n, block, width = lay.slab, lay.block, lay.width
    span = lay.slots * lay.head

    small = jnp.concatenate([norm_gains[0], biases[0]], axis=1).astype(F32).T
    small = jnp.stack([small[i] for i in (0, 1, 2, 6, 5, 7, 3, 4)])
    small = jnp.concatenate([small, fc_bias[0].reshape(-1, block).astype(F32)])
    small = jnp.pad(small, ((0, 0), (0, 128 - block)))
    places = jnp.pad(positions.astype(F32), ((0, 0), (0, 128 - lay.rows)))
    small = jnp.concatenate([small, places])
    small = jnp.pad(small, ((0, -small.shape[0] % 8), (0, 0)))
    qkv_cut, wo_cut, fc_cut, proj_cut, w_qkv, w_out, h, g, row, *smalls = run_start(
        0, lay, small, w_qkv[0], w_attn_out[0], w_fc[0], w_proj[0], inputs[:, 0], cotangent[:, 0]
    )
    smalls = [smalls[3 * layer : 3 * layer + 3] for layer in range(lay.sections)]
    col = row.reshape(lay.tokens, 1)
    outs, keeps, params = [], [], []
    for layer in range(lay.sections):
        last = layer == lay.sections - 1
        vec, bias, unit = smalls[layer]
        w_qkv = w_qkv.reshape(width, 3 * span)
        (full, qkv, attended, logs, mid, normed_two), (w_fc, w_proj) = run_attention_forward(
            1 + 2 * layer,
            lay.head,
            gather_side([fc_cut[layer], proj_cut[layer]], (lay.zs - 1, lay.zs - 2)),
            h,
            w_qkv,
            w_out,
            bias,
            col,
            row,
            vec,
        )
        w_fc = w_fc.reshape(width, -1)
        if last:
            side = route_side(0, lay, outs[0])
        else:
            side = gather_side([wo_cut[layer + 1], qkv_cut[layer + 1]], turn=span)
        (full_two, slope, activated, result, w_proj), later = run_feed_forward(
            2 + 2 * layer, side, normed_two, mid, w_fc, w_proj, unit, vec
        )
        params.append((w_qkv, w_out, w_fc, w_proj.reshape(-1, width)))
        if last:
            routed = [later[0]]
        else:
            w_out, w_qkv = later
        keeps.append((h, full, qkv, attended, logs, mid, full_two, slope, activated))
        h = result
        outs.append(h)

    rings = Rings(lay)
    plans = {
        ("feed", 1): [("proj", 1, 1)],
        ("attention", 1): [("proj", 1, 2), ("fc", 1, 2)],
        ("feed", 0): [("qkv", 1, 3), ("fc", 1, 1), ("proj", 0, 1)],
        ("attention", 0): [("fc", 0, 3), ("proj", 0, 2), ("out", 1, 3)],
    }
    grad_rows, sums = [None] * lay.sections, [None] * lay.sections
    grad_out = None
    for layer in reversed(range(lay.sections)):
        w_qkv, w_out, w_fc, w_proj = params[layer]
        vec = smalls[layer][0]
        h, full, qkv, attended, logs, mid, full_two, slope, activated = keeps[layer]
        full, full_two = (a.reshape(lay.tokens, width) for a in (full, full_two))
        name = 1 + 4 * lay.sections - 2 * layer
        side = rings.side(plans["feed", layer], {"proj": (lay.half, width)}, grad_out, lay.cols)
        side = both_sides(side, route_side(1, lay, outs[1] if grad_out is None else g))
        (grad_mid, attn_rows, grad_proj, grad_fc, feed_sums, unit_sums), done = run_feed_backward(
            name, side, g, mid, w_fc, w_proj, slope, activated, full_two, vec
        )
        rings.put("proj", layer, grad_proj)
        rings.put("fc", layer, grad_fc)
        rings.done(plans["feed", layer], done)
        routed.append(done[-1])
        if grad_out is not None:
            rings.put("out", layer + 1, done[-2])
        side = rings.side(plans["attention", layer])
        (g, grad_qkv, grad_out, attn_sums, head_sums), done = run_attention_backward(
            name + 1, lay.head, side, attn_rows, grad_mid, h, w_qkv, w_out, qkv, attended, logs, full, col, row, vec
        )
        rings.done(plans["attention", layer], done)
        rings.put("qkv", layer, grad_qkv)
        grad_rows[layer] = g
        sums[layer] = (feed_sums, unit_sums, attn_sums, head_sums)
    rows = []
    for layer in range(lay.sections):
        feed_sums, unit_sums, attn_sums, head_sums = sums[layer]
        feed_sums, attn_sums = lay.restore(feed_sums), lay.restore(attn_sums)
        zero = jnp.zeros((n * span,), jnp.float32)
        s_q = lax.dynamic_update_slice_in_dim(zero, head_sums[0, :span], lay.t * span, 0)[:width]
        s_v = lax.dynamic_update_slice_in_dim(zero, head_sums[0, 2 * span :], lay.t * span, 0)[:width]
        cols = [attn_sums[0], feed_sums[0], attn_sums[1], s_q, s_v, feed_sums[3], feed_sums[1], feed_sums[2]]
        cols = jnp.stack(cols, axis=1).reshape(lay.shards, block * 8)
        spots = jnp.zeros((n, lay.zs, lay.half), jnp.float32)
        spots = lax.dynamic_update_index_in_dim(
            spots, unit_sums.reshape(lay.zs, lay.half), lay.t, 0
        )
        spots = spots.reshape(lay.sections, lay.cores, lay.rest, lay.zs, lay.half)
        spots = spots.transpose(1, 3, 2, 0, 4).reshape(lay.shards, lay.unit_block)
        rows.append(jnp.concatenate([cols, spots], axis=1))
    rows = jnp.stack(rows).reshape(lay.sections, lay.cores, lay.zs, lay.rest, -1)
    used = rows.shape[-1]
    rows = jnp.pad(jnp.swapaxes(rows, 2, 3), ((0, 0),) * 4 + ((0, -used % 1024),))
    rows = rows.reshape(n, lay.zs, -1, 128)
    out_qkv, out_attn, out_fc, out_proj, rows, routed_grad = run_end(
        3 + 4 * lay.sections,
        lay,
        rings.state["qkv", 0][0],
        grad_out,
        rings.state["qkv", 1][1],
        rings.state["out", 1][1],
        [rings.state["fc", layer][1] for layer in range(2)],
        [rings.state["proj", layer][1] for layer in range(2)],
        rows,
        g,
    )
    first = lay.x == 0
    section_out = lay.restore(jnp.where(first, routed[0], routed[1]))[None, :, None]
    section_grad = lay.restore(jnp.where(first, routed_grad, routed[2]))[None, :, None]
    rows = rows.reshape(-1)[:used]
    cols = rows[: block * 8].reshape(block, 8)
    return (
        section_out,
        section_grad,
        out_qkv[None],
        out_attn[None],
        out_fc[None],
        out_proj[None],
        cols[None, :, :2],
        cols[None, :, 2:],
        rows[None, block * 8 :],
    )


def solution(mesh):
    sections, cores, contexts = (mesh.shape[a] for a in ("section", "dp", "ctx"))
    zs = sections * cores
    shape = (sections, cores, zs, contexts // zs)
    inner = Mesh(mesh.devices.reshape(shape), ALL)
    tokens = P(None, "dp", ("z", "r"), None)
    rows = P("section", ("dp", "z", "r"), None)
    units = P("section", ("dp", "z", "r"))
    out_tokens = P("section", None, "dp", ("z", "r"), None)
    return jax.shard_map(
        on_device,
        mesh=inner,
        in_specs=(tokens, tokens, P(None, ("z", "r"))) + (rows,) * 6 + (units,),
        out_specs=(out_tokens, out_tokens) + (rows,) * 6 + (units,),
        check_vma=False,
    )
```

```python
import functools

import jax
import jax.numpy as jnp
from jax import lax
from jax.experimental import pallas as pl
from jax.experimental.pallas import tpu as pltpu
from jax.sharding import Mesh
from jax.sharding import PartitionSpec as P

HEADS = 25
EPSILON = 1e-05

SLAB = ("section", "dp", "r")
ALL = ("section", "dp", "z", "r")
MESH = pl.DeviceIdType.MESH


class Layout:
    def __init__(self, inputs, w_fc):
        self.micros, _, self.rows, self.width = inputs.shape
        self.sections = lax.axis_size("section")
        self.cores = lax.axis_size("dp")
        self.zs = lax.axis_size("z")
        self.rest = lax.axis_size("r")
        self.slab = self.sections * self.cores * self.rest
        self.shards = self.cores * self.zs * self.rest
        self.units = w_fc.shape[2]
        self.tokens = self.rows * self.slab
        self.seqs = self.cores
        self.head = self.width // HEADS
        self.slots = -(-HEADS // self.slab)
        self.block = self.width // self.shards
        self.unit_block = self.units // self.shards
        self.half = self.unit_block // self.sections
        self.cols = self.width // self.slab
        self.x = lax.axis_index("section")
        self.c = lax.axis_index("dp")
        self.z = lax.axis_index("z")
        self.r = lax.axis_index("r")
        self.t = (self.x * self.cores + self.c) * self.rest + self.r

    def number(self, x, c, z, r):
        return ((x * self.cores + c) * self.zs + z) * self.rest + r

    def order(self, a):
        lead = a.shape[:-1]
        a = a.reshape(*lead, self.cores, self.zs, self.rest * self.block)
        return jnp.swapaxes(a, -3, -2).reshape(*lead, self.width)

    def restore(self, a):
        lead = a.shape[:-1]
        a = a.reshape(*lead, self.zs, self.cores, self.rest * self.block)
        return jnp.swapaxes(a, -3, -2).reshape(*lead, self.width)

    def routes(self, micro):
        pairs = []
        for x in range(self.sections):
            for c in range(self.cores):
                for s in range(self.seqs):
                    for r in range(self.rest):
                        place = x * self.cores + c
                        pairs.append(((x, s, place, r), (x, c, micro * self.seqs + s, r)))
        return pairs

    def tokens_in(self, a):
        got = []
        for micro in range(self.micros):
            route = [(self.number(*f), self.number(*g)) for f, g in self.routes(micro)]
            got.append(lax.ppermute(a[micro, 0], ALL, route))
        out = got[0]
        for micro in range(1, self.micros):
            out = jnp.where(self.z // self.seqs == micro, got[micro], out)
        return out

    def tokens_out(self, parts):
        result = []
        for micro in range(self.micros):
            got = []
            for layer, part in enumerate(parts):
                route = [
                    (self.number(*g), self.number(layer, *f[1:])) for f, g in self.routes(micro)
                ]
                got.append(lax.ppermute(part, ALL, route))
            out = got[0]
            for layer in range(1, len(parts)):
                out = jnp.where(self.x == layer, got[layer], out)
            result.append(out)
        return jnp.stack(result)[None, :, None]


LOW = -1e30
BF = jnp.bfloat16
F32 = jnp.float32


class Peers:
    def __init__(self):
        self.sections, self.rest = lax.axis_size("section"), lax.axis_size("r")
        self.chips = self.sections * self.rest
        self.x, self.c, self.r = (lax.axis_index(a) for a in ("section", "dp", "r"))
        self.chip = self.x * self.rest + self.r

    def away(self, k, sign):
        x = lax.rem(self.x + self.sections + sign * (k // self.rest), self.sections)
        r = lax.rem(self.r + self.rest + sign * (k % self.rest), self.rest)
        return x, r

    def ahead(self, k):
        x, r = self.away(k, 1)
        return {"section": x, "dp": self.c, "r": r}

    def behind(self, k):
        x, r = self.away(k, -1)
        return {"section": x, "dp": self.c, "r": r}

    def sibling(self):
        return {"section": self.x, "dp": 1 - self.c, "r": self.r}

    def behind_chip(self, k):
        x, r = self.away(k, -1)
        return x * self.rest + r

    def other(self, dx, dc, dr):
        x = lax.rem(self.x + self.sections + dx, self.sections)
        c = lax.rem(self.c + 2 + dc, 2)
        r = lax.rem(self.r + self.rest + dr, self.rest)
        return {"section": x, "dp": c, "r": r}, (x * 2 + c) * self.rest + r

    def offsets(self):
        every = [(x, c, r) for x in range(self.sections) for c in range(2) for r in range(self.rest)]
        return list(enumerate(every))[1:]

    def greet(self, zs=1, work=None):
        barrier = pltpu.get_barrier_semaphore()
        z = lax.axis_index("z")
        size = lax.axis_size("z")
        for k in range(1, zs):
            pl.semaphore_signal(barrier, inc=1, device_id={"z": lax.rem(z + size - k, size)}, device_id_type=MESH)
        others = self.offsets()
        for _, place in others:
            pl.semaphore_signal(barrier, inc=1, device_id=self.other(*place)[0], device_id_type=MESH)
        more = 0 if work is None else work.greet()
        pl.semaphore_wait(barrier, len(others) + zs - 1 + more)


def remote(src, dst, send, recv, device):
    return pltpu.make_async_remote_copy(
        src_ref=src, dst_ref=dst, send_sem=send, recv_sem=recv, device_id=device, device_id_type=MESH
    )


class Gather:
    def __init__(self, peers, full, sems):
        self.peers, self.full = peers, full
        self.chip_send, self.chip_recv, self.core_send, self.core_recv = sems
        self.sent = []

    def start(self, src):
        p = self.peers
        mine = self.full.at[p.chip, p.c]
        mine[...] = src if isinstance(src, jax.Array) else src[...]
        for k in range(1, p.chips):
            self.send(remote(mine, mine, self.chip_send.at[k], self.chip_recv.at[k], p.ahead(k)))
        self.send(remote(mine, mine, self.core_send.at[0], self.core_recv.at[0], p.sibling()))

    def send(self, copy):
        copy.start()
        self.sent.append(copy)

    def forward(self, k):
        p = self.peers
        block = self.full.at[p.behind_chip(k), p.c]
        remote(block, block, self.chip_send.at[k], self.chip_recv.at[k], p.sibling()).wait_recv()
        self.send(remote(block, block, self.core_send.at[k], self.core_recv.at[k], p.sibling()))

    def chip(self, k):
        p = self.peers
        block = self.full.at[p.behind_chip(k), 1 - p.c]
        remote(block, block, self.core_send.at[k], self.core_recv.at[k], p.sibling()).wait_recv()
        return p.behind_chip(k)

    def arrivals(self):
        yield 0, self.chip(0)
        chips = self.peers.chips
        for k in range(1, chips):
            for later in (1, 2) if k == 1 else (k + 1,):
                if later < chips:
                    self.forward(later)
            yield k, self.chip(k)

    def finish(self):
        for copy in self.sent:
            copy.wait_send()


class Reduce:
    def __init__(self, peers, mine, stage, other, going, coming, sems):
        self.peers = peers
        self.mine, self.stage, self.other, self.going, self.coming = mine, stage, other, going, coming
        self.chip_send, self.chip_recv, self.core_send, self.core_recv = sems
        self.sent = []

    def send(self, copy):
        copy.start()
        self.sent.append(copy)

    def put(self, k, both):
        p = self.peers
        rows = both.shape[0] // 2
        low, high = both[:rows], both[rows:]
        first = p.c == 0
        self.mine[k] = jnp.where(first, low, high)
        self.stage[k] = jnp.where(first, high, low).astype(BF)
        self.send(remote(self.stage.at[k], self.other.at[k], self.core_send.at[k], self.core_recv.at[k], p.sibling()))

    def arrived(self, k):
        p = self.peers
        remote(self.stage.at[k], self.other.at[k], self.core_send.at[k], self.core_recv.at[k], p.sibling()).wait_recv()
        return self.mine[k] + self.other[k].astype(F32)

    def push(self, k):
        p = self.peers
        if k:
            self.going[k - 1] = self.arrived(k).astype(BF)
            self.send(remote(self.going.at[k - 1], self.coming.at[k - 1], self.chip_send.at[k], self.chip_recv.at[k], p.behind(k)))

    def total(self):
        p = self.peers
        out = self.arrived(0)
        for k in range(1, p.chips):
            remote(self.going.at[k - 1], self.coming.at[k - 1], self.chip_send.at[k], self.chip_recv.at[k], p.sibling()).wait_recv()
            out = out + self.coming[k - 1].astype(F32)
        return out

    def finish(self):
        for copy in self.sent:
            copy.wait_send()


class RingGather:
    def greet(self):
        return 0

    def __init__(self, pieces, local, send, recv):
        self.pieces, self.local, self.send_sem, self.recv_sem = pieces, local, send, recv
        self.zs, self.z = lax.axis_size("z"), lax.axis_index("z")
        every = [(p, s) for s in range(self.zs - 1) for p in range(len(pieces)) if s < pieces[p][2]]
        self.steps = [(p, s) for p, s in every if s < pieces[p][2] - 1] + [(p, s) for p, s in every if s == pieces[p][2] - 1]
        self.forwards = len(every) - len(pieces)
        self.sent = []

    def block(self, step):
        return lax.rem(self.z + self.zs - step, self.zs)

    def send(self, p, step, src):
        dst = self.pieces[p][1].at[self.block(step)]
        copy = remote(src, dst, self.send_sem.at[p, step], self.recv_sem.at[p, step], {"z": lax.rem(self.z + 1, self.zs)})
        copy.start()
        self.sent.append(copy)

    def start(self):
        for p, (shard, full, _) in enumerate(self.pieces):
            self.send(p, 0, shard)
            pltpu.make_async_copy(shard, full.at[self.z], self.local.at[p]).start()

    def tick(self, count=1):
        for _ in range(min(count, self.forwards)):
            self.forwards -= 1
            self.take()

    def take(self):
        p, step = self.steps.pop(0)
        shard, full, count = self.pieces[p]
        block = full.at[self.block(step + 1)]
        remote(block, block, self.send_sem.at[p, step], self.recv_sem.at[p, step], {"z": lax.rem(self.z + 1, self.zs)}).wait_recv()
        if step < count - 1:
            self.send(p, step + 1, block)
            return None
        pltpu.make_async_copy(shard, full.at[self.z], self.local.at[p]).wait()
        return p

    def finish(self):
        while self.steps:
            self.take()
        for copy in self.sent:
            copy.wait_send()


class RingSum:
    def greet(self):
        return 0

    def __init__(self, pieces, send, recv):
        self.pieces, self.send_sem, self.recv_sem = pieces, send, recv
        self.zs, self.z = lax.axis_size("z"), lax.axis_index("z")
        self.steps, self.sent = [], []
        self.late = [p for p, piece in enumerate(pieces) if piece[0] is None]
        ready = [p for p in range(len(pieces)) if p not in self.late]
        self.steps = [(p, i) for i in range(self.zs - 1) for p in ready if i < pieces[p][5] - 1]
        self.forwards = len(self.steps)
        self.steps += [(p, pieces[p][5] - 1) for p in ready]
        self.parts = [piece[0] for piece in pieces]

    def copy(self, p, i, src):
        dst = self.pieces[p][2].at[i]
        return remote(src, dst, self.send_sem.at[p, i], self.recv_sem.at[p, i], {"z": lax.rem(self.z + 1, self.zs)})

    def send(self, p, i, src):
        copy = self.copy(p, i, src)
        copy.start()
        self.sent.append(copy)

    def launch(self, p):
        acc, first = self.pieces[p][1], self.pieces[p][4]
        self.send(p, 0, far(acc) if first else far(self.parts[p]).at[lax.rem(self.z + self.zs - 1, self.zs)])

    def start(self):
        for p in range(len(self.pieces)):
            if p not in self.late:
                self.launch(p)

    def made(self, part):
        if self.late:
            p = self.late.pop(0)
            self.parts[p] = part
            self.launch(p)
            count = self.pieces[p][5]
            self.steps[self.forwards : self.forwards] = [(p, i) for i in range(count - 1)]
            self.forwards += count - 1
            self.steps.append((p, count - 1))

    def tick(self, count=1):
        for _ in range(min(count, self.forwards)):
            self.forwards -= 1
            self.take()

    def take(self):
        p, i = self.steps.pop(0)
        part, acc, came, out, first, count = self.pieces[p]
        self.copy(p, i, came.at[i]).wait_recv()
        own = self.parts[p][lax.rem(self.z + 2 * self.zs - 2 - first - i, self.zs)]
        total = (came[i].astype(F32) + own.astype(F32)).astype(BF)
        if i < count - 1:
            came[i] = total
            self.send(p, i + 1, came.at[i])
        else:
            out[...] = total

    def middle(self):
        pass

    def finish(self):
        while self.steps:
            self.take()
        for copy in self.sent:
            copy.wait_send()


class TurnBack:
    def __init__(self, peers, turned, part, pieces, came, send, recv):
        self.peers, self.turned, self.part, self.pieces, self.came = peers, turned, part, pieces, came
        self.send_sem, self.recv_sem = send, recv
        self.sent = []

    def start(self):
        slab, _, cols = self.pieces.shape
        for t in range(slab):
            self.pieces[t] = self.turned[:, t * cols : (t + 1) * cols]
        _, me = self.peers.other(0, 0, 0)
        for i, place in self.peers.offsets():
            device, t = self.peers.other(*place)
            copy = remote(self.pieces.at[t], self.came.at[me], self.send_sem.at[i], self.recv_sem.at[i], device)
            copy.start()
            self.sent.append(copy)
        self.came[me] = self.pieces[me]

    def finish(self):
        for i, place in self.peers.offsets():
            device, t = self.peers.other(*(-d for d in place))
            block = self.came.at[t]
            remote(block, block, self.send_sem.at[i], self.recv_sem.at[i], device).wait_recv()
        zs, rows, _ = self.part.shape
        wide, span = rows // 2, self.came.shape[1]
        for c in range(2):
            for k in range(zs):
                at, done = (c * zs + k) * wide, 0
                while done < wide:
                    t, row = divmod(at + done, span)
                    count = min(wide - done, span - row)
                    self.part[k, c * wide + done : c * wide + done + count, :] = self.came[t, row : row + count, :]
                    done += count
        for copy in self.sent:
            copy.wait_send()


class SumAndTurn:
    def greet(self):
        return 0

    def __init__(self, ring, turn):
        self.ring, self.turn = ring, turn
        self.start, self.tick, self.made = ring.start, ring.tick, ring.made

    def middle(self):
        self.turn.start()

    def finish(self):
        self.turn.finish()
        self.ring.finish()


class Turn:
    def __init__(self, peers, full, nat, land, w_out, send, recv):
        self.peers, self.full, self.nat, self.land, self.w_out = peers, full, nat, land, w_out
        self.send_sem, self.recv_sem = send, recv
        self.sent = []

    def start(self):
        zs, rows, cols = self.full.shape
        part, span = rows // 2, self.w_out.shape[0]
        for c in range(2):
            for z in range(zs):
                at = (c * zs + z) * part
                self.nat[at : at + part, :] = self.full[z, c * part : (c + 1) * part, :]
        used = zs * rows
        if used < self.nat.shape[0]:
            self.nat[used:, :] = jnp.zeros((self.nat.shape[0] - used, cols), BF)
        _, me = self.peers.other(0, 0, 0)
        for i, place in self.peers.offsets():
            device, t = self.peers.other(*place)
            src = self.nat.at[pl.ds(pl.multiple_of(t * span, span), span)]
            copy = remote(src, self.land.at[me], self.send_sem.at[i], self.recv_sem.at[i], device)
            copy.start()
            self.sent.append(copy)
        self.land[me] = self.nat[pl.ds(pl.multiple_of(me * span, span), span), :]

    def finish(self):
        for i, place in self.peers.offsets():
            device, t = self.peers.other(*(-d for d in place))
            block = self.land.at[t]
            remote(block, block, self.send_sem.at[i], self.recv_sem.at[i], device).wait_recv()
        slab, _, cols = self.land.shape
        for t in range(slab):
            self.w_out[:, t * cols : (t + 1) * cols] = self.land[t]
        for copy in self.sent:
            copy.wait_send()


class Route:
    def __init__(self, seqs, src, out, local, send, recv, when="start"):
        self.when = when
        self.seqs, self.src, self.out = seqs, src, out
        self.local, self.send_sem, self.recv_sem = local, send, recv
        x, c, z = (lax.axis_index(a) for a in ("section", "dp", "z"))
        self.here = lax.rem(z, 2) == x
        place = c * 2 + x
        self.to = {"dp": lax.rem(z, seqs), "z": place}
        self.micro = z // seqs
        self.same = (lax.rem(z, seqs) == c) & (place == z)
        self.sources = []
        for micro in range(out.shape[0]):
            src_c, src_z = z // 2, micro * seqs + c
            self.sources.append(({"dp": src_c, "z": src_z}, (src_c == c) & (src_z == z)))

    def greet(self):
        barrier = pltpu.get_barrier_semaphore()
        for device, same in self.sources:

            @pl.when(self.here & jnp.logical_not(same))
            def _(device=device):
                pl.semaphore_signal(barrier, inc=1, device_id=device, device_id_type=MESH)

        return jnp.where(self.same, 0, 1)

    def copy(self):
        return remote(self.src, self.out.at[self.micro], self.send_sem, self.recv_sem.at[self.micro], self.to)

    def own(self):
        return pltpu.make_async_copy(self.src, self.out.at[self.micro], self.local)

    def start(self):
        if self.when == "start":
            self.go()

    def middle(self):
        pass

    def go(self):
        @pl.when(jnp.logical_not(self.same))
        def _():
            self.copy().start()

        @pl.when(self.same)
        def _():
            self.own().start()

    def tick(self, point):
        if self.when == point:
            self.go()

    def made(self, part):
        pass

    def arrived(self):
        for micro, (device, same) in enumerate(self.sources):

            @pl.when(self.here & jnp.logical_not(same))
            def _(micro=micro, device=device):
                block = self.out.at[micro]
                remote(block, block, self.send_sem, self.recv_sem.at[micro], device).wait_recv()

        @pl.when(self.same)
        def _():
            self.own().wait()

    def sent(self):
        @pl.when(jnp.logical_not(self.same))
        def _():
            self.copy().wait_send()

    def finish(self):
        self.arrived()
        self.sent()


class Across:
    def __init__(self, layer, src, out, send, recv):
        self.src, self.out, self.send_sem, self.recv_sem = src, out, send, recv
        x, z = lax.axis_index("section"), lax.axis_index("z")
        self.layer = layer
        self.sends = (x != layer) & (lax.rem(z, 2) == x)
        self.takes = (x == layer) & (lax.rem(z, 2) != x)
        self.going = False

    def greet(self):
        barrier = pltpu.get_barrier_semaphore()

        @pl.when(self.takes)
        def _():
            pl.semaphore_signal(barrier, inc=1, device_id={"section": 1 - self.layer}, device_id_type=MESH)

        return jnp.where(self.sends, 1, 0)

    def copy(self):
        return remote(self.src, self.out, self.send_sem, self.recv_sem, {"section": jnp.int32(self.layer)})

    def back(self):
        return remote(self.out, self.out, self.send_sem, self.recv_sem, {"section": jnp.int32(1 - self.layer)})

    def start(self):
        pass

    def tick(self, point):
        if not self.going:
            self.going = True

            @pl.when(self.sends)
            def _():
                self.copy().start()

    def made(self, part):
        pass

    def middle(self):
        pass

    def finish(self):
        self.tick("end")

        @pl.when(self.takes)
        def _():
            self.back().wait_recv()

        @pl.when(self.sends)
        def _():
            self.copy().wait_send()


class RouteIn:
    def __init__(self, seqs, pairs, local, send, recv):
        self.pairs, self.local, self.send_sem, self.recv_sem = pairs, local, send, recv
        x, c, z = (lax.axis_index(a) for a in ("section", "dp", "z"))
        self.sends = lax.rem(z, 2) == x
        self.targets = []
        for micro in range(pairs[0][0].shape[0]):
            to_c, to_z = z // 2, micro * seqs + c
            self.targets.append(({"dp": to_c, "z": to_z}, (to_c == c) & (to_z == z)))
        self.micro = z // seqs
        self.source = {"dp": lax.rem(z, seqs), "z": c * 2 + x}
        self.same = (lax.rem(z, seqs) == c) & (c * 2 + x == z)

    def greet(self):
        barrier = pltpu.get_barrier_semaphore()

        @pl.when(jnp.logical_not(self.same))
        def _():
            pl.semaphore_signal(barrier, inc=1, device_id=self.source, device_id_type=MESH)

        return sum(jnp.where(self.sends & jnp.logical_not(same), 1, 0) for _, same in self.targets)

    def far(self, i, micro):
        src, dst = self.pairs[i]
        return remote(src.at[micro, 0], dst, self.send_sem.at[i, micro], self.recv_sem.at[i], self.targets[micro][0])

    def near(self, i, micro):
        src, dst = self.pairs[i]
        return pltpu.make_async_copy(src.at[micro, 0], dst, self.local.at[i])

    def start(self, i=0):
        for micro, (_, same) in enumerate(self.targets):

            @pl.when(self.sends & jnp.logical_not(same))
            def _(micro=micro):
                self.far(i, micro).start()

            @pl.when(self.sends & same)
            def _(micro=micro):
                self.near(i, micro).start()

    def tick(self, point):
        pass

    def made(self, part):
        pass

    def middle(self):
        pass

    def arrived(self, i):
        dst = self.pairs[i][1]

        @pl.when(jnp.logical_not(self.same))
        def _():
            remote(dst, dst, self.send_sem.at[i, 0], self.recv_sem.at[i], self.source).wait_recv()

        for micro, (_, same) in enumerate(self.targets):

            @pl.when(self.sends & same)
            def _(micro=micro):
                self.near(i, micro).wait()

    def finish(self):
        for i in range(len(self.pairs)):
            for micro, (_, same) in enumerate(self.targets):

                @pl.when(self.sends & jnp.logical_not(same))
                def _(i=i, micro=micro):
                    self.far(i, micro).wait_send()


def reorder(raw, ordered, zs, wide):
    for c in range(2):
        for k in range(zs):
            at, to = (c * zs + k) * wide, (k * 2 + c) * wide
            ordered[:, to : to + wide] = raw[:, at : at + wide]


class Shared:
    def __init__(self, src, gather, points):
        self.src, self.gather, self.points = src, gather, points

    def greet(self):
        return 0

    def start(self):
        pass

    def made(self, part):
        pass

    def middle(self):
        pass

    def tick(self, point):
        if point == self.points[0]:
            self.gather.start(self.src)
        if point == self.points[1]:
            for k in range(1, self.gather.peers.chips):
                self.gather.forward(k)

    def finish(self):
        for k in range(self.gather.peers.chips):
            self.gather.chip(k)
        self.gather.finish()


class Several:
    def __init__(self, works):
        self.works = works

    def greet(self):
        return sum(work.greet() for work in self.works)

    def start(self):
        for work in self.works:
            work.start()

    def tick(self, point):
        for work in self.works:
            work.tick(point)

    def made(self, part):
        for work in self.works:
            work.made(part)

    def middle(self):
        for work in self.works:
            work.middle()

    def finish(self):
        for work in self.works:
            work.finish()


class NoSide:
    def greet(self):
        return 0

    def start(self):
        pass

    def tick(self, point):
        pass

    def made(self, part):
        pass

    def middle(self):
        pass

    def finish(self):
        pass


class Both:
    def greet(self):
        return 0

    def __init__(self, ring, turn):
        self.ring, self.turn, self.turned = ring, turn, False

    def start(self):
        self.ring.start()

    def tick(self, count=1):
        self.ring.tick(count)

    def finish(self):
        while self.ring.steps:
            if self.ring.take() == 0:
                self.turn.start()
        self.ring.finish()
        self.turn.finish()


class Fetch:
    def __init__(self, far, near, sem):
        self.far, self.near = far, near
        self.copy = pltpu.make_async_copy(far, near, sem)
        self.copy.start()
        self.here = False
        self.shape = near.shape

    def __getitem__(self, index):
        if not self.here:
            self.copy.wait()
            self.here = True
        return self.near[index]

    def finish(self):
        if not self.here:
            self.copy.wait()


def far(ref):
    return ref.far if isinstance(ref, Fetch) else ref


class Paced:
    def __init__(self, work, pace):
        self.work, self.pace = work, pace
        self.greet, self.start, self.finish = work.greet, work.start, work.finish
        self.middle = getattr(work, "middle", lambda: None)
        self.part = None

    def made(self, part):
        self.part = part
        if "launch" not in self.pace:
            self.work.made(part)

    def tick(self, point):
        self.work.tick(self.pace.get(point, 0))
        if self.part is not None and self.pace.get("launch") == point:
            self.work.made(self.part)


class SideWork:
    def __init__(self, operands=(), in_hbm=(), outs=(), out_hbm=(), scratch=(), build=None):
        self.operands, self.in_hbm, self.outs, self.out_hbm = operands, in_hbm, outs, out_hbm
        self.scratch, self.build = scratch, build
        self.zs = 1 if build is None else 2

    def make(self, peers, ins, outs, scratch):
        return NoSide() if self.build is None else self.build(peers, ins, outs, scratch)


def route_side(lay, src, when):
    dma = pltpu.SemaphoreType.DMA
    outs = [((lay.micros, *src.shape), BF)]

    def build(peers, ins, outs, scratch):
        return Route(lay.seqs, ins[0], outs[0], *scratch, when)

    return SideWork([src], (True,), outs, (True,), [dma, dma, dma((lay.micros,))], build)


def share_side(lay, a, points):
    chips = lay.slab // 2

    def build(peers, ins, outs, scratch):
        return Shared(ins[0], Gather(peers, outs[0], scratch), points)

    return SideWork([a], (False,), [((chips, 2, *a.shape), BF)], (False,), [pltpu.SemaphoreType.DMA((chips,))] * 4, build)


def across_side(layer, a):
    dma = pltpu.SemaphoreType.DMA

    def build(peers, ins, outs, scratch):
        return Across(layer, ins[0], outs[0], *scratch)

    return SideWork([a], (True,), [(a.shape, a.dtype)], (True,), [dma, dma], build)


def both_sides(*sides):
    sides = [side for side in sides if side.build is not None]
    joined = [[], [], [], [], []]
    for side in sides:
        for into, more in zip(joined, (side.operands, side.in_hbm, side.outs, side.out_hbm, side.scratch)):
            into += list(more)

    def build(peers, ins, outs, scratch):
        works = []
        for side in sides:
            a, b, c = len(side.operands), len(side.outs), len(side.scratch)
            works.append(side.build(peers, ins[:a], outs[:b], scratch[:c]))
            ins, outs, scratch = ins[a:], outs[b:], scratch[c:]
        return Several(works)

    return SideWork(*joined, build)


def gather_side(shards, pace, counts=None, turn=None):
    zs = lax.axis_size("z")
    n = len(shards)
    counts = counts or (zs - 1,) * n
    places = [a[1] if isinstance(a, tuple) else None for a in shards]
    shards = [a[0] if isinstance(a, tuple) else a for a in shards]
    outs = [((zs, *a.shape[-2:]), BF) for a in shards]
    sems = [pltpu.SemaphoreType.DMA((n,))] + [pltpu.SemaphoreType.DMA((n, zs - 1))] * 2
    if turn is None:

        def build(peers, ins, outs, scratch):
            ins = [a if place is None else a.at[place] for a, place in zip(ins, places)]
            return Paced(RingGather(list(zip(ins, outs, counts)), *scratch), pace)

        return SideWork(shards, (True,) * n, outs, (True,) * n, sems, build)
    slab = 2 * lax.axis_size("section") * lax.axis_size("r")
    cols = shards[0].shape[1]
    outs[0] = ((turn, slab * cols), BF)
    more = [
        pltpu.VMEM((zs, *shards[0].shape), BF),
        pltpu.VMEM((slab * turn, cols), BF),
        pltpu.VMEM((slab, turn, cols), BF),
    ] + [pltpu.SemaphoreType.DMA((slab,))] * 2

    def build_turn(peers, ins, outs, scratch):
        pieces = list(zip(ins, [scratch[3], *outs[1:]], counts))
        turning = Turn(peers, scratch[3], scratch[4], scratch[5], outs[0], *scratch[6:8])
        return Paced(Both(RingGather(pieces, *scratch[:3]), turning), pace)

    return SideWork(shards, (True,) * n, outs, (False,) + (True,) * (n - 1), sems + more, build_turn)


def sum_side(pieces, pace, turned=None, cols=0):
    zs = lax.axis_size("z")
    n = len(pieces)
    operands, outs, scratch = [], [], []
    for part, shape, acc, first, count in pieces:
        operands += [a for a in (part, acc) if a is not None]
        outs.append((shape, BF))
        scratch.append(pltpu.VMEM((count, *shape), BF))
    scratch += [pltpu.SemaphoreType.DMA((n, zs - 1))] * 2
    if turned is not None:
        operands.append(turned)
        slab = turned.shape[1] // cols
        rows = turned.shape[1] // zs
        outs.append(((zs, rows, cols), BF))
        scratch += [pltpu.VMEM((slab, turned.shape[0], cols), BF)] * 2 + [pltpu.SemaphoreType.DMA((slab,))] * 2

    def build(peers, ins, outs, scratch):
        ins, made = list(ins), []
        for i, (part, shape, acc, first, count) in enumerate(pieces):
            part_ref = None if part is None else ins.pop(0)
            acc_ref = None if acc is None else ins.pop(0)
            made.append((part_ref, acc_ref, scratch[i], outs[i], first, count))
        ring = RingSum(made, *scratch[n : n + 2])
        if turned is None:
            return Paced(ring, pace)
        return Paced(SumAndTurn(ring, TurnBack(peers, ins.pop(0), outs[n], *scratch[n + 2 :])), pace)

    return SideWork(operands, (False,) * len(operands), outs, (False,) * len(outs), scratch, build)


def gather_scratch(chips, rows, width):
    return [pltpu.VMEM((chips, 2, rows, width), BF)] + [pltpu.SemaphoreType.DMA((chips,))] * 4


def reduce_scratch(chips, rows, width):
    return [
        pltpu.VMEM((chips, rows, width), F32),
        pltpu.VMEM((chips, rows, width), BF),
        pltpu.VMEM((chips, rows, width), BF),
        pltpu.VMEM((chips - 1, rows, width), BF),
        pltpu.VMEM((chips - 1, rows, width), BF),
    ] + [pltpu.SemaphoreType.DMA((chips,))] * 4


def norm_parts(v):
    centred = v - jnp.mean(v, axis=-1, keepdims=True)
    spread = jnp.mean(centred * centred, axis=-1, keepdims=True)
    scale = lax.rsqrt(spread + EPSILON)
    return centred * scale, scale


def norm_back(v, gain, grad):
    unit, scale = norm_parts(v)
    scaled = grad * gain
    part = scaled - jnp.mean(scaled, axis=-1, keepdims=True)
    part = part - unit * jnp.mean(scaled * unit, axis=-1, keepdims=True)
    return part * scale, jnp.sum(grad * unit, axis=0, keepdims=True), jnp.sum(grad, axis=0, keepdims=True)


def dot(a, b, ca=1, cb=0):
    return lax.dot_general(a, b, (((ca,), (cb,)), ((), ())), preferred_element_type=F32)


def chip_rows(chip, rows):
    return pl.ds(pl.multiple_of(chip * (2 * rows), 2 * rows), 2 * rows)


def groups(span, head):
    wide = 128 if span % 128 == 0 else span
    for g in range(span // wide):
        yield slice(g * wide, (g + 1) * wide), [(g * wide // head + i, i * head) for i in range(wide // head)]


def only(a, start, head):
    lane = lax.broadcasted_iota(jnp.int32, a.shape, 1)
    return jnp.where((lane >= start) & (lane < start + head), a, jnp.zeros_like(a))


def attention_forward(head, side, *refs):
    (h, w_qkv, w_out, bias, col, row, vec) = refs[:7]
    ins, refs = refs[7 : 7 + len(side.operands)], refs[7 + len(side.operands) :]
    (normed, qkv, attended, logs, mid, normed_two), refs = refs[:6], refs[6:]
    side_outs, refs = refs[: len(side.outs)], refs[len(side.outs) :]
    gather_refs, reduce_refs, side_refs = refs[:5], refs[5 : 14 + 1], refs[14 + 1 :]
    rows, width = h.shape
    span = w_out.shape[0]
    peers = Peers()
    gather = Gather(peers, gather_refs[0], gather_refs[1:])
    reduce = Reduce(peers, *reduce_refs[:5], reduce_refs[5:9])
    kept_sem = reduce_refs[9]
    full = gather.full
    work = side.make(peers, ins, side_outs, side_refs)
    peers.greet(side.zs, work)
    gather.start((norm_parts(h[...].astype(F32))[0] * vec[0:1, :] + vec[2:3, :]).astype(BF))
    work.start()
    for k, chip in gather.arrivals():
        part = dot(full[chip].reshape(2 * rows, width), w_qkv[...]) + bias[...]
        qkv[chip_rows(chip, rows), :] = part.astype(BF)
    work.tick("qkv")
    kept = pltpu.make_async_copy(full, normed, kept_sem)
    kept.start()
    scale = head ** (-0.5)
    order = list(range(1, peers.chips)) + [0]
    before = None
    for k in order:
        chip = peers.behind_chip(k)
        here = chip_rows(chip, rows)
        block = jnp.where(col[...] <= row[:, here], 0.0, LOW).astype(F32)
        for lanes, heads in groups(span, head):
            q = qkv[here, lanes]
            keys = qkv[:, slice(span + lanes.start, span + lanes.stop)]
            values = qkv[:, slice(2 * span + lanes.start, 2 * span + lanes.stop)]
            merged = None
            for slot, start in heads:
                scores = dot(keys, only(q, start, head) * scale, 1, 1) + block
                top = jnp.max(scores, axis=0, keepdims=True)
                weights = jnp.exp(scores - top)
                total = jnp.sum(weights, axis=0, keepdims=True)
                logs[slot : slot + 1, here] = top + jnp.log(total)
                mixed = dot(values, weights.astype(BF), 0, 0) / total
                lane = lax.broadcasted_iota(jnp.int32, mixed.shape, 0)
                merged = mixed if merged is None else jnp.where(lane >= start, mixed, merged)
            attended[here, lanes] = merged.T.astype(BF)
        reduce.put(k, dot(attended[here, :], w_out[...]))
        if before is not None:
            reduce.push(before)
        work.tick("q%d" % order.index(k))
        before = k
    reduce.push(before)
    out = h[...].astype(F32) + (reduce.total() + vec[4:5, :])
    mid[...] = out
    normed_two[...] = (norm_parts(out)[0] * vec[1:2, :] + vec[3:4, :]).astype(BF)
    work.finish()
    gather.finish()
    reduce.finish()
    kept.wait()


ROOT = 0.7978845608028654


def feed_forward(side, *refs):
    (src, mid, w_fc, w_proj, bias, vec) = refs[:6]
    ins, refs = refs[6 : 6 + len(side.operands)], refs[6 + len(side.operands) :]
    (normed_two, slope, activated, result, proj_out), refs = refs[:5], refs[5:]
    side_outs, refs = refs[: len(side.outs)], refs[len(side.outs) :]
    gather_refs, reduce_refs, side_refs = refs[:5], refs[5 : 14 + 6], refs[14 + 6 :]
    rows, width = src.shape
    peers = Peers()
    gather = Gather(peers, gather_refs[0], gather_refs[1:])
    reduce = Reduce(peers, *reduce_refs[:5], reduce_refs[5:9])
    kept_sem, proj, proj_local, proj_send, proj_recv, proj_sem = reduce_refs[9:15]
    full = gather.full
    work = side.make(peers, ins, side_outs, side_refs)
    zs, z = lax.axis_size("z"), lax.axis_index("z")
    half = proj.shape[1]
    peers.greet(2, work)
    gather.start(src)
    there = lax.rem(z + 2, zs)
    last = remote(w_proj.at[there], proj.at[there], proj_send, proj_recv, {"z": lax.rem(z + 1, zs)})
    last.start()
    here = [lax.rem(z + zs - i, zs) for i in range(zs - 1)]
    placed = [pltpu.make_async_copy(w_proj.at[b], proj.at[b], proj_local.at[i]) for i, b in enumerate(here)]
    for copy in placed:
        copy.start()
    before = None
    for k, chip in gather.arrivals():
        if k == 0:
            last.wait_recv()
            work.start()
            for copy in placed:
                copy.wait()
            proj_kept = pltpu.make_async_copy(proj, proj_out, proj_sem)
            proj_kept.start()
        here = chip_rows(chip, rows)
        u = dot(full[chip].reshape(2 * rows, width), w_fc[...]) + bias[...]
        bend = jnp.tanh(ROOT * (u + 0.044715 * (u * u * u)))
        slope[here, :] = (0.5 * (1.0 + bend) + 0.5 * u * (1.0 - bend * bend) * (ROOT * (1.0 + 3 * 0.044715 * (u * u)))).astype(BF)
        act = (0.5 * u * (1.0 + bend)).astype(BF)
        activated[here, :] = act
        back = dot(act[:, :half], proj[0])
        for b in range(1, zs):
            back = back + dot(act[:, b * half : (b + 1) * half], proj[b])
        reduce.put(k, back)
        if before is not None:
            reduce.push(before)
        work.tick("k%d" % k)
        before = k
    kept = pltpu.make_async_copy(full, normed_two, kept_sem)
    kept.start()
    reduce.push(before)
    work.tick("sent")
    out = (mid[...] + (reduce.total() + vec[5:6, :])).astype(BF)
    result[...] = out
    last.wait_send()
    proj_kept.wait()
    work.finish()
    gather.finish()
    reduce.finish()
    kept.wait()


def chunks(size, step):
    return [(a, min(a + step, size)) for a in range(0, size, step)]


def feed_backward(side, ready, *refs):
    (src, mid, w_fc, w_proj, slope, activated, normed_two, vec, *given) = refs[: 8 + ready]
    refs = refs[8 + ready :]
    ins, refs = refs[: len(side.operands)], refs[len(side.operands) :]
    (grad_mid, attn_rows, grad_proj, grad_fc, sums, unit_sums), refs = refs[:6], refs[6:]
    side_outs, refs = refs[: len(side.outs)], refs[len(side.outs) :]
    gather_refs, reduce_refs, side_refs = refs[:5], refs[5 : 14 + 1], refs[14 + 1 :]
    hidden, = reduce_refs[9:10]
    rows, width = src.shape
    tokens = slope.shape[0]
    peers = Peers()
    gather = Gather(peers, gather_refs[0], gather_refs[1:])
    reduce = Reduce(peers, *reduce_refs[:5], reduce_refs[5:9])
    full = given[0] if ready else gather.full
    work = side.make(peers, ins, side_outs, side_refs)
    peers.greet(side.zs, work)
    half = grad_proj.shape[1]

    def proj_terms():
        branch = full[...].reshape(tokens, width)
        for b in range(grad_proj.shape[0]):
            grad_proj[b] = dot(activated[:, b * half : (b + 1) * half], branch, 0, 0).astype(BF)
        work.made(grad_proj)

    if ready:
        order = [(k, peers.behind_chip(k)) for k in (*range(1, peers.chips), 0)]
    else:
        gather.start(src)
        order = gather.arrivals()
    work.start()
    if ready:
        proj_terms()
    before = None
    for k, chip in order:
        here = chip_rows(chip, rows)
        back = dot(full[chip].reshape(2 * rows, width), w_proj[...], 1, 1) * slope[here, :].astype(F32)
        back = back.astype(BF)
        hidden[here, :] = back
        reduce.put(k, dot(back, w_fc[...], 1, 1))
        if before is not None:
            reduce.push(before)
        work.tick("k%d" % k)
        before = k
    reduce.push(before)
    work.middle()
    if not ready:
        proj_terms()
    work.tick("proj")
    back = hidden[...]
    for a, b in chunks(width, 512):
        grad_fc[a:b, :] = dot(normed_two[:, a:b], back, 0, 0).astype(BF)
    work.tick("fc")
    unit_sums[...] = jnp.sum(back.astype(F32), axis=0, keepdims=True)
    own = src[...].astype(F32)
    part, gain, shift = norm_back(mid[...], vec[1:2, :], reduce.total())
    out = own + part
    grad_mid[...] = out
    low = out.astype(BF)
    attn_rows[...] = low
    sums[0:1, :] = gain
    sums[1:2, :] = shift
    sums[2:3, :] = jnp.sum(own, axis=0, keepdims=True)
    sums[3:4, :] = jnp.sum(low.astype(F32), axis=0, keepdims=True)
    sums[4:8, :] = jnp.zeros((4, width), F32)
    work.finish()
    if not ready:
        gather.finish()
    reduce.finish()


def attention_backward(head, side, *refs):
    (src, grad_mid, h, w_qkv, w_out, qkv, attended, logs, normed, col, row, vec) = refs[:12]
    ins, refs = refs[12 : 12 + len(side.operands)], refs[12 + len(side.operands) :]
    (grad_in, grad_qkv, grad_out, sums, head_sums), refs = refs[:5], refs[5:]
    side_outs, refs = refs[: len(side.outs)], refs[len(side.outs) :]
    gather_refs, reduce_refs, side_refs = refs[:5], refs[5 : 14 + 3], refs[14 + 3 :]
    joint, key_sum, value_sum = reduce_refs[9:12]
    rows, width = src.shape
    tokens, span = attended.shape
    scale = head ** (-0.5)
    peers = Peers()
    gather = Gather(peers, gather_refs[0], gather_refs[1:])
    reduce = Reduce(peers, *reduce_refs[:5], reduce_refs[5:9])
    full = gather.full
    work = side.make(peers, ins, side_outs, side_refs)
    peers.greet(side.zs, work)
    gather.start(src)
    work.start()
    for k, chip in gather.arrivals():
        here = chip_rows(chip, rows)
        g_all = dot(full[chip].reshape(2 * rows, width), w_out[...], 1, 1).astype(BF)
        block = jnp.where(col[...] <= row[:, here], 0.0, LOW).astype(F32)
        for lanes, heads in groups(span, head):
            q = qkv[here, lanes]
            g = g_all[:, lanes]
            keys = qkv[:, slice(span + lanes.start, span + lanes.stop)]
            values = qkv[:, slice(2 * span + lanes.start, 2 * span + lanes.stop)]
            merged = None
            key_term, value_term = 0.0, 0.0
            for slot, start in heads:
                q_one, g_one = only(q, start, head) * scale, only(g, start, head)
                probs = jnp.exp(dot(keys, q_one, 1, 1) + block - logs[slot : slot + 1, here])
                g_probs = dot(values, g_one, 1, 1)
                both = probs * g_probs
                centre = jnp.sum(both, axis=0, keepdims=True)
                g_scores = (both - probs * centre).astype(BF)
                value_term += dot(probs.astype(BF), g_one)
                key_term += dot(g_scores, q_one)
                g_query = dot(keys, g_scores, 0, 0)
                lane = lax.broadcasted_iota(jnp.int32, g_query.shape, 0)
                merged = g_query if merged is None else jnp.where(lane >= start, g_query, merged)
            joint[here, lanes] = (merged.T * scale).astype(BF)
            if k == 0:
                key_sum[:, lanes] = key_term
                value_sum[:, lanes] = value_term
            else:
                key_sum[:, lanes] += key_term
                value_sum[:, lanes] += value_term
        work.tick("k%d" % k)
    joint[:, span : 2 * span] = key_sum[...].astype(BF)
    joint[:, 2 * span :] = value_sum[...].astype(BF)
    order = list(range(1, peers.chips)) + [0]
    before = None
    for k in order:
        reduce.put(k, dot(joint[chip_rows(peers.behind_chip(k), rows), :], w_qkv[...], 1, 1))
        if before is not None:
            reduce.push(before)
        before = k
    work.tick("sent")
    grads = joint[...]
    for a, b in chunks(width, 512):
        grad_qkv[a:b, :] = dot(normed[:, a:b], grads, 0, 0).astype(BF)
    work.tick("grad")
    grad_out[...] = dot(attended[...], full[...].reshape(tokens, width), 0, 0).astype(BF)
    head_sums[...] = jnp.sum(grads.astype(F32), axis=0, keepdims=True)
    part, gain, shift = norm_back(h[...].astype(F32), vec[0:1, :], reduce.total())
    grad_in[...] = (grad_mid[...] + part).astype(BF)
    sums[0:1, :] = gain
    sums[1:2, :] = shift
    sums[2:8, :] = jnp.zeros((6, width), F32)
    work.finish()
    gather.finish()
    reduce.finish()


def call(kernel, name, outs, operands, side, kept, scratch, keep=()):
    chips = lax.axis_size("section") * lax.axis_size("r")
    rows, width = operands[0].shape
    vmem, hbm = pl.BlockSpec(memory_space=pltpu.VMEM), pl.BlockSpec(memory_space=pl.ANY)
    every = [*operands, *side.operands]
    fetched = [i for i in range(len(every)) if i not in keep and not (i >= len(operands) and side.in_hbm[i - len(operands)])]
    work = gather_scratch(chips, rows, width) + reduce_scratch(chips, rows, width) + scratch + list(side.scratch)

    def body(*refs):
        refs = list(refs)
        near, sems = refs[-1 - len(fetched) : -1], refs[-1]
        for k, i in enumerate(fetched):
            refs[i] = Fetch(refs[i], near[k], sems.at[k])
        kernel(*refs[: -1 - len(fetched)])
        for i in fetched:
            refs[i].finish()

    out = pl.pallas_call(
        body,
        out_shape=[jax.ShapeDtypeStruct(*o) for o in (*outs, *side.outs)],
        in_specs=[hbm] * len(every),
        out_specs=[hbm if i in kept else vmem for i in range(len(outs))] + [hbm if i else vmem for i in side.out_hbm],
        scratch_shapes=work
        + [pltpu.VMEM(every[i].shape, every[i].dtype) for i in fetched]
        + [pltpu.SemaphoreType.DMA((len(fetched),))],
        compiler_params=pltpu.CompilerParams(collective_id=name, has_side_effects=True, vmem_limit_bytes=60 * 2**20),
    )(*every)
    return out[: len(outs)], out[len(outs) :]


def run_attention_forward(name, head, side, *operands):
    h, w_qkv, w_out, bias, col, row, vec = operands
    rows, width = h.shape
    tokens, span = col.shape[0], w_out.shape[0]
    slots = -(-(span // head) // 8) * 8
    chips = tokens // (2 * rows)
    outs = [
        ((chips, 2, rows, width), BF),
        ((tokens, 3 * span), BF),
        ((tokens, span), BF),
        ((slots, tokens), F32),
        ((rows, width), F32),
        ((rows, width), BF),
    ]
    return call(functools.partial(attention_forward, head, side), name, outs, operands, side, (0,), [pltpu.SemaphoreType.DMA])


def run_feed_forward(name, side, *operands):
    src, mid, w_fc, w_proj, bias, vec = operands
    rows, width = src.shape
    units = w_fc.shape[1]
    chips = lax.axis_size("section") * lax.axis_size("r")
    tokens = 2 * chips * rows
    outs = [
        ((chips, 2, rows, width), BF),
        ((tokens, units), BF),
        ((tokens, units), BF),
        ((rows, width), BF),
        (w_proj.shape, BF),
    ]
    dma = pltpu.SemaphoreType.DMA
    scratch = [dma, pltpu.VMEM(w_proj.shape, BF), dma((w_proj.shape[0],)), dma, dma, dma]
    return call(functools.partial(feed_forward, side), name, outs, operands, side, (0, 4), scratch, (3,))


def run_feed_backward(name, side, *operands):
    src, mid, w_fc, w_proj, slope, activated, normed_two, vec, *given = operands
    rows, width = src.shape
    tokens, units = slope.shape
    zs = lax.axis_size("z")
    outs = [
        ((rows, width), F32),
        ((rows, width), BF),
        ((zs, units // zs, width), BF),
        ((width, units), BF),
        ((8, width), F32),
        ((1, units), F32),
    ]
    return call(functools.partial(feed_backward, side, len(given)), name, outs, operands, side, (), [pltpu.VMEM((tokens, units), BF)])


def run_attention_backward(name, head, side, *operands):
    src, grad_mid, h, w_qkv, w_out, qkv, attended, logs, normed, col, row, vec = operands
    rows, width = src.shape
    tokens, span = attended.shape
    outs = [
        ((rows, width), BF),
        ((width, 3 * span), BF),
        ((span, width), BF),
        ((8, width), F32),
        ((1, 3 * span), F32),
    ]
    scratch = [pltpu.VMEM((tokens, 3 * span), BF), pltpu.VMEM((tokens, span), F32), pltpu.VMEM((tokens, span), F32)]
    return call(functools.partial(attention_backward, head, side), name, outs, operands, side, (), scratch)


def start_kernel(sizes, *refs):
    block, span, half, seqs, micros = sizes
    (tiny, w_qkv, w_attn, w_fc, w_proj, inputs, cotangent), refs = refs[:7], refs[7:]
    (qkv, wo, fc, (proj, qkv_full, w_out, h, g, row, *smalls)), refs = (refs[0:2], refs[2:4], refs[4:6], refs[6:18]), refs[18:]
    tiny_out, stage, h_raw, g_raw, natural, proj_cut = refs[:6]
    cuts, lands, (wo_full, nat, land), refs = refs[6:9], refs[9:12], refs[12:15], refs[15:]
    z_send, z_recv, *sems = refs[:6]
    all_send, all_recv, far_send, far_recv, turn_send, turn_recv = refs[6:12]
    ring_local, ring_send, ring_recv, *route_sems = refs[12:]
    peers = Peers()
    zs, z = lax.axis_size("z"), lax.axis_index("z")
    x, rest, slab = peers.x, peers.rest, 2 * peers.chips
    sections = peers.sections
    spot = peers.c * rest + peers.r
    width, wide = w_attn.shape[1], rest * block
    _, me = peers.other(0, 0, 0)
    route = RouteIn(seqs, [(inputs, h_raw), (cotangent, g_raw)], *route_sems)
    peers.greet(zs, route)
    sent = []

    def send(copy):
        copy.start()
        sent.append(copy)

    for k in range(1, zs):
        send(remote(tiny, stage.at[z], z_send.at[k], z_recv.at[k], {"z": lax.rem(z + k, zs)}))
    stage[z] = tiny[...]
    route.start(0)
    route.start(1)

    def share(a):
        for i, place in peers.offsets():
            device, t = peers.other(*place)
            send(remote(cuts[a].at[t], lands[a].at[x, spot], all_send.at[a, i], all_recv.at[a, i], device))
        lands[a][x, spot] = cuts[a][me]

    def settle(a, shard):
        for i, place in peers.offsets():
            device, _ = peers.other(*(-d for d in place))
            came = lands[a].at[device["section"], device["dp"] * rest + device["r"]]
            remote(came, came, all_send.at[a, i], all_recv.at[a, i], device).wait_recv()
        for layer in range(sections):
            for i in range(2 * rest):
                shard[layer][i * block : (i + 1) * block, :] = lands[a][layer, i, :block, :]

    cols = width // slab
    for t in range(slab):
        big, off = divmod(t * cols, wide)
        at = (big % 2 * zs + big // 2) * wide + off
        cuts[0][t, :block, :] = w_attn[:, at : at + cols]
    share(0)
    for t in range(slab):
        count = max(0, min(span, width - t * span))
        for p in range(3):
            if count:
                at = p * width + t * span
                cuts[1][t, :block, p * span : p * span + count] = w_qkv[:, at : at + count]
            if count < span:
                cuts[1][t, :block, p * span + count : (p + 1) * span] = jnp.zeros((block, span - count), BF)
    share(1)
    for t in range(slab):
        a, c, r = t // (2 * rest), t // rest % 2, t % rest
        for k in range(zs):
            at = ((c * zs + k) * rest + r) * (sections * half) + a * half
            cuts[2][t, :block, k * half : (k + 1) * half] = w_fc[:, at : at + half]
    for a in range(sections):
        for c in range(2):
            for k in range(zs):
                at, to = (c * zs + k) * wide, (k * 2 + c) * wide
                proj_cut[a, :, to : to + wide] = w_proj[a * half : (a + 1) * half, at : at + wide]
    for k in range(1, zs):
        came = stage.at[lax.rem(z + zs - k, zs)]
        remote(came, came, z_send.at[k], z_recv.at[k], {"z": lax.rem(z + k, zs)}).wait_recv()
    gather = Gather(peers, tiny_out, sems)
    gather.start(stage)
    settle(0, wo)
    settle(1, qkv)
    turn = Turn(peers, wo_full, nat, land, w_out, turn_send, turn_recv)
    ring = RingGather([(wo[0], wo_full, zs - 1), (qkv[0], qkv_full, zs - 1)], ring_local, ring_send, ring_recv)
    work = Both(ring, turn)
    work.start()
    share(2)
    for d in range(1, sections):
        device, _ = peers.other(d, 0, 0)
        there = lax.rem(x + d, sections)
        send(remote(proj_cut.at[there], proj.at[x], far_send.at[d], far_recv.at[d], device))
    proj[x] = proj_cut[x]
    for _ in gather.arrivals():
        pass

    per_row, halves = sections * half // block, half // block
    for layer in range(sections):
        vec, bias, unit = smalls[3 * layer : 3 * layer + 3]
        natural[...] = jnp.zeros_like(natural)
        for c in range(2):
            for k in range(zs):
                for r in range(rest):
                    at = ((k * 2 + c) * rest + r) * block
                    vec[:, at : at + block] = tiny_out[layer * rest + r, c, k, 0:8, :block]
                    at = ((c * zs + k) * rest + r) * block
                    natural[:, at : at + block] = tiny_out[layer * rest + r, c, k, 0:8, :block]
        own = jnp.zeros((8, span), F32)
        for t in range(slab):
            own = jnp.where(me == t, natural[:, t * span : (t + 1) * span], own)
        bias[:, :span] = own[6:7]
        bias[:, span : 2 * span] = jnp.zeros((1, span), F32)
        bias[:, 2 * span :] = own[7:8]
        for k in range(zs):
            for j in range(halves):
                line = tiny_out[layer * rest + peers.r, peers.c, k, pl.ds(8 + x * halves + j, 1), :block]
                unit[:, k * half + j * block : k * half + (j + 1) * block] = line
    rows = h.shape[0]
    for a in range(sections):
        for r in range(rest):
            for c in range(2):
                at = ((a * rest + r) * 2 + c) * rows
                line = tiny_out[r, 0, c * 2 + a, pl.ds(8 + per_row + z // seqs, 1), :rows]
                row[:, at : at + rows] = line.astype(jnp.int32)
    work.tick()
    settle(2, fc)
    work.tick()
    for i, (raw, ordered) in enumerate([(h_raw, h), (g_raw, g)]):
        route.arrived(i)
        reorder(raw, ordered, zs, wide)
    for d in range(1, sections):
        device, _ = peers.other(-d, 0, 0)
        came = proj.at[device["section"]]
        remote(came, came, far_send.at[d], far_recv.at[d], device).wait_recv()
    work.finish()
    route.finish()
    gather.finish()
    for copy in sent:
        copy.wait_send()


def run_start(name, lay, tiny, w_qkv, w_attn, w_fc, w_proj, inputs, cotangent):
    zs, n, chips, sections = lay.zs, lay.slab, lay.slab // 2, lay.sections
    span, block = lay.slots * lay.head, lay.block
    spots = lay.cores * lay.rest
    rows, tall = spots * block, -(-block // 16) * 16
    vmem, hbm = pl.BlockSpec(memory_space=pltpu.VMEM), pl.BlockSpec(memory_space=pl.ANY)
    units = lay.units // n
    widths = [lay.cols, 3 * span, units]
    flat = inputs.shape[2:]
    outs = [((rows, m), BF) for m in (3 * span, lay.cols, units) for _ in range(sections)]
    outs += [((sections, lay.half, lay.width), BF), ((zs, rows, 3 * span), BF), ((span, lay.width), BF)]
    outs += [(flat, BF), (flat, BF), ((1, lay.tokens), jnp.int32)]
    outs += [((8, lay.width), F32), ((1, 3 * span), F32), ((1, units), F32)] * sections
    dma = pltpu.SemaphoreType.DMA
    return pl.pallas_call(
        functools.partial(start_kernel, (block, span, lay.half, lay.seqs, lay.micros)),
        out_shape=[jax.ShapeDtypeStruct(*o) for o in outs],
        in_specs=[vmem] * 7,
        out_specs=[vmem] * (1 + 3 * sections) + [hbm] + [vmem] * (4 + 3 * sections),
        scratch_shapes=[
            pltpu.VMEM((chips, 2, zs, *tiny.shape), F32),
            pltpu.VMEM((zs, *tiny.shape), F32),
            pltpu.VMEM(flat, BF),
            pltpu.VMEM(flat, BF),
            pltpu.VMEM((8, n * span), F32),
            pltpu.VMEM((sections, lay.half, lay.width), BF),
        ]
        + [pltpu.VMEM((n, tall, m), BF) for m in widths]
        + [pltpu.VMEM((sections, spots, tall, m), BF) for m in widths]
        + [pltpu.VMEM((zs, rows, lay.cols), BF), pltpu.VMEM((n * span, lay.cols), BF), pltpu.VMEM((n, span, lay.cols), BF)]
        + [dma((zs,))] * 2
        + [dma((chips,))] * 4
        + [dma((3, n))] * 2
        + [dma((sections,))] * 2
        + [dma((n,))] * 2
        + [dma((2,))]
        + [dma((2, zs - 1))] * 2
        + [dma((2,)), dma((2, lay.micros)), dma((2,))],
        compiler_params=pltpu.CompilerParams(collective_id=name, has_side_effects=True, vmem_limit_bytes=60 * 2**20),
    )(tiny, w_qkv, w_attn, w_fc, w_proj, inputs, cotangent)


def end_kernel(sizes, *refs):
    block, width, units, seqs = sizes
    (part, turned, qkv_one, wo_one, fc_zero, fc_one, proj_zero, proj_one), refs = refs[:8], refs[8:]
    sums, (last_rows, *ready), refs = refs[:8], refs[8:15], refs[15:]
    (out_qkv, out_wo, out_fc, out_proj, out_small, section_out, section_grad, home, out_rows), refs = refs[:9], refs[9:]
    (qkv_total, wo_part, wo_total, wo_cut, wo_back, proj_both, proj_land), refs = refs[:7], refs[7:]
    stages, lands, refs = refs[:3], refs[3:6], refs[6:]
    (small_land, small_sum, z_land, came_qkv, came_wo, small, natural, rows_buf), refs = refs[:8], refs[8:]
    all_send, all_recv, far_send, far_recv, z_send, z_recv, turn_send, turn_recv, ring_send, ring_recv, late_send, late_recv, *route_sems, rows_sem = refs
    peers = Peers()
    zs, z = lax.axis_size("z"), lax.axis_index("z")
    x, rest, slab = peers.x, peers.rest, 2 * peers.chips
    spot = peers.c * rest + peers.r
    span, cols = turned.shape[0], wo_total.shape[1]
    half, wide = proj_zero.shape[0], rest * block
    _, me = peers.other(0, 0, 0)
    offsets = peers.offsets()
    route = Route(seqs, last_rows, home, *route_sems[:3])
    across = Across(0, home, out_rows, *route_sems[3:5])
    peers.greet(zs, Several([route, across]))
    sent = []

    def send(copy):
        copy.start()
        sent.append(copy)

    ring = RingSum([(part, None, came_qkv, qkv_total, 0, zs - 1)], ring_send, ring_recv)
    ring.start()

    def restore(first_crossed, second, first_home, out):
        whole = lax.rem(z, 2) == x
        for layer, choice in enumerate([(first_home, first_crossed), second]):
            for kind, src in enumerate(choice):

                @pl.when((x == layer) & (whole if kind == 0 else jnp.logical_not(whole)))
                def _(src=src):
                    pltpu.make_async_copy(src, rows_buf, rows_sem).start()

        pltpu.make_async_copy(first_home, rows_buf, rows_sem).wait()
        for micro in range(out.shape[0]):
            for c in range(2):
                for k in range(zs):
                    at, of = (c * zs + k) * wide, (k * 2 + c) * wide
                    out[micro, :, at : at + wide] = rows_buf[micro, :, of : of + wide]

    turn = TurnBack(peers, turned, wo_part, wo_cut, wo_back, turn_send, turn_recv)
    turn.start()
    small[...] = jnp.zeros_like(small)
    halves = half // block
    for layer in range(2):
        feed, attn, heads, unit = sums[4 * layer : 4 * layer + 4]
        for t in range(slab):
            natural[0:1, t * span : (t + 1) * span] = jnp.where(me == t, heads[:, :span], 0.0)
            natural[1:2, t * span : (t + 1) * span] = jnp.where(me == t, heads[:, 2 * span :], 0.0)
        for c in range(2):
            for k in range(zs):
                for r in range(rest):
                    to = small.at[(layer * 2 + c) * rest + r, k]
                    at = slice(((k * 2 + c) * rest + r) * block, ((k * 2 + c) * rest + r + 1) * block)
                    to[0:1, :block] = attn[0:1, at]
                    to[1:2, :block] = feed[0:1, at]
                    to[2:3, :block] = attn[1:2, at]
                    to[5:6, :block] = feed[3:4, at]
                    to[6:8, :block] = feed[1:3, at]
                    at = ((c * zs + k) * rest + r) * block
                    to[3:5, :block] = natural[0:2, at : at + block]
                    own = (peers.c == c) & (peers.r == r)
                    for h in range(2):
                        for j in range(halves):
                            line = unit[0:1, k * half + j * block : k * half + (j + 1) * block]
                            spot_row = 8 + h * halves + j
                            to[spot_row : spot_row + 1, :block] = jnp.where(own & (x == h), line, 0.0)
    for i, place in offsets:
        device, t = peers.other(*place)
        send(remote(small.at[t], small_land.at[me], all_send.at[3, i], all_recv.at[3, i], device))
    small_land[me] = small[me]

    def cut(a, totals):
        for layer, total in enumerate(totals):
            for i in range(2 * rest):
                stages[a][layer, i, :block, :] = total[i * block : (i + 1) * block, :]
        for i, place in offsets:
            device, t = peers.other(*place)
            src = stages[a].at[device["section"], device["dp"] * rest + device["r"]]
            send(remote(src, lands[a].at[me], all_send.at[a, i], all_recv.at[a, i], device))
        lands[a][me] = stages[a][x, spot]

    def settle(a, land):
        for i, place in offsets:
            device, t = peers.other(*(-d for d in place))
            came = land.at[t]
            remote(came, came, all_send.at[a, i], all_recv.at[a, i], device).wait_recv()

    route.start()
    cut(0, (fc_zero, fc_one))
    proj_both[0] = proj_zero[...]
    proj_both[1] = proj_one[...]
    device, _ = peers.other(1, 0, 0)
    send(remote(proj_both.at[1 - x], proj_land.at[x], far_send, far_recv, device))
    proj_land[x] = proj_both[x]

    turn.finish()
    wo_ring = RingSum([(wo_part, None, came_wo, wo_total, 0, zs - 1)], late_send, late_recv)
    wo_ring.start()
    settle(3, small_land)
    total = small_land[0]
    for t in range(1, slab):
        total = total + small_land[t]
    small_sum[...] = total
    for k in range(1, zs):
        there = lax.rem(z + k, zs)
        send(remote(small_sum.at[there], z_land.at[z], z_send.at[k], z_recv.at[k], {"z": there}))
    z_land[z] = small_sum[z]
    ring.tick()
    wo_ring.tick()
    route.arrived()
    across.tick("middle")
    settle(0, lands[0])
    for t in range(slab):
        h, c, r = t // (2 * rest), t // rest % 2, t % rest
        for k in range(zs):
            at = ((c * zs + k) * rest + r) * (units // (2 * zs * rest)) + h * half
            out_fc[:, at : at + half] = lands[0][t, :block, k * half : (k + 1) * half]
    ring.tick()
    wo_ring.tick()
    restore(ready[1], ready[2:4], ready[0], section_out)
    came = proj_land.at[1 - x]
    remote(came, came, far_send, far_recv, device).wait_recv()
    for h in range(2):
        for c in range(2):
            for k in range(zs):
                at, of = (c * zs + k) * wide, (k * 2 + c) * wide
                out_proj[h * half : (h + 1) * half, at : at + wide] = proj_land[h, :, of : of + wide]
    for k in range(1, zs):
        came = z_land.at[lax.rem(z + zs - k, zs)]
        remote(came, came, z_send.at[k], z_recv.at[k], {"z": lax.rem(z + k, zs)}).wait_recv()
    total = z_land[0]
    for k in range(1, zs):
        total = total + z_land[k]
    out_small[...] = total
    wo_ring.finish()
    cut(2, (wo_total, wo_one))
    ring.finish()
    cut(1, (qkv_total, qkv_one))
    settle(2, lands[2])
    for t in range(slab):
        big, off = divmod(t * cols, wide)
        at = (big % 2 * zs + big // 2) * wide + off
        out_wo[:, at : at + cols] = lands[2][t, :block, :]
    settle(1, lands[1])
    for t in range(slab):
        count = min(span, width - t * span)
        for p in range(3):
            if count > 0:
                at = p * width + t * span
                out_qkv[:, at : at + count] = lands[1][t, :block, p * span : p * span + count]
    route.sent()
    across.finish()
    restore(out_rows, ready[4:], home, section_grad)
    for copy in sent:
        copy.wait_send()


def run_end(name, lay, part, turned, qkv_one, wo_one, fcs, projs, sums, last_rows, ready):
    zs, n = lay.zs, lay.slab
    span, width, block = lay.slots * lay.head, lay.width, lay.block
    rows = part.shape[1]
    spots = lay.cores * lay.rest
    tall = -(-block // 16) * 16
    vmem = pl.BlockSpec(memory_space=pltpu.VMEM)
    dma = pltpu.SemaphoreType.DMA
    widths = [fcs[0].shape[1], part.shape[2], lay.cols]
    half = projs[0].shape[0]
    tile = (-(-(8 + lay.unit_block // block) // 8) * 8, 128)
    outs = [(block, 3 * width), (block, width), (block, lay.units), (lay.unit_block, width), tile]
    return pl.pallas_call(
        functools.partial(end_kernel, (block, width, lay.units, lay.seqs)),
        out_shape=[jax.ShapeDtypeStruct(o, BF) for o in outs[:4]] + [jax.ShapeDtypeStruct(outs[4], F32)]
        + [jax.ShapeDtypeStruct((lay.micros, *last_rows.shape), BF)] * 4,
        in_specs=[vmem] * 16 + [pl.BlockSpec(memory_space=pl.ANY)] * 7,
        out_specs=[vmem] * 7 + [pl.BlockSpec(memory_space=pl.ANY)] * 2,
        scratch_shapes=[
            pltpu.VMEM((rows, part.shape[2]), BF),
            pltpu.VMEM((zs, rows, lay.cols), BF),
            pltpu.VMEM((rows, lay.cols), BF),
            pltpu.VMEM((n, span, lay.cols), BF),
            pltpu.VMEM((n, span, lay.cols), BF),
            pltpu.VMEM((2, half, width), BF),
            pltpu.VMEM((2, half, width), BF),
        ]
        + [pltpu.VMEM((lay.sections, spots, tall, m), BF) for m in widths]
        + [pltpu.VMEM((n, tall, m), BF) for m in widths]
        + [
            pltpu.VMEM((n, zs, *tile), F32),
            pltpu.VMEM((zs, *tile), F32),
            pltpu.VMEM((zs, *tile), F32),
            pltpu.VMEM((zs - 1, rows, part.shape[2]), BF),
            pltpu.VMEM((zs - 1, rows, lay.cols), BF),
            pltpu.VMEM((n, zs, *tile), F32),
            pltpu.VMEM((8, n * span), F32),
            pltpu.VMEM((lay.micros, *last_rows.shape), BF),
        ]
        + [dma((4, n))] * 2
        + [dma] * 2
        + [dma((zs,))] * 2
        + [dma((n,))] * 2
        + [dma((2, zs - 1))] * 4
        + [dma, dma, dma((lay.micros,)), dma, dma, dma],
        compiler_params=pltpu.CompilerParams(collective_id=name, has_side_effects=True, vmem_limit_bytes=60 * 2**20),
    )(part, turned, qkv_one, wo_one, *fcs, *projs, *sums, last_rows, *ready)


class Rings:
    def __init__(self, lay):
        self.zs = lay.zs
        self.state = {}

    def put(self, kind, layer, part):
        if part.ndim == 2:
            part = part.reshape(self.zs, part.shape[0] // self.zs, part.shape[1])
        _, acc, steps = self.state.get((kind, layer), (None, None, 0))
        self.state[kind, layer] = (part, acc, steps)

    def side(self, plan, pace, makes={}, turned=None, cols=0):
        pieces = []
        for kind, layer, count in plan:
            part, acc, steps = self.state.get((kind, layer), (None, None, 0))
            shape = makes[kind] if part is None else part.shape[1:]
            pieces.append((part, shape, acc, steps, count))
        return sum_side(pieces, pace, turned, cols)

    def done(self, plan, outs):
        for (kind, layer, count), acc in zip(plan, outs):
            part, _, steps = self.state[kind, layer]
            self.state[kind, layer] = (part, acc, steps + count)


def on_device(
    inputs, cotangent, positions, w_qkv, w_attn_out, w_fc, w_proj, norm_gains, biases, fc_bias
):
    lay = Layout(inputs, w_fc)
    n, block, width = lay.slab, lay.block, lay.width
    span = lay.slots * lay.head

    small = jnp.concatenate([norm_gains[0], biases[0]], axis=1).astype(F32).T
    small = jnp.stack([small[i] for i in (0, 1, 2, 6, 5, 7, 3, 4)])
    small = jnp.concatenate([small, fc_bias[0].reshape(-1, block).astype(F32)])
    small = jnp.pad(small, ((0, 0), (0, 128 - block)))
    places = jnp.pad(positions.astype(F32), ((0, 0), (0, 128 - lay.rows)))
    small = jnp.concatenate([small, places])
    small = jnp.pad(small, ((0, -small.shape[0] % 8), (0, 0)))
    *cut, proj_cut, w_qkv, w_out, h, g, row, vec_0, bias_0, unit_0, vec_1, bias_1, unit_1 = run_start(
        0, lay, small, w_qkv[0], w_attn_out[0], w_fc[0], w_proj[0], inputs, cotangent
    )
    qkv_cut, wo_cut, fc_cut = cut[0:2], cut[2:4], cut[4:6]
    smalls = [(vec_0, bias_0, unit_0), (vec_1, bias_1, unit_1)]
    col = row.reshape(lay.tokens, 1)
    outs, keeps, params = [], [], []
    for layer in range(lay.sections):
        last = layer == lay.sections - 1
        vec, bias, unit = smalls[layer]
        w_qkv = w_qkv.reshape(width, 3 * span)
        side = gather_side([fc_cut[layer], (proj_cut, layer)], {"qkv": 1, "q0": 1, "q3": 1}, (lay.zs - 1, lay.zs - 2))
        if last:
            side = both_sides(side, share_side(lay, g, ("qkv", "q3")))
        (full, qkv, attended, logs, mid, normed_two), (w_fc, w_proj, *shared) = run_attention_forward(
            1 + 2 * layer,
            lay.head,
            side,
            h,
            w_qkv,
            w_out,
            bias,
            col,
            row,
            vec,
        )
        w_fc = w_fc.reshape(width, -1)
        if last:
            side = route_side(lay, outs[0], "start")
        else:
            side = gather_side([wo_cut[layer + 1], qkv_cut[layer + 1]], {"k3": 2}, turn=span)
        (full_two, slope, activated, result, w_proj), later = run_feed_forward(
            2 + 2 * layer, side, normed_two, mid, w_fc, w_proj, unit, vec
        )
        params.append((w_qkv, w_out, w_fc, w_proj.reshape(-1, width)))
        if last:
            (home,), (branch,) = later, shared
        else:
            w_out, w_qkv = later
        keeps.append((h, full, qkv, attended, logs, mid, full_two, slope, activated))
        h = result
        outs.append(h)

    rings = Rings(lay)
    plans = {
        ("feed", 1): [("proj", 1, 3)],
        ("attention", 1): [("fc", 1, 3)],
        ("feed", 0): [("qkv", 1, 3), ("proj", 0, 1)],
        ("attention", 0): [("fc", 0, 3), ("proj", 0, 2), ("out", 1, 3)],
    }
    paces = {
        ("feed", 1): {"proj": 1, "fc": 1},
        ("attention", 1): {"k2": 1, "grad": 1},
        ("feed", 0): {"k2": 1, "fc": 1, "launch": "fc"},
        ("attention", 0): {"k3": 3},
    }
    crossed = {}
    sums = [None] * lay.sections
    grad_out = None
    for layer in reversed(range(lay.sections)):
        w_qkv, w_out, w_fc, w_proj = params[layer]
        vec = smalls[layer][0]
        h, full, qkv, attended, logs, mid, full_two, slope, activated = keeps[layer]
        full, full_two = (a.reshape(lay.tokens, width) for a in (full, full_two))
        name = 1 + 4 * lay.sections - 2 * layer
        side = rings.side(plans["feed", layer], paces["feed", layer], {"proj": (lay.half, width)}, grad_out, lay.cols)
        late = grad_out is None
        if late:
            side = both_sides(side, route_side(lay, outs[1], "start"), across_side(0, home))
        else:
            side = both_sides(side, route_side(lay, g, "fc"))
        (grad_mid, attn_rows, grad_proj, grad_fc, feed_sums, unit_sums), done = run_feed_backward(
            name, side, g, mid, w_fc, w_proj, slope, activated, full_two, vec, *([branch] if late else [])
        )
        rings.put("proj", layer, grad_proj)
        rings.put("fc", layer, grad_fc)
        rings.done(plans["feed", layer], done)
        if late:
            crossed["out", 0] = (home, done[-1])
            home = done[-2]
        else:
            home = done[-1]
            rings.put("out", layer + 1, done[-2])
        side = both_sides(rings.side(plans["attention", layer], paces["attention", layer]), across_side(1, home))
        (g, grad_qkv, grad_out, attn_sums, head_sums), done = run_attention_backward(
            name + 1, lay.head, side, attn_rows, grad_mid, h, w_qkv, w_out, qkv, attended, logs, full, col, row, vec
        )
        rings.done(plans["attention", layer], done)
        crossed["out" if late else "grad", 1] = (home, done[-1])
        rings.put("qkv", layer, grad_qkv)
        sums[layer] = (feed_sums, attn_sums, head_sums, unit_sums)
    out_qkv, out_attn, out_fc, out_proj, rows, section_out, section_grad, *_ = run_end(
        3 + 4 * lay.sections,
        lay,
        rings.state["qkv", 0][0],
        grad_out,
        rings.state["qkv", 1][1],
        rings.state["out", 1][1],
        [rings.state["fc", layer][1] for layer in range(2)],
        [rings.state["proj", layer][1] for layer in range(2)],
        [a for layer in range(2) for a in sums[layer]],
        g,
        [*crossed["out", 0], *crossed["out", 1], *crossed["grad", 1]],
    )
    cols = rows[:8, :block].T
    return (
        section_out[None, :, None],
        section_grad[None, :, None],
        out_qkv.astype(F32)[None],
        out_attn.astype(F32)[None],
        out_fc.astype(F32)[None],
        out_proj.astype(F32)[None],
        cols[None, :, :2],
        cols[None, :, 2:],
        rows[8 : 8 + lay.unit_block // block, :block].reshape(1, lay.unit_block),
    )


def solution(mesh):
    sections, cores, contexts = (mesh.shape[a] for a in ("section", "dp", "ctx"))
    zs = sections * cores
    shape = (sections, cores, zs, contexts // zs)
    inner = Mesh(mesh.devices.reshape(shape), ALL)
    tokens = P(None, "dp", ("z", "r"), None)
    rows = P("section", ("dp", "z", "r"), None)
    units = P("section", ("dp", "z", "r"))
    out_tokens = P("section", None, "dp", ("z", "r"), None)
    return jax.shard_map(
        on_device,
        mesh=inner,
        in_specs=(tokens, tokens, P(None, ("z", "r"))) + (rows,) * 6 + (units,),
        out_specs=(out_tokens, out_tokens) + (rows,) * 6 + (units,),
        check_vma=False,
    )
```

```python
import functools

import jax
import jax.numpy as jnp
from jax import lax
from jax.experimental import pallas as pl
from jax.experimental.pallas import tpu as pltpu
from jax.sharding import Mesh
from jax.sharding import PartitionSpec as P

HEADS = 25
EPSILON = 1e-05

SLAB = ("section", "dp", "r")
ALL = ("section", "dp", "z", "r")
MESH = pl.DeviceIdType.MESH


class Layout:
    def __init__(self, inputs, w_fc):
        self.micros, _, self.rows, self.width = inputs.shape
        self.sections = lax.axis_size("section")
        self.cores = lax.axis_size("dp")
        self.zs = lax.axis_size("z")
        self.rest = lax.axis_size("r")
        self.slab = self.sections * self.cores * self.rest
        self.shards = self.cores * self.zs * self.rest
        self.units = w_fc.shape[2]
        self.tokens = self.rows * self.slab
        self.seqs = self.cores
        self.head = self.width // HEADS
        self.slots = -(-HEADS // self.slab)
        self.block = self.width // self.shards
        self.unit_block = self.units // self.shards
        self.half = self.unit_block // self.sections
        self.cols = self.width // self.slab
        self.x = lax.axis_index("section")
        self.c = lax.axis_index("dp")
        self.z = lax.axis_index("z")
        self.r = lax.axis_index("r")
        self.t = (self.x * self.cores + self.c) * self.rest + self.r

    def number(self, x, c, z, r):
        return ((x * self.cores + c) * self.zs + z) * self.rest + r

    def order(self, a):
        lead = a.shape[:-1]
        a = a.reshape(*lead, self.cores, self.zs, self.rest * self.block)
        return jnp.swapaxes(a, -3, -2).reshape(*lead, self.width)

    def restore(self, a):
        lead = a.shape[:-1]
        a = a.reshape(*lead, self.zs, self.cores, self.rest * self.block)
        return jnp.swapaxes(a, -3, -2).reshape(*lead, self.width)

    def routes(self, micro):
        pairs = []
        for x in range(self.sections):
            for c in range(self.cores):
                for s in range(self.seqs):
                    for r in range(self.rest):
                        place = x * self.cores + c
                        pairs.append(((x, s, place, r), (x, c, micro * self.seqs + s, r)))
        return pairs

    def tokens_in(self, a):
        got = []
        for micro in range(self.micros):
            route = [(self.number(*f), self.number(*g)) for f, g in self.routes(micro)]
            got.append(lax.ppermute(a[micro, 0], ALL, route))
        out = got[0]
        for micro in range(1, self.micros):
            out = jnp.where(self.z // self.seqs == micro, got[micro], out)
        return out

    def tokens_out(self, parts):
        result = []
        for micro in range(self.micros):
            got = []
            for layer, part in enumerate(parts):
                route = [
                    (self.number(*g), self.number(layer, *f[1:])) for f, g in self.routes(micro)
                ]
                got.append(lax.ppermute(part, ALL, route))
            out = got[0]
            for layer in range(1, len(parts)):
                out = jnp.where(self.x == layer, got[layer], out)
            result.append(out)
        return jnp.stack(result)[None, :, None]


LOW = -1e30
BF = jnp.bfloat16
F32 = jnp.float32


class Peers:
    def __init__(self):
        self.sections, self.rest = lax.axis_size("section"), lax.axis_size("r")
        self.chips = self.sections * self.rest
        self.x, self.c, self.r = (lax.axis_index(a) for a in ("section", "dp", "r"))
        self.chip = self.x * self.rest + self.r

    def away(self, k, sign):
        x = lax.rem(self.x + self.sections + sign * (k // self.rest), self.sections)
        r = lax.rem(self.r + self.rest + sign * (k % self.rest), self.rest)
        return x, r

    def ahead(self, k):
        x, r = self.away(k, 1)
        return {"section": x, "dp": self.c, "r": r}

    def behind(self, k):
        x, r = self.away(k, -1)
        return {"section": x, "dp": self.c, "r": r}

    def sibling(self):
        return {"section": self.x, "dp": 1 - self.c, "r": self.r}

    def behind_chip(self, k):
        x, r = self.away(k, -1)
        return x * self.rest + r

    def other(self, dx, dc, dr):
        x = lax.rem(self.x + self.sections + dx, self.sections)
        c = lax.rem(self.c + 2 + dc, 2)
        r = lax.rem(self.r + self.rest + dr, self.rest)
        return {"section": x, "dp": c, "r": r}, (x * 2 + c) * self.rest + r

    def offsets(self):
        every = [(x, c, r) for x in range(self.sections) for c in range(2) for r in range(self.rest)]
        return list(enumerate(every))[1:]

    def greet(self, zs=1, work=None):
        barrier = pltpu.get_barrier_semaphore()
        z = lax.axis_index("z")
        size = lax.axis_size("z")
        for k in range(1, zs):
            pl.semaphore_signal(barrier, inc=1, device_id={"z": lax.rem(z + size - k, size)}, device_id_type=MESH)
        others = self.offsets()
        for _, place in others:
            pl.semaphore_signal(barrier, inc=1, device_id=self.other(*place)[0], device_id_type=MESH)
        more = 0 if work is None else work.greet()
        pl.semaphore_wait(barrier, len(others) + zs - 1 + more)


def remote(src, dst, send, recv, device):
    return pltpu.make_async_remote_copy(
        src_ref=src, dst_ref=dst, send_sem=send, recv_sem=recv, device_id=device, device_id_type=MESH
    )


class Gather:
    def __init__(self, peers, full, sems):
        self.peers, self.full = peers, full
        self.chip_send, self.chip_recv, self.core_send, self.core_recv = sems
        self.sent = []

    def start(self, src):
        p = self.peers
        mine = self.full.at[p.chip, p.c]
        mine[...] = src if isinstance(src, jax.Array) else src[...]
        for k in range(1, p.chips):
            self.send(remote(mine, mine, self.chip_send.at[k], self.chip_recv.at[k], p.ahead(k)))
        self.send(remote(mine, mine, self.core_send.at[0], self.core_recv.at[0], p.sibling()))

    def send(self, copy):
        copy.start()
        self.sent.append(copy)

    def forward(self, k):
        p = self.peers
        block = self.full.at[p.behind_chip(k), p.c]
        remote(block, block, self.chip_send.at[k], self.chip_recv.at[k], p.sibling()).wait_recv()
        self.send(remote(block, block, self.core_send.at[k], self.core_recv.at[k], p.sibling()))

    def chip(self, k):
        p = self.peers
        block = self.full.at[p.behind_chip(k), 1 - p.c]
        remote(block, block, self.core_send.at[k], self.core_recv.at[k], p.sibling()).wait_recv()
        return p.behind_chip(k)

    def arrivals(self):
        yield 0, self.chip(0)
        chips = self.peers.chips
        for k in range(1, chips):
            for later in (1, 2) if k == 1 else (k + 1,):
                if later < chips:
                    self.forward(later)
            yield k, self.chip(k)

    def finish(self):
        for copy in self.sent:
            copy.wait_send()


class Reduce:
    def __init__(self, peers, mine, stage, other, going, coming, sems):
        self.peers = peers
        self.mine, self.stage, self.other, self.going, self.coming = mine, stage, other, going, coming
        self.chip_send, self.chip_recv, self.core_send, self.core_recv = sems
        self.sent = []

    def send(self, copy):
        copy.start()
        self.sent.append(copy)

    def put(self, k, both):
        p = self.peers
        rows = both.shape[0] // 2
        low, high = both[:rows], both[rows:]
        first = p.c == 0
        self.mine[k] = jnp.where(first, low, high)
        self.stage[k] = jnp.where(first, high, low).astype(BF)
        self.send(remote(self.stage.at[k], self.other.at[k], self.core_send.at[k], self.core_recv.at[k], p.sibling()))

    def arrived(self, k):
        p = self.peers
        remote(self.stage.at[k], self.other.at[k], self.core_send.at[k], self.core_recv.at[k], p.sibling()).wait_recv()
        return self.mine[k] + self.other[k].astype(F32)

    def push(self, k):
        p = self.peers
        if k:
            self.going[k - 1] = self.arrived(k).astype(BF)
            self.send(remote(self.going.at[k - 1], self.coming.at[k - 1], self.chip_send.at[k], self.chip_recv.at[k], p.behind(k)))

    def total(self):
        p = self.peers
        out = self.arrived(0)
        for k in range(1, p.chips):
            remote(self.going.at[k - 1], self.coming.at[k - 1], self.chip_send.at[k], self.chip_recv.at[k], p.sibling()).wait_recv()
            out = out + self.coming[k - 1].astype(F32)
        return out

    def finish(self):
        for copy in self.sent:
            copy.wait_send()


class RingGather:
    def greet(self):
        return 0

    def __init__(self, pieces, local, send, recv):
        self.pieces, self.local, self.send_sem, self.recv_sem = pieces, local, send, recv
        self.zs, self.z = lax.axis_size("z"), lax.axis_index("z")
        every = [(p, s) for s in range(self.zs - 1) for p in range(len(pieces)) if s < pieces[p][2]]
        self.steps = [(p, s) for p, s in every if s < pieces[p][2] - 1] + [(p, s) for p, s in every if s == pieces[p][2] - 1]
        self.forwards = len(every) - len(pieces)
        self.sent = []

    def block(self, step):
        return lax.rem(self.z + self.zs - step, self.zs)

    def send(self, p, step, src):
        dst = self.pieces[p][1].at[self.block(step)]
        copy = remote(src, dst, self.send_sem.at[p, step], self.recv_sem.at[p, step], {"z": lax.rem(self.z + 1, self.zs)})
        copy.start()
        self.sent.append(copy)

    def start(self):
        for p in range(len(self.pieces)):
            self.launch(p)

    def launch(self, p):
        shard, full, _ = self.pieces[p]
        self.send(p, 0, shard)
        pltpu.make_async_copy(shard, full.at[self.z], self.local.at[p]).start()

    def tick(self, count=1):
        for _ in range(min(count, self.forwards)):
            self.forwards -= 1
            self.take()

    def take(self):
        p, step = self.steps.pop(0)
        shard, full, count = self.pieces[p]
        block = full.at[self.block(step + 1)]
        remote(block, block, self.send_sem.at[p, step], self.recv_sem.at[p, step], {"z": lax.rem(self.z + 1, self.zs)}).wait_recv()
        if step < count - 1:
            self.send(p, step + 1, block)
            return None
        pltpu.make_async_copy(shard, full.at[self.z], self.local.at[p]).wait()
        return p

    def finish(self):
        while self.steps:
            self.take()
        for copy in self.sent:
            copy.wait_send()


class RingSum:
    def greet(self):
        return 0

    def __init__(self, pieces, send, recv):
        self.pieces, self.send_sem, self.recv_sem = pieces, send, recv
        self.zs, self.z = lax.axis_size("z"), lax.axis_index("z")
        self.steps, self.sent = [], []
        self.late = [p for p, piece in enumerate(pieces) if piece[0] is None]
        ready = [p for p in range(len(pieces)) if p not in self.late]
        self.steps = [(p, i) for i in range(self.zs - 1) for p in ready if i < pieces[p][5] - 1]
        self.forwards = len(self.steps)
        self.steps += [(p, pieces[p][5] - 1) for p in ready]
        self.parts = [piece[0] for piece in pieces]

    def copy(self, p, i, src):
        dst = self.pieces[p][2].at[i]
        return remote(src, dst, self.send_sem.at[p, i], self.recv_sem.at[p, i], {"z": lax.rem(self.z + 1, self.zs)})

    def send(self, p, i, src):
        copy = self.copy(p, i, src)
        copy.start()
        self.sent.append(copy)

    def launch(self, p):
        acc, first = self.pieces[p][1], self.pieces[p][4]
        self.send(p, 0, far(acc) if first else far(self.parts[p]).at[lax.rem(self.z + self.zs - 1, self.zs)])

    def start(self):
        for p in range(len(self.pieces)):
            if p not in self.late:
                self.launch(p)

    def made(self, part):
        if self.late:
            p = self.late.pop(0)
            self.parts[p] = part
            self.launch(p)
            count = self.pieces[p][5]
            self.steps[self.forwards : self.forwards] = [(p, i) for i in range(count - 1)]
            self.forwards += count - 1
            self.steps.append((p, count - 1))

    def tick(self, count=1):
        for _ in range(min(count, self.forwards)):
            self.forwards -= 1
            self.take()

    def take(self):
        p, i = self.steps.pop(0)
        part, acc, came, out, first, count = self.pieces[p]
        self.copy(p, i, came.at[i]).wait_recv()
        own = self.parts[p][lax.rem(self.z + 2 * self.zs - 2 - first - i, self.zs)]
        total = (came[i].astype(F32) + own.astype(F32)).astype(BF)
        if i < count - 1:
            came[i] = total
            self.send(p, i + 1, came.at[i])
        else:
            out[...] = total

    def middle(self):
        pass

    def finish(self):
        while self.steps:
            self.take()
        for copy in self.sent:
            copy.wait_send()


class TurnBack:
    def __init__(self, peers, part, pieces, came, send, recv, given=None):
        self.given = given
        self.peers, self.part, self.pieces, self.came = peers, part, pieces, came
        self.send_sem, self.recv_sem = send, recv
        self.sent = []

    def greet(self):
        return 0

    def start(self):
        pass

    def tick(self, point):
        pass

    def middle(self):
        if self.given is not None:
            self.share(self.given)

    def made(self, turned):
        if self.given is None:
            self.share(turned)

    def share(self, turned):
        slab, _, cols = self.pieces.shape
        for t in range(slab):
            self.pieces[t] = turned[:, t * cols : (t + 1) * cols]
        _, me = self.peers.other(0, 0, 0)
        for i, place in self.peers.offsets():
            device, t = self.peers.other(*place)
            copy = remote(self.pieces.at[t], self.came.at[me], self.send_sem.at[i], self.recv_sem.at[i], device)
            copy.start()
            self.sent.append(copy)
        self.came[me] = self.pieces[me]

    def finish(self):
        for i, place in self.peers.offsets():
            device, t = self.peers.other(*(-d for d in place))
            block = self.came.at[t]
            remote(block, block, self.send_sem.at[i], self.recv_sem.at[i], device).wait_recv()
        zs, rows, _ = self.part.shape
        wide, span = rows // 2, self.came.shape[1]
        for c in range(2):
            for k in range(zs):
                at, done = (c * zs + k) * wide, 0
                while done < wide:
                    t, row = divmod(at + done, span)
                    count = min(wide - done, span - row)
                    self.part[k, c * wide + done : c * wide + done + count, :] = self.came[t, row : row + count, :]
                    done += count
        for copy in self.sent:
            copy.wait_send()


class Turn:
    def __init__(self, peers, full, nat, land, w_out, send, recv):
        self.peers, self.full, self.nat, self.land, self.w_out = peers, full, nat, land, w_out
        self.send_sem, self.recv_sem = send, recv
        self.sent = []

    def start(self):
        zs, rows, cols = self.full.shape
        part, span = rows // 2, self.w_out.shape[0]
        for c in range(2):
            for z in range(zs):
                at = (c * zs + z) * part
                self.nat[at : at + part, :] = self.full[z, c * part : (c + 1) * part, :]
        used = zs * rows
        if used < self.nat.shape[0]:
            self.nat[used:, :] = jnp.zeros((self.nat.shape[0] - used, cols), BF)
        _, me = self.peers.other(0, 0, 0)
        for i, place in self.peers.offsets():
            device, t = self.peers.other(*place)
            src = self.nat.at[pl.ds(pl.multiple_of(t * span, span), span)]
            copy = remote(src, self.land.at[me], self.send_sem.at[i], self.recv_sem.at[i], device)
            copy.start()
            self.sent.append(copy)
        self.land[me] = self.nat[pl.ds(pl.multiple_of(me * span, span), span), :]

    def finish(self):
        for i, place in self.peers.offsets():
            device, t = self.peers.other(*(-d for d in place))
            block = self.land.at[t]
            remote(block, block, self.send_sem.at[i], self.recv_sem.at[i], device).wait_recv()
        slab, _, cols = self.land.shape
        for t in range(slab):
            self.w_out[:, t * cols : (t + 1) * cols] = self.land[t]
        for copy in self.sent:
            copy.wait_send()


class Route:
    def __init__(self, seqs, src, out, local, send, recv, when="start"):
        self.when = when
        self.seqs, self.src, self.out = seqs, src, out
        self.local, self.send_sem, self.recv_sem = local, send, recv
        x, c, z = (lax.axis_index(a) for a in ("section", "dp", "z"))
        self.here = lax.rem(z, 2) == x
        place = c * 2 + x
        self.to = {"dp": lax.rem(z, seqs), "z": place}
        self.micro = z // seqs
        self.same = (lax.rem(z, seqs) == c) & (place == z)
        self.sources = []
        for micro in range(out.shape[0]):
            src_c, src_z = z // 2, micro * seqs + c
            self.sources.append(({"dp": src_c, "z": src_z}, (src_c == c) & (src_z == z)))

    def greet(self):
        barrier = pltpu.get_barrier_semaphore()
        for device, same in self.sources:

            @pl.when(self.here & jnp.logical_not(same))
            def _(device=device):
                pl.semaphore_signal(barrier, inc=1, device_id=device, device_id_type=MESH)

        return jnp.where(self.same, 0, 1)

    def copy(self):
        return remote(self.src, self.out.at[self.micro], self.send_sem, self.recv_sem.at[self.micro], self.to)

    def own(self):
        return pltpu.make_async_copy(self.src, self.out.at[self.micro], self.local)

    def start(self):
        if self.when == "start":
            self.go()

    def middle(self):
        pass

    def go(self):
        @pl.when(jnp.logical_not(self.same))
        def _():
            self.copy().start()

        @pl.when(self.same)
        def _():
            self.own().start()

    def tick(self, point):
        if self.when == point:
            self.go()

    def made(self, part):
        pass

    def arrived(self):
        for micro, (device, same) in enumerate(self.sources):

            @pl.when(self.here & jnp.logical_not(same))
            def _(micro=micro, device=device):
                block = self.out.at[micro]
                remote(block, block, self.send_sem, self.recv_sem.at[micro], device).wait_recv()

        @pl.when(self.same)
        def _():
            self.own().wait()

    def sent(self):
        @pl.when(jnp.logical_not(self.same))
        def _():
            self.copy().wait_send()

    def finish(self):
        self.arrived()
        self.sent()


class Across:
    def __init__(self, layer, src, out, send, recv):
        self.src, self.out, self.send_sem, self.recv_sem = src, out, send, recv
        x, z = lax.axis_index("section"), lax.axis_index("z")
        self.layer = layer
        self.sends = (x != layer) & (lax.rem(z, 2) == x)
        self.takes = (x == layer) & (lax.rem(z, 2) != x)
        self.going = False

    def greet(self):
        barrier = pltpu.get_barrier_semaphore()

        @pl.when(self.takes)
        def _():
            pl.semaphore_signal(barrier, inc=1, device_id={"section": 1 - self.layer}, device_id_type=MESH)

        return jnp.where(self.sends, 1, 0)

    def copy(self):
        return remote(self.src, self.out, self.send_sem, self.recv_sem, {"section": jnp.int32(self.layer)})

    def back(self):
        return remote(self.out, self.out, self.send_sem, self.recv_sem, {"section": jnp.int32(1 - self.layer)})

    def start(self):
        pass

    def tick(self, point):
        if not self.going:
            self.going = True

            @pl.when(self.sends)
            def _():
                self.copy().start()

    def made(self, part):
        pass

    def middle(self):
        pass

    def finish(self):
        self.tick("end")

        @pl.when(self.takes)
        def _():
            self.back().wait_recv()

        @pl.when(self.sends)
        def _():
            self.copy().wait_send()


class RouteIn:
    def __init__(self, seqs, pairs, local, send, recv):
        self.pairs, self.local, self.send_sem, self.recv_sem = pairs, local, send, recv
        x, c, z = (lax.axis_index(a) for a in ("section", "dp", "z"))
        self.sends = lax.rem(z, 2) == x
        self.targets = []
        for micro in range(pairs[0][0].shape[0]):
            to_c, to_z = z // 2, micro * seqs + c
            self.targets.append(({"dp": to_c, "z": to_z}, (to_c == c) & (to_z == z)))
        self.micro = z // seqs
        self.source = {"dp": lax.rem(z, seqs), "z": c * 2 + x}
        self.same = (lax.rem(z, seqs) == c) & (c * 2 + x == z)

    def greet(self):
        barrier = pltpu.get_barrier_semaphore()

        @pl.when(jnp.logical_not(self.same))
        def _():
            pl.semaphore_signal(barrier, inc=1, device_id=self.source, device_id_type=MESH)

        return sum(jnp.where(self.sends & jnp.logical_not(same), 1, 0) for _, same in self.targets)

    def far(self, i, micro):
        src, dst = self.pairs[i]
        return remote(src.at[micro, 0], dst, self.send_sem.at[i, micro], self.recv_sem.at[i], self.targets[micro][0])

    def near(self, i, micro):
        src, dst = self.pairs[i]
        return pltpu.make_async_copy(src.at[micro, 0], dst, self.local.at[i])

    def start(self, i=0):
        for micro, (_, same) in enumerate(self.targets):

            @pl.when(self.sends & jnp.logical_not(same))
            def _(micro=micro):
                self.far(i, micro).start()

            @pl.when(self.sends & same)
            def _(micro=micro):
                self.near(i, micro).start()

    def tick(self, point):
        pass

    def made(self, part):
        pass

    def middle(self):
        pass

    def arrived(self, i):
        dst = self.pairs[i][1]

        @pl.when(jnp.logical_not(self.same))
        def _():
            remote(dst, dst, self.send_sem.at[i, 0], self.recv_sem.at[i], self.source).wait_recv()

        for micro, (_, same) in enumerate(self.targets):

            @pl.when(self.sends & same)
            def _(micro=micro):
                self.near(i, micro).wait()

    def finish(self):
        for i in range(len(self.pairs)):
            for micro, (_, same) in enumerate(self.targets):

                @pl.when(self.sends & jnp.logical_not(same))
                def _(i=i, micro=micro):
                    self.far(i, micro).wait_send()


def reorder(raw, ordered, zs, wide):
    for c in range(2):
        for k in range(zs):
            at, to = (c * zs + k) * wide, (k * 2 + c) * wide
            ordered[:, to : to + wide] = raw[at : at + wide, :].astype(F32).T.astype(BF)


class Shared:
    def __init__(self, src, gather, points):
        self.src, self.gather, self.points = src, gather, points

    def greet(self):
        return 0

    def start(self):
        pass

    def made(self, part):
        pass

    def middle(self):
        pass

    def tick(self, point):
        if point == self.points[0]:
            self.gather.start(self.src)
        if point == self.points[1]:
            for k in range(1, self.gather.peers.chips):
                self.gather.forward(k)

    def finish(self):
        for k in range(self.gather.peers.chips):
            self.gather.chip(k)
        self.gather.finish()


class Several:
    def __init__(self, works):
        self.works = works

    def greet(self):
        return sum(work.greet() for work in self.works)

    def start(self):
        for work in self.works:
            work.start()

    def tick(self, point):
        for work in self.works:
            work.tick(point)

    def made(self, part):
        for work in self.works:
            work.made(part)

    def middle(self):
        for work in self.works:
            work.middle()

    def finish(self):
        for work in self.works:
            work.finish()


class NoSide:
    def greet(self):
        return 0

    def start(self):
        pass

    def tick(self, point):
        pass

    def made(self, part):
        pass

    def middle(self):
        pass

    def finish(self):
        pass


class Both:
    def greet(self):
        return 0

    def __init__(self, ring, turn, ahead):
        self.ring, self.turn = ring, turn
        if ahead:
            ring.steps.sort(key=lambda step: step[1] if step[0] else step[1] * 0.5 - 0.6)

    def start(self):
        self.ring.start()

    def tick(self, count=1):
        for _ in range(count):
            self.take()

    def take(self):
        if self.ring.take() == 0:
            self.turn.start()

    def finish(self):
        while self.ring.steps:
            self.take()
        self.ring.finish()
        self.turn.finish()


class Fetch:
    def __init__(self, far, near, sem):
        self.far, self.near = far, near
        self.copy = pltpu.make_async_copy(far, near, sem)
        self.copy.start()
        self.here = False
        self.shape = near.shape

    def __getitem__(self, index):
        if not self.here:
            self.copy.wait()
            self.here = True
        return self.near[index]

    def finish(self):
        if not self.here:
            self.copy.wait()


def far(ref):
    return ref.far if isinstance(ref, Fetch) else ref


class Paced:
    def __init__(self, work, pace):
        self.work, self.pace = work, pace
        self.greet, self.start, self.finish = work.greet, work.start, work.finish
        self.middle = getattr(work, "middle", lambda: None)
        self.part = None

    def made(self, part):
        self.part = part
        if "launch" not in self.pace:
            self.work.made(part)

    def tick(self, point):
        self.work.tick(self.pace.get(point, 0))
        if self.part is not None and self.pace.get("launch") == point:
            self.work.made(self.part)


class SideWork:
    def __init__(self, operands=(), in_hbm=(), outs=(), out_hbm=(), scratch=(), build=None):
        self.operands, self.in_hbm, self.outs, self.out_hbm = operands, in_hbm, outs, out_hbm
        self.scratch, self.build = scratch, build
        self.zs = 1 if build is None else 2

    def make(self, peers, ins, outs, scratch):
        return NoSide() if self.build is None else self.build(peers, ins, outs, scratch)


def route_side(lay, src, when):
    dma = pltpu.SemaphoreType.DMA
    outs = [((lay.micros, *src.shape), BF)]

    def build(peers, ins, outs, scratch):
        return Route(lay.seqs, ins[0], outs[0], *scratch, when)

    return SideWork([src], (True,), outs, (True,), [dma, dma, dma((lay.micros,))], build)


def turn_side(lay, turned=None):
    n, span = lay.slab, lay.slots * lay.head
    outs = [((lay.zs, lay.width // lay.zs, lay.cols), BF)]
    scratch = [pltpu.VMEM((n, span, lay.cols), BF)] * 2 + [pltpu.SemaphoreType.DMA((n,))] * 2

    def build(peers, ins, outs, scratch):
        return TurnBack(peers, outs[0], *scratch, ins[0] if ins else None)

    operands = [] if turned is None else [turned]
    return SideWork(operands, (False,) * len(operands), outs, (False,), scratch, build)


def share_side(lay, a, points):
    chips = lay.slab // 2

    def build(peers, ins, outs, scratch):
        return Shared(ins[0], Gather(peers, outs[0], scratch), points)

    return SideWork([a], (False,), [((chips, 2, *a.shape), BF)], (False,), [pltpu.SemaphoreType.DMA((chips,))] * 4, build)


def across_side(layer, a):
    dma = pltpu.SemaphoreType.DMA

    def build(peers, ins, outs, scratch):
        return Across(layer, ins[0], outs[0], *scratch)

    return SideWork([a], (True,), [(a.shape, a.dtype)], (True,), [dma, dma], build)


def both_sides(*sides):
    sides = [side for side in sides if side.build is not None]
    joined = [[], [], [], [], []]
    for side in sides:
        for into, more in zip(joined, (side.operands, side.in_hbm, side.outs, side.out_hbm, side.scratch)):
            into += list(more)

    def build(peers, ins, outs, scratch):
        works = []
        for side in sides:
            a, b, c = len(side.operands), len(side.outs), len(side.scratch)
            works.append(side.build(peers, ins[:a], outs[:b], scratch[:c]))
            ins, outs, scratch = ins[a:], outs[b:], scratch[c:]
        return Several(works)

    return SideWork(*joined, build)


def gather_side(shards, pace, counts=None, turn=None):
    zs = lax.axis_size("z")
    n = len(shards)
    counts = counts or (zs - 1,) * n
    places = [a[1] if isinstance(a, tuple) else None for a in shards]
    shards = [a[0] if isinstance(a, tuple) else a for a in shards]
    outs = [((zs, *a.shape[-2:]), BF) for a in shards]
    sems = [pltpu.SemaphoreType.DMA((n,))] + [pltpu.SemaphoreType.DMA((n, zs - 1))] * 2
    if turn is None:

        def build(peers, ins, outs, scratch):
            ins = [a if place is None else a.at[place] for a, place in zip(ins, places)]
            return Paced(RingGather(list(zip(ins, outs, counts)), *scratch), pace)

        return SideWork(shards, (True,) * n, outs, (True,) * n, sems, build)
    slab = 2 * lax.axis_size("section") * lax.axis_size("r")
    cols = shards[0].shape[1]
    outs[0] = ((turn, slab * cols), BF)
    more = [
        pltpu.VMEM((zs, *shards[0].shape), BF),
        pltpu.VMEM((slab * turn, cols), BF),
        pltpu.VMEM((slab, turn, cols), BF),
    ] + [pltpu.SemaphoreType.DMA((slab,))] * 2

    def build_turn(peers, ins, outs, scratch):
        pieces = list(zip(ins, [scratch[3], *outs[1:]], counts))
        turning = Turn(peers, scratch[3], scratch[4], scratch[5], outs[0], *scratch[6:8])
        return Paced(Both(RingGather(pieces, *scratch[:3]), turning, False), pace)

    return SideWork(shards, (True,) * n, outs, (False,) + (True,) * (n - 1), sems + more, build_turn)


def sum_side(pieces, pace):
    zs = lax.axis_size("z")
    n = len(pieces)
    operands, outs, scratch = [], [], []
    for part, shape, acc, first, count in pieces:
        operands += [a for a in (part, acc) if a is not None]
        outs.append((shape, BF))
        scratch.append(pltpu.VMEM((count, *shape), BF))
    scratch += [pltpu.SemaphoreType.DMA((n, zs - 1))] * 2
    def build(peers, ins, outs, scratch):
        ins, made = list(ins), []
        for i, (part, shape, acc, first, count) in enumerate(pieces):
            part_ref = None if part is None else ins.pop(0)
            acc_ref = None if acc is None else ins.pop(0)
            made.append((part_ref, acc_ref, scratch[i], outs[i], first, count))
        ring = RingSum(made, *scratch[n : n + 2])
        return Paced(ring, pace)

    return SideWork(operands, (False,) * len(operands), outs, (False,) * len(outs), scratch, build)


def gather_scratch(chips, rows, width):
    return [pltpu.VMEM((chips, 2, rows, width), BF)] + [pltpu.SemaphoreType.DMA((chips,))] * 4


def reduce_scratch(chips, rows, width):
    return [
        pltpu.VMEM((chips, rows, width), F32),
        pltpu.VMEM((chips, rows, width), BF),
        pltpu.VMEM((chips, rows, width), BF),
        pltpu.VMEM((chips - 1, rows, width), BF),
        pltpu.VMEM((chips - 1, rows, width), BF),
    ] + [pltpu.SemaphoreType.DMA((chips,))] * 4


def norm_parts(v):
    centred = v - jnp.mean(v, axis=-1, keepdims=True)
    spread = jnp.mean(centred * centred, axis=-1, keepdims=True)
    scale = lax.rsqrt(spread + EPSILON)
    return centred * scale, scale


def norm_back(v, gain, grad):
    unit, scale = norm_parts(v)
    scaled = grad * gain
    part = scaled - jnp.mean(scaled, axis=-1, keepdims=True)
    part = part - unit * jnp.mean(scaled * unit, axis=-1, keepdims=True)
    return part * scale, jnp.sum(grad * unit, axis=0, keepdims=True), jnp.sum(grad, axis=0, keepdims=True)


def dot(a, b, ca=1, cb=0):
    return lax.dot_general(a, b, (((ca,), (cb,)), ((), ())), preferred_element_type=F32)


def chip_rows(chip, rows):
    return pl.ds(pl.multiple_of(chip * (2 * rows), 2 * rows), 2 * rows)


def groups(span, head):
    wide = 128 if span % 128 == 0 else span
    for g in range(span // wide):
        yield slice(g * wide, (g + 1) * wide), [(g * wide // head + i, i * head) for i in range(wide // head)]


def only(a, start, head):
    lane = lax.broadcasted_iota(jnp.int32, a.shape, 1)
    return jnp.where((lane >= start) & (lane < start + head), a, jnp.zeros_like(a))


def attention_forward(head, side, *refs):
    (h, w_qkv, w_out, bias, col, row, vec) = refs[:7]
    ins, refs = refs[7 : 7 + len(side.operands)], refs[7 + len(side.operands) :]
    (normed, qkv, attended, logs, mid, normed_two), refs = refs[:6], refs[6:]
    side_outs, refs = refs[: len(side.outs)], refs[len(side.outs) :]
    gather_refs, reduce_refs, side_refs = refs[:5], refs[5 : 14 + 1], refs[14 + 1 :]
    rows, width = h.shape
    span = w_out.shape[0]
    peers = Peers()
    gather = Gather(peers, gather_refs[0], gather_refs[1:])
    reduce = Reduce(peers, *reduce_refs[:5], reduce_refs[5:9])
    kept_sem = reduce_refs[9]
    full = gather.full
    work = side.make(peers, ins, side_outs, side_refs)
    peers.greet(side.zs, work)
    gather.start((norm_parts(h[...].astype(F32))[0] * vec[0:1, :] + vec[2:3, :]).astype(BF))
    work.start()
    for k, chip in gather.arrivals():
        part = dot(full[chip].reshape(2 * rows, width), w_qkv[...]) + bias[...]
        qkv[chip_rows(chip, rows), :] = part.astype(BF)
    work.tick("qkv")
    kept = pltpu.make_async_copy(full, normed, kept_sem)
    kept.start()
    scale = head ** (-0.5)
    order = list(range(1, peers.chips)) + [0]
    before = None
    for k in order:
        chip = peers.behind_chip(k)
        here = chip_rows(chip, rows)
        block = jnp.where(col[...] <= row[:, here], 0.0, LOW).astype(F32)
        for lanes, heads in groups(span, head):
            q = qkv[here, lanes]
            keys = qkv[:, slice(span + lanes.start, span + lanes.stop)]
            values = qkv[:, slice(2 * span + lanes.start, 2 * span + lanes.stop)]
            merged = None
            for slot, start in heads:
                scores = dot(keys, only(q, start, head) * scale, 1, 1) + block
                top = jnp.max(scores, axis=0, keepdims=True)
                weights = jnp.exp(scores - top)
                total = jnp.sum(weights, axis=0, keepdims=True)
                logs[slot : slot + 1, here] = top + jnp.log(total)
                mixed = dot(values, weights.astype(BF), 0, 0) / total
                lane = lax.broadcasted_iota(jnp.int32, mixed.shape, 0)
                merged = mixed if merged is None else jnp.where(lane >= start, mixed, merged)
            attended[here, lanes] = merged.T.astype(BF)
        reduce.put(k, dot(attended[here, :], w_out[...]))
        if before is not None:
            reduce.push(before)
        work.tick("q%d" % order.index(k))
        before = k
    reduce.push(before)
    out = h[...].astype(F32) + (reduce.total() + vec[4:5, :])
    mid[...] = out
    normed_two[...] = (norm_parts(out)[0] * vec[1:2, :] + vec[3:4, :]).astype(BF)
    work.finish()
    gather.finish()
    reduce.finish()
    kept.wait()


ROOT = 0.7978845608028654


def feed_forward(side, *refs):
    (src, mid, fc_packed, w_proj, bias, vec) = refs[:6]
    ins, refs = refs[6 : 6 + len(side.operands)], refs[6 + len(side.operands) :]
    (normed_two, slope, activated, result, proj_out, fc_out), refs = refs[:6], refs[6:]
    side_outs, refs = refs[: len(side.outs)], refs[len(side.outs) :]
    gather_refs, reduce_refs, side_refs = refs[:5], refs[5 : 14 + 8], refs[14 + 8 :]
    rows, width = src.shape
    peers = Peers()
    gather = Gather(peers, gather_refs[0], gather_refs[1:])
    reduce = Reduce(peers, *reduce_refs[:5], reduce_refs[5:9])
    kept_sem, proj, proj_local, proj_send, proj_recv, proj_sem, w_fc, fc_sem = reduce_refs[9:17]
    full = gather.full
    work = side.make(peers, ins, side_outs, side_refs)
    zs, z = lax.axis_size("z"), lax.axis_index("z")
    half = proj.shape[1]
    peers.greet(2, work)
    gather.start(src)
    there = lax.rem(z + 2, zs)
    last = remote(w_proj.at[there], proj.at[there], proj_send, proj_recv, {"z": lax.rem(z + 1, zs)})
    last.start()
    here = [lax.rem(z + zs - i, zs) for i in range(zs - 1)]
    placed = [pltpu.make_async_copy(w_proj.at[b], proj.at[b], proj_local.at[i]) for i, b in enumerate(here)]
    for copy in placed:
        copy.start()
    rows_of, units = fc_packed.shape[1], w_fc.shape[1]
    for b in range(zs):
        for c in range(2):
            at = (b * 2 + c) * rows_of
            w_fc[at : at + rows_of, :] = fc_packed[b, :, c * units : (c + 1) * units]
    fc_kept = pltpu.make_async_copy(w_fc, fc_out, fc_sem)
    fc_kept.start()
    before = None
    for k, chip in gather.arrivals():
        if k == 0:
            last.wait_recv()
            work.start()
            for copy in placed:
                copy.wait()
            proj_kept = pltpu.make_async_copy(proj, proj_out, proj_sem)
            proj_kept.start()
        here = chip_rows(chip, rows)
        u = dot(full[chip].reshape(2 * rows, width), w_fc[...]) + bias[...]
        bend = jnp.tanh(ROOT * (u + 0.044715 * (u * u * u)))
        slope[here, :] = (0.5 * (1.0 + bend) + 0.5 * u * (1.0 - bend * bend) * (ROOT * (1.0 + 3 * 0.044715 * (u * u)))).astype(BF)
        act = (0.5 * u * (1.0 + bend)).astype(BF)
        activated[here, :] = act
        back = dot(act[:, :half], proj[0])
        for b in range(1, zs):
            back = back + dot(act[:, b * half : (b + 1) * half], proj[b])
        reduce.put(k, back)
        if before is not None:
            reduce.push(before)
        work.tick("k%d" % k)
        before = k
    kept = pltpu.make_async_copy(full, normed_two, kept_sem)
    kept.start()
    reduce.push(before)
    work.tick("sent")
    out = (mid[...] + (reduce.total() + vec[5:6, :])).astype(BF)
    result[...] = out
    last.wait_send()
    proj_kept.wait()
    fc_kept.wait()
    work.finish()
    gather.finish()
    reduce.finish()
    kept.wait()


def chunks(size, step):
    return [(a, min(a + step, size)) for a in range(0, size, step)]


def feed_backward(side, ready, *refs):
    (src, mid, w_fc, w_proj, slope, activated, normed_two, vec, *given) = refs[: 8 + ready]
    refs = refs[8 + ready :]
    ins, refs = refs[: len(side.operands)], refs[len(side.operands) :]
    (grad_mid, attn_rows, grad_proj, grad_fc, sums, unit_sums), refs = refs[:6], refs[6:]
    side_outs, refs = refs[: len(side.outs)], refs[len(side.outs) :]
    gather_refs, reduce_refs, side_refs = refs[:5], refs[5 : 14 + 1], refs[14 + 1 :]
    hidden, = reduce_refs[9:10]
    rows, width = src.shape
    tokens = slope.shape[0]
    peers = Peers()
    gather = Gather(peers, gather_refs[0], gather_refs[1:])
    reduce = Reduce(peers, *reduce_refs[:5], reduce_refs[5:9])
    full = given[0] if ready else gather.full
    work = side.make(peers, ins, side_outs, side_refs)
    peers.greet(side.zs, work)
    half = grad_proj.shape[1]

    def proj_terms():
        branch = full[...].reshape(tokens, width)
        for b in range(grad_proj.shape[0]):
            grad_proj[b] = dot(activated[:, b * half : (b + 1) * half], branch, 0, 0).astype(BF)
        work.made(grad_proj)

    if ready:
        order = [(k, peers.behind_chip(k)) for k in (*range(1, peers.chips), 0)]
    else:
        gather.start(src)
        order = gather.arrivals()
    work.start()
    if ready:
        proj_terms()
    before = None
    for k, chip in order:
        here = chip_rows(chip, rows)
        back = dot(full[chip].reshape(2 * rows, width), w_proj[...], 1, 1) * slope[here, :].astype(F32)
        back = back.astype(BF)
        hidden[here, :] = back
        reduce.put(k, dot(back, w_fc[...], 1, 1))
        if before is not None:
            reduce.push(before)
        work.tick("k%d" % k)
        before = k
    reduce.push(before)
    work.middle()
    if not ready:
        proj_terms()
    work.tick("proj")
    back = hidden[...]
    blocks, rows_of, units = grad_fc.shape[0], grad_fc.shape[1], back.shape[1]
    for b in range(blocks):
        at = b * 2 * rows_of
        part = dot(normed_two[:, at : at + 2 * rows_of], back, 0, 0).astype(BF)
        for c in range(2):
            grad_fc[b, :, c * units : (c + 1) * units] = part[c * rows_of : (c + 1) * rows_of]
    work.tick("fc")
    unit_sums[...] = jnp.sum(back.astype(F32), axis=0, keepdims=True)
    own = src[...].astype(F32)
    part, gain, shift = norm_back(mid[...], vec[1:2, :], reduce.total())
    out = own + part
    grad_mid[...] = out
    low = out.astype(BF)
    attn_rows[...] = low
    sums[0:1, :] = gain
    sums[1:2, :] = shift
    sums[2:3, :] = jnp.sum(own, axis=0, keepdims=True)
    sums[3:4, :] = jnp.sum(low.astype(F32), axis=0, keepdims=True)
    sums[4:8, :] = jnp.zeros((4, width), F32)
    work.finish()
    if not ready:
        gather.finish()
    reduce.finish()


def attention_backward(head, side, *refs):
    (src, grad_mid, h, w_qkv, w_out, qkv, attended, logs, normed, col, row, vec) = refs[:12]
    ins, refs = refs[12 : 12 + len(side.operands)], refs[12 + len(side.operands) :]
    (grad_in, *grad_parts, grad_out, sums, head_sums), refs = refs[:7], refs[7:]
    side_outs, refs = refs[: len(side.outs)], refs[len(side.outs) :]
    gather_refs, reduce_refs, side_refs = refs[:5], refs[5 : 14 + 3], refs[14 + 3 :]
    joint, key_sum, value_sum = reduce_refs[9:12]
    rows, width = src.shape
    tokens, span = attended.shape
    scale = head ** (-0.5)
    peers = Peers()
    gather = Gather(peers, gather_refs[0], gather_refs[1:])
    reduce = Reduce(peers, *reduce_refs[:5], reduce_refs[5:9])
    full = gather.full
    work = side.make(peers, ins, side_outs, side_refs)
    peers.greet(side.zs, work)
    gather.start(src)
    work.start()
    for k, chip in gather.arrivals():
        here = chip_rows(chip, rows)
        g_all = dot(full[chip].reshape(2 * rows, width), w_out[...], 1, 1).astype(BF)
        block = jnp.where(col[...] <= row[:, here], 0.0, LOW).astype(F32)
        for lanes, heads in groups(span, head):
            q = qkv[here, lanes]
            g = g_all[:, lanes]
            keys = qkv[:, slice(span + lanes.start, span + lanes.stop)]
            values = qkv[:, slice(2 * span + lanes.start, 2 * span + lanes.stop)]
            merged = None
            key_term, value_term = 0.0, 0.0
            for slot, start in heads:
                q_one, g_one = only(q, start, head) * scale, only(g, start, head)
                probs = jnp.exp(dot(keys, q_one, 1, 1) + block - logs[slot : slot + 1, here])
                g_probs = dot(values, g_one, 1, 1)
                both = probs * g_probs
                centre = jnp.sum(both, axis=0, keepdims=True)
                g_scores = (both - probs * centre).astype(BF)
                value_term += dot(probs.astype(BF), g_one)
                key_term += dot(g_scores, q_one)
                g_query = dot(keys, g_scores, 0, 0)
                lane = lax.broadcasted_iota(jnp.int32, g_query.shape, 0)
                merged = g_query if merged is None else jnp.where(lane >= start, g_query, merged)
            joint[here, lanes] = (merged.T * scale).astype(BF)
            if k == 0:
                key_sum[:, lanes] = key_term
                value_sum[:, lanes] = value_term
            else:
                key_sum[:, lanes] += key_term
                value_sum[:, lanes] += value_term
        work.tick("k%d" % k)
    joint[:, span : 2 * span] = key_sum[...].astype(BF)
    joint[:, 2 * span :] = value_sum[...].astype(BF)
    order = list(range(1, peers.chips)) + [0]
    before = None
    for k in order:
        reduce.put(k, dot(joint[chip_rows(peers.behind_chip(k), rows), :], w_qkv[...], 1, 1))
        if before is not None:
            reduce.push(before)
        before = k
    work.tick("sent")
    grads = joint[...]
    grad_out[...] = dot(attended[...], full[...].reshape(tokens, width), 0, 0).astype(BF)
    work.made(grad_out)
    for a, b in chunks(width, 512):
        part = dot(normed[:, a:b], grads, 0, 0).astype(BF)
        for i, grad in enumerate(grad_parts):
            grad[a:b, :] = part[:, i * span : (i + 1) * span]
    work.tick("grad")
    head_sums[...] = jnp.sum(grads.astype(F32), axis=0, keepdims=True)
    part, gain, shift = norm_back(h[...].astype(F32), vec[0:1, :], reduce.total())
    grad_in[...] = (grad_mid[...] + part).astype(BF)
    sums[0:1, :] = gain
    sums[1:2, :] = shift
    sums[2:8, :] = jnp.zeros((6, width), F32)
    work.finish()
    gather.finish()
    reduce.finish()


def call(kernel, name, outs, operands, side, kept, scratch, keep=()):
    chips = lax.axis_size("section") * lax.axis_size("r")
    rows, width = operands[0].shape
    vmem, hbm = pl.BlockSpec(memory_space=pltpu.VMEM), pl.BlockSpec(memory_space=pl.ANY)
    every = [*operands, *side.operands]
    fetched = [i for i in range(len(every)) if i not in keep and not (i >= len(operands) and side.in_hbm[i - len(operands)])]
    work = gather_scratch(chips, rows, width) + reduce_scratch(chips, rows, width) + scratch + list(side.scratch)

    def body(*refs):
        refs = list(refs)
        near, sems = refs[-1 - len(fetched) : -1], refs[-1]
        for k, i in enumerate(fetched):
            refs[i] = Fetch(refs[i], near[k], sems.at[k])
        kernel(*refs[: -1 - len(fetched)])
        for i in fetched:
            refs[i].finish()

    out = pl.pallas_call(
        body,
        out_shape=[jax.ShapeDtypeStruct(*o) for o in (*outs, *side.outs)],
        in_specs=[hbm] * len(every),
        out_specs=[hbm if i in kept else vmem for i in range(len(outs))] + [hbm if i else vmem for i in side.out_hbm],
        scratch_shapes=work
        + [pltpu.VMEM(every[i].shape, every[i].dtype) for i in fetched]
        + [pltpu.SemaphoreType.DMA((len(fetched),))],
        compiler_params=pltpu.CompilerParams(collective_id=name, has_side_effects=True, vmem_limit_bytes=60 * 2**20),
    )(*every)
    return out[: len(outs)], out[len(outs) :]


def run_attention_forward(name, head, side, *operands):
    h, w_qkv, w_out, bias, col, row, vec = operands
    rows, width = h.shape
    tokens, span = col.shape[0], w_out.shape[0]
    slots = -(-(span // head) // 8) * 8
    chips = tokens // (2 * rows)
    outs = [
        ((chips, 2, rows, width), BF),
        ((tokens, 3 * span), BF),
        ((tokens, span), BF),
        ((slots, tokens), F32),
        ((rows, width), F32),
        ((rows, width), BF),
    ]
    return call(functools.partial(attention_forward, head, side), name, outs, operands, side, (0,), [pltpu.SemaphoreType.DMA])


def run_feed_forward(name, side, *operands):
    src, mid, w_fc, w_proj, bias, vec = operands
    rows, width = src.shape
    units = w_fc.shape[2] // 2
    chips = lax.axis_size("section") * lax.axis_size("r")
    tokens = 2 * chips * rows
    outs = [
        ((chips, 2, rows, width), BF),
        ((tokens, units), BF),
        ((tokens, units), BF),
        ((rows, width), BF),
        (w_proj.shape, BF),
        ((width, units), BF),
    ]
    dma = pltpu.SemaphoreType.DMA
    scratch = [dma, pltpu.VMEM(w_proj.shape, BF), dma((w_proj.shape[0],)), dma, dma, dma, pltpu.VMEM((width, units), BF), dma]
    return call(functools.partial(feed_forward, side), name, outs, operands, side, (0, 4, 5), scratch, (3,))


def run_feed_backward(name, side, *operands):
    src, mid, w_fc, w_proj, slope, activated, normed_two, vec, *given = operands
    rows, width = src.shape
    tokens, units = slope.shape
    zs = lax.axis_size("z")
    outs = [
        ((rows, width), F32),
        ((rows, width), BF),
        ((zs, units // zs, width), BF),
        ((zs, width // (2 * zs), 2 * units), BF),
        ((8, width), F32),
        ((1, units), F32),
    ]
    return call(functools.partial(feed_backward, side, len(given)), name, outs, operands, side, (), [pltpu.VMEM((tokens, units), BF)])


def run_attention_backward(name, head, side, *operands):
    src, grad_mid, h, w_qkv, w_out, qkv, attended, logs, normed, col, row, vec = operands
    rows, width = src.shape
    tokens, span = attended.shape
    outs = [
        ((rows, width), BF),
        ((width, span), BF),
        ((width, span), BF),
        ((width, span), BF),
        ((span, width), BF),
        ((8, width), F32),
        ((1, 3 * span), F32),
    ]
    scratch = [pltpu.VMEM((tokens, 3 * span), BF), pltpu.VMEM((tokens, span), F32), pltpu.VMEM((tokens, span), F32)]
    return call(functools.partial(attention_backward, head, side), name, outs, operands, side, (), scratch)


def start_kernel(sizes, *refs):
    block, span, half, seqs, micros = sizes
    (tiny, w_qkv, w_attn, w_fc, w_proj, inputs, cotangent), refs = refs[:7], refs[7:]
    (qkv, wo, fc, (proj, qkv_full, w_out, h, g, row, col, *smalls)), refs = (refs[0:2], refs[2:4], refs[4:6], refs[6:19]), refs[19:]
    tiny_out, stage, h_raw, g_raw, natural, proj_cut = refs[:6]
    cuts, lands, (wo_full, nat, land), refs = refs[6:9], refs[9:12], refs[12:15], refs[15:]
    z_send, z_recv, *sems = refs[:6]
    all_send, all_recv, far_send, far_recv, turn_send, turn_recv = refs[6:12]
    ring_local, ring_send, ring_recv, *route_sems = refs[12:]
    peers = Peers()
    zs, z = lax.axis_size("z"), lax.axis_index("z")
    x, rest, slab = peers.x, peers.rest, 2 * peers.chips
    sections = peers.sections
    spot = peers.c * rest + peers.r
    width, wide = w_attn.shape[1], rest * block
    _, me = peers.other(0, 0, 0)
    route = RouteIn(seqs, [(inputs, h_raw), (cotangent, g_raw)], *route_sems)
    peers.greet(zs, route)
    sent = []

    def send(copy):
        copy.start()
        sent.append(copy)

    for k in range(1, zs):
        send(remote(tiny, stage.at[z], z_send.at[k], z_recv.at[k], {"z": lax.rem(z + k, zs)}))
    stage[z] = tiny[...]
    route.start(0)
    route.start(1)

    def share(a):
        for i, place in peers.offsets():
            device, t = peers.other(*place)
            send(remote(cuts[a].at[t], lands[a].at[x, spot], all_send.at[a, i], all_recv.at[a, i], device))
        lands[a][x, spot] = cuts[a][me]

    def settle(a, shard):
        for i, place in peers.offsets():
            device, _ = peers.other(*(-d for d in place))
            came = lands[a].at[device["section"], device["dp"] * rest + device["r"]]
            remote(came, came, all_send.at[a, i], all_recv.at[a, i], device).wait_recv()
        for layer in range(sections):
            for i in range(2 * rest):
                rows_at, lanes_at = i * block, 0
                if a == 2:
                    rows_at, lanes_at = i % rest * block, i // rest * lands[a].shape[3]
                to = shard[layer].at[rows_at : rows_at + block, lanes_at : lanes_at + lands[a].shape[3]]
                to[...] = lands[a][layer, i, :block, :]

    cols = width // slab
    for t in range(slab):
        big, off = divmod(t * cols, wide)
        at = (big % 2 * zs + big // 2) * wide + off
        cuts[0][t, :block, :] = w_attn[:, at : at + cols]
    share(0)
    for t in range(slab):
        count = max(0, min(span, width - t * span))
        for p in range(3):
            if count:
                at = p * width + t * span
                cuts[1][t, :block, p * span : p * span + count] = w_qkv[:, at : at + count]
            if count < span:
                cuts[1][t, :block, p * span + count : (p + 1) * span] = jnp.zeros((block, span - count), BF)
    share(1)
    for t in range(slab):
        a, c, r = t // (2 * rest), t // rest % 2, t % rest
        for k in range(zs):
            at = ((c * zs + k) * rest + r) * (sections * half) + a * half
            cuts[2][t, :block, k * half : (k + 1) * half] = w_fc[:, at : at + half]
    for a in range(sections):
        for c in range(2):
            for k in range(zs):
                at, to = (c * zs + k) * wide, (k * 2 + c) * wide
                proj_cut[a, :, to : to + wide] = w_proj[a * half : (a + 1) * half, at : at + wide]
    for k in range(1, zs):
        came = stage.at[lax.rem(z + zs - k, zs)]
        remote(came, came, z_send.at[k], z_recv.at[k], {"z": lax.rem(z + k, zs)}).wait_recv()
    gather = Gather(peers, tiny_out, sems)
    gather.start(stage)
    settle(0, wo)
    turn = Turn(peers, wo_full, nat, land, w_out, turn_send, turn_recv)
    ring = RingGather([(wo[0], wo_full, zs - 1), (qkv[0], qkv_full, zs - 1)], ring_local, ring_send, ring_recv)
    work = Both(ring, turn, True)
    ring.launch(0)
    settle(1, qkv)
    ring.launch(1)
    share(2)
    for d in range(1, sections):
        device, _ = peers.other(d, 0, 0)
        there = lax.rem(x + d, sections)
        send(remote(proj_cut.at[there], proj.at[x], far_send.at[d], far_recv.at[d], device))
    proj[x] = proj_cut[x]
    work.tick()
    for _ in gather.arrivals():
        pass
    work.tick()

    per_row, halves = sections * half // block, half // block
    for layer in range(sections):
        vec, bias, unit = smalls[3 * layer : 3 * layer + 3]
        natural[...] = jnp.zeros_like(natural)
        for c in range(2):
            for k in range(zs):
                for r in range(rest):
                    at = ((k * 2 + c) * rest + r) * block
                    vec[:, at : at + block] = tiny_out[layer * rest + r, c, k, 0:8, :block]
                    at = ((c * zs + k) * rest + r) * block
                    natural[:, at : at + block] = tiny_out[layer * rest + r, c, k, 0:8, :block]
        own = jnp.zeros((8, span), F32)
        for t in range(slab):
            own = jnp.where(me == t, natural[:, t * span : (t + 1) * span], own)
        bias[:, :span] = own[6:7]
        bias[:, span : 2 * span] = jnp.zeros((1, span), F32)
        bias[:, 2 * span :] = own[7:8]
        for k in range(zs):
            for j in range(halves):
                line = tiny_out[layer * rest + peers.r, peers.c, k, pl.ds(8 + x * halves + j, 1), :block]
                unit[:, k * half + j * block : k * half + (j + 1) * block] = line
    rows = h.shape[0]
    for a in range(sections):
        for r in range(rest):
            for c in range(2):
                at = ((a * rest + r) * 2 + c) * rows
                line = tiny_out[r, 0, c * 2 + a, pl.ds(8 + per_row + z // seqs, 1), :rows]
                row[:, at : at + rows] = line.astype(jnp.int32)
                col[at : at + rows, :] = jnp.broadcast_to(line, (8, rows)).T[:, :1].astype(jnp.int32)
    work.tick(2)
    settle(2, fc)
    work.tick()
    for i, (raw, ordered) in enumerate([(h_raw, h), (g_raw, g)]):
        route.arrived(i)
        reorder(raw, ordered, zs, wide)
    for d in range(1, sections):
        device, _ = peers.other(-d, 0, 0)
        came = proj.at[device["section"]]
        remote(came, came, far_send.at[d], far_recv.at[d], device).wait_recv()
    work.finish()
    route.finish()
    gather.finish()
    for copy in sent:
        copy.wait_send()


def run_start(name, lay, tiny, w_qkv, w_attn, w_fc, w_proj, inputs, cotangent):
    zs, n, chips, sections = lay.zs, lay.slab, lay.slab // 2, lay.sections
    span, block = lay.slots * lay.head, lay.block
    spots = lay.cores * lay.rest
    rows, tall = spots * block, -(-block // 16) * 16
    vmem, hbm = pl.BlockSpec(memory_space=pltpu.VMEM), pl.BlockSpec(memory_space=pl.ANY)
    units = lay.units // n
    widths = [lay.cols, 3 * span, units]
    flat = (lay.rows, lay.width)
    outs = [(a, BF) for a in ((rows, 3 * span), (rows, lay.cols), (rows // 2, 2 * units)) for _ in range(sections)]
    outs += [((sections, lay.half, lay.width), BF), ((zs, rows, 3 * span), BF), ((span, lay.width), BF)]
    outs += [(flat, BF), (flat, BF), ((1, lay.tokens), jnp.int32), ((lay.tokens, 1), jnp.int32)]
    outs += [((8, lay.width), F32), ((1, 3 * span), F32), ((1, units), F32)] * sections
    dma = pltpu.SemaphoreType.DMA
    return pl.pallas_call(
        functools.partial(start_kernel, (block, span, lay.half, lay.seqs, lay.micros)),
        out_shape=[jax.ShapeDtypeStruct(*o) for o in outs],
        in_specs=[vmem] * 7,
        out_specs=[vmem] * (1 + 3 * sections) + [hbm] + [vmem] * (5 + 3 * sections),
        scratch_shapes=[
            pltpu.VMEM((chips, 2, zs, *tiny.shape), F32),
            pltpu.VMEM((zs, *tiny.shape), F32),
            pltpu.VMEM(flat[::-1], BF),
            pltpu.VMEM(flat[::-1], BF),
            pltpu.VMEM((8, n * span), F32),
            pltpu.VMEM((sections, lay.half, lay.width), BF),
        ]
        + [pltpu.VMEM((n, tall, m), BF) for m in widths]
        + [pltpu.VMEM((sections, spots, tall, m), BF) for m in widths]
        + [pltpu.VMEM((zs, rows, lay.cols), BF), pltpu.VMEM((n * span, lay.cols), BF), pltpu.VMEM((n, span, lay.cols), BF)]
        + [dma((zs,))] * 2
        + [dma((chips,))] * 4
        + [dma((3, n))] * 2
        + [dma((sections,))] * 2
        + [dma((n,))] * 2
        + [dma((2,))]
        + [dma((2, zs - 1))] * 2
        + [dma((2,)), dma((2, lay.micros)), dma((2,))],
        compiler_params=pltpu.CompilerParams(collective_id=name, has_side_effects=True, vmem_limit_bytes=60 * 2**20),
    )(tiny, w_qkv, w_attn, w_fc, w_proj, inputs, cotangent)


def end_kernel(sizes, *refs):
    block, width, units, seqs = sizes
    parts, (q_one, k_one, v_one, wo_one), (fc_zero, fc_one, proj_zero, proj_one), refs = refs[:4], refs[4:8], refs[8:12], refs[12:]
    sums, (last_rows, *ready), refs = refs[:8], refs[8:15], refs[15:]
    (out_qkv, out_wo, out_fc, out_proj, out_small, section_out, section_grad, home, out_rows), refs = refs[:9], refs[9:]
    totals, (proj_both, proj_land), refs = refs[:4], refs[4:6], refs[6:]
    stages, lands, refs = refs[:5], refs[5:10], refs[10:]
    (small_land, small_sum, z_land), came, (small, natural, rows_buf), refs = refs[:3], refs[3:7], refs[7:10], refs[10:]
    all_send, all_recv, far_send, far_recv, z_send, z_recv, ring_send, ring_recv, late_send, late_recv, *route_sems, rows_sem = refs
    peers = Peers()
    zs, z = lax.axis_size("z"), lax.axis_index("z")
    x, rest, slab = peers.x, peers.rest, 2 * peers.chips
    spot = peers.c * rest + peers.r
    span, cols = q_one.shape[1], wo_one.shape[1]
    half, wide = proj_zero.shape[0], rest * block
    _, me = peers.other(0, 0, 0)
    offsets = peers.offsets()
    route = Route(seqs, last_rows, home, *route_sems[:3])
    across = Across(0, home, out_rows, *route_sems[3:5])
    peers.greet(zs, Several([route, across]))
    sent = []

    def send(copy):
        copy.start()
        sent.append(copy)

    pieces = [(parts[p], None, came[p], totals[p], 0, zs - 1) for p in range(4)]
    ring = RingSum(pieces[:2], ring_send, ring_recv)
    ring.start()
    route.start()

    def restore(first_crossed, second, first_home, out):
        whole = lax.rem(z, 2) == x
        for layer, choice in enumerate([(first_home, first_crossed), second]):
            for kind, src in enumerate(choice):

                @pl.when((x == layer) & (whole if kind == 0 else jnp.logical_not(whole)))
                def _(src=src):
                    pltpu.make_async_copy(src, rows_buf, rows_sem).start()

        pltpu.make_async_copy(first_home, rows_buf, rows_sem).wait()
        for micro in range(out.shape[0]):
            for c in range(2):
                for k in range(zs):
                    at, of = (c * zs + k) * wide, (k * 2 + c) * wide
                    out[micro, at : at + wide, :] = rows_buf[micro, :, of : of + wide].astype(F32).T.astype(BF)

    def cut(a, totals):
        for layer, total in enumerate(totals):
            for i in range(2 * rest):
                wide_at, rows_at = 0, i * block
                if a == 0:
                    wide_at, rows_at = i // rest * stages[a].shape[3], i % rest * block
                stages[a][layer, i, :block, :] = total[rows_at : rows_at + block, wide_at : wide_at + stages[a].shape[3]]
        for i, place in offsets:
            device, t = peers.other(*place)
            src = stages[a].at[device["section"], device["dp"] * rest + device["r"]]
            line = a + a // 3
            send(remote(src, lands[a].at[me], all_send.at[line, i], all_recv.at[line, i], device))
        lands[a][me] = stages[a][x, spot]

    def settle(a, land):
        for i, place in offsets:
            device, t = peers.other(*(-d for d in place))
            came = land.at[t]
            remote(came, came, all_send.at[a, i], all_recv.at[a, i], device).wait_recv()

    cut(0, (fc_zero, fc_one))
    proj_both[0] = proj_zero[...]
    proj_both[1] = proj_one[...]
    device, _ = peers.other(1, 0, 0)
    send(remote(proj_both.at[1 - x], proj_land.at[x], far_send, far_recv, device))
    proj_land[x] = proj_both[x]
    ring.tick(2)
    small[...] = jnp.zeros_like(small)
    halves = half // block
    for layer in range(2):
        feed, attn, heads, unit = sums[4 * layer : 4 * layer + 4]
        for t in range(slab):
            natural[0:1, t * span : (t + 1) * span] = jnp.where(me == t, heads[:, :span], 0.0)
            natural[1:2, t * span : (t + 1) * span] = jnp.where(me == t, heads[:, 2 * span :], 0.0)
        for c in range(2):
            for k in range(zs):
                for r in range(rest):
                    to = small.at[(layer * 2 + c) * rest + r, k]
                    at = slice(((k * 2 + c) * rest + r) * block, ((k * 2 + c) * rest + r + 1) * block)
                    to[0:1, :block] = attn[0:1, at]
                    to[1:2, :block] = feed[0:1, at]
                    to[2:3, :block] = attn[1:2, at]
                    to[5:6, :block] = feed[3:4, at]
                    to[6:8, :block] = feed[1:3, at]
                    at = ((c * zs + k) * rest + r) * block
                    to[3:5, :block] = natural[0:2, at : at + block]
                    own = (peers.c == c) & (peers.r == r)
                    for h in range(2):
                        for j in range(halves):
                            line = unit[0:1, k * half + j * block : k * half + (j + 1) * block]
                            spot_row = 8 + h * halves + j
                            to[spot_row : spot_row + 1, :block] = jnp.where(own & (x == h), line, 0.0)
    for i, place in offsets:
        device, t = peers.other(*place)
        send(remote(small.at[t], small_land.at[me], all_send.at[3, i], all_recv.at[3, i], device))
    small_land[me] = small[me]

    ring.tick(2)
    late_ring = RingSum(pieces[2:], late_send, late_recv)
    late_ring.start()
    settle(0, lands[0])
    for t in range(slab):
        h, c, r = t // (2 * rest), t // rest % 2, t % rest
        for k in range(zs):
            at = ((c * zs + k) * rest + r) * (units // (2 * zs * rest)) + h * half
            out_fc[:, at : at + half] = lands[0][t, :block, k * half : (k + 1) * half]
    settle(3, small_land)
    total = small_land[0]
    for t in range(1, slab):
        total = total + small_land[t]
    small_sum[...] = total
    for k in range(1, zs):
        there = lax.rem(z + k, zs)
        send(remote(small_sum.at[there], z_land.at[z], z_send.at[k], z_recv.at[k], {"z": there}))
    z_land[z] = small_sum[z]
    ring.finish()
    cut(1, (totals[0], q_one))
    cut(2, (totals[1], k_one))
    late_ring.tick(2)
    route.arrived()
    across.tick("middle")
    restore(ready[1], ready[2:4], ready[0], section_out)
    came_proj = proj_land.at[1 - x]
    remote(came_proj, came_proj, far_send, far_recv, device).wait_recv()
    for h in range(2):
        for c in range(2):
            for k in range(zs):
                at, of = (c * zs + k) * wide, (k * 2 + c) * wide
                out_proj[h * half : (h + 1) * half, at : at + wide] = proj_land[h, :, of : of + wide]
    late_ring.tick(2)
    for k in range(1, zs):
        block_in = z_land.at[lax.rem(z + zs - k, zs)]
        remote(block_in, block_in, z_send.at[k], z_recv.at[k], {"z": lax.rem(z + k, zs)}).wait_recv()
    total = z_land[0]
    for k in range(1, zs):
        total = total + z_land[k]
    out_small[...] = total

    def place(p):
        for t in range(slab):
            count = min(span, width - t * span)
            if count > 0:
                at = p * width + t * span
                out_qkv[:, at : at + count] = lands[1 + p][t, :block, :count]

    for p in range(2):
        settle(1 + p, lands[1 + p])
        place(p)
    late_ring.finish()
    cut(3, (totals[2], v_one))
    cut(4, (totals[3], wo_one))
    route.sent()
    across.finish()
    restore(out_rows, ready[4:], home, section_grad)
    settle(4, lands[3])
    place(2)
    settle(5, lands[4])
    for t in range(slab):
        big, off = divmod(t * cols, wide)
        at = (big % 2 * zs + big // 2) * wide + off
        out_wo[:, at : at + cols] = lands[4][t, :block, :]
    for copy in sent:
        copy.wait_send()


def run_end(name, lay, parts, ones, fcs, projs, sums, last_rows, ready):
    zs, n = lay.zs, lay.slab
    span, width, block = lay.slots * lay.head, lay.width, lay.block
    rows = parts[0].shape[1]
    spots = lay.cores * lay.rest
    tall = -(-block // 16) * 16
    vmem = pl.BlockSpec(memory_space=pltpu.VMEM)
    dma = pltpu.SemaphoreType.DMA
    widths = [fcs[0].shape[1] // 2, span, span, span, lay.cols]
    half = projs[0].shape[0]
    tile = (-(-(8 + lay.unit_block // block) // 8) * 8, 128)
    outs = [(block, 3 * width), (block, width), (block, lay.units), (lay.unit_block, width), tile]
    return pl.pallas_call(
        functools.partial(end_kernel, (block, width, lay.units, lay.seqs)),
        out_shape=[jax.ShapeDtypeStruct(o, BF) for o in outs[:4]] + [jax.ShapeDtypeStruct(outs[4], F32)]
        + [jax.ShapeDtypeStruct((lay.micros, lay.width, lay.rows), BF)] * 2
        + [jax.ShapeDtypeStruct((lay.micros, *last_rows.shape), BF)] * 2,
        in_specs=[vmem] * 20 + [pl.BlockSpec(memory_space=pl.ANY)] * 7,
        out_specs=[vmem] * 7 + [pl.BlockSpec(memory_space=pl.ANY)] * 2,
        scratch_shapes=[
            *[pltpu.VMEM((rows, a.shape[2]), BF) for a in parts],
            pltpu.VMEM((2, half, width), BF),
            pltpu.VMEM((2, half, width), BF),
        ]
        + [pltpu.VMEM((lay.sections, spots, tall, m), BF) for m in widths]
        + [pltpu.VMEM((n, tall, m), BF) for m in widths]
        + [
            pltpu.VMEM((n, zs, *tile), F32),
            pltpu.VMEM((zs, *tile), F32),
            pltpu.VMEM((zs, *tile), F32),
            *[pltpu.VMEM((zs - 1, rows, a.shape[2]), BF) for a in parts],
            pltpu.VMEM((n, zs, *tile), F32),
            pltpu.VMEM((8, n * span), F32),
            pltpu.VMEM((lay.micros, *last_rows.shape), BF),
        ]
        + [dma((6, n))] * 2
        + [dma] * 2
        + [dma((zs,))] * 2
        + [dma((2, zs - 1))] * 4
        + [dma, dma, dma((lay.micros,)), dma, dma, dma],
        compiler_params=pltpu.CompilerParams(collective_id=name, has_side_effects=True, vmem_limit_bytes=60 * 2**20),
    )(*parts, *ones, *fcs, *projs, *sums, last_rows, *ready)


class Rings:
    def __init__(self, lay):
        self.zs = lay.zs
        self.state = {}

    def put(self, kind, layer, part):
        if part.ndim == 2:
            part = part.reshape(self.zs, part.shape[0] // self.zs, part.shape[1])
        _, acc, steps = self.state.get((kind, layer), (None, None, 0))
        self.state[kind, layer] = (part, acc, steps)

    def side(self, plan, pace, makes={}):
        pieces = []
        for kind, layer, count in plan:
            part, acc, steps = self.state.get((kind, layer), (None, None, 0))
            shape = makes[kind] if part is None else part.shape[1:]
            pieces.append((part, shape, acc, steps, count))
        return sum_side(pieces, pace)

    def done(self, plan, outs):
        for (kind, layer, count), acc in zip(plan, outs):
            part, _, steps = self.state[kind, layer]
            self.state[kind, layer] = (part, acc, steps + count)


def on_device(
    inputs, cotangent, positions, w_qkv, w_attn_out, w_fc, w_proj, norm_gains, biases, fc_bias
):
    lay = Layout(inputs, w_fc)
    n, block, width = lay.slab, lay.block, lay.width
    span = lay.slots * lay.head

    small = jnp.concatenate([norm_gains[0], biases[0]], axis=1).astype(F32).T
    small = jnp.stack([small[i] for i in (0, 1, 2, 6, 5, 7, 3, 4)])
    small = jnp.concatenate([small, fc_bias[0].reshape(-1, block).astype(F32)])
    small = jnp.pad(small, ((0, 0), (0, 128 - block)))
    places = jnp.pad(positions.astype(F32), ((0, 0), (0, 128 - lay.rows)))
    small = jnp.concatenate([small, places])
    small = jnp.pad(small, ((0, -small.shape[0] % 8), (0, 0)))
    *cut, proj_cut, w_qkv, w_out, h, g, row, col, vec_0, bias_0, unit_0, vec_1, bias_1, unit_1 = run_start(
        0, lay, small, w_qkv[0], w_attn_out[0], w_fc[0], w_proj[0], jnp.swapaxes(inputs, 2, 3), jnp.swapaxes(cotangent, 2, 3)
    )
    qkv_cut, wo_cut, fc_cut = cut[0:2], cut[2:4], cut[4:6]
    smalls = [(vec_0, bias_0, unit_0), (vec_1, bias_1, unit_1)]
    outs, keeps, params = [], [], []
    for layer in range(lay.sections):
        last = layer == lay.sections - 1
        vec, bias, unit = smalls[layer]
        w_qkv = w_qkv.reshape(width, 3 * span)
        side = gather_side([fc_cut[layer], (proj_cut, layer)], {"qkv": 1, "q0": 1, "q3": 1}, (lay.zs - 1, lay.zs - 2))
        if last:
            side = both_sides(side, share_side(lay, g, ("qkv", "q3")))
        (full, qkv, attended, logs, mid, normed_two), (w_fc, w_proj, *shared) = run_attention_forward(
            1 + 2 * layer,
            lay.head,
            side,
            h,
            w_qkv,
            w_out,
            bias,
            col,
            row,
            vec,
        )
        if last:
            side = route_side(lay, outs[0], "start")
        else:
            side = gather_side([wo_cut[layer + 1], qkv_cut[layer + 1]], {"k3": 2, "sent": 1}, turn=span)
        (full_two, slope, activated, result, w_proj, w_fc), later = run_feed_forward(
            2 + 2 * layer, side, normed_two, mid, w_fc, w_proj, unit, vec
        )
        params.append((w_qkv, w_out, w_fc, w_proj.reshape(-1, width)))
        if last:
            (home,), (branch,) = later, shared
        else:
            w_out, w_qkv = later
        keeps.append((h, full, qkv, attended, logs, mid, full_two, slope, activated))
        h = result
        outs.append(h)

    rings = Rings(lay)
    plans = {
        ("feed", 1): [("proj", 1, 3)],
        ("attention", 1): [("fc", 1, 3)],
        ("feed", 0): [("q", 1, 3), ("k", 1, 3), ("v", 1, 3), ("proj", 0, 1)],
        ("attention", 0): [("fc", 0, 3), ("proj", 0, 2), ("out", 1, 3)],
    }
    paces = {
        ("feed", 1): {"proj": 1, "fc": 1},
        ("attention", 1): {"k2": 1, "grad": 1},
        ("feed", 0): {"k3": 3},
        ("attention", 0): {"k3": 3},
    }
    crossed = {}
    sums = [None] * lay.sections
    for layer in reversed(range(lay.sections)):
        w_qkv, w_out, w_fc, w_proj = params[layer]
        vec = smalls[layer][0]
        h, full, qkv, attended, logs, mid, full_two, slope, activated = keeps[layer]
        full, full_two = (a.reshape(lay.tokens, width) for a in (full, full_two))
        name = 1 + 4 * lay.sections - 2 * layer
        side = rings.side(plans["feed", layer], paces["feed", layer], {"proj": (lay.half, width)})
        late = layer == lay.sections - 1
        turn = SideWork() if late else turn_side(lay, grad_out)
        side = both_sides(side, turn, across_side(0 if late else 1, home), route_side(lay, outs[1] if late else g, "start"))
        (grad_mid, attn_rows, grad_proj, grad_fc, feed_sums, unit_sums), done = run_feed_backward(
            name, side, g, mid, w_fc, w_proj, slope, activated, full_two, vec, *([branch] if late else [])
        )
        rings.put("proj", layer, grad_proj)
        rings.put("fc", layer, grad_fc)
        rings.done(plans["feed", layer], done)
        if late:
            crossed["out", 0] = (home, done[-2])
        else:
            crossed["out", 1] = (home, done[-2])
            rings.put("out", 1, done[-3])
        home = done[-1]
        side = rings.side(plans["attention", layer], paces["attention", layer])
        if not late:
            side = both_sides(side, turn_side(lay), across_side(1, home))
        (g, *grad_parts, grad_out, attn_sums, head_sums), done = run_attention_backward(
            name + 1, lay.head, side, attn_rows, grad_mid, h, w_qkv, w_out, qkv, attended, logs, full, col, row, vec
        )
        rings.done(plans["attention", layer], done)
        if not late:
            rings.put("out", layer, done[-2])
            crossed["grad", 1] = (home, done[-1])
        for kind, part in zip("qkv", grad_parts):
            rings.put(kind, layer, part)
        sums[layer] = (feed_sums, attn_sums, head_sums, unit_sums)
    out_qkv, out_attn, out_fc, out_proj, rows, section_out, section_grad, *_ = run_end(
        3 + 4 * lay.sections,
        lay,
        [rings.state[kind, 0][0] for kind in ("q", "k", "v", "out")],
        [rings.state[kind, 1][1] for kind in ("q", "k", "v", "out")],
        [rings.state["fc", layer][1] for layer in range(2)],
        [rings.state["proj", layer][1] for layer in range(2)],
        [a for layer in range(2) for a in sums[layer]],
        g,
        [*crossed["out", 0], *crossed["out", 1], *crossed["grad", 1]],
    )
    cols = rows[:8, :block].T
    return (
        jnp.swapaxes(section_out, 1, 2)[None, :, None],
        jnp.swapaxes(section_grad, 1, 2)[None, :, None],
        out_qkv.astype(F32)[None],
        out_attn.astype(F32)[None],
        out_fc.astype(F32)[None],
        out_proj.astype(F32)[None],
        cols[None, :, :2],
        cols[None, :, 2:],
        rows[8 : 8 + lay.unit_block // block, :block].reshape(1, lay.unit_block),
    )


def solution(mesh):
    sections, cores, contexts = (mesh.shape[a] for a in ("section", "dp", "ctx"))
    zs = sections * cores
    shape = (sections, cores, zs, contexts // zs)
    inner = Mesh(mesh.devices.reshape(shape), ALL)
    tokens = P(None, "dp", ("z", "r"), None)
    rows = P("section", ("dp", "z", "r"), None)
    units = P("section", ("dp", "z", "r"))
    out_tokens = P("section", None, "dp", ("z", "r"), None)
    return jax.shard_map(
        on_device,
        mesh=inner,
        in_specs=(tokens, tokens, P(None, ("z", "r"))) + (rows,) * 6 + (units,),
        out_specs=(out_tokens, out_tokens) + (rows,) * 6 + (units,),
        check_vma=False,
    )
```

```python
import functools

import jax
import jax.numpy as jnp
from jax import lax
from jax.experimental import pallas as pl
from jax.experimental.pallas import tpu as pltpu
from jax.sharding import Mesh
from jax.sharding import PartitionSpec as P

HEADS = 25
EPSILON = 1e-05

SLAB = ("section", "dp", "r")
ALL = ("section", "dp", "z", "r")
MESH = pl.DeviceIdType.MESH


class Layout:
    def __init__(self, inputs, w_fc):
        self.micros, _, self.rows, self.width = inputs.shape
        self.sections = lax.axis_size("section")
        self.cores = lax.axis_size("dp")
        self.zs = lax.axis_size("z")
        self.rest = lax.axis_size("r")
        self.slab = self.sections * self.cores * self.rest
        self.shards = self.cores * self.zs * self.rest
        self.units = w_fc.shape[2]
        self.tokens = self.rows * self.slab
        self.seqs = self.cores
        self.head = self.width // HEADS
        self.slots = -(-HEADS // self.slab)
        self.block = self.width // self.shards
        self.unit_block = self.units // self.shards
        self.half = self.unit_block // self.sections
        self.cols = self.width // self.slab
        self.x = lax.axis_index("section")
        self.c = lax.axis_index("dp")
        self.z = lax.axis_index("z")
        self.r = lax.axis_index("r")
        self.t = (self.x * self.cores + self.c) * self.rest + self.r

    def number(self, x, c, z, r):
        return ((x * self.cores + c) * self.zs + z) * self.rest + r

    def order(self, a):
        lead = a.shape[:-1]
        a = a.reshape(*lead, self.cores, self.zs, self.rest * self.block)
        return jnp.swapaxes(a, -3, -2).reshape(*lead, self.width)

    def restore(self, a):
        lead = a.shape[:-1]
        a = a.reshape(*lead, self.zs, self.cores, self.rest * self.block)
        return jnp.swapaxes(a, -3, -2).reshape(*lead, self.width)

    def routes(self, micro):
        pairs = []
        for x in range(self.sections):
            for c in range(self.cores):
                for s in range(self.seqs):
                    for r in range(self.rest):
                        place = x * self.cores + c
                        pairs.append(((x, s, place, r), (x, c, micro * self.seqs + s, r)))
        return pairs

    def tokens_in(self, a):
        got = []
        for micro in range(self.micros):
            route = [(self.number(*f), self.number(*g)) for f, g in self.routes(micro)]
            got.append(lax.ppermute(a[micro, 0], ALL, route))
        out = got[0]
        for micro in range(1, self.micros):
            out = jnp.where(self.z // self.seqs == micro, got[micro], out)
        return out

    def tokens_out(self, parts):
        result = []
        for micro in range(self.micros):
            got = []
            for layer, part in enumerate(parts):
                route = [
                    (self.number(*g), self.number(layer, *f[1:])) for f, g in self.routes(micro)
                ]
                got.append(lax.ppermute(part, ALL, route))
            out = got[0]
            for layer in range(1, len(parts)):
                out = jnp.where(self.x == layer, got[layer], out)
            result.append(out)
        return jnp.stack(result)[None, :, None]


LOW = -1e30
BF = jnp.bfloat16
F32 = jnp.float32


class Peers:
    def __init__(self):
        self.sections, self.rest = lax.axis_size("section"), lax.axis_size("r")
        self.chips = self.sections * self.rest
        self.x, self.c, self.r = (lax.axis_index(a) for a in ("section", "dp", "r"))
        self.chip = self.x * self.rest + self.r

    def away(self, k, sign):
        x = lax.rem(self.x + self.sections + sign * (k // self.rest), self.sections)
        r = lax.rem(self.r + self.rest + sign * (k % self.rest), self.rest)
        return x, r

    def ahead(self, k):
        x, r = self.away(k, 1)
        return {"section": x, "dp": self.c, "r": r}

    def behind(self, k):
        x, r = self.away(k, -1)
        return {"section": x, "dp": self.c, "r": r}

    def sibling(self):
        return {"section": self.x, "dp": 1 - self.c, "r": self.r}

    def behind_chip(self, k):
        x, r = self.away(k, -1)
        return x * self.rest + r

    def other(self, dx, dc, dr):
        x = lax.rem(self.x + self.sections + dx, self.sections)
        c = lax.rem(self.c + 2 + dc, 2)
        r = lax.rem(self.r + self.rest + dr, self.rest)
        return {"section": x, "dp": c, "r": r}, (x * 2 + c) * self.rest + r

    def offsets(self):
        every = [(x, c, r) for x in range(self.sections) for c in range(2) for r in range(self.rest)]
        return list(enumerate(every))[1:]

    def greet(self, zs=1, work=None):
        barrier = pltpu.get_barrier_semaphore()
        z = lax.axis_index("z")
        size = lax.axis_size("z")
        for k in range(1, zs):
            pl.semaphore_signal(barrier, inc=1, device_id={"z": lax.rem(z + size - k, size)}, device_id_type=MESH)
        others = self.offsets()
        for _, place in others:
            pl.semaphore_signal(barrier, inc=1, device_id=self.other(*place)[0], device_id_type=MESH)
        more = 0 if work is None else work.greet()
        pl.semaphore_wait(barrier, len(others) + zs - 1 + more)


def remote(src, dst, send, recv, device):
    return pltpu.make_async_remote_copy(
        src_ref=src, dst_ref=dst, send_sem=send, recv_sem=recv, device_id=device, device_id_type=MESH
    )


class Gather:
    def __init__(self, peers, full, sems):
        self.peers, self.full = peers, full
        self.chip_send, self.chip_recv, self.core_send, self.core_recv = sems
        self.sent = []

    def start(self, src):
        p = self.peers
        mine = self.full.at[p.chip, p.c]
        mine[...] = src if isinstance(src, jax.Array) else src[...]
        for k in range(1, p.chips):
            self.send(remote(mine, mine, self.chip_send.at[k], self.chip_recv.at[k], p.ahead(k)))
        self.send(remote(mine, mine, self.core_send.at[0], self.core_recv.at[0], p.sibling()))

    def send(self, copy):
        copy.start()
        self.sent.append(copy)

    def forward(self, k):
        p = self.peers
        block = self.full.at[p.behind_chip(k), p.c]
        remote(block, block, self.chip_send.at[k], self.chip_recv.at[k], p.sibling()).wait_recv()
        self.send(remote(block, block, self.core_send.at[k], self.core_recv.at[k], p.sibling()))

    def chip(self, k):
        p = self.peers
        block = self.full.at[p.behind_chip(k), 1 - p.c]
        remote(block, block, self.core_send.at[k], self.core_recv.at[k], p.sibling()).wait_recv()
        return p.behind_chip(k)

    def arrivals(self):
        yield 0, self.chip(0)
        chips = self.peers.chips
        for k in range(1, chips):
            for later in (1, 2) if k == 1 else (k + 1,):
                if later < chips:
                    self.forward(later)
            yield k, self.chip(k)

    def finish(self):
        for copy in self.sent:
            copy.wait_send()


class Reduce:
    def __init__(self, peers, mine, stage, other, going, coming, sems):
        self.peers = peers
        self.mine, self.stage, self.other, self.going, self.coming = mine, stage, other, going, coming
        self.chip_send, self.chip_recv, self.core_send, self.core_recv = sems
        self.sent = []

    def send(self, copy):
        copy.start()
        self.sent.append(copy)

    def put(self, k, both):
        p = self.peers
        rows = both.shape[0] // 2
        low, high = both[:rows], both[rows:]
        first = p.c == 0
        self.mine[k] = jnp.where(first, low, high)
        self.stage[k] = jnp.where(first, high, low).astype(BF)
        self.send(remote(self.stage.at[k], self.other.at[k], self.core_send.at[k], self.core_recv.at[k], p.sibling()))

    def arrived(self, k):
        p = self.peers
        remote(self.stage.at[k], self.other.at[k], self.core_send.at[k], self.core_recv.at[k], p.sibling()).wait_recv()
        return self.mine[k] + self.other[k].astype(F32)

    def push(self, k):
        p = self.peers
        if k:
            self.going[k - 1] = self.arrived(k).astype(BF)
            self.send(remote(self.going.at[k - 1], self.coming.at[k - 1], self.chip_send.at[k], self.chip_recv.at[k], p.behind(k)))

    def total(self):
        p = self.peers
        out = self.arrived(0)
        for k in range(1, p.chips):
            remote(self.going.at[k - 1], self.coming.at[k - 1], self.chip_send.at[k], self.chip_recv.at[k], p.sibling()).wait_recv()
            out = out + self.coming[k - 1].astype(F32)
        return out

    def finish(self):
        for copy in self.sent:
            copy.wait_send()


class RingGather:
    def greet(self):
        return 0

    def __init__(self, pieces, local, send, recv):
        self.pieces, self.local, self.send_sem, self.recv_sem = pieces, local, send, recv
        self.zs, self.z = lax.axis_size("z"), lax.axis_index("z")
        every = [(p, s) for s in range(self.zs - 1) for p in range(len(pieces)) if s < pieces[p][2]]
        self.steps = [(p, s) for p, s in every if s < pieces[p][2] - 1] + [(p, s) for p, s in every if s == pieces[p][2] - 1]
        self.forwards = len(every) - len(pieces)
        self.sent = []

    def block(self, step):
        return lax.rem(self.z + self.zs - step, self.zs)

    def send(self, p, step, src):
        dst = self.pieces[p][1].at[self.block(step)]
        copy = remote(src, dst, self.send_sem.at[p, step], self.recv_sem.at[p, step], {"z": lax.rem(self.z + 1, self.zs)})
        copy.start()
        self.sent.append(copy)

    def start(self):
        for p in range(len(self.pieces)):
            self.launch(p)

    def launch(self, p):
        shard, full, _ = self.pieces[p]
        self.send(p, 0, shard)
        pltpu.make_async_copy(shard, full.at[self.z], self.local.at[p]).start()

    def tick(self, count=1):
        for _ in range(min(count, self.forwards)):
            self.forwards -= 1
            self.take()

    def take(self):
        p, step = self.steps.pop(0)
        shard, full, count = self.pieces[p]
        block = full.at[self.block(step + 1)]
        remote(block, block, self.send_sem.at[p, step], self.recv_sem.at[p, step], {"z": lax.rem(self.z + 1, self.zs)}).wait_recv()
        if step < count - 1:
            self.send(p, step + 1, block)
            return None
        pltpu.make_async_copy(shard, full.at[self.z], self.local.at[p]).wait()
        return p

    def finish(self):
        while self.steps:
            self.take()
        for copy in self.sent:
            copy.wait_send()


class RingSum:
    def greet(self):
        return 0

    def __init__(self, pieces, send, recv):
        self.pieces, self.send_sem, self.recv_sem = pieces, send, recv
        self.zs, self.z = lax.axis_size("z"), lax.axis_index("z")
        self.steps, self.sent = [], []
        self.late = [p for p, piece in enumerate(pieces) if piece[0] is None]
        ready = [p for p in range(len(pieces)) if p not in self.late]
        self.steps = [(p, i) for i in range(self.zs - 1) for p in ready if i < pieces[p][5] - 1]
        self.forwards = len(self.steps)
        self.steps += [(p, pieces[p][5] - 1) for p in ready]
        self.parts = [piece[0] for piece in pieces]

    def copy(self, p, i, src):
        dst = self.pieces[p][2].at[i]
        return remote(src, dst, self.send_sem.at[p, i], self.recv_sem.at[p, i], {"z": lax.rem(self.z + 1, self.zs)})

    def send(self, p, i, src):
        copy = self.copy(p, i, src)
        copy.start()
        self.sent.append(copy)

    def launch(self, p):
        acc, first = self.pieces[p][1], self.pieces[p][4]
        self.send(p, 0, far(acc) if first else far(self.parts[p]).at[lax.rem(self.z + self.zs - 1, self.zs)])

    def start(self):
        for p in range(len(self.pieces)):
            if p not in self.late:
                self.launch(p)

    def made(self, part):
        if self.late:
            p = self.late.pop(0)
            self.parts[p] = part
            self.launch(p)
            count = self.pieces[p][5]
            self.steps[self.forwards : self.forwards] = [(p, i) for i in range(count - 1)]
            self.forwards += count - 1
            self.steps.append((p, count - 1))

    def tick(self, count=1):
        for _ in range(min(count, self.forwards)):
            self.forwards -= 1
            self.take()

    def take(self):
        p, i = self.steps.pop(0)
        part, acc, came, out, first, count = self.pieces[p]
        self.copy(p, i, came.at[i]).wait_recv()
        own = self.parts[p][lax.rem(self.z + 2 * self.zs - 2 - first - i, self.zs)]
        total = (came[i].astype(F32) + own.astype(F32)).astype(BF)
        if i < count - 1:
            came[i] = total
            self.send(p, i + 1, came.at[i])
        else:
            out[...] = total

    def middle(self):
        pass

    def finish(self):
        while self.steps:
            self.take()
        for copy in self.sent:
            copy.wait_send()


GROUPS = 5


def groups_of(rows, start, count):
    tall, at = rows // GROUPS, start
    while at < start + count:
        group, row = divmod(at, tall)
        some = min(tall - row, start + count - at)
        yield at - start, group, row, some
        at += some


class TurnBack:
    def __init__(self, peers, part, pieces, came, send, recv, given=None):
        self.given = given
        self.peers, self.part, self.pieces, self.came = peers, part, pieces, came
        self.send_sem, self.recv_sem = send, recv
        self.sent = []

    def greet(self):
        return 0

    def start(self):
        pass

    def tick(self, point):
        pass

    def middle(self):
        if self.given is not None:
            self.share(self.given)

    def made(self, turned):
        if self.given is None:
            self.share(turned)

    def share(self, turned):
        slab, _, cols = self.pieces.shape
        for t in range(slab):
            self.pieces[t] = turned[:, t * cols : (t + 1) * cols]
        _, me = self.peers.other(0, 0, 0)
        for i, place in self.peers.offsets():
            device, t = self.peers.other(*place)
            copy = remote(self.pieces.at[t], self.came.at[me], self.send_sem.at[i], self.recv_sem.at[i], device)
            copy.start()
            self.sent.append(copy)
        self.came[me] = self.pieces[me]

    def finish(self):
        for i, place in self.peers.offsets():
            device, t = self.peers.other(*(-d for d in place))
            block = self.came.at[t]
            remote(block, block, self.send_sem.at[i], self.recv_sem.at[i], device).wait_recv()
        zs, rows, cols = self.part.shape[0], self.part.shape[1] * GROUPS, self.came.shape[2]
        wide, span = rows // 2, self.came.shape[1]
        for c in range(2):
            for k in range(zs):
                at, done = (c * zs + k) * wide, 0
                while done < wide:
                    t, row = divmod(at + done, span)
                    count = min(wide - done, span - row)
                    for first, group, to, some in groups_of(rows, c * wide + done, count):
                        lanes = slice(group * cols, (group + 1) * cols)
                        self.part[k, to : to + some, lanes] = self.came[t, row + first : row + first + some, :]
                    done += count
        for copy in self.sent:
            copy.wait_send()


class Turn:
    def __init__(self, peers, full, nat, land, w_out, send, recv):
        self.peers, self.full, self.nat, self.land, self.w_out = peers, full, nat, land, w_out
        self.send_sem, self.recv_sem = send, recv
        self.sent = []

    def start(self):
        zs, rows, cols = self.full.shape[0], self.full.shape[1] * GROUPS, self.nat.shape[1]
        part, span = rows // 2, self.w_out.shape[0]
        for c in range(2):
            for z in range(zs):
                at = (c * zs + z) * part
                for first, group, row, some in groups_of(rows, c * part, part):
                    lanes = slice(group * cols, (group + 1) * cols)
                    self.nat[at + first : at + first + some, :] = self.full[z, row : row + some, lanes]
        used = zs * rows
        if used < self.nat.shape[0]:
            self.nat[used:, :] = jnp.zeros((self.nat.shape[0] - used, cols), BF)
        _, me = self.peers.other(0, 0, 0)
        for i, place in self.peers.offsets():
            device, t = self.peers.other(*place)
            src = self.nat.at[pl.ds(pl.multiple_of(t * span, span), span)]
            copy = remote(src, self.land.at[me], self.send_sem.at[i], self.recv_sem.at[i], device)
            copy.start()
            self.sent.append(copy)
        self.land[me] = self.nat[pl.ds(pl.multiple_of(me * span, span), span), :]

    def finish(self):
        for i, place in self.peers.offsets():
            device, t = self.peers.other(*(-d for d in place))
            block = self.land.at[t]
            remote(block, block, self.send_sem.at[i], self.recv_sem.at[i], device).wait_recv()
        slab, _, cols = self.land.shape
        for t in range(slab):
            self.w_out[:, t * cols : (t + 1) * cols] = self.land[t]
        for copy in self.sent:
            copy.wait_send()


class Route:
    def __init__(self, seqs, src, out, local, send, recv, when="start"):
        self.when = when
        self.seqs, self.src, self.out = seqs, src, out
        self.local, self.send_sem, self.recv_sem = local, send, recv
        x, c, z = (lax.axis_index(a) for a in ("section", "dp", "z"))
        self.here = lax.rem(z, 2) == x
        place = c * 2 + x
        self.to = {"dp": lax.rem(z, seqs), "z": place}
        self.micro = z // seqs
        self.same = (lax.rem(z, seqs) == c) & (place == z)
        self.sources = []
        for micro in range(out.shape[0]):
            src_c, src_z = z // 2, micro * seqs + c
            self.sources.append(({"dp": src_c, "z": src_z}, (src_c == c) & (src_z == z)))

    def greet(self):
        barrier = pltpu.get_barrier_semaphore()
        for device, same in self.sources:

            @pl.when(self.here & jnp.logical_not(same))
            def _(device=device):
                pl.semaphore_signal(barrier, inc=1, device_id=device, device_id_type=MESH)

        return jnp.where(self.same, 0, 1)

    def copy(self):
        return remote(self.src, self.out.at[self.micro], self.send_sem, self.recv_sem.at[self.micro], self.to)

    def own(self):
        return pltpu.make_async_copy(self.src, self.out.at[self.micro], self.local)

    def start(self):
        if self.when == "start":
            self.go()

    def middle(self):
        pass

    def go(self):
        @pl.when(jnp.logical_not(self.same))
        def _():
            self.copy().start()

        @pl.when(self.same)
        def _():
            self.own().start()

    def tick(self, point):
        if self.when == point:
            self.go()

    def made(self, part):
        pass

    def arrived(self):
        for micro, (device, same) in enumerate(self.sources):

            @pl.when(self.here & jnp.logical_not(same))
            def _(micro=micro, device=device):
                block = self.out.at[micro]
                remote(block, block, self.send_sem, self.recv_sem.at[micro], device).wait_recv()

        @pl.when(self.same)
        def _():
            self.own().wait()

    def sent(self):
        @pl.when(jnp.logical_not(self.same))
        def _():
            self.copy().wait_send()

    def finish(self):
        self.arrived()
        self.sent()


class Across:
    def __init__(self, layer, src, out, send, recv):
        self.src, self.out, self.send_sem, self.recv_sem = src, out, send, recv
        x, z = lax.axis_index("section"), lax.axis_index("z")
        self.layer = layer
        self.sends = (x != layer) & (lax.rem(z, 2) == x)
        self.takes = (x == layer) & (lax.rem(z, 2) != x)
        self.going = False

    def greet(self):
        barrier = pltpu.get_barrier_semaphore()

        @pl.when(self.takes)
        def _():
            pl.semaphore_signal(barrier, inc=1, device_id={"section": 1 - self.layer}, device_id_type=MESH)

        return jnp.where(self.sends, 1, 0)

    def copy(self):
        return remote(self.src, self.out, self.send_sem, self.recv_sem, {"section": jnp.int32(self.layer)})

    def back(self):
        return remote(self.out, self.out, self.send_sem, self.recv_sem, {"section": jnp.int32(1 - self.layer)})

    def start(self):
        pass

    def tick(self, point):
        if not self.going:
            self.going = True

            @pl.when(self.sends)
            def _():
                self.copy().start()

    def made(self, part):
        pass

    def middle(self):
        pass

    def finish(self):
        self.tick("end")

        @pl.when(self.takes)
        def _():
            self.back().wait_recv()

        @pl.when(self.sends)
        def _():
            self.copy().wait_send()


class RouteIn:
    def __init__(self, seqs, pairs, local, send, recv):
        self.pairs, self.local, self.send_sem, self.recv_sem = pairs, local, send, recv
        x, c, z = (lax.axis_index(a) for a in ("section", "dp", "z"))
        self.sends = lax.rem(z, 2) == x
        self.targets = []
        for micro in range(pairs[0][0].shape[0]):
            to_c, to_z = z // 2, micro * seqs + c
            self.targets.append(({"dp": to_c, "z": to_z}, (to_c == c) & (to_z == z)))
        self.micro = z // seqs
        self.source = {"dp": lax.rem(z, seqs), "z": c * 2 + x}
        self.same = (lax.rem(z, seqs) == c) & (c * 2 + x == z)

    def greet(self):
        barrier = pltpu.get_barrier_semaphore()

        @pl.when(jnp.logical_not(self.same))
        def _():
            pl.semaphore_signal(barrier, inc=1, device_id=self.source, device_id_type=MESH)

        return sum(jnp.where(self.sends & jnp.logical_not(same), 1, 0) for _, same in self.targets)

    def far(self, i, micro):
        src, dst = self.pairs[i]
        return remote(src.at[micro, 0], dst, self.send_sem.at[i, micro], self.recv_sem.at[i], self.targets[micro][0])

    def near(self, i, micro):
        src, dst = self.pairs[i]
        return pltpu.make_async_copy(src.at[micro, 0], dst, self.local.at[i])

    def start(self, i=0):
        for micro, (_, same) in enumerate(self.targets):

            @pl.when(self.sends & jnp.logical_not(same))
            def _(micro=micro):
                self.far(i, micro).start()

            @pl.when(self.sends & same)
            def _(micro=micro):
                self.near(i, micro).start()

    def tick(self, point):
        pass

    def made(self, part):
        pass

    def middle(self):
        pass

    def arrived(self, i):
        dst = self.pairs[i][1]

        @pl.when(jnp.logical_not(self.same))
        def _():
            remote(dst, dst, self.send_sem.at[i, 0], self.recv_sem.at[i], self.source).wait_recv()

        for micro, (_, same) in enumerate(self.targets):

            @pl.when(self.sends & same)
            def _(micro=micro):
                self.near(i, micro).wait()

    def finish(self):
        for i in range(len(self.pairs)):
            for micro, (_, same) in enumerate(self.targets):

                @pl.when(self.sends & jnp.logical_not(same))
                def _(i=i, micro=micro):
                    self.far(i, micro).wait_send()


def reorder(raw, ordered, zs, wide):
    for c in range(2):
        for k in range(zs):
            at, to = (c * zs + k) * wide, (k * 2 + c) * wide
            ordered[:, to : to + wide] = raw[at : at + wide, :].astype(F32).T.astype(BF)


class Shared:
    def __init__(self, src, gather, points):
        self.src, self.gather, self.points = src, gather, points

    def greet(self):
        return 0

    def start(self):
        pass

    def made(self, part):
        pass

    def middle(self):
        pass

    def tick(self, point):
        if point == self.points[0]:
            self.gather.start(self.src)
        if point == self.points[1]:
            for k in range(1, self.gather.peers.chips):
                self.gather.forward(k)

    def finish(self):
        for k in range(self.gather.peers.chips):
            self.gather.chip(k)
        self.gather.finish()


class Several:
    def __init__(self, works):
        self.works = works

    def greet(self):
        return sum(work.greet() for work in self.works)

    def start(self):
        for work in self.works:
            work.start()

    def tick(self, point):
        for work in self.works:
            work.tick(point)

    def made(self, part):
        for work in self.works:
            work.made(part)

    def middle(self):
        for work in self.works:
            work.middle()

    def finish(self):
        for work in self.works:
            work.finish()


class NoSide:
    def greet(self):
        return 0

    def start(self):
        pass

    def tick(self, point):
        pass

    def made(self, part):
        pass

    def middle(self):
        pass

    def finish(self):
        pass


class Both:
    def greet(self):
        return 0

    def __init__(self, ring, turn, ahead):
        self.ring, self.turn = ring, turn
        if ahead:
            ring.steps.sort(key=lambda step: step[1] if step[0] else step[1] * 0.5 - 0.6)

    def start(self):
        self.ring.start()

    def tick(self, count=1):
        for _ in range(count):
            self.take()

    def take(self):
        if self.ring.take() == 0:
            self.turn.start()

    def finish(self):
        while self.ring.steps:
            self.take()
        self.ring.finish()
        self.turn.finish()


class Fetch:
    def __init__(self, far, near, sem):
        self.far, self.near = far, near
        self.copy = pltpu.make_async_copy(far, near, sem)
        self.copy.start()
        self.here = False
        self.shape = near.shape

    def __getitem__(self, index):
        if not self.here:
            self.copy.wait()
            self.here = True
        return self.near[index]

    def finish(self):
        if not self.here:
            self.copy.wait()


def far(ref):
    return ref.far if isinstance(ref, Fetch) else ref


class Paced:
    def __init__(self, work, pace):
        self.work, self.pace = work, pace
        self.greet, self.start, self.finish = work.greet, work.start, work.finish
        self.middle = getattr(work, "middle", lambda: None)
        self.part = None

    def made(self, part):
        self.part = part
        if "launch" not in self.pace:
            self.work.made(part)

    def tick(self, point):
        self.work.tick(self.pace.get(point, 0))
        if self.part is not None and self.pace.get("launch") == point:
            self.work.made(self.part)


class SideWork:
    def __init__(self, operands=(), in_hbm=(), outs=(), out_hbm=(), scratch=(), build=None):
        self.operands, self.in_hbm, self.outs, self.out_hbm = operands, in_hbm, outs, out_hbm
        self.scratch, self.build = scratch, build
        self.zs = 1 if build is None else 2

    def make(self, peers, ins, outs, scratch):
        return NoSide() if self.build is None else self.build(peers, ins, outs, scratch)


def route_side(lay, src, when):
    dma = pltpu.SemaphoreType.DMA
    outs = [((lay.micros, *src.shape), BF)]

    def build(peers, ins, outs, scratch):
        return Route(lay.seqs, ins[0], outs[0], *scratch, when)

    return SideWork([src], (True,), outs, (True,), [dma, dma, dma((lay.micros,))], build)


def turn_side(lay, turned=None):
    n, span = lay.slab, lay.slots * lay.head
    outs = [((lay.zs, lay.width // lay.zs // GROUPS, GROUPS * lay.cols), BF)]
    scratch = [pltpu.VMEM((n, span, lay.cols), BF)] * 2 + [pltpu.SemaphoreType.DMA((n,))] * 2

    def build(peers, ins, outs, scratch):
        return TurnBack(peers, outs[0], *scratch, ins[0] if ins else None)

    operands = [] if turned is None else [turned]
    return SideWork(operands, (False,) * len(operands), outs, (False,), scratch, build)


def share_side(lay, a, points):
    chips = lay.slab // 2

    def build(peers, ins, outs, scratch):
        return Shared(ins[0], Gather(peers, outs[0], scratch), points)

    return SideWork([a], (False,), [((chips, 2, *a.shape), BF)], (False,), [pltpu.SemaphoreType.DMA((chips,))] * 4, build)


def across_side(layer, a):
    dma = pltpu.SemaphoreType.DMA

    def build(peers, ins, outs, scratch):
        return Across(layer, ins[0], outs[0], *scratch)

    return SideWork([a], (True,), [(a.shape, a.dtype)], (True,), [dma, dma], build)


def both_sides(*sides):
    sides = [side for side in sides if side.build is not None]
    joined = [[], [], [], [], []]
    for side in sides:
        for into, more in zip(joined, (side.operands, side.in_hbm, side.outs, side.out_hbm, side.scratch)):
            into += list(more)

    def build(peers, ins, outs, scratch):
        works = []
        for side in sides:
            a, b, c = len(side.operands), len(side.outs), len(side.scratch)
            works.append(side.build(peers, ins[:a], outs[:b], scratch[:c]))
            ins, outs, scratch = ins[a:], outs[b:], scratch[c:]
        return Several(works)

    return SideWork(*joined, build)


def gather_side(shards, pace, counts=None, turn=None):
    zs = lax.axis_size("z")
    n = len(shards)
    counts = counts or (zs - 1,) * n
    places = [a[1] if isinstance(a, tuple) else None for a in shards]
    shards = [a[0] if isinstance(a, tuple) else a for a in shards]
    outs = [((zs, *a.shape[-2:]), BF) for a in shards]
    sems = [pltpu.SemaphoreType.DMA((n,))] + [pltpu.SemaphoreType.DMA((n, zs - 1))] * 2
    if turn is None:

        def build(peers, ins, outs, scratch):
            ins = [a if place is None else a.at[place] for a, place in zip(ins, places)]
            return Paced(RingGather(list(zip(ins, outs, counts)), *scratch), pace)

        return SideWork(shards, (True,) * n, outs, (True,) * n, sems, build)
    slab = 2 * lax.axis_size("section") * lax.axis_size("r")
    cols = shards[0].shape[1] // GROUPS
    outs[0] = ((turn, slab * cols), BF)
    more = [
        pltpu.VMEM((zs, *shards[0].shape), BF),
        pltpu.VMEM((slab * turn, cols), BF),
        pltpu.VMEM((slab, turn, cols), BF),
    ] + [pltpu.SemaphoreType.DMA((slab,))] * 2

    def build_turn(peers, ins, outs, scratch):
        pieces = list(zip(ins, [scratch[3], *outs[1:]], counts))
        turning = Turn(peers, scratch[3], scratch[4], scratch[5], outs[0], *scratch[6:8])
        return Paced(Both(RingGather(pieces, *scratch[:3]), turning, False), pace)

    return SideWork(shards, (True,) * n, outs, (False,) + (True,) * (n - 1), sems + more, build_turn)


def sum_side(pieces, pace):
    zs = lax.axis_size("z")
    n = len(pieces)
    operands, outs, scratch = [], [], []
    for part, shape, acc, first, count in pieces:
        operands += [a for a in (part, acc) if a is not None]
        outs.append((shape, BF))
        scratch.append(pltpu.VMEM((count, *shape), BF))
    scratch += [pltpu.SemaphoreType.DMA((n, zs - 1))] * 2
    def build(peers, ins, outs, scratch):
        ins, made = list(ins), []
        for i, (part, shape, acc, first, count) in enumerate(pieces):
            part_ref = None if part is None else ins.pop(0)
            acc_ref = None if acc is None else ins.pop(0)
            made.append((part_ref, acc_ref, scratch[i], outs[i], first, count))
        ring = RingSum(made, *scratch[n : n + 2])
        return Paced(ring, pace)

    return SideWork(operands, (False,) * len(operands), outs, (False,) * len(outs), scratch, build)


def gather_scratch(chips, rows, width):
    return [pltpu.VMEM((chips, 2, rows, width), BF)] + [pltpu.SemaphoreType.DMA((chips,))] * 4


def reduce_scratch(chips, rows, width):
    return [
        pltpu.VMEM((chips, rows, width), F32),
        pltpu.VMEM((chips, rows, width), BF),
        pltpu.VMEM((chips, rows, width), BF),
        pltpu.VMEM((chips - 1, rows, width), BF),
        pltpu.VMEM((chips - 1, rows, width), BF),
    ] + [pltpu.SemaphoreType.DMA((chips,))] * 4


def norm_parts(v):
    centred = v - jnp.mean(v, axis=-1, keepdims=True)
    spread = jnp.mean(centred * centred, axis=-1, keepdims=True)
    scale = lax.rsqrt(spread + EPSILON)
    return centred * scale, scale


def norm_back(v, gain, grad):
    unit, scale = norm_parts(v)
    scaled = grad * gain
    part = scaled - jnp.mean(scaled, axis=-1, keepdims=True)
    part = part - unit * jnp.mean(scaled * unit, axis=-1, keepdims=True)
    return part * scale, jnp.sum(grad * unit, axis=0, keepdims=True), jnp.sum(grad, axis=0, keepdims=True)


def dot(a, b, ca=1, cb=0):
    return lax.dot_general(a, b, (((ca,), (cb,)), ((), ())), preferred_element_type=F32)


def chip_rows(chip, rows):
    return pl.ds(pl.multiple_of(chip * (2 * rows), 2 * rows), 2 * rows)


def groups(span, head):
    wide = 128 if span % 128 == 0 else span
    for g in range(span // wide):
        yield slice(g * wide, (g + 1) * wide), [(g * wide // head + i, i * head) for i in range(wide // head)]


def only(a, start, head):
    lane = lax.broadcasted_iota(jnp.int32, a.shape, 1)
    return jnp.where((lane >= start) & (lane < start + head), a, jnp.zeros_like(a))


def attention_forward(head, side, *refs):
    (h, w_qkv, w_out, bias, col, row, vec) = refs[:7]
    ins, refs = refs[7 : 7 + len(side.operands)], refs[7 + len(side.operands) :]
    (normed, qkv, attended, logs, mid, normed_two), refs = refs[:6], refs[6:]
    side_outs, refs = refs[: len(side.outs)], refs[len(side.outs) :]
    gather_refs, reduce_refs, side_refs = refs[:5], refs[5 : 14 + 1], refs[14 + 1 :]
    rows, width = h.shape
    span = w_out.shape[0]
    peers = Peers()
    gather = Gather(peers, gather_refs[0], gather_refs[1:])
    reduce = Reduce(peers, *reduce_refs[:5], reduce_refs[5:9])
    kept_sem = reduce_refs[9]
    full = gather.full
    work = side.make(peers, ins, side_outs, side_refs)
    peers.greet(side.zs, work)
    gather.start((norm_parts(h[...].astype(F32))[0] * vec[0:1, :] + vec[2:3, :]).astype(BF))
    work.start()
    for k, chip in gather.arrivals():
        part = dot(full[chip].reshape(2 * rows, width), w_qkv[...]) + bias[...]
        qkv[chip_rows(chip, rows), :] = part.astype(BF)
    work.tick("qkv")
    kept = pltpu.make_async_copy(full, normed, kept_sem)
    kept.start()
    scale = head ** (-0.5)
    order = list(range(1, peers.chips)) + [0]
    before = None
    for k in order:
        chip = peers.behind_chip(k)
        here = chip_rows(chip, rows)
        block = jnp.where(col[...] <= row[:, here], 0.0, LOW).astype(F32)
        for lanes, heads in groups(span, head):
            q = qkv[here, lanes]
            keys = qkv[:, slice(span + lanes.start, span + lanes.stop)]
            values = qkv[:, slice(2 * span + lanes.start, 2 * span + lanes.stop)]
            merged = None
            for slot, start in heads:
                scores = dot(keys, only(q, start, head) * scale, 1, 1) + block
                top = jnp.max(scores, axis=0, keepdims=True)
                weights = jnp.exp(scores - top)
                total = jnp.sum(weights, axis=0, keepdims=True)
                logs[slot : slot + 1, here] = top + jnp.log(total)
                mixed = dot(values, weights.astype(BF), 0, 0) / total
                lane = lax.broadcasted_iota(jnp.int32, mixed.shape, 0)
                merged = mixed if merged is None else jnp.where(lane >= start, mixed, merged)
            attended[here, lanes] = merged.T.astype(BF)
        reduce.put(k, dot(attended[here, :], w_out[...]))
        if before is not None:
            reduce.push(before)
        work.tick("q%d" % order.index(k))
        before = k
    reduce.push(before)
    out = h[...].astype(F32) + (reduce.total() + vec[4:5, :])
    mid[...] = out
    normed_two[...] = (norm_parts(out)[0] * vec[1:2, :] + vec[3:4, :]).astype(BF)
    work.finish()
    gather.finish()
    reduce.finish()
    kept.wait()


ROOT = 0.7978845608028654


def feed_forward(side, *refs):
    (src, mid, fc_packed, w_proj, bias, vec) = refs[:6]
    ins, refs = refs[6 : 6 + len(side.operands)], refs[6 + len(side.operands) :]
    (normed_two, slope, activated, result, proj_out, fc_out), refs = refs[:6], refs[6:]
    side_outs, refs = refs[: len(side.outs)], refs[len(side.outs) :]
    gather_refs, reduce_refs, side_refs = refs[:5], refs[5 : 14 + 8], refs[14 + 8 :]
    rows, width = src.shape
    peers = Peers()
    gather = Gather(peers, gather_refs[0], gather_refs[1:])
    reduce = Reduce(peers, *reduce_refs[:5], reduce_refs[5:9])
    kept_sem, proj, proj_local, proj_send, proj_recv, proj_sem, w_fc, fc_sem = reduce_refs[9:17]
    full = gather.full
    work = side.make(peers, ins, side_outs, side_refs)
    zs, z = lax.axis_size("z"), lax.axis_index("z")
    half = proj.shape[1]
    peers.greet(2, work)
    gather.start(src)
    there = lax.rem(z + 2, zs)
    last = remote(w_proj.at[there], proj.at[there], proj_send, proj_recv, {"z": lax.rem(z + 1, zs)})
    last.start()
    here = [lax.rem(z + zs - i, zs) for i in range(zs - 1)]
    placed = [pltpu.make_async_copy(w_proj.at[b], proj.at[b], proj_local.at[i]) for i, b in enumerate(here)]
    for copy in placed:
        copy.start()
    rows_of, units = fc_packed.shape[1], w_fc.shape[1]
    for b in range(zs):
        for c in range(2):
            at = (b * 2 + c) * rows_of
            w_fc[at : at + rows_of, :] = fc_packed[b, :, c * units : (c + 1) * units]
    fc_kept = pltpu.make_async_copy(w_fc, fc_out, fc_sem)
    fc_kept.start()
    before = None
    for k, chip in gather.arrivals():
        if k == 0:
            last.wait_recv()
            work.start()
            for copy in placed:
                copy.wait()
            proj_kept = pltpu.make_async_copy(proj, proj_out, proj_sem)
            proj_kept.start()
        here = chip_rows(chip, rows)
        u = dot(full[chip].reshape(2 * rows, width), w_fc[...]) + bias[...]
        bend = jnp.tanh(ROOT * (u + 0.044715 * (u * u * u)))
        slope[here, :] = (0.5 * (1.0 + bend) + 0.5 * u * (1.0 - bend * bend) * (ROOT * (1.0 + 3 * 0.044715 * (u * u)))).astype(BF)
        act = (0.5 * u * (1.0 + bend)).astype(BF)
        activated[here, :] = act
        back = dot(act[:, :half], proj[0])
        for b in range(1, zs):
            back = back + dot(act[:, b * half : (b + 1) * half], proj[b])
        reduce.put(k, back)
        if before is not None:
            reduce.push(before)
        work.tick("k%d" % k)
        before = k
    kept = pltpu.make_async_copy(full, normed_two, kept_sem)
    kept.start()
    reduce.push(before)
    work.tick("sent")
    out = (mid[...] + (reduce.total() + vec[5:6, :])).astype(BF)
    result[...] = out
    last.wait_send()
    proj_kept.wait()
    fc_kept.wait()
    work.finish()
    gather.finish()
    reduce.finish()
    kept.wait()


def chunks(size, step):
    return [(a, min(a + step, size)) for a in range(0, size, step)]


def feed_backward(side, ready, *refs):
    (src, mid, w_fc, w_proj, slope, activated, normed_two, vec, *given) = refs[: 8 + ready]
    refs = refs[8 + ready :]
    ins, refs = refs[: len(side.operands)], refs[len(side.operands) :]
    (grad_mid, attn_rows, grad_proj, grad_fc, sums, unit_sums), refs = refs[:6], refs[6:]
    side_outs, refs = refs[: len(side.outs)], refs[len(side.outs) :]
    gather_refs, reduce_refs, side_refs = refs[:5], refs[5 : 14 + 1], refs[14 + 1 :]
    hidden, = reduce_refs[9:10]
    rows, width = src.shape
    tokens = slope.shape[0]
    peers = Peers()
    gather = Gather(peers, gather_refs[0], gather_refs[1:])
    reduce = Reduce(peers, *reduce_refs[:5], reduce_refs[5:9])
    full = given[0] if ready else gather.full
    work = side.make(peers, ins, side_outs, side_refs)
    peers.greet(side.zs, work)
    half = grad_proj.shape[1]

    def proj_terms():
        branch = full[...].reshape(tokens, width)
        for b in range(grad_proj.shape[0]):
            grad_proj[b] = dot(activated[:, b * half : (b + 1) * half], branch, 0, 0).astype(BF)
        work.made(grad_proj)

    if ready:
        order = [(k, peers.behind_chip(k)) for k in (*range(1, peers.chips), 0)]
    else:
        gather.start(src)
        order = gather.arrivals()
    work.start()
    if ready:
        proj_terms()
    before = None
    for k, chip in order:
        here = chip_rows(chip, rows)
        back = dot(full[chip].reshape(2 * rows, width), w_proj[...], 1, 1) * slope[here, :].astype(F32)
        back = back.astype(BF)
        hidden[here, :] = back
        reduce.put(k, dot(back, w_fc[...], 1, 1))
        if before is not None:
            reduce.push(before)
        work.tick("k%d" % k)
        before = k
    reduce.push(before)
    work.middle()
    if not ready:
        proj_terms()
    work.tick("proj")
    back = hidden[...]
    blocks, rows_of, units = grad_fc.shape[0], grad_fc.shape[1], back.shape[1]
    for b in range(blocks):
        at = b * 2 * rows_of
        part = dot(normed_two[:, at : at + 2 * rows_of], back, 0, 0).astype(BF)
        for c in range(2):
            grad_fc[b, :, c * units : (c + 1) * units] = part[c * rows_of : (c + 1) * rows_of]
    work.tick("fc")
    unit_sums[...] = jnp.sum(back.astype(F32), axis=0, keepdims=True)
    own = src[...].astype(F32)
    part, gain, shift = norm_back(mid[...], vec[1:2, :], reduce.total())
    out = own + part
    grad_mid[...] = out
    low = out.astype(BF)
    attn_rows[...] = low
    sums[0:1, :] = gain
    sums[1:2, :] = shift
    sums[2:3, :] = jnp.sum(own, axis=0, keepdims=True)
    sums[3:4, :] = jnp.sum(low.astype(F32), axis=0, keepdims=True)
    sums[4:8, :] = jnp.zeros((4, width), F32)
    work.finish()
    if not ready:
        gather.finish()
    reduce.finish()


def attention_backward(head, side, *refs):
    (src, grad_mid, h, w_qkv, w_out, qkv, attended, logs, normed, col, row, vec) = refs[:12]
    ins, refs = refs[12 : 12 + len(side.operands)], refs[12 + len(side.operands) :]
    (grad_in, *grad_parts, grad_out, sums, head_sums), refs = refs[:7], refs[7:]
    side_outs, refs = refs[: len(side.outs)], refs[len(side.outs) :]
    gather_refs, reduce_refs, side_refs = refs[:5], refs[5 : 14 + 3], refs[14 + 3 :]
    joint, key_sum, value_sum = reduce_refs[9:12]
    rows, width = src.shape
    tokens, span = attended.shape
    scale = head ** (-0.5)
    peers = Peers()
    gather = Gather(peers, gather_refs[0], gather_refs[1:])
    reduce = Reduce(peers, *reduce_refs[:5], reduce_refs[5:9])
    full = gather.full
    work = side.make(peers, ins, side_outs, side_refs)
    peers.greet(side.zs, work)
    gather.start(src)
    work.start()
    for k, chip in gather.arrivals():
        here = chip_rows(chip, rows)
        g_all = dot(full[chip].reshape(2 * rows, width), w_out[...], 1, 1).astype(BF)
        block = jnp.where(col[...] <= row[:, here], 0.0, LOW).astype(F32)
        for lanes, heads in groups(span, head):
            q = qkv[here, lanes]
            g = g_all[:, lanes]
            keys = qkv[:, slice(span + lanes.start, span + lanes.stop)]
            values = qkv[:, slice(2 * span + lanes.start, 2 * span + lanes.stop)]
            merged = None
            key_term, value_term = 0.0, 0.0
            for slot, start in heads:
                q_one, g_one = only(q, start, head) * scale, only(g, start, head)
                probs = jnp.exp(dot(keys, q_one, 1, 1) + block - logs[slot : slot + 1, here])
                g_probs = dot(values, g_one, 1, 1)
                both = probs * g_probs
                centre = jnp.sum(both, axis=0, keepdims=True)
                g_scores = (both - probs * centre).astype(BF)
                value_term += dot(probs.astype(BF), g_one)
                key_term += dot(g_scores, q_one)
                g_query = dot(keys, g_scores, 0, 0)
                lane = lax.broadcasted_iota(jnp.int32, g_query.shape, 0)
                merged = g_query if merged is None else jnp.where(lane >= start, g_query, merged)
            joint[here, lanes] = (merged.T * scale).astype(BF)
            if k == 0:
                key_sum[:, lanes] = key_term
                value_sum[:, lanes] = value_term
            else:
                key_sum[:, lanes] += key_term
                value_sum[:, lanes] += value_term
        work.tick("k%d" % k)
    joint[:, span : 2 * span] = key_sum[...].astype(BF)
    joint[:, 2 * span :] = value_sum[...].astype(BF)
    order = list(range(1, peers.chips)) + [0]
    before = None
    for k in order:
        reduce.put(k, dot(joint[chip_rows(peers.behind_chip(k), rows), :], w_qkv[...], 1, 1))
        if before is not None:
            reduce.push(before)
        before = k
    work.tick("sent")
    grads = joint[...]
    grad_out[...] = dot(attended[...], full[...].reshape(tokens, width), 0, 0).astype(BF)
    work.made(grad_out)
    for a, b in chunks(width, 512):
        part = dot(normed[:, a:b], grads, 0, 0).astype(BF)
        for i, grad in enumerate(grad_parts):
            grad[a:b, :] = part[:, i * span : (i + 1) * span]
    work.tick("grad")
    head_sums[...] = jnp.sum(grads.astype(F32), axis=0, keepdims=True)
    part, gain, shift = norm_back(h[...].astype(F32), vec[0:1, :], reduce.total())
    grad_in[...] = (grad_mid[...] + part).astype(BF)
    sums[0:1, :] = gain
    sums[1:2, :] = shift
    sums[2:8, :] = jnp.zeros((6, width), F32)
    work.finish()
    gather.finish()
    reduce.finish()


def call(kernel, name, outs, operands, side, kept, scratch, keep=()):
    chips = lax.axis_size("section") * lax.axis_size("r")
    rows, width = operands[0].shape
    vmem, hbm = pl.BlockSpec(memory_space=pltpu.VMEM), pl.BlockSpec(memory_space=pl.ANY)
    every = [*operands, *side.operands]
    fetched = [i for i in range(len(every)) if i not in keep and not (i >= len(operands) and side.in_hbm[i - len(operands)])]
    work = gather_scratch(chips, rows, width) + reduce_scratch(chips, rows, width) + scratch + list(side.scratch)

    def body(*refs):
        refs = list(refs)
        near, sems = refs[-1 - len(fetched) : -1], refs[-1]
        for k, i in enumerate(fetched):
            refs[i] = Fetch(refs[i], near[k], sems.at[k])
        kernel(*refs[: -1 - len(fetched)])
        for i in fetched:
            refs[i].finish()

    out = pl.pallas_call(
        body,
        out_shape=[jax.ShapeDtypeStruct(*o) for o in (*outs, *side.outs)],
        in_specs=[hbm] * len(every),
        out_specs=[hbm if i in kept else vmem for i in range(len(outs))] + [hbm if i else vmem for i in side.out_hbm],
        scratch_shapes=work
        + [pltpu.VMEM(every[i].shape, every[i].dtype) for i in fetched]
        + [pltpu.SemaphoreType.DMA((len(fetched),))],
        compiler_params=pltpu.CompilerParams(collective_id=name, has_side_effects=True, vmem_limit_bytes=60 * 2**20),
    )(*every)
    return out[: len(outs)], out[len(outs) :]


def run_attention_forward(name, head, side, *operands):
    h, w_qkv, w_out, bias, col, row, vec = operands
    rows, width = h.shape
    tokens, span = col.shape[0], w_out.shape[0]
    slots = -(-(span // head) // 8) * 8
    chips = tokens // (2 * rows)
    outs = [
        ((chips, 2, rows, width), BF),
        ((tokens, 3 * span), BF),
        ((tokens, span), BF),
        ((slots, tokens), F32),
        ((rows, width), F32),
        ((rows, width), BF),
    ]
    return call(functools.partial(attention_forward, head, side), name, outs, operands, side, (0,), [pltpu.SemaphoreType.DMA])


def run_feed_forward(name, side, *operands):
    src, mid, w_fc, w_proj, bias, vec = operands
    rows, width = src.shape
    units = w_fc.shape[2] // 2
    chips = lax.axis_size("section") * lax.axis_size("r")
    tokens = 2 * chips * rows
    outs = [
        ((chips, 2, rows, width), BF),
        ((tokens, units), BF),
        ((tokens, units), BF),
        ((rows, width), BF),
        (w_proj.shape, BF),
        ((width, units), BF),
    ]
    dma = pltpu.SemaphoreType.DMA
    scratch = [dma, pltpu.VMEM(w_proj.shape, BF), dma((w_proj.shape[0],)), dma, dma, dma, pltpu.VMEM((width, units), BF), dma]
    return call(functools.partial(feed_forward, side), name, outs, operands, side, (0, 4, 5), scratch, (3,))


def run_feed_backward(name, side, *operands):
    src, mid, w_fc, w_proj, slope, activated, normed_two, vec, *given = operands
    rows, width = src.shape
    tokens, units = slope.shape
    zs = lax.axis_size("z")
    outs = [
        ((rows, width), F32),
        ((rows, width), BF),
        ((zs, units // zs, width), BF),
        ((zs, width // (2 * zs), 2 * units), BF),
        ((8, width), F32),
        ((1, units), F32),
    ]
    return call(functools.partial(feed_backward, side, len(given)), name, outs, operands, side, (), [pltpu.VMEM((tokens, units), BF)])


def run_attention_backward(name, head, side, *operands):
    src, grad_mid, h, w_qkv, w_out, qkv, attended, logs, normed, col, row, vec = operands
    rows, width = src.shape
    tokens, span = attended.shape
    outs = [
        ((rows, width), BF),
        ((width, span), BF),
        ((width, span), BF),
        ((width, span), BF),
        ((span, width), BF),
        ((8, width), F32),
        ((1, 3 * span), F32),
    ]
    scratch = [pltpu.VMEM((tokens, 3 * span), BF), pltpu.VMEM((tokens, span), F32), pltpu.VMEM((tokens, span), F32)]
    return call(functools.partial(attention_backward, head, side), name, outs, operands, side, (), scratch)


def start_kernel(sizes, *refs):
    block, span, half, seqs, micros = sizes
    (tiny, w_qkv, w_attn, w_fc, w_proj, inputs, cotangent), refs = refs[:7], refs[7:]
    (qkv, wo, fc, (proj, qkv_full, w_out, h, g, row, col, *smalls)), refs = (refs[0:2], refs[2:4], refs[4:6], refs[6:19]), refs[19:]
    tiny_out, stage, h_raw, g_raw, natural, proj_cut = refs[:6]
    cuts, lands, (wo_full, nat, land), refs = refs[6:9], refs[9:12], refs[12:15], refs[15:]
    z_send, z_recv, *sems = refs[:6]
    all_send, all_recv, far_send, far_recv, turn_send, turn_recv = refs[6:12]
    ring_local, ring_send, ring_recv, *route_sems = refs[12:]
    peers = Peers()
    zs, z = lax.axis_size("z"), lax.axis_index("z")
    x, rest, slab = peers.x, peers.rest, 2 * peers.chips
    sections = peers.sections
    spot = peers.c * rest + peers.r
    width, wide = w_attn.shape[1], rest * block
    _, me = peers.other(0, 0, 0)
    route = RouteIn(seqs, [(inputs, h_raw), (cotangent, g_raw)], *route_sems)
    peers.greet(zs, route)
    sent = []

    def send(copy):
        copy.start()
        sent.append(copy)

    for k in range(1, zs):
        send(remote(tiny, stage.at[z], z_send.at[k], z_recv.at[k], {"z": lax.rem(z + k, zs)}))
    stage[z] = tiny[...]
    route.start(0)
    route.start(1)

    def share(a):
        for i, place in peers.offsets():
            device, t = peers.other(*place)
            send(remote(cuts[a].at[t], lands[a].at[x, spot], all_send.at[a, i], all_recv.at[a, i], device))
        lands[a][x, spot] = cuts[a][me]

    def settle(a, shard):
        for i, place in peers.offsets():
            device, _ = peers.other(*(-d for d in place))
            came = lands[a].at[device["section"], device["dp"] * rest + device["r"]]
            remote(came, came, all_send.at[a, i], all_recv.at[a, i], device).wait_recv()
        for layer in range(sections):
            for i in range(2 * rest):
                if a == 0:
                    for first, group, row, some in groups_of(2 * rest * block, i * block, block):
                        to = shard[layer].at[row : row + some, group * cols : (group + 1) * cols]
                        to[...] = lands[a][layer, i, first : first + some, :]
                    continue
                rows_at, lanes_at = i * block, 0
                if a == 2:
                    rows_at, lanes_at = i % rest * block, i // rest * lands[a].shape[3]
                to = shard[layer].at[rows_at : rows_at + block, lanes_at : lanes_at + lands[a].shape[3]]
                to[...] = lands[a][layer, i, :block, :]

    cols = width // slab
    for t in range(slab):
        big, off = divmod(t * cols, wide)
        at = (big % 2 * zs + big // 2) * wide + off
        cuts[0][t, :block, :] = w_attn[:, at : at + cols]
    share(0)
    for t in range(slab):
        count = max(0, min(span, width - t * span))
        for p in range(3):
            if count:
                at = p * width + t * span
                cuts[1][t, :block, p * span : p * span + count] = w_qkv[:, at : at + count]
            if count < span:
                cuts[1][t, :block, p * span + count : (p + 1) * span] = jnp.zeros((block, span - count), BF)
    share(1)
    for t in range(slab):
        a, c, r = t // (2 * rest), t // rest % 2, t % rest
        for k in range(zs):
            at = ((c * zs + k) * rest + r) * (sections * half) + a * half
            cuts[2][t, :block, k * half : (k + 1) * half] = w_fc[:, at : at + half]
    for a in range(sections):
        for c in range(2):
            for k in range(zs):
                at, to = (c * zs + k) * wide, (k * 2 + c) * wide
                proj_cut[a, :, to : to + wide] = w_proj[a * half : (a + 1) * half, at : at + wide]
    for k in range(1, zs):
        came = stage.at[lax.rem(z + zs - k, zs)]
        remote(came, came, z_send.at[k], z_recv.at[k], {"z": lax.rem(z + k, zs)}).wait_recv()
    gather = Gather(peers, tiny_out, sems)
    gather.start(stage)
    settle(0, wo)
    turn = Turn(peers, wo_full, nat, land, w_out, turn_send, turn_recv)
    ring = RingGather([(wo[0], wo_full, zs - 1), (qkv[0], qkv_full, zs - 1)], ring_local, ring_send, ring_recv)
    work = Both(ring, turn, True)
    ring.launch(0)
    settle(1, qkv)
    ring.launch(1)
    share(2)
    for d in range(1, sections):
        device, _ = peers.other(d, 0, 0)
        there = lax.rem(x + d, sections)
        send(remote(proj_cut.at[there], proj.at[x], far_send.at[d], far_recv.at[d], device))
    proj[x] = proj_cut[x]
    work.tick()
    for _ in gather.arrivals():
        pass
    work.tick()

    per_row, halves = sections * half // block, half // block
    for layer in range(sections):
        vec, bias, unit = smalls[3 * layer : 3 * layer + 3]
        natural[...] = jnp.zeros_like(natural)
        for c in range(2):
            for k in range(zs):
                for r in range(rest):
                    at = ((k * 2 + c) * rest + r) * block
                    vec[:, at : at + block] = tiny_out[layer * rest + r, c, k, 0:8, :block]
                    at = ((c * zs + k) * rest + r) * block
                    natural[:, at : at + block] = tiny_out[layer * rest + r, c, k, 0:8, :block]
        own = jnp.zeros((8, span), F32)
        for t in range(slab):
            own = jnp.where(me == t, natural[:, t * span : (t + 1) * span], own)
        bias[:, :span] = own[6:7]
        bias[:, span : 2 * span] = jnp.zeros((1, span), F32)
        bias[:, 2 * span :] = own[7:8]
        for k in range(zs):
            for j in range(halves):
                line = tiny_out[layer * rest + peers.r, peers.c, k, pl.ds(8 + x * halves + j, 1), :block]
                unit[:, k * half + j * block : k * half + (j + 1) * block] = line
    rows = h.shape[0]
    for a in range(sections):
        for r in range(rest):
            for c in range(2):
                at = ((a * rest + r) * 2 + c) * rows
                line = tiny_out[r, 0, c * 2 + a, pl.ds(8 + per_row + z // seqs, 1), :rows]
                row[:, at : at + rows] = line.astype(jnp.int32)
                col[at : at + rows, :] = jnp.broadcast_to(line, (8, rows)).T[:, :1].astype(jnp.int32)
    work.tick(2)
    settle(2, fc)
    work.tick()
    for i, (raw, ordered) in enumerate([(h_raw, h), (g_raw, g)]):
        route.arrived(i)
        reorder(raw, ordered, zs, wide)
    for d in range(1, sections):
        device, _ = peers.other(-d, 0, 0)
        came = proj.at[device["section"]]
        remote(came, came, far_send.at[d], far_recv.at[d], device).wait_recv()
    work.finish()
    route.finish()
    gather.finish()
    for copy in sent:
        copy.wait_send()


def run_start(name, lay, tiny, w_qkv, w_attn, w_fc, w_proj, inputs, cotangent):
    zs, n, chips, sections = lay.zs, lay.slab, lay.slab // 2, lay.sections
    span, block = lay.slots * lay.head, lay.block
    spots = lay.cores * lay.rest
    rows, tall = spots * block, -(-block // 16) * 16
    vmem, hbm = pl.BlockSpec(memory_space=pltpu.VMEM), pl.BlockSpec(memory_space=pl.ANY)
    units = lay.units // n
    widths = [lay.cols, 3 * span, units]
    flat = (lay.rows, lay.width)
    outs = [(a, BF) for a in ((rows, 3 * span), (rows // GROUPS, GROUPS * lay.cols), (rows // 2, 2 * units)) for _ in range(sections)]
    outs += [((sections, lay.half, lay.width), BF), ((zs, rows, 3 * span), BF), ((span, lay.width), BF)]
    outs += [(flat, BF), (flat, BF), ((1, lay.tokens), jnp.int32), ((lay.tokens, 1), jnp.int32)]
    outs += [((8, lay.width), F32), ((1, 3 * span), F32), ((1, units), F32)] * sections
    dma = pltpu.SemaphoreType.DMA
    return pl.pallas_call(
        functools.partial(start_kernel, (block, span, lay.half, lay.seqs, lay.micros)),
        out_shape=[jax.ShapeDtypeStruct(*o) for o in outs],
        in_specs=[vmem] * 7,
        out_specs=[vmem] * (1 + 3 * sections) + [hbm] + [vmem] * (5 + 3 * sections),
        scratch_shapes=[
            pltpu.VMEM((chips, 2, zs, *tiny.shape), F32),
            pltpu.VMEM((zs, *tiny.shape), F32),
            pltpu.VMEM(flat[::-1], BF),
            pltpu.VMEM(flat[::-1], BF),
            pltpu.VMEM((8, n * span), F32),
            pltpu.VMEM((sections, lay.half, lay.width), BF),
        ]
        + [pltpu.VMEM((n, tall, m), BF) for m in widths]
        + [pltpu.VMEM((sections, spots, tall, m), BF) for m in widths]
        + [pltpu.VMEM((zs, rows // GROUPS, GROUPS * lay.cols), BF), pltpu.VMEM((n * span, lay.cols), BF), pltpu.VMEM((n, span, lay.cols), BF)]
        + [dma((zs,))] * 2
        + [dma((chips,))] * 4
        + [dma((3, n))] * 2
        + [dma((sections,))] * 2
        + [dma((n,))] * 2
        + [dma((2,))]
        + [dma((2, zs - 1))] * 2
        + [dma((2,)), dma((2, lay.micros)), dma((2,))],
        compiler_params=pltpu.CompilerParams(collective_id=name, has_side_effects=True, vmem_limit_bytes=60 * 2**20),
    )(tiny, w_qkv, w_attn, w_fc, w_proj, inputs, cotangent)


def end_kernel(sizes, *refs):
    block, width, units, seqs = sizes
    parts, (q_one, k_one, v_one, wo_one), (fc_zero, fc_one, proj_zero, proj_one), refs = refs[:4], refs[4:8], refs[8:12], refs[12:]
    sums, (last_rows, *ready), refs = refs[:8], refs[8:15], refs[15:]
    (out_qkv, out_wo, out_fc, out_proj, out_small, section_out, section_grad, home, out_rows), refs = refs[:9], refs[9:]
    totals, (proj_both, proj_land), refs = refs[:4], refs[4:6], refs[6:]
    stages, lands, refs = refs[:5], refs[5:10], refs[10:]
    (small_land, small_sum, z_land), came, (small, natural, rows_buf), refs = refs[:3], refs[3:7], refs[7:10], refs[10:]
    all_send, all_recv, far_send, far_recv, z_send, z_recv, ring_send, ring_recv, late_send, late_recv, *route_sems, rows_sem = refs
    peers = Peers()
    zs, z = lax.axis_size("z"), lax.axis_index("z")
    x, rest, slab = peers.x, peers.rest, 2 * peers.chips
    spot = peers.c * rest + peers.r
    span, cols = q_one.shape[1], wo_one.shape[1] // GROUPS
    half, wide = proj_zero.shape[0], rest * block
    _, me = peers.other(0, 0, 0)
    offsets = peers.offsets()
    route = Route(seqs, last_rows, home, *route_sems[:3])
    across = Across(0, home, out_rows, *route_sems[3:5])
    peers.greet(zs, Several([route, across]))
    sent = []

    def send(copy):
        copy.start()
        sent.append(copy)

    pieces = [(parts[p], None, came[p], totals[p], 0, zs - 1) for p in range(4)]
    ring = RingSum(pieces[:2], ring_send, ring_recv)
    ring.start()
    route.start()

    def restore(first_crossed, second, first_home, out):
        whole = lax.rem(z, 2) == x
        for layer, choice in enumerate([(first_home, first_crossed), second]):
            for kind, src in enumerate(choice):

                @pl.when((x == layer) & (whole if kind == 0 else jnp.logical_not(whole)))
                def _(src=src):
                    pltpu.make_async_copy(src, rows_buf, rows_sem).start()

        pltpu.make_async_copy(first_home, rows_buf, rows_sem).wait()
        for micro in range(out.shape[0]):
            for c in range(2):
                for k in range(zs):
                    at, of = (c * zs + k) * wide, (k * 2 + c) * wide
                    out[micro, at : at + wide, :] = rows_buf[micro, :, of : of + wide].astype(F32).T.astype(BF)

    def cut(a, totals):
        for layer, total in enumerate(totals):
            for i in range(2 * rest):
                if a == 4:
                    for first, group, row, some in groups_of(2 * rest * block, i * block, block):
                        lanes = slice(group * cols, (group + 1) * cols)
                        stages[a][layer, i, first : first + some, :] = total[row : row + some, lanes]
                    continue
                wide_at, rows_at = 0, i * block
                if a == 0:
                    wide_at, rows_at = i // rest * stages[a].shape[3], i % rest * block
                stages[a][layer, i, :block, :] = total[rows_at : rows_at + block, wide_at : wide_at + stages[a].shape[3]]
        for i, place in offsets:
            device, t = peers.other(*place)
            src = stages[a].at[device["section"], device["dp"] * rest + device["r"]]
            line = a + a // 3
            send(remote(src, lands[a].at[me], all_send.at[line, i], all_recv.at[line, i], device))
        lands[a][me] = stages[a][x, spot]

    def settle(a, land):
        for i, place in offsets:
            device, t = peers.other(*(-d for d in place))
            came = land.at[t]
            remote(came, came, all_send.at[a, i], all_recv.at[a, i], device).wait_recv()

    cut(0, (fc_zero, fc_one))
    proj_both[0] = proj_zero[...]
    proj_both[1] = proj_one[...]
    device, _ = peers.other(1, 0, 0)
    send(remote(proj_both.at[1 - x], proj_land.at[x], far_send, far_recv, device))
    proj_land[x] = proj_both[x]
    ring.tick(2)
    small[...] = jnp.zeros_like(small)
    halves = half // block
    for layer in range(2):
        feed, attn, heads, unit = sums[4 * layer : 4 * layer + 4]
        for t in range(slab):
            natural[0:1, t * span : (t + 1) * span] = jnp.where(me == t, heads[:, :span], 0.0)
            natural[1:2, t * span : (t + 1) * span] = jnp.where(me == t, heads[:, 2 * span :], 0.0)
        for c in range(2):
            for k in range(zs):
                for r in range(rest):
                    to = small.at[(layer * 2 + c) * rest + r, k]
                    at = slice(((k * 2 + c) * rest + r) * block, ((k * 2 + c) * rest + r + 1) * block)
                    to[0:1, :block] = attn[0:1, at]
                    to[1:2, :block] = feed[0:1, at]
                    to[2:3, :block] = attn[1:2, at]
                    to[5:6, :block] = feed[3:4, at]
                    to[6:8, :block] = feed[1:3, at]
                    at = ((c * zs + k) * rest + r) * block
                    to[3:5, :block] = natural[0:2, at : at + block]
                    own = (peers.c == c) & (peers.r == r)
                    for h in range(2):
                        for j in range(halves):
                            line = unit[0:1, k * half + j * block : k * half + (j + 1) * block]
                            spot_row = 8 + h * halves + j
                            to[spot_row : spot_row + 1, :block] = jnp.where(own & (x == h), line, 0.0)
    for i, place in offsets:
        device, t = peers.other(*place)
        send(remote(small.at[t], small_land.at[me], all_send.at[3, i], all_recv.at[3, i], device))
    small_land[me] = small[me]

    ring.tick(2)
    late_ring = RingSum(pieces[2:], late_send, late_recv)
    late_ring.start()
    settle(0, lands[0])
    for t in range(slab):
        h, c, r = t // (2 * rest), t // rest % 2, t % rest
        for k in range(zs):
            at = ((c * zs + k) * rest + r) * (units // (2 * zs * rest)) + h * half
            out_fc[:, 0, at : at + half] = lands[0][t, :block, k * half : (k + 1) * half].astype(F32)
    settle(3, small_land)
    total = small_land[0]
    for t in range(1, slab):
        total = total + small_land[t]
    small_sum[...] = total
    for k in range(1, zs):
        there = lax.rem(z + k, zs)
        send(remote(small_sum.at[there], z_land.at[z], z_send.at[k], z_recv.at[k], {"z": there}))
    z_land[z] = small_sum[z]
    ring.finish()
    cut(1, (totals[0], q_one))
    cut(2, (totals[1], k_one))
    late_ring.tick(2)
    route.arrived()
    across.tick("middle")
    restore(ready[1], ready[2:4], ready[0], section_out)
    came_proj = proj_land.at[1 - x]
    remote(came_proj, came_proj, far_send, far_recv, device).wait_recv()
    for h in range(2):
        for c in range(2):
            for k in range(zs):
                at, of = (c * zs + k) * wide, (k * 2 + c) * wide
                out_proj[h * half : (h + 1) * half, at : at + wide] = proj_land[h, :, of : of + wide]
    late_ring.tick(2)
    for k in range(1, zs):
        block_in = z_land.at[lax.rem(z + zs - k, zs)]
        remote(block_in, block_in, z_send.at[k], z_recv.at[k], {"z": lax.rem(z + k, zs)}).wait_recv()
    total = z_land[0]
    for k in range(1, zs):
        total = total + z_land[k]
    out_small[...] = total

    def place(p):
        for t in range(slab):
            count = min(span, width - t * span)
            if count > 0:
                at = p * width + t * span
                out_qkv[:, 0, at : at + count] = lands[1 + p][t, :block, :count].astype(F32)

    for p in range(2):
        settle(1 + p, lands[1 + p])
        place(p)
    late_ring.finish()
    cut(3, (totals[2], v_one))
    cut(4, (totals[3], wo_one))
    route.sent()
    across.finish()
    restore(out_rows, ready[4:], home, section_grad)
    settle(4, lands[3])
    place(2)
    settle(5, lands[4])
    for t in range(slab):
        big, off = divmod(t * cols, wide)
        at = (big % 2 * zs + big // 2) * wide + off
        out_wo[:, 0, at : at + cols] = lands[4][t, :block, :].astype(F32)
    for copy in sent:
        copy.wait_send()


def run_end(name, lay, parts, ones, fcs, projs, sums, last_rows, ready):
    zs, n = lay.zs, lay.slab
    span, width, block = lay.slots * lay.head, lay.width, lay.block
    spots = lay.cores * lay.rest
    tall = -(-block // 16) * 16
    vmem = pl.BlockSpec(memory_space=pltpu.VMEM)
    dma = pltpu.SemaphoreType.DMA
    widths = [fcs[0].shape[1] // 2, span, span, span, lay.cols]
    half = projs[0].shape[0]
    tile = (-(-(8 + lay.unit_block // block) // 8) * 8, 128)
    outs = [(block, 1, 3 * width), (block, 1, width), (block, 1, lay.units), (lay.unit_block, width), tile]
    return pl.pallas_call(
        functools.partial(end_kernel, (block, width, lay.units, lay.seqs)),
        out_shape=[jax.ShapeDtypeStruct(o, BF if i == 3 else F32) for i, o in enumerate(outs)]
        + [jax.ShapeDtypeStruct((lay.micros, lay.width, lay.rows), BF)] * 2
        + [jax.ShapeDtypeStruct((lay.micros, *last_rows.shape), BF)] * 2,
        in_specs=[vmem] * 20 + [pl.BlockSpec(memory_space=pl.ANY)] * 7,
        out_specs=[vmem] * 7 + [pl.BlockSpec(memory_space=pl.ANY)] * 2,
        scratch_shapes=[
            *[pltpu.VMEM(a.shape[1:], BF) for a in parts],
            pltpu.VMEM((2, half, width), BF),
            pltpu.VMEM((2, half, width), BF),
        ]
        + [pltpu.VMEM((lay.sections, spots, tall, m), BF) for m in widths]
        + [pltpu.VMEM((n, tall, m), BF) for m in widths]
        + [
            pltpu.VMEM((n, zs, *tile), F32),
            pltpu.VMEM((zs, *tile), F32),
            pltpu.VMEM((zs, *tile), F32),
            *[pltpu.VMEM((zs - 1, *a.shape[1:]), BF) for a in parts],
            pltpu.VMEM((n, zs, *tile), F32),
            pltpu.VMEM((8, n * span), F32),
            pltpu.VMEM((lay.micros, *last_rows.shape), BF),
        ]
        + [dma((6, n))] * 2
        + [dma] * 2
        + [dma((zs,))] * 2
        + [dma((2, zs - 1))] * 4
        + [dma, dma, dma((lay.micros,)), dma, dma, dma],
        compiler_params=pltpu.CompilerParams(collective_id=name, has_side_effects=True, vmem_limit_bytes=60 * 2**20),
    )(*parts, *ones, *fcs, *projs, *sums, last_rows, *ready)


class Rings:
    def __init__(self, lay):
        self.zs = lay.zs
        self.state = {}

    def put(self, kind, layer, part):
        if part.ndim == 2:
            part = part.reshape(self.zs, part.shape[0] // self.zs, part.shape[1])
        _, acc, steps = self.state.get((kind, layer), (None, None, 0))
        self.state[kind, layer] = (part, acc, steps)

    def side(self, plan, pace, makes={}):
        pieces = []
        for kind, layer, count in plan:
            part, acc, steps = self.state.get((kind, layer), (None, None, 0))
            shape = makes[kind] if part is None else part.shape[1:]
            pieces.append((part, shape, acc, steps, count))
        return sum_side(pieces, pace)

    def done(self, plan, outs):
        for (kind, layer, count), acc in zip(plan, outs):
            part, _, steps = self.state[kind, layer]
            self.state[kind, layer] = (part, acc, steps + count)


def on_device(
    inputs, cotangent, positions, w_qkv, w_attn_out, w_fc, w_proj, norm_gains, biases, fc_bias
):
    lay = Layout(inputs, w_fc)
    n, block, width = lay.slab, lay.block, lay.width
    span = lay.slots * lay.head

    small = jnp.concatenate([norm_gains[0], biases[0]], axis=1).astype(F32).T
    small = jnp.stack([small[i] for i in (0, 1, 2, 6, 5, 7, 3, 4)])
    small = jnp.concatenate([small, fc_bias[0].reshape(-1, block).astype(F32)])
    small = jnp.pad(small, ((0, 0), (0, 128 - block)))
    places = jnp.pad(positions.astype(F32), ((0, 0), (0, 128 - lay.rows)))
    small = jnp.concatenate([small, places])
    small = jnp.pad(small, ((0, -small.shape[0] % 8), (0, 0)))
    *cut, proj_cut, w_qkv, w_out, h, g, row, col, vec_0, bias_0, unit_0, vec_1, bias_1, unit_1 = run_start(
        0, lay, small, w_qkv[0], w_attn_out[0], w_fc[0], w_proj[0], jnp.swapaxes(inputs, 2, 3), jnp.swapaxes(cotangent, 2, 3)
    )
    qkv_cut, wo_cut, fc_cut = cut[0:2], cut[2:4], cut[4:6]
    smalls = [(vec_0, bias_0, unit_0), (vec_1, bias_1, unit_1)]
    outs, keeps, params = [], [], []
    for layer in range(lay.sections):
        last = layer == lay.sections - 1
        vec, bias, unit = smalls[layer]
        w_qkv = w_qkv.reshape(width, 3 * span)
        side = gather_side([fc_cut[layer], (proj_cut, layer)], {"qkv": 1, "q0": 1, "q3": 1}, (lay.zs - 1, lay.zs - 2))
        if last:
            side = both_sides(side, share_side(lay, g, ("qkv", "q3")))
        (full, qkv, attended, logs, mid, normed_two), (w_fc, w_proj, *shared) = run_attention_forward(
            1 + 2 * layer,
            lay.head,
            side,
            h,
            w_qkv,
            w_out,
            bias,
            col,
            row,
            vec,
        )
        if last:
            side = route_side(lay, outs[0], "start")
        else:
            side = gather_side([wo_cut[layer + 1], qkv_cut[layer + 1]], {"k3": 2, "sent": 1}, turn=span)
        (full_two, slope, activated, result, w_proj, w_fc), later = run_feed_forward(
            2 + 2 * layer, side, normed_two, mid, w_fc, w_proj, unit, vec
        )
        params.append((w_qkv, w_out, w_fc, w_proj.reshape(-1, width)))
        if last:
            (home,), (branch,) = later, shared
        else:
            w_out, w_qkv = later
        keeps.append((h, full, qkv, attended, logs, mid, full_two, slope, activated))
        h = result
        outs.append(h)

    rings = Rings(lay)
    plans = {
        ("feed", 1): [("proj", 1, 3)],
        ("attention", 1): [("fc", 1, 3)],
        ("feed", 0): [("q", 1, 3), ("k", 1, 3), ("v", 1, 3), ("proj", 0, 1)],
        ("attention", 0): [("fc", 0, 3), ("proj", 0, 2), ("out", 1, 3)],
    }
    paces = {
        ("feed", 1): {"proj": 1, "fc": 1},
        ("attention", 1): {"k2": 1, "grad": 1},
        ("feed", 0): {"k3": 3},
        ("attention", 0): {"k3": 3},
    }
    crossed = {}
    sums = [None] * lay.sections
    for layer in reversed(range(lay.sections)):
        w_qkv, w_out, w_fc, w_proj = params[layer]
        vec = smalls[layer][0]
        h, full, qkv, attended, logs, mid, full_two, slope, activated = keeps[layer]
        full, full_two = (a.reshape(lay.tokens, width) for a in (full, full_two))
        name = 1 + 4 * lay.sections - 2 * layer
        side = rings.side(plans["feed", layer], paces["feed", layer], {"proj": (lay.half, width)})
        late = layer == lay.sections - 1
        turn = SideWork() if late else turn_side(lay, grad_out)
        side = both_sides(side, turn, across_side(0 if late else 1, home), route_side(lay, outs[1] if late else g, "start"))
        (grad_mid, attn_rows, grad_proj, grad_fc, feed_sums, unit_sums), done = run_feed_backward(
            name, side, g, mid, w_fc, w_proj, slope, activated, full_two, vec, *([branch] if late else [])
        )
        rings.put("proj", layer, grad_proj)
        rings.put("fc", layer, grad_fc)
        rings.done(plans["feed", layer], done)
        if late:
            crossed["out", 0] = (home, done[-2])
        else:
            crossed["out", 1] = (home, done[-2])
            rings.put("out", 1, done[-3])
        home = done[-1]
        side = rings.side(plans["attention", layer], paces["attention", layer])
        if not late:
            side = both_sides(side, turn_side(lay), across_side(1, home))
        (g, *grad_parts, grad_out, attn_sums, head_sums), done = run_attention_backward(
            name + 1, lay.head, side, attn_rows, grad_mid, h, w_qkv, w_out, qkv, attended, logs, full, col, row, vec
        )
        rings.done(plans["attention", layer], done)
        if not late:
            rings.put("out", layer, done[-2])
            crossed["grad", 1] = (home, done[-1])
        for kind, part in zip("qkv", grad_parts):
            rings.put(kind, layer, part)
        sums[layer] = (feed_sums, attn_sums, head_sums, unit_sums)
    out_qkv, out_attn, out_fc, out_proj, rows, section_out, section_grad, *_ = run_end(
        3 + 4 * lay.sections,
        lay,
        [rings.state[kind, 0][0] for kind in ("q", "k", "v", "out")],
        [rings.state[kind, 1][1] for kind in ("q", "k", "v", "out")],
        [rings.state["fc", layer][1] for layer in range(2)],
        [rings.state["proj", layer][1] for layer in range(2)],
        [a for layer in range(2) for a in sums[layer]],
        g,
        [*crossed["out", 0], *crossed["out", 1], *crossed["grad", 1]],
    )
    cols = rows[:8, :block].T
    return (
        jnp.swapaxes(section_out, 1, 2)[None, :, None],
        jnp.swapaxes(section_grad, 1, 2)[None, :, None],
        jnp.swapaxes(out_qkv, 0, 1),
        jnp.swapaxes(out_attn, 0, 1),
        jnp.swapaxes(out_fc, 0, 1),
        out_proj.astype(F32)[None],
        cols[None, :, :2],
        cols[None, :, 2:],
        rows[8 : 8 + lay.unit_block // block, :block].reshape(1, lay.unit_block),
    )


def solution(mesh):
    sections, cores, contexts = (mesh.shape[a] for a in ("section", "dp", "ctx"))
    zs = sections * cores
    shape = (sections, cores, zs, contexts // zs)
    inner = Mesh(mesh.devices.reshape(shape), ALL)
    tokens = P(None, "dp", ("z", "r"), None)
    rows = P("section", ("dp", "z", "r"), None)
    units = P("section", ("dp", "z", "r"))
    out_tokens = P("section", None, "dp", ("z", "r"), None)
    return jax.shard_map(
        on_device,
        mesh=inner,
        in_specs=(tokens, tokens, P(None, ("z", "r"))) + (rows,) * 6 + (units,),
        out_specs=(out_tokens, out_tokens) + (rows,) * 6 + (units,),
        check_vma=False,
    )
```

```python
import functools

import jax
import jax.numpy as jnp
from jax import lax
from jax.experimental import pallas as pl
from jax.experimental.pallas import tpu as pltpu
from jax.sharding import Mesh
from jax.sharding import PartitionSpec as P

HEADS = 25
EPSILON = 1e-05

SLAB = ("section", "dp", "r")
ALL = ("section", "dp", "z", "r")
MESH = pl.DeviceIdType.MESH


class Layout:
    def __init__(self, inputs, w_fc):
        self.micros, _, self.rows, self.width = inputs.shape
        self.sections = lax.axis_size("section")
        self.cores = lax.axis_size("dp")
        self.zs = lax.axis_size("z")
        self.rest = lax.axis_size("r")
        self.slab = self.sections * self.cores * self.rest
        self.shards = self.cores * self.zs * self.rest
        self.units = w_fc.shape[2]
        self.tokens = self.rows * self.slab
        self.seqs = self.cores
        self.head = self.width // HEADS
        self.slots = -(-HEADS // self.slab)
        self.block = self.width // self.shards
        self.unit_block = self.units // self.shards
        self.half = self.unit_block // self.sections
        self.cols = self.width // self.slab
        self.x = lax.axis_index("section")
        self.c = lax.axis_index("dp")
        self.z = lax.axis_index("z")
        self.r = lax.axis_index("r")
        self.t = (self.x * self.cores + self.c) * self.rest + self.r

    def number(self, x, c, z, r):
        return ((x * self.cores + c) * self.zs + z) * self.rest + r

    def order(self, a):
        lead = a.shape[:-1]
        a = a.reshape(*lead, self.cores, self.zs, self.rest * self.block)
        return jnp.swapaxes(a, -3, -2).reshape(*lead, self.width)

    def restore(self, a):
        lead = a.shape[:-1]
        a = a.reshape(*lead, self.zs, self.cores, self.rest * self.block)
        return jnp.swapaxes(a, -3, -2).reshape(*lead, self.width)

    def routes(self, micro):
        pairs = []
        for x in range(self.sections):
            for c in range(self.cores):
                for s in range(self.seqs):
                    for r in range(self.rest):
                        place = x * self.cores + c
                        pairs.append(((x, s, place, r), (x, c, micro * self.seqs + s, r)))
        return pairs

    def tokens_in(self, a):
        got = []
        for micro in range(self.micros):
            route = [(self.number(*f), self.number(*g)) for f, g in self.routes(micro)]
            got.append(lax.ppermute(a[micro, 0], ALL, route))
        out = got[0]
        for micro in range(1, self.micros):
            out = jnp.where(self.z // self.seqs == micro, got[micro], out)
        return out

    def tokens_out(self, parts):
        result = []
        for micro in range(self.micros):
            got = []
            for layer, part in enumerate(parts):
                route = [
                    (self.number(*g), self.number(layer, *f[1:])) for f, g in self.routes(micro)
                ]
                got.append(lax.ppermute(part, ALL, route))
            out = got[0]
            for layer in range(1, len(parts)):
                out = jnp.where(self.x == layer, got[layer], out)
            result.append(out)
        return jnp.stack(result)[None, :, None]


LOW = -1e30
BF = jnp.bfloat16
F32 = jnp.float32


class Peers:
    def __init__(self):
        self.sections, self.rest = lax.axis_size("section"), lax.axis_size("r")
        self.chips = self.sections * self.rest
        self.x, self.c, self.r = (lax.axis_index(a) for a in ("section", "dp", "r"))
        self.chip = self.x * self.rest + self.r

    def away(self, k, sign):
        x = lax.rem(self.x + self.sections + sign * (k // self.rest), self.sections)
        r = lax.rem(self.r + self.rest + sign * (k % self.rest), self.rest)
        return x, r

    def ahead(self, k):
        x, r = self.away(k, 1)
        return {"section": x, "dp": self.c, "r": r}

    def behind(self, k):
        x, r = self.away(k, -1)
        return {"section": x, "dp": self.c, "r": r}

    def sibling(self):
        return {"section": self.x, "dp": 1 - self.c, "r": self.r}

    def behind_chip(self, k):
        x, r = self.away(k, -1)
        return x * self.rest + r

    def other(self, dx, dc, dr):
        x = lax.rem(self.x + self.sections + dx, self.sections)
        c = lax.rem(self.c + 2 + dc, 2)
        r = lax.rem(self.r + self.rest + dr, self.rest)
        return {"section": x, "dp": c, "r": r}, (x * 2 + c) * self.rest + r

    def offsets(self):
        every = [(x, c, r) for x in range(self.sections) for c in range(2) for r in range(self.rest)]
        return list(enumerate(every))[1:]

    def greet(self, zs=1, work=None):
        barrier = pltpu.get_barrier_semaphore()
        z = lax.axis_index("z")
        size = lax.axis_size("z")
        for k in range(1, zs):
            pl.semaphore_signal(barrier, inc=1, device_id={"z": lax.rem(z + size - k, size)}, device_id_type=MESH)
        others = self.offsets()
        for _, place in others:
            pl.semaphore_signal(barrier, inc=1, device_id=self.other(*place)[0], device_id_type=MESH)
        more = 0 if work is None else work.greet()
        pl.semaphore_wait(barrier, len(others) + zs - 1 + more)


def remote(src, dst, send, recv, device):
    return pltpu.make_async_remote_copy(
        src_ref=src, dst_ref=dst, send_sem=send, recv_sem=recv, device_id=device, device_id_type=MESH
    )


class Gather:
    def __init__(self, peers, full, sems):
        self.peers, self.full = peers, full
        self.chip_send, self.chip_recv, self.core_send, self.core_recv = sems
        self.sent = []

    def start(self, src):
        p = self.peers
        mine = self.full.at[p.chip, p.c]
        mine[...] = src if isinstance(src, jax.Array) else src[...]
        for k in range(1, p.chips):
            self.send(remote(mine, mine, self.chip_send.at[k], self.chip_recv.at[k], p.ahead(k)))
        self.send(remote(mine, mine, self.core_send.at[0], self.core_recv.at[0], p.sibling()))

    def send(self, copy):
        copy.start()
        self.sent.append(copy)

    def forward(self, k):
        p = self.peers
        block = self.full.at[p.behind_chip(k), p.c]
        remote(block, block, self.chip_send.at[k], self.chip_recv.at[k], p.sibling()).wait_recv()
        self.send(remote(block, block, self.core_send.at[k], self.core_recv.at[k], p.sibling()))

    def chip(self, k):
        p = self.peers
        block = self.full.at[p.behind_chip(k), 1 - p.c]
        remote(block, block, self.core_send.at[k], self.core_recv.at[k], p.sibling()).wait_recv()
        return p.behind_chip(k)

    def arrivals(self):
        yield 0, self.chip(0)
        chips = self.peers.chips
        for k in range(1, chips):
            for later in (1, 2) if k == 1 else (k + 1,):
                if later < chips:
                    self.forward(later)
            yield k, self.chip(k)

    def finish(self):
        for copy in self.sent:
            copy.wait_send()


class Reduce:
    def __init__(self, peers, mine, stage, other, going, coming, sems):
        self.peers = peers
        self.mine, self.stage, self.other, self.going, self.coming = mine, stage, other, going, coming
        self.chip_send, self.chip_recv, self.core_send, self.core_recv = sems
        self.sent = []

    def send(self, copy):
        copy.start()
        self.sent.append(copy)

    def put(self, k, both):
        p = self.peers
        rows = both.shape[0] // 2
        low, high = both[:rows], both[rows:]
        first = p.c == 0
        self.mine[k] = jnp.where(first, low, high)
        self.stage[k] = jnp.where(first, high, low).astype(BF)
        self.send(remote(self.stage.at[k], self.other.at[k], self.core_send.at[k], self.core_recv.at[k], p.sibling()))

    def arrived(self, k):
        p = self.peers
        remote(self.stage.at[k], self.other.at[k], self.core_send.at[k], self.core_recv.at[k], p.sibling()).wait_recv()
        return self.mine[k] + self.other[k].astype(F32)

    def push(self, k):
        p = self.peers
        if k:
            self.going[k - 1] = self.arrived(k).astype(BF)
            self.send(remote(self.going.at[k - 1], self.coming.at[k - 1], self.chip_send.at[k], self.chip_recv.at[k], p.behind(k)))

    def total(self):
        p = self.peers
        out = self.arrived(0)
        for k in range(1, p.chips):
            remote(self.going.at[k - 1], self.coming.at[k - 1], self.chip_send.at[k], self.chip_recv.at[k], p.sibling()).wait_recv()
            out = out + self.coming[k - 1].astype(F32)
        return out

    def finish(self):
        for copy in self.sent:
            copy.wait_send()


class RingGather:
    def greet(self):
        return 0

    def __init__(self, pieces, local, send, recv):
        self.pieces, self.local, self.send_sem, self.recv_sem = pieces, local, send, recv
        self.zs, self.z = lax.axis_size("z"), lax.axis_index("z")
        every = [(p, s) for s in range(self.zs - 1) for p in range(len(pieces)) if s < pieces[p][2]]
        self.steps = [(p, s) for p, s in every if s < pieces[p][2] - 1] + [(p, s) for p, s in every if s == pieces[p][2] - 1]
        self.forwards = len(every) - len(pieces)
        self.sent = []

    def block(self, step):
        return lax.rem(self.z + self.zs - step, self.zs)

    def send(self, p, step, src):
        dst = self.pieces[p][1].at[self.block(step)]
        copy = remote(src, dst, self.send_sem.at[p, step], self.recv_sem.at[p, step], {"z": lax.rem(self.z + 1, self.zs)})
        copy.start()
        self.sent.append(copy)

    def start(self):
        for p in range(len(self.pieces)):
            self.launch(p)

    def launch(self, p):
        shard, full, _ = self.pieces[p]
        self.send(p, 0, shard)
        pltpu.make_async_copy(shard, full.at[self.z], self.local.at[p]).start()

    def tick(self, count=1):
        for _ in range(min(count, self.forwards)):
            self.forwards -= 1
            self.take()

    def take(self):
        p, step = self.steps.pop(0)
        shard, full, count = self.pieces[p]
        block = full.at[self.block(step + 1)]
        remote(block, block, self.send_sem.at[p, step], self.recv_sem.at[p, step], {"z": lax.rem(self.z + 1, self.zs)}).wait_recv()
        if step < count - 1:
            self.send(p, step + 1, block)
            return None
        pltpu.make_async_copy(shard, full.at[self.z], self.local.at[p]).wait()
        return p

    def finish(self):
        while self.steps:
            self.take()
        for copy in self.sent:
            copy.wait_send()


class RingSum:
    def greet(self):
        return 0

    def __init__(self, pieces, send, recv):
        self.pieces, self.send_sem, self.recv_sem = pieces, send, recv
        self.zs, self.z = lax.axis_size("z"), lax.axis_index("z")
        self.steps, self.sent = [], []
        self.late = [p for p, piece in enumerate(pieces) if piece[0] is None]
        ready = [p for p in range(len(pieces)) if p not in self.late]
        self.steps = [(p, i) for i in range(self.zs - 1) for p in ready if i < pieces[p][5] - 1]
        self.forwards = len(self.steps)
        self.steps += [(p, pieces[p][5] - 1) for p in ready]
        self.parts = [piece[0] for piece in pieces]

    def copy(self, p, i, src):
        dst = self.pieces[p][2].at[i]
        return remote(src, dst, self.send_sem.at[p, i], self.recv_sem.at[p, i], {"z": lax.rem(self.z + 1, self.zs)})

    def send(self, p, i, src):
        copy = self.copy(p, i, src)
        copy.start()
        self.sent.append(copy)

    def launch(self, p):
        acc, first = self.pieces[p][1], self.pieces[p][4]
        self.send(p, 0, far(acc) if first else far(self.parts[p]).at[lax.rem(self.z + self.zs - 1, self.zs)])

    def start(self):
        for p in range(len(self.pieces)):
            if p not in self.late:
                self.launch(p)

    def made(self, part):
        if self.late:
            p = self.late.pop(0)
            self.parts[p] = part
            self.launch(p)
            count = self.pieces[p][5]
            self.steps[self.forwards : self.forwards] = [(p, i) for i in range(count - 1)]
            self.forwards += count - 1
            self.steps.append((p, count - 1))

    def tick(self, count=1):
        for _ in range(min(count, self.forwards)):
            self.forwards -= 1
            self.take()

    def take(self):
        p, i = self.steps.pop(0)
        part, acc, came, out, first, count = self.pieces[p]
        self.copy(p, i, came.at[i]).wait_recv()
        own = self.parts[p][lax.rem(self.z + 2 * self.zs - 2 - first - i, self.zs)]
        total = (came[i].astype(F32) + own.astype(F32)).astype(BF)
        if i < count - 1:
            came[i] = total
            self.send(p, i + 1, came.at[i])
        else:
            out[...] = total

    def middle(self):
        pass

    def finish(self):
        while self.steps:
            self.take()
        for copy in self.sent:
            copy.wait_send()


GROUPS = 5


def groups_of(rows, start, count):
    tall, at = rows // GROUPS, start
    while at < start + count:
        group, row = divmod(at, tall)
        some = min(tall - row, start + count - at)
        yield at - start, group, row, some
        at += some


class TurnBack:
    def __init__(self, peers, part, pieces, came, send, recv, given=None):
        self.given = given
        self.peers, self.part, self.pieces, self.came = peers, part, pieces, came
        self.send_sem, self.recv_sem = send, recv
        self.sent = []

    def greet(self):
        return 0

    def start(self):
        pass

    def tick(self, point):
        pass

    def middle(self):
        if self.given is not None:
            self.share(self.given)

    def made(self, turned):
        if self.given is None:
            self.share(turned)

    def share(self, turned):
        slab, _, cols = self.pieces.shape
        for t in range(slab):
            self.pieces[t] = turned[:, t * cols : (t + 1) * cols]
        _, me = self.peers.other(0, 0, 0)
        for i, place in self.peers.offsets():
            device, t = self.peers.other(*place)
            copy = remote(self.pieces.at[t], self.came.at[me], self.send_sem.at[i], self.recv_sem.at[i], device)
            copy.start()
            self.sent.append(copy)
        self.came[me] = self.pieces[me]

    def finish(self):
        for i, place in self.peers.offsets():
            device, t = self.peers.other(*(-d for d in place))
            block = self.came.at[t]
            remote(block, block, self.send_sem.at[i], self.recv_sem.at[i], device).wait_recv()
        zs, rows, cols = self.part.shape[0], self.part.shape[1] * GROUPS, self.came.shape[2]
        wide, span = rows // 2, self.came.shape[1]
        for c in range(2):
            for k in range(zs):
                at, done = (c * zs + k) * wide, 0
                while done < wide:
                    t, row = divmod(at + done, span)
                    count = min(wide - done, span - row)
                    for first, group, to, some in groups_of(rows, c * wide + done, count):
                        lanes = slice(group * cols, (group + 1) * cols)
                        self.part[k, to : to + some, lanes] = self.came[t, row + first : row + first + some, :]
                    done += count
        for copy in self.sent:
            copy.wait_send()


class Turn:
    def __init__(self, peers, full, nat, land, w_out, send, recv):
        self.peers, self.full, self.nat, self.land, self.w_out = peers, full, nat, land, w_out
        self.send_sem, self.recv_sem = send, recv
        self.sent = []

    def start(self):
        zs, rows, cols = self.full.shape[0], self.full.shape[1] * GROUPS, self.nat.shape[1]
        part, span = rows // 2, self.w_out.shape[0]
        for c in range(2):
            for z in range(zs):
                at = (c * zs + z) * part
                for first, group, row, some in groups_of(rows, c * part, part):
                    lanes = slice(group * cols, (group + 1) * cols)
                    self.nat[at + first : at + first + some, :] = self.full[z, row : row + some, lanes]
        used = zs * rows
        if used < self.nat.shape[0]:
            self.nat[used:, :] = jnp.zeros((self.nat.shape[0] - used, cols), BF)
        _, me = self.peers.other(0, 0, 0)
        for i, place in self.peers.offsets():
            device, t = self.peers.other(*place)
            src = self.nat.at[pl.ds(pl.multiple_of(t * span, span), span)]
            copy = remote(src, self.land.at[me], self.send_sem.at[i], self.recv_sem.at[i], device)
            copy.start()
            self.sent.append(copy)
        self.land[me] = self.nat[pl.ds(pl.multiple_of(me * span, span), span), :]

    def finish(self):
        for i, place in self.peers.offsets():
            device, t = self.peers.other(*(-d for d in place))
            block = self.land.at[t]
            remote(block, block, self.send_sem.at[i], self.recv_sem.at[i], device).wait_recv()
        slab, _, cols = self.land.shape
        for t in range(slab):
            self.w_out[:, t * cols : (t + 1) * cols] = self.land[t]
        for copy in self.sent:
            copy.wait_send()


class Route:
    def __init__(self, seqs, src, out, local, send, recv, when="start"):
        self.when = when
        self.seqs, self.src, self.out = seqs, src, out
        self.local, self.send_sem, self.recv_sem = local, send, recv
        x, c, z = (lax.axis_index(a) for a in ("section", "dp", "z"))
        self.here = lax.rem(z, 2) == x
        place = c * 2 + x
        self.to = {"dp": lax.rem(z, seqs), "z": place}
        self.micro = z // seqs
        self.same = (lax.rem(z, seqs) == c) & (place == z)
        self.sources = []
        for micro in range(out.shape[0]):
            src_c, src_z = z // 2, micro * seqs + c
            self.sources.append(({"dp": src_c, "z": src_z}, (src_c == c) & (src_z == z)))

    def greet(self):
        barrier = pltpu.get_barrier_semaphore()
        for device, same in self.sources:

            @pl.when(self.here & jnp.logical_not(same))
            def _(device=device):
                pl.semaphore_signal(barrier, inc=1, device_id=device, device_id_type=MESH)

        return jnp.where(self.same, 0, 1)

    def copy(self):
        return remote(self.src, self.out.at[self.micro], self.send_sem, self.recv_sem.at[self.micro], self.to)

    def own(self):
        return pltpu.make_async_copy(self.src, self.out.at[self.micro], self.local)

    def start(self):
        if self.when == "start":
            self.go()

    def middle(self):
        pass

    def go(self):
        @pl.when(jnp.logical_not(self.same))
        def _():
            self.copy().start()

        @pl.when(self.same)
        def _():
            self.own().start()

    def tick(self, point):
        if self.when == point:
            self.go()

    def made(self, part):
        pass

    def arrived(self):
        for micro, (device, same) in enumerate(self.sources):

            @pl.when(self.here & jnp.logical_not(same))
            def _(micro=micro, device=device):
                block = self.out.at[micro]
                remote(block, block, self.send_sem, self.recv_sem.at[micro], device).wait_recv()

        @pl.when(self.same)
        def _():
            self.own().wait()

    def sent(self):
        @pl.when(jnp.logical_not(self.same))
        def _():
            self.copy().wait_send()

    def finish(self):
        self.arrived()
        self.sent()


class Across:
    def __init__(self, layer, src, out, send, recv):
        self.src, self.out, self.send_sem, self.recv_sem = src, out, send, recv
        x, z = lax.axis_index("section"), lax.axis_index("z")
        self.layer = layer
        self.sends = (x != layer) & (lax.rem(z, 2) == x)
        self.takes = (x == layer) & (lax.rem(z, 2) != x)
        self.going = False

    def greet(self):
        barrier = pltpu.get_barrier_semaphore()

        @pl.when(self.takes)
        def _():
            pl.semaphore_signal(barrier, inc=1, device_id={"section": 1 - self.layer}, device_id_type=MESH)

        return jnp.where(self.sends, 1, 0)

    def copy(self):
        return remote(self.src, self.out, self.send_sem, self.recv_sem, {"section": jnp.int32(self.layer)})

    def back(self):
        return remote(self.out, self.out, self.send_sem, self.recv_sem, {"section": jnp.int32(1 - self.layer)})

    def start(self):
        pass

    def tick(self, point):
        if not self.going:
            self.going = True

            @pl.when(self.sends)
            def _():
                self.copy().start()

    def made(self, part):
        pass

    def middle(self):
        pass

    def finish(self):
        self.tick("end")

        @pl.when(self.takes)
        def _():
            self.back().wait_recv()

        @pl.when(self.sends)
        def _():
            self.copy().wait_send()


class RouteIn:
    def __init__(self, seqs, pairs, local, send, recv):
        self.pairs, self.local, self.send_sem, self.recv_sem = pairs, local, send, recv
        x, c, z = (lax.axis_index(a) for a in ("section", "dp", "z"))
        self.sends = lax.rem(z, 2) == x
        self.targets = []
        for micro in range(pairs[0][0].shape[0]):
            to_c, to_z = z // 2, micro * seqs + c
            self.targets.append(({"dp": to_c, "z": to_z}, (to_c == c) & (to_z == z)))
        self.micro = z // seqs
        self.source = {"dp": lax.rem(z, seqs), "z": c * 2 + x}
        self.same = (lax.rem(z, seqs) == c) & (c * 2 + x == z)

    def greet(self):
        barrier = pltpu.get_barrier_semaphore()

        @pl.when(jnp.logical_not(self.same))
        def _():
            pl.semaphore_signal(barrier, inc=1, device_id=self.source, device_id_type=MESH)

        return sum(jnp.where(self.sends & jnp.logical_not(same), 1, 0) for _, same in self.targets)

    def far(self, i, micro):
        src, dst = self.pairs[i]
        return remote(src.at[micro, 0], dst, self.send_sem.at[i, micro], self.recv_sem.at[i], self.targets[micro][0])

    def near(self, i, micro):
        src, dst = self.pairs[i]
        return pltpu.make_async_copy(src.at[micro, 0], dst, self.local.at[i])

    def start(self, i=0):
        for micro, (_, same) in enumerate(self.targets):

            @pl.when(self.sends & jnp.logical_not(same))
            def _(micro=micro):
                self.far(i, micro).start()

            @pl.when(self.sends & same)
            def _(micro=micro):
                self.near(i, micro).start()

    def tick(self, point):
        pass

    def made(self, part):
        pass

    def middle(self):
        pass

    def arrived(self, i):
        dst = self.pairs[i][1]

        @pl.when(jnp.logical_not(self.same))
        def _():
            remote(dst, dst, self.send_sem.at[i, 0], self.recv_sem.at[i], self.source).wait_recv()

        for micro, (_, same) in enumerate(self.targets):

            @pl.when(self.sends & same)
            def _(micro=micro):
                self.near(i, micro).wait()

    def finish(self):
        for i in range(len(self.pairs)):
            for micro, (_, same) in enumerate(self.targets):

                @pl.when(self.sends & jnp.logical_not(same))
                def _(i=i, micro=micro):
                    self.far(i, micro).wait_send()


def reorder(raw, ordered, zs, wide):
    for c in range(2):
        for k in range(zs):
            at, to = (c * zs + k) * wide, (k * 2 + c) * wide
            ordered[:, to : to + wide] = raw[at : at + wide, :].astype(F32).T.astype(BF)


class Shared:
    def __init__(self, src, gather, points):
        self.src, self.gather, self.points = src, gather, points

    def greet(self):
        return 0

    def start(self):
        pass

    def made(self, part):
        pass

    def middle(self):
        pass

    def tick(self, point):
        if point == self.points[0]:
            self.gather.start(self.src)
        if point == self.points[1]:
            for k in range(1, self.gather.peers.chips):
                self.gather.forward(k)

    def finish(self):
        for k in range(self.gather.peers.chips):
            self.gather.chip(k)
        self.gather.finish()


class Several:
    def __init__(self, works):
        self.works = works

    def greet(self):
        return sum(work.greet() for work in self.works)

    def start(self):
        for work in self.works:
            work.start()

    def tick(self, point):
        for work in self.works:
            work.tick(point)

    def made(self, part):
        for work in self.works:
            work.made(part)

    def middle(self):
        for work in self.works:
            work.middle()

    def finish(self):
        for work in self.works:
            work.finish()


class NoSide:
    def greet(self):
        return 0

    def start(self):
        pass

    def tick(self, point):
        pass

    def made(self, part):
        pass

    def middle(self):
        pass

    def finish(self):
        pass


class Both:
    def greet(self):
        return 0

    def __init__(self, ring, turn, ahead):
        self.ring, self.turn = ring, turn
        if ahead:
            ring.steps.sort(key=lambda step: step[1] if step[0] else step[1] * 0.5 - 0.6)

    def start(self):
        self.ring.start()

    def tick(self, count=1):
        for _ in range(count):
            self.take()

    def take(self):
        if self.ring.take() == 0:
            self.turn.start()

    def finish(self):
        while self.ring.steps:
            self.take()
        self.ring.finish()
        self.turn.finish()


class Fetch:
    def __init__(self, far, near, sem):
        self.far, self.near = far, near
        self.copy = pltpu.make_async_copy(far, near, sem)
        self.copy.start()
        self.here = False
        self.shape = near.shape

    def __getitem__(self, index):
        if not self.here:
            self.copy.wait()
            self.here = True
        return self.near[index]

    def finish(self):
        if not self.here:
            self.copy.wait()


class Store:
    def __init__(self, far, near, sem):
        self.copy = pltpu.make_async_copy(near, far, sem)
        self.near, self.gone = near, False
        self.shape, self.at = near.shape, near.at

    def __getitem__(self, index):
        return self.near[index]

    def __setitem__(self, index, value):
        self.near[index] = value

    def flush(self):
        self.gone = True
        self.copy.start()

    def finish(self):
        if not self.gone:
            self.flush()
        self.copy.wait()


def far(ref):
    return ref.far if isinstance(ref, Fetch) else ref


class Paced:
    def __init__(self, work, pace):
        self.work, self.pace = work, pace
        self.greet, self.start, self.finish = work.greet, work.start, work.finish
        self.middle = getattr(work, "middle", lambda: None)
        self.part = None

    def made(self, part):
        self.part = part
        if "launch" not in self.pace:
            self.work.made(part)

    def tick(self, point):
        self.work.tick(self.pace.get(point, 0))
        if self.part is not None and self.pace.get("launch") == point:
            self.work.made(self.part)


class SideWork:
    def __init__(self, operands=(), in_hbm=(), outs=(), out_hbm=(), scratch=(), build=None):
        self.operands, self.in_hbm, self.outs, self.out_hbm = operands, in_hbm, outs, out_hbm
        self.scratch, self.build = scratch, build
        self.zs = 1 if build is None else 2

    def make(self, peers, ins, outs, scratch):
        return NoSide() if self.build is None else self.build(peers, ins, outs, scratch)


def route_side(lay, src, when):
    dma = pltpu.SemaphoreType.DMA
    outs = [((lay.micros, *src.shape), BF)]

    def build(peers, ins, outs, scratch):
        return Route(lay.seqs, ins[0], outs[0], *scratch, when)

    return SideWork([src], (True,), outs, (True,), [dma, dma, dma((lay.micros,))], build)


def turn_side(lay, turned=None):
    n, span = lay.slab, lay.slots * lay.head
    outs = [((lay.zs, lay.width // lay.zs // GROUPS, GROUPS * lay.cols), BF)]
    scratch = [pltpu.VMEM((n, span, lay.cols), BF)] * 2 + [pltpu.SemaphoreType.DMA((n,))] * 2

    def build(peers, ins, outs, scratch):
        return TurnBack(peers, outs[0], *scratch, ins[0] if ins else None)

    operands = [] if turned is None else [turned]
    return SideWork(operands, (False,) * len(operands), outs, (False,), scratch, build)


def share_side(lay, a, points):
    chips = lay.slab // 2

    def build(peers, ins, outs, scratch):
        return Shared(ins[0], Gather(peers, outs[0], scratch), points)

    return SideWork([a], (False,), [((chips, 2, *a.shape), BF)], (False,), [pltpu.SemaphoreType.DMA((chips,))] * 4, build)


def across_side(layer, a):
    dma = pltpu.SemaphoreType.DMA

    def build(peers, ins, outs, scratch):
        return Across(layer, ins[0], outs[0], *scratch)

    return SideWork([a], (True,), [(a.shape, a.dtype)], (True,), [dma, dma], build)


def both_sides(*sides):
    sides = [side for side in sides if side.build is not None]
    joined = [[], [], [], [], []]
    for side in sides:
        for into, more in zip(joined, (side.operands, side.in_hbm, side.outs, side.out_hbm, side.scratch)):
            into += list(more)

    def build(peers, ins, outs, scratch):
        works = []
        for side in sides:
            a, b, c = len(side.operands), len(side.outs), len(side.scratch)
            works.append(side.build(peers, ins[:a], outs[:b], scratch[:c]))
            ins, outs, scratch = ins[a:], outs[b:], scratch[c:]
        return Several(works)

    return SideWork(*joined, build)


def gather_side(shards, pace, counts=None, turn=None):
    zs = lax.axis_size("z")
    n = len(shards)
    counts = counts or (zs - 1,) * n
    places = [a[1] if isinstance(a, tuple) else None for a in shards]
    shards = [a[0] if isinstance(a, tuple) else a for a in shards]
    outs = [((zs, *a.shape[-2:]), BF) for a in shards]
    sems = [pltpu.SemaphoreType.DMA((n,))] + [pltpu.SemaphoreType.DMA((n, zs - 1))] * 2
    if turn is None:

        def build(peers, ins, outs, scratch):
            ins = [a if place is None else a.at[place] for a, place in zip(ins, places)]
            return Paced(RingGather(list(zip(ins, outs, counts)), *scratch), pace)

        return SideWork(shards, (True,) * n, outs, (True,) * n, sems, build)
    slab = 2 * lax.axis_size("section") * lax.axis_size("r")
    cols = shards[0].shape[1] // GROUPS
    outs[0] = ((turn, slab * cols), BF)
    more = [
        pltpu.VMEM((zs, *shards[0].shape), BF),
        pltpu.VMEM((slab * turn, cols), BF),
        pltpu.VMEM((slab, turn, cols), BF),
    ] + [pltpu.SemaphoreType.DMA((slab,))] * 2

    def build_turn(peers, ins, outs, scratch):
        pieces = list(zip(ins, [scratch[3], *outs[1:]], counts))
        turning = Turn(peers, scratch[3], scratch[4], scratch[5], outs[0], *scratch[6:8])
        return Paced(Both(RingGather(pieces, *scratch[:3]), turning, False), pace)

    return SideWork(shards, (True,) * n, outs, (False,) + (True,) * (n - 1), sems + more, build_turn)


def sum_side(pieces, pace):
    zs = lax.axis_size("z")
    n = len(pieces)
    operands, outs, scratch = [], [], []
    for part, shape, acc, first, count in pieces:
        operands += [a for a in (part, acc) if a is not None]
        outs.append((shape, BF))
        scratch.append(pltpu.VMEM((count, *shape), BF))
    scratch += [pltpu.SemaphoreType.DMA((n, zs - 1))] * 2
    def build(peers, ins, outs, scratch):
        ins, made = list(ins), []
        for i, (part, shape, acc, first, count) in enumerate(pieces):
            part_ref = None if part is None else ins.pop(0)
            acc_ref = None if acc is None else ins.pop(0)
            made.append((part_ref, acc_ref, scratch[i], outs[i], first, count))
        ring = RingSum(made, *scratch[n : n + 2])
        return Paced(ring, pace)

    return SideWork(operands, (False,) * len(operands), outs, (False,) * len(outs), scratch, build)


def gather_scratch(chips, rows, width):
    return [pltpu.VMEM((chips, 2, rows, width), BF)] + [pltpu.SemaphoreType.DMA((chips,))] * 4


def reduce_scratch(chips, rows, width):
    return [
        pltpu.VMEM((chips, rows, width), F32),
        pltpu.VMEM((chips, rows, width), BF),
        pltpu.VMEM((chips, rows, width), BF),
        pltpu.VMEM((chips - 1, rows, width), BF),
        pltpu.VMEM((chips - 1, rows, width), BF),
    ] + [pltpu.SemaphoreType.DMA((chips,))] * 4


def norm_parts(v):
    centred = v - jnp.mean(v, axis=-1, keepdims=True)
    spread = jnp.mean(centred * centred, axis=-1, keepdims=True)
    scale = lax.rsqrt(spread + EPSILON)
    return centred * scale, scale


def norm_back(v, gain, grad):
    unit, scale = norm_parts(v)
    scaled = grad * gain
    part = scaled - jnp.mean(scaled, axis=-1, keepdims=True)
    part = part - unit * jnp.mean(scaled * unit, axis=-1, keepdims=True)
    return part * scale, jnp.sum(grad * unit, axis=0, keepdims=True), jnp.sum(grad, axis=0, keepdims=True)


def dot(a, b, ca=1, cb=0):
    return lax.dot_general(a, b, (((ca,), (cb,)), ((), ())), preferred_element_type=F32)


def chip_rows(chip, rows):
    return pl.ds(pl.multiple_of(chip * (2 * rows), 2 * rows), 2 * rows)


def groups(span, head):
    wide = 128 if span % 128 == 0 else span
    for g in range(span // wide):
        yield slice(g * wide, (g + 1) * wide), [(g * wide // head + i, i * head) for i in range(wide // head)]


def only(a, start, head):
    lane = lax.broadcasted_iota(jnp.int32, a.shape, 1)
    return jnp.where((lane >= start) & (lane < start + head), a, jnp.zeros_like(a))


def attention_forward(head, side, *refs):
    (h, w_qkv, w_out, bias, col, row, vec) = refs[:7]
    ins, refs = refs[7 : 7 + len(side.operands)], refs[7 + len(side.operands) :]
    (normed, qkv, attended, logs, mid, normed_two), refs = refs[:6], refs[6:]
    side_outs, refs = refs[: len(side.outs)], refs[len(side.outs) :]
    gather_refs, reduce_refs, side_refs = refs[:5], refs[5 : 14 + 1], refs[14 + 1 :]
    rows, width = h.shape
    span = w_out.shape[0]
    peers = Peers()
    gather = Gather(peers, gather_refs[0], gather_refs[1:])
    reduce = Reduce(peers, *reduce_refs[:5], reduce_refs[5:9])
    kept_sem = reduce_refs[9]
    full = gather.full
    work = side.make(peers, ins, side_outs, side_refs)
    peers.greet(side.zs, work)
    gather.start((norm_parts(h[...].astype(F32))[0] * vec[0:1, :] + vec[2:3, :]).astype(BF))
    work.start()
    for k, chip in gather.arrivals():
        part = dot(full[chip].reshape(2 * rows, width), w_qkv[...]) + bias[...]
        qkv[chip_rows(chip, rows), :] = part.astype(BF)
    work.tick("qkv")
    kept = pltpu.make_async_copy(full, normed, kept_sem)
    kept.start()
    qkv.flush()
    scale = head ** (-0.5)
    order = list(range(1, peers.chips)) + [0]
    before = None
    for k in order:
        chip = peers.behind_chip(k)
        here = chip_rows(chip, rows)
        block = jnp.where(col[...] <= row[:, here], 0.0, LOW).astype(F32)
        for lanes, heads in groups(span, head):
            q = qkv[here, lanes]
            keys = qkv[:, slice(span + lanes.start, span + lanes.stop)]
            values = qkv[:, slice(2 * span + lanes.start, 2 * span + lanes.stop)]
            merged = None
            for slot, start in heads:
                scores = dot(keys, only(q, start, head) * scale, 1, 1) + block
                top = jnp.max(scores, axis=0, keepdims=True)
                weights = jnp.exp(scores - top)
                total = jnp.sum(weights, axis=0, keepdims=True)
                logs[slot : slot + 1, here] = top + jnp.log(total)
                mixed = dot(values, weights.astype(BF), 0, 0) / total
                lane = lax.broadcasted_iota(jnp.int32, mixed.shape, 0)
                merged = mixed if merged is None else jnp.where(lane >= start, mixed, merged)
            attended[here, lanes] = merged.T.astype(BF)
        reduce.put(k, dot(attended[here, :], w_out[...]))
        if before is not None:
            reduce.push(before)
        work.tick("q%d" % order.index(k))
        before = k
    attended.flush()
    reduce.push(before)
    out = h[...].astype(F32) + (reduce.total() + vec[4:5, :])
    mid[...] = out
    normed_two[...] = (norm_parts(out)[0] * vec[1:2, :] + vec[3:4, :]).astype(BF)
    work.finish()
    gather.finish()
    reduce.finish()
    kept.wait()


ROOT = 0.7978845608028654


def feed_forward(side, *refs):
    (src, mid, fc_packed, w_proj, bias, vec) = refs[:6]
    ins, refs = refs[6 : 6 + len(side.operands)], refs[6 + len(side.operands) :]
    (normed_two, slope, activated, result, proj_out, fc_out), refs = refs[:6], refs[6:]
    side_outs, refs = refs[: len(side.outs)], refs[len(side.outs) :]
    gather_refs, reduce_refs, side_refs = refs[:5], refs[5 : 14 + 8], refs[14 + 8 :]
    rows, width = src.shape
    peers = Peers()
    gather = Gather(peers, gather_refs[0], gather_refs[1:])
    reduce = Reduce(peers, *reduce_refs[:5], reduce_refs[5:9])
    kept_sem, proj, proj_local, proj_send, proj_recv, proj_sem, w_fc, fc_sem = reduce_refs[9:17]
    full = gather.full
    work = side.make(peers, ins, side_outs, side_refs)
    zs, z = lax.axis_size("z"), lax.axis_index("z")
    half = proj.shape[1]
    peers.greet(2, work)
    gather.start(src)
    there = lax.rem(z + 2, zs)
    last = remote(w_proj.at[there], proj.at[there], proj_send, proj_recv, {"z": lax.rem(z + 1, zs)})
    last.start()
    here = [lax.rem(z + zs - i, zs) for i in range(zs - 1)]
    placed = [pltpu.make_async_copy(w_proj.at[b], proj.at[b], proj_local.at[i]) for i, b in enumerate(here)]
    for copy in placed:
        copy.start()
    rows_of, units = fc_packed.shape[1], w_fc.shape[1]
    for b in range(zs):
        for c in range(2):
            at = (b * 2 + c) * rows_of
            w_fc[at : at + rows_of, :] = fc_packed[b, :, c * units : (c + 1) * units]
    fc_kept = pltpu.make_async_copy(w_fc, fc_out, fc_sem)
    fc_kept.start()
    before = None
    for k, chip in gather.arrivals():
        if k == 0:
            last.wait_recv()
            work.start()
            for copy in placed:
                copy.wait()
            proj_kept = pltpu.make_async_copy(proj, proj_out, proj_sem)
            proj_kept.start()
        here = chip_rows(chip, rows)
        u = dot(full[chip].reshape(2 * rows, width), w_fc[...]) + bias[...]
        bend = jnp.tanh(ROOT * (u + 0.044715 * (u * u * u)))
        slope[here, :] = (0.5 * (1.0 + bend) + 0.5 * u * (1.0 - bend * bend) * (ROOT * (1.0 + 3 * 0.044715 * (u * u)))).astype(BF)
        act = (0.5 * u * (1.0 + bend)).astype(BF)
        activated[here, :] = act
        back = dot(act[:, :half], proj[0])
        for b in range(1, zs):
            back = back + dot(act[:, b * half : (b + 1) * half], proj[b])
        reduce.put(k, back)
        if before is not None:
            reduce.push(before)
        work.tick("k%d" % k)
        before = k
    kept = pltpu.make_async_copy(full, normed_two, kept_sem)
    kept.start()
    slope.flush()
    activated.flush()
    reduce.push(before)
    work.tick("sent")
    out = (mid[...] + (reduce.total() + vec[5:6, :])).astype(BF)
    result[...] = out
    last.wait_send()
    proj_kept.wait()
    fc_kept.wait()
    work.finish()
    gather.finish()
    reduce.finish()
    kept.wait()


def chunks(size, step):
    return [(a, min(a + step, size)) for a in range(0, size, step)]


def feed_backward(side, ready, *refs):
    (src, mid, w_fc, w_proj, slope, activated, normed_two, vec, *given) = refs[: 8 + ready]
    refs = refs[8 + ready :]
    ins, refs = refs[: len(side.operands)], refs[len(side.operands) :]
    (grad_mid, attn_rows, grad_proj, grad_fc, sums, unit_sums), refs = refs[:6], refs[6:]
    side_outs, refs = refs[: len(side.outs)], refs[len(side.outs) :]
    gather_refs, reduce_refs, side_refs = refs[:5], refs[5 : 14 + 1], refs[14 + 1 :]
    hidden, = reduce_refs[9:10]
    rows, width = src.shape
    tokens = slope.shape[0]
    peers = Peers()
    gather = Gather(peers, gather_refs[0], gather_refs[1:])
    reduce = Reduce(peers, *reduce_refs[:5], reduce_refs[5:9])
    full = given[0] if ready else gather.full
    work = side.make(peers, ins, side_outs, side_refs)
    peers.greet(side.zs, work)
    half = grad_proj.shape[1]

    def proj_terms():
        branch = full[...].reshape(tokens, width)
        for b in range(grad_proj.shape[0]):
            grad_proj[b] = dot(activated[:, b * half : (b + 1) * half], branch, 0, 0).astype(BF)
        grad_proj.flush()
        work.made(grad_proj)

    if ready:
        order = [(k, peers.behind_chip(k)) for k in (*range(1, peers.chips), 0)]
    else:
        gather.start(src)
        order = gather.arrivals()
    work.start()
    if ready:
        proj_terms()
    before = None
    for k, chip in order:
        here = chip_rows(chip, rows)
        back = dot(full[chip].reshape(2 * rows, width), w_proj[...], 1, 1) * slope[here, :].astype(F32)
        back = back.astype(BF)
        hidden[here, :] = back
        reduce.put(k, dot(back, w_fc[...], 1, 1))
        if before is not None:
            reduce.push(before)
        work.tick("k%d" % k)
        before = k
    reduce.push(before)
    work.middle()
    if not ready:
        proj_terms()
    work.tick("proj")
    back = hidden[...]
    blocks, rows_of, units = grad_fc.shape[0], grad_fc.shape[1], back.shape[1]
    for b in range(blocks):
        at = b * 2 * rows_of
        part = dot(normed_two[:, at : at + 2 * rows_of], back, 0, 0).astype(BF)
        for c in range(2):
            grad_fc[b, :, c * units : (c + 1) * units] = part[c * rows_of : (c + 1) * rows_of]
    grad_fc.flush()
    work.tick("fc")
    unit_sums[...] = jnp.sum(back.astype(F32), axis=0, keepdims=True)
    own = src[...].astype(F32)
    part, gain, shift = norm_back(mid[...], vec[1:2, :], reduce.total())
    out = own + part
    grad_mid[...] = out
    low = out.astype(BF)
    attn_rows[...] = low
    sums[0:1, :] = gain
    sums[1:2, :] = shift
    sums[2:3, :] = jnp.sum(own, axis=0, keepdims=True)
    sums[3:4, :] = jnp.sum(low.astype(F32), axis=0, keepdims=True)
    sums[4:8, :] = jnp.zeros((4, width), F32)
    work.finish()
    if not ready:
        gather.finish()
    reduce.finish()


def attention_backward(head, side, *refs):
    (src, grad_mid, h, w_qkv, w_out, qkv, attended, logs, normed, col, row, vec) = refs[:12]
    ins, refs = refs[12 : 12 + len(side.operands)], refs[12 + len(side.operands) :]
    (grad_in, *grad_parts, grad_out, sums, head_sums), refs = refs[:7], refs[7:]
    side_outs, refs = refs[: len(side.outs)], refs[len(side.outs) :]
    gather_refs, reduce_refs, side_refs = refs[:5], refs[5 : 14 + 3], refs[14 + 3 :]
    joint, key_sum, value_sum = reduce_refs[9:12]
    rows, width = src.shape
    tokens, span = attended.shape
    scale = head ** (-0.5)
    peers = Peers()
    gather = Gather(peers, gather_refs[0], gather_refs[1:])
    reduce = Reduce(peers, *reduce_refs[:5], reduce_refs[5:9])
    full = gather.full
    work = side.make(peers, ins, side_outs, side_refs)
    peers.greet(side.zs, work)
    gather.start(src)
    work.start()
    for k, chip in gather.arrivals():
        here = chip_rows(chip, rows)
        g_all = dot(full[chip].reshape(2 * rows, width), w_out[...], 1, 1).astype(BF)
        block = jnp.where(col[...] <= row[:, here], 0.0, LOW).astype(F32)
        for lanes, heads in groups(span, head):
            q = qkv[here, lanes]
            g = g_all[:, lanes]
            keys = qkv[:, slice(span + lanes.start, span + lanes.stop)]
            values = qkv[:, slice(2 * span + lanes.start, 2 * span + lanes.stop)]
            merged = None
            key_term, value_term = 0.0, 0.0
            for slot, start in heads:
                q_one, g_one = only(q, start, head) * scale, only(g, start, head)
                probs = jnp.exp(dot(keys, q_one, 1, 1) + block - logs[slot : slot + 1, here])
                g_probs = dot(values, g_one, 1, 1)
                both = probs * g_probs
                centre = jnp.sum(both, axis=0, keepdims=True)
                g_scores = (both - probs * centre).astype(BF)
                value_term += dot(probs.astype(BF), g_one)
                key_term += dot(g_scores, q_one)
                g_query = dot(keys, g_scores, 0, 0)
                lane = lax.broadcasted_iota(jnp.int32, g_query.shape, 0)
                merged = g_query if merged is None else jnp.where(lane >= start, g_query, merged)
            joint[here, lanes] = (merged.T * scale).astype(BF)
            if k == 0:
                key_sum[:, lanes] = key_term
                value_sum[:, lanes] = value_term
            else:
                key_sum[:, lanes] += key_term
                value_sum[:, lanes] += value_term
        work.tick("k%d" % k)
    joint[:, span : 2 * span] = key_sum[...].astype(BF)
    joint[:, 2 * span :] = value_sum[...].astype(BF)
    order = list(range(1, peers.chips)) + [0]
    before = None
    for k in order:
        reduce.put(k, dot(joint[chip_rows(peers.behind_chip(k), rows), :], w_qkv[...], 1, 1))
        if before is not None:
            reduce.push(before)
        before = k
    work.tick("sent")
    grads = joint[...]
    grad_out[...] = dot(attended[...], full[...].reshape(tokens, width), 0, 0).astype(BF)
    grad_out.flush()
    work.made(grad_out)
    for a, b in chunks(width, 512):
        part = dot(normed[:, a:b], grads, 0, 0).astype(BF)
        for i, grad in enumerate(grad_parts):
            grad[a:b, :] = part[:, i * span : (i + 1) * span]
    for grad in grad_parts:
        grad.flush()
    work.tick("grad")
    head_sums[...] = jnp.sum(grads.astype(F32), axis=0, keepdims=True)
    part, gain, shift = norm_back(h[...].astype(F32), vec[0:1, :], reduce.total())
    grad_in[...] = (grad_mid[...] + part).astype(BF)
    sums[0:1, :] = gain
    sums[1:2, :] = shift
    sums[2:8, :] = jnp.zeros((6, width), F32)
    work.finish()
    gather.finish()
    reduce.finish()


def call(kernel, name, outs, operands, side, kept, scratch, keep=(), early=()):
    chips = lax.axis_size("section") * lax.axis_size("r")
    rows, width = operands[0].shape
    vmem, hbm = pl.BlockSpec(memory_space=pltpu.VMEM), pl.BlockSpec(memory_space=pl.ANY)
    every = [*operands, *side.operands]
    fetched = [i for i in range(len(every)) if i not in keep and not (i >= len(operands) and side.in_hbm[i - len(operands)])]
    work = gather_scratch(chips, rows, width) + reduce_scratch(chips, rows, width) + scratch + list(side.scratch)

    def body(*refs):
        refs = list(refs)
        count = len(fetched) + len(early)
        near, sems = refs[-1 - count : -1], refs[-1]
        for k, i in enumerate(fetched):
            refs[i] = Fetch(refs[i], near[k], sems.at[k])
        for k, i in enumerate(early):
            k += len(fetched)
            refs[len(every) + i] = Store(refs[len(every) + i], near[k], sems.at[k])
        kernel(*refs[: -1 - count])
        for i in fetched:
            refs[i].finish()
        for i in early:
            refs[len(every) + i].finish()

    out = pl.pallas_call(
        body,
        out_shape=[jax.ShapeDtypeStruct(*o) for o in (*outs, *side.outs)],
        in_specs=[hbm] * len(every),
        out_specs=[hbm if i in kept or i in early else vmem for i in range(len(outs))] + [hbm if i else vmem for i in side.out_hbm],
        scratch_shapes=work
        + [pltpu.VMEM(every[i].shape, every[i].dtype) for i in fetched]
        + [pltpu.VMEM(*outs[i]) for i in early]
        + [pltpu.SemaphoreType.DMA((len(fetched) + len(early),))],
        compiler_params=pltpu.CompilerParams(collective_id=name, has_side_effects=True, vmem_limit_bytes=60 * 2**20),
    )(*every)
    return out[: len(outs)], out[len(outs) :]


def run_attention_forward(name, head, side, *operands):
    h, w_qkv, w_out, bias, col, row, vec = operands
    rows, width = h.shape
    tokens, span = col.shape[0], w_out.shape[0]
    slots = -(-(span // head) // 8) * 8
    chips = tokens // (2 * rows)
    outs = [
        ((chips, 2, rows, width), BF),
        ((tokens, 3 * span), BF),
        ((tokens, span), BF),
        ((slots, tokens), F32),
        ((rows, width), F32),
        ((rows, width), BF),
    ]
    return call(functools.partial(attention_forward, head, side), name, outs, operands, side, (0,), [pltpu.SemaphoreType.DMA], (), (1, 2))


def run_feed_forward(name, side, *operands):
    src, mid, w_fc, w_proj, bias, vec = operands
    rows, width = src.shape
    units = w_fc.shape[2] // 2
    chips = lax.axis_size("section") * lax.axis_size("r")
    tokens = 2 * chips * rows
    outs = [
        ((chips, 2, rows, width), BF),
        ((tokens, units), BF),
        ((tokens, units), BF),
        ((rows, width), BF),
        (w_proj.shape, BF),
        ((width, units), BF),
    ]
    dma = pltpu.SemaphoreType.DMA
    scratch = [dma, pltpu.VMEM(w_proj.shape, BF), dma((w_proj.shape[0],)), dma, dma, dma, pltpu.VMEM((width, units), BF), dma]
    return call(functools.partial(feed_forward, side), name, outs, operands, side, (0, 4, 5), scratch, (3,), (1, 2))


def run_feed_backward(name, side, *operands):
    src, mid, w_fc, w_proj, slope, activated, normed_two, vec, *given = operands
    rows, width = src.shape
    tokens, units = slope.shape
    zs = lax.axis_size("z")
    outs = [
        ((rows, width), F32),
        ((rows, width), BF),
        ((zs, units // zs, width), BF),
        ((zs, width // (2 * zs), 2 * units), BF),
        ((8, width), F32),
        ((1, units), F32),
    ]
    return call(functools.partial(feed_backward, side, len(given)), name, outs, operands, side, (), [pltpu.VMEM((tokens, units), BF)], (), (2, 3))


def run_attention_backward(name, head, side, *operands):
    src, grad_mid, h, w_qkv, w_out, qkv, attended, logs, normed, col, row, vec = operands
    rows, width = src.shape
    tokens, span = attended.shape
    outs = [
        ((rows, width), BF),
        ((width, span), BF),
        ((width, span), BF),
        ((width, span), BF),
        ((span, width), BF),
        ((8, width), F32),
        ((1, 3 * span), F32),
    ]
    scratch = [pltpu.VMEM((tokens, 3 * span), BF), pltpu.VMEM((tokens, span), F32), pltpu.VMEM((tokens, span), F32)]
    return call(functools.partial(attention_backward, head, side), name, outs, operands, side, (), scratch, (), (1, 2, 3, 4))


def start_kernel(sizes, *refs):
    block, span, half, seqs, micros = sizes
    (tiny, w_qkv, w_attn, w_fc, w_proj, inputs, cotangent), refs = refs[:7], refs[7:]
    (qkv, wo, fc, (proj, qkv_full, w_out, h, g, row, col, *smalls)), refs = (refs[0:2], refs[2:4], refs[4:6], refs[6:19]), refs[19:]
    tiny_out, stage, h_raw, g_raw, natural, proj_cut = refs[:6]
    cuts, lands, (wo_full, nat, land), refs = refs[6:9], refs[9:12], refs[12:15], refs[15:]
    z_send, z_recv, *sems = refs[:6]
    all_send, all_recv, far_send, far_recv, turn_send, turn_recv = refs[6:12]
    ring_local, ring_send, ring_recv, *route_sems = refs[12:]
    peers = Peers()
    zs, z = lax.axis_size("z"), lax.axis_index("z")
    x, rest, slab = peers.x, peers.rest, 2 * peers.chips
    sections = peers.sections
    spot = peers.c * rest + peers.r
    width, wide = w_attn.shape[1], rest * block
    _, me = peers.other(0, 0, 0)
    route = RouteIn(seqs, [(inputs, h_raw), (cotangent, g_raw)], *route_sems)
    peers.greet(zs, route)
    sent = []

    def send(copy):
        copy.start()
        sent.append(copy)

    for k in range(1, zs):
        send(remote(tiny, stage.at[z], z_send.at[k], z_recv.at[k], {"z": lax.rem(z + k, zs)}))
    stage[z] = tiny[...]
    route.start(0)
    route.start(1)

    def share(a):
        for i, place in peers.offsets():
            device, t = peers.other(*place)
            send(remote(cuts[a].at[t], lands[a].at[x, spot], all_send.at[a, i], all_recv.at[a, i], device))
        lands[a][x, spot] = cuts[a][me]

    def settle(a, shard):
        for i, place in peers.offsets():
            device, _ = peers.other(*(-d for d in place))
            came = lands[a].at[device["section"], device["dp"] * rest + device["r"]]
            remote(came, came, all_send.at[a, i], all_recv.at[a, i], device).wait_recv()
        for layer in range(sections):
            for i in range(2 * rest):
                if a == 0:
                    for first, group, row, some in groups_of(2 * rest * block, i * block, block):
                        to = shard[layer].at[row : row + some, group * cols : (group + 1) * cols]
                        to[...] = lands[a][layer, i, first : first + some, :]
                    continue
                rows_at, lanes_at = i * block, 0
                if a == 2:
                    rows_at, lanes_at = i % rest * block, i // rest * lands[a].shape[3]
                to = shard[layer].at[rows_at : rows_at + block, lanes_at : lanes_at + lands[a].shape[3]]
                to[...] = lands[a][layer, i, :block, :]

    cols = width // slab
    for t in range(slab):
        big, off = divmod(t * cols, wide)
        at = (big % 2 * zs + big // 2) * wide + off
        cuts[0][t, :block, :] = w_attn[:, at : at + cols]
    share(0)
    for t in range(slab):
        count = max(0, min(span, width - t * span))
        for p in range(3):
            if count:
                at = p * width + t * span
                cuts[1][t, :block, p * span : p * span + count] = w_qkv[:, at : at + count]
            if count < span:
                cuts[1][t, :block, p * span + count : (p + 1) * span] = jnp.zeros((block, span - count), BF)
    share(1)
    for t in range(slab):
        a, c, r = t // (2 * rest), t // rest % 2, t % rest
        for k in range(zs):
            at = ((c * zs + k) * rest + r) * (sections * half) + a * half
            cuts[2][t, :block, k * half : (k + 1) * half] = w_fc[:, at : at + half]
    for a in range(sections):
        for c in range(2):
            for k in range(zs):
                at, to = (c * zs + k) * wide, (k * 2 + c) * wide
                proj_cut[a, :, to : to + wide] = w_proj[a * half : (a + 1) * half, at : at + wide]
    for k in range(1, zs):
        came = stage.at[lax.rem(z + zs - k, zs)]
        remote(came, came, z_send.at[k], z_recv.at[k], {"z": lax.rem(z + k, zs)}).wait_recv()
    gather = Gather(peers, tiny_out, sems)
    gather.start(stage)
    settle(0, wo)
    turn = Turn(peers, wo_full, nat, land, w_out, turn_send, turn_recv)
    ring = RingGather([(wo[0], wo_full, zs - 1), (qkv[0], qkv_full, zs - 1)], ring_local, ring_send, ring_recv)
    work = Both(ring, turn, True)
    ring.launch(0)
    settle(1, qkv)
    ring.launch(1)
    share(2)
    for d in range(1, sections):
        device, _ = peers.other(d, 0, 0)
        there = lax.rem(x + d, sections)
        send(remote(proj_cut.at[there], proj.at[x], far_send.at[d], far_recv.at[d], device))
    proj[x] = proj_cut[x]
    work.tick()
    for _ in gather.arrivals():
        pass
    work.tick()

    per_row, halves = sections * half // block, half // block
    for layer in range(sections):
        vec, bias, unit = smalls[3 * layer : 3 * layer + 3]
        natural[...] = jnp.zeros_like(natural)
        for c in range(2):
            for k in range(zs):
                for r in range(rest):
                    at = ((k * 2 + c) * rest + r) * block
                    vec[:, at : at + block] = tiny_out[layer * rest + r, c, k, 0:8, :block]
                    at = ((c * zs + k) * rest + r) * block
                    natural[:, at : at + block] = tiny_out[layer * rest + r, c, k, 0:8, :block]
        own = jnp.zeros((8, span), F32)
        for t in range(slab):
            own = jnp.where(me == t, natural[:, t * span : (t + 1) * span], own)
        bias[:, :span] = own[6:7]
        bias[:, span : 2 * span] = jnp.zeros((1, span), F32)
        bias[:, 2 * span :] = own[7:8]
        for k in range(zs):
            for j in range(halves):
                line = tiny_out[layer * rest + peers.r, peers.c, k, pl.ds(8 + x * halves + j, 1), :block]
                unit[:, k * half + j * block : k * half + (j + 1) * block] = line
    rows = h.shape[0]
    for a in range(sections):
        for r in range(rest):
            for c in range(2):
                at = ((a * rest + r) * 2 + c) * rows
                line = tiny_out[r, 0, c * 2 + a, pl.ds(8 + per_row + z // seqs, 1), :rows]
                row[:, at : at + rows] = line.astype(jnp.int32)
                col[at : at + rows, :] = jnp.broadcast_to(line, (8, rows)).T[:, :1].astype(jnp.int32)
    work.tick(2)
    settle(2, fc)
    work.tick()
    for i, (raw, ordered) in enumerate([(h_raw, h), (g_raw, g)]):
        route.arrived(i)
        reorder(raw, ordered, zs, wide)
    for d in range(1, sections):
        device, _ = peers.other(-d, 0, 0)
        came = proj.at[device["section"]]
        remote(came, came, far_send.at[d], far_recv.at[d], device).wait_recv()
    work.finish()
    route.finish()
    gather.finish()
    for copy in sent:
        copy.wait_send()


def run_start(name, lay, tiny, w_qkv, w_attn, w_fc, w_proj, inputs, cotangent):
    zs, n, chips, sections = lay.zs, lay.slab, lay.slab // 2, lay.sections
    span, block = lay.slots * lay.head, lay.block
    spots = lay.cores * lay.rest
    rows, tall = spots * block, -(-block // 16) * 16
    vmem, hbm = pl.BlockSpec(memory_space=pltpu.VMEM), pl.BlockSpec(memory_space=pl.ANY)
    units = lay.units // n
    widths = [lay.cols, 3 * span, units]
    flat = (lay.rows, lay.width)
    outs = [(a, BF) for a in ((rows, 3 * span), (rows // GROUPS, GROUPS * lay.cols), (rows // 2, 2 * units)) for _ in range(sections)]
    outs += [((sections, lay.half, lay.width), BF), ((zs, rows, 3 * span), BF), ((span, lay.width), BF)]
    outs += [(flat, BF), (flat, BF), ((1, lay.tokens), jnp.int32), ((lay.tokens, 1), jnp.int32)]
    outs += [((8, lay.width), F32), ((1, 3 * span), F32), ((1, units), F32)] * sections
    dma = pltpu.SemaphoreType.DMA
    return pl.pallas_call(
        functools.partial(start_kernel, (block, span, lay.half, lay.seqs, lay.micros)),
        out_shape=[jax.ShapeDtypeStruct(*o) for o in outs],
        in_specs=[vmem] * 7,
        out_specs=[vmem] * (1 + 3 * sections) + [hbm] + [vmem] * (5 + 3 * sections),
        scratch_shapes=[
            pltpu.VMEM((chips, 2, zs, *tiny.shape), F32),
            pltpu.VMEM((zs, *tiny.shape), F32),
            pltpu.VMEM(flat[::-1], BF),
            pltpu.VMEM(flat[::-1], BF),
            pltpu.VMEM((8, n * span), F32),
            pltpu.VMEM((sections, lay.half, lay.width), BF),
        ]
        + [pltpu.VMEM((n, tall, m), BF) for m in widths]
        + [pltpu.VMEM((sections, spots, tall, m), BF) for m in widths]
        + [pltpu.VMEM((zs, rows // GROUPS, GROUPS * lay.cols), BF), pltpu.VMEM((n * span, lay.cols), BF), pltpu.VMEM((n, span, lay.cols), BF)]
        + [dma((zs,))] * 2
        + [dma((chips,))] * 4
        + [dma((3, n))] * 2
        + [dma((sections,))] * 2
        + [dma((n,))] * 2
        + [dma((2,))]
        + [dma((2, zs - 1))] * 2
        + [dma((2,)), dma((2, lay.micros)), dma((2,))],
        compiler_params=pltpu.CompilerParams(collective_id=name, has_side_effects=True, vmem_limit_bytes=60 * 2**20),
    )(tiny, w_qkv, w_attn, w_fc, w_proj, inputs, cotangent)


def end_kernel(sizes, *refs):
    count = 20
    refs = list(refs)
    near, sems = refs[-1 - count : -1], refs[-1]
    fetched = [Fetch(refs[i], near[i], sems.at[i]) for i in range(count)]
    refs = fetched + refs[count : -1 - count]
    block, width, units, seqs = sizes
    parts, (q_one, k_one, v_one, wo_one), (fc_zero, fc_one, proj_zero, proj_one), refs = refs[:4], refs[4:8], refs[8:12], refs[12:]
    sums, (last_rows, *ready), refs = refs[:8], refs[8:15], refs[15:]
    (out_qkv, out_wo, out_fc, out_proj, out_small, section_out, section_grad, home, out_rows), refs = refs[:9], refs[9:]
    totals, (proj_both, proj_land), refs = refs[:4], refs[4:6], refs[6:]
    stages, lands, refs = refs[:5], refs[5:10], refs[10:]
    (small_land, small_sum, z_land), came, (small, natural, rows_buf), refs = refs[:3], refs[3:7], refs[7:10], refs[10:]
    all_send, all_recv, far_send, far_recv, z_send, z_recv, ring_send, ring_recv, late_send, late_recv, *route_sems, rows_sem = refs
    peers = Peers()
    zs, z = lax.axis_size("z"), lax.axis_index("z")
    x, rest, slab = peers.x, peers.rest, 2 * peers.chips
    spot = peers.c * rest + peers.r
    span, cols = q_one.shape[1], wo_one.shape[1] // GROUPS
    half, wide = proj_zero.shape[0], rest * block
    _, me = peers.other(0, 0, 0)
    offsets = peers.offsets()
    route = Route(seqs, last_rows, home, *route_sems[:3])
    across = Across(0, home, out_rows, *route_sems[3:5])
    peers.greet(zs, Several([route, across]))
    sent = []

    def send(copy):
        copy.start()
        sent.append(copy)

    pieces = [(parts[p], None, came[p], totals[p], 0, zs - 1) for p in range(4)]
    ring = RingSum(pieces[:2], ring_send, ring_recv)
    ring.start()
    route.start()

    def restore(first_crossed, second, first_home, out):
        whole = lax.rem(z, 2) == x
        for layer, choice in enumerate([(first_home, first_crossed), second]):
            for kind, src in enumerate(choice):

                @pl.when((x == layer) & (whole if kind == 0 else jnp.logical_not(whole)))
                def _(src=src):
                    pltpu.make_async_copy(src, rows_buf, rows_sem).start()

        pltpu.make_async_copy(first_home, rows_buf, rows_sem).wait()
        for micro in range(out.shape[0]):
            for c in range(2):
                for k in range(zs):
                    at, of = (c * zs + k) * wide, (k * 2 + c) * wide
                    out[micro, at : at + wide, :] = rows_buf[micro, :, of : of + wide].astype(F32).T.astype(BF)

    def cut(a, totals):
        for layer, total in enumerate(totals):
            for i in range(2 * rest):
                if a == 4:
                    for first, group, row, some in groups_of(2 * rest * block, i * block, block):
                        lanes = slice(group * cols, (group + 1) * cols)
                        stages[a][layer, i, first : first + some, :] = total[row : row + some, lanes]
                    continue
                wide_at, rows_at = 0, i * block
                if a == 0:
                    wide_at, rows_at = i // rest * stages[a].shape[3], i % rest * block
                stages[a][layer, i, :block, :] = total[rows_at : rows_at + block, wide_at : wide_at + stages[a].shape[3]]
        for i, place in offsets:
            device, t = peers.other(*place)
            src = stages[a].at[device["section"], device["dp"] * rest + device["r"]]
            line = a + a // 3
            send(remote(src, lands[a].at[me], all_send.at[line, i], all_recv.at[line, i], device))
        lands[a][me] = stages[a][x, spot]

    def settle(a, land):
        for i, place in offsets:
            device, t = peers.other(*(-d for d in place))
            came = land.at[t]
            remote(came, came, all_send.at[a, i], all_recv.at[a, i], device).wait_recv()

    cut(0, (fc_zero, fc_one))
    proj_both[0] = proj_zero[...]
    proj_both[1] = proj_one[...]
    device, _ = peers.other(1, 0, 0)
    send(remote(proj_both.at[1 - x], proj_land.at[x], far_send, far_recv, device))
    proj_land[x] = proj_both[x]
    ring.tick(2)
    small[...] = jnp.zeros_like(small)
    halves = half // block
    for layer in range(2):
        feed, attn, heads, unit = sums[4 * layer : 4 * layer + 4]
        for t in range(slab):
            natural[0:1, t * span : (t + 1) * span] = jnp.where(me == t, heads[:, :span], 0.0)
            natural[1:2, t * span : (t + 1) * span] = jnp.where(me == t, heads[:, 2 * span :], 0.0)
        for c in range(2):
            for k in range(zs):
                for r in range(rest):
                    to = small.at[(layer * 2 + c) * rest + r, k]
                    at = slice(((k * 2 + c) * rest + r) * block, ((k * 2 + c) * rest + r + 1) * block)
                    to[0:1, :block] = attn[0:1, at]
                    to[1:2, :block] = feed[0:1, at]
                    to[2:3, :block] = attn[1:2, at]
                    to[5:6, :block] = feed[3:4, at]
                    to[6:8, :block] = feed[1:3, at]
                    at = ((c * zs + k) * rest + r) * block
                    to[3:5, :block] = natural[0:2, at : at + block]
                    own = (peers.c == c) & (peers.r == r)
                    for h in range(2):
                        for j in range(halves):
                            line = unit[0:1, k * half + j * block : k * half + (j + 1) * block]
                            spot_row = 8 + h * halves + j
                            to[spot_row : spot_row + 1, :block] = jnp.where(own & (x == h), line, 0.0)
    for i, place in offsets:
        device, t = peers.other(*place)
        send(remote(small.at[t], small_land.at[me], all_send.at[3, i], all_recv.at[3, i], device))
    small_land[me] = small[me]

    ring.tick(2)
    late_ring = RingSum(pieces[2:], late_send, late_recv)
    late_ring.start()
    settle(0, lands[0])
    for t in range(slab):
        h, c, r = t // (2 * rest), t // rest % 2, t % rest
        for k in range(zs):
            at = ((c * zs + k) * rest + r) * (units // (2 * zs * rest)) + h * half
            out_fc[:, 0, at : at + half] = lands[0][t, :block, k * half : (k + 1) * half].astype(F32)
    settle(3, small_land)
    total = small_land[0]
    for t in range(1, slab):
        total = total + small_land[t]
    small_sum[...] = total
    for k in range(1, zs):
        there = lax.rem(z + k, zs)
        send(remote(small_sum.at[there], z_land.at[z], z_send.at[k], z_recv.at[k], {"z": there}))
    z_land[z] = small_sum[z]
    ring.finish()
    cut(1, (totals[0], q_one))
    cut(2, (totals[1], k_one))
    late_ring.tick(2)
    route.arrived()
    across.tick("middle")
    restore(ready[1], ready[2:4], ready[0], section_out)
    came_proj = proj_land.at[1 - x]
    remote(came_proj, came_proj, far_send, far_recv, device).wait_recv()
    for h in range(2):
        for c in range(2):
            for k in range(zs):
                at, of = (c * zs + k) * wide, (k * 2 + c) * wide
                out_proj[h * half : (h + 1) * half, at : at + wide] = proj_land[h, :, of : of + wide]
    late_ring.tick(2)
    for k in range(1, zs):
        block_in = z_land.at[lax.rem(z + zs - k, zs)]
        remote(block_in, block_in, z_send.at[k], z_recv.at[k], {"z": lax.rem(z + k, zs)}).wait_recv()
    total = z_land[0]
    for k in range(1, zs):
        total = total + z_land[k]
    out_small[...] = total

    def place(p):
        for t in range(slab):
            count = min(span, width - t * span)
            if count > 0:
                at = p * width + t * span
                out_qkv[:, 0, at : at + count] = lands[1 + p][t, :block, :count].astype(F32)

    for p in range(2):
        settle(1 + p, lands[1 + p])
        place(p)
    late_ring.finish()
    cut(3, (totals[2], v_one))
    cut(4, (totals[3], wo_one))
    route.sent()
    across.finish()
    for operand in fetched:
        operand.finish()
    restore(out_rows, ready[4:], home, section_grad)
    settle(4, lands[3])
    place(2)
    settle(5, lands[4])
    for t in range(slab):
        big, off = divmod(t * cols, wide)
        at = (big % 2 * zs + big // 2) * wide + off
        out_wo[:, 0, at : at + cols] = lands[4][t, :block, :].astype(F32)
    for copy in sent:
        copy.wait_send()


def run_end(name, lay, parts, ones, fcs, projs, sums, last_rows, ready):
    zs, n = lay.zs, lay.slab
    span, width, block = lay.slots * lay.head, lay.width, lay.block
    spots = lay.cores * lay.rest
    tall = -(-block // 16) * 16
    vmem = pl.BlockSpec(memory_space=pltpu.VMEM)
    dma = pltpu.SemaphoreType.DMA
    widths = [fcs[0].shape[1] // 2, span, span, span, lay.cols]
    half = projs[0].shape[0]
    tile = (-(-(8 + lay.unit_block // block) // 8) * 8, 128)
    outs = [(block, 1, 3 * width), (block, 1, width), (block, 1, lay.units), (lay.unit_block, width), tile]
    return pl.pallas_call(
        functools.partial(end_kernel, (block, width, lay.units, lay.seqs)),
        out_shape=[jax.ShapeDtypeStruct(o, BF if i == 3 else F32) for i, o in enumerate(outs)]
        + [jax.ShapeDtypeStruct((lay.micros, lay.width, lay.rows), BF)] * 2
        + [jax.ShapeDtypeStruct((lay.micros, *last_rows.shape), BF)] * 2,
        in_specs=[pl.BlockSpec(memory_space=pl.ANY)] * 27,
        out_specs=[vmem] * 7 + [pl.BlockSpec(memory_space=pl.ANY)] * 2,
        scratch_shapes=[
            *[pltpu.VMEM(a.shape[1:], BF) for a in parts],
            pltpu.VMEM((2, half, width), BF),
            pltpu.VMEM((2, half, width), BF),
        ]
        + [pltpu.VMEM((lay.sections, spots, tall, m), BF) for m in widths]
        + [pltpu.VMEM((n, tall, m), BF) for m in widths]
        + [
            pltpu.VMEM((n, zs, *tile), F32),
            pltpu.VMEM((zs, *tile), F32),
            pltpu.VMEM((zs, *tile), F32),
            *[pltpu.VMEM((zs - 1, *a.shape[1:]), BF) for a in parts],
            pltpu.VMEM((n, zs, *tile), F32),
            pltpu.VMEM((8, n * span), F32),
            pltpu.VMEM((lay.micros, *last_rows.shape), BF),
        ]
        + [dma((6, n))] * 2
        + [dma] * 2
        + [dma((zs,))] * 2
        + [dma((2, zs - 1))] * 4
        + [dma, dma, dma((lay.micros,)), dma, dma, dma]
        + [pltpu.VMEM(a.shape, a.dtype) for a in (*parts, *ones, *fcs, *projs, *sums)]
        + [dma((20,))],
        compiler_params=pltpu.CompilerParams(collective_id=name, has_side_effects=True, vmem_limit_bytes=60 * 2**20),
    )(*parts, *ones, *fcs, *projs, *sums, last_rows, *ready)


class Rings:
    def __init__(self, lay):
        self.zs = lay.zs
        self.state = {}

    def put(self, kind, layer, part):
        if part.ndim == 2:
            part = part.reshape(self.zs, part.shape[0] // self.zs, part.shape[1])
        _, acc, steps = self.state.get((kind, layer), (None, None, 0))
        self.state[kind, layer] = (part, acc, steps)

    def side(self, plan, pace, makes={}):
        pieces = []
        for kind, layer, count in plan:
            part, acc, steps = self.state.get((kind, layer), (None, None, 0))
            shape = makes[kind] if part is None else part.shape[1:]
            pieces.append((part, shape, acc, steps, count))
        return sum_side(pieces, pace)

    def done(self, plan, outs):
        for (kind, layer, count), acc in zip(plan, outs):
            part, _, steps = self.state[kind, layer]
            self.state[kind, layer] = (part, acc, steps + count)


def on_device(
    inputs, cotangent, positions, w_qkv, w_attn_out, w_fc, w_proj, norm_gains, biases, fc_bias
):
    lay = Layout(inputs, w_fc)
    n, block, width = lay.slab, lay.block, lay.width
    span = lay.slots * lay.head

    small = jnp.concatenate([norm_gains[0], biases[0]], axis=1).astype(F32).T
    small = jnp.stack([small[i] for i in (0, 1, 2, 6, 5, 7, 3, 4)])
    small = jnp.concatenate([small, fc_bias[0].reshape(-1, block).astype(F32)])
    small = jnp.pad(small, ((0, 0), (0, 128 - block)))
    places = jnp.pad(positions.astype(F32), ((0, 0), (0, 128 - lay.rows)))
    small = jnp.concatenate([small, places])
    small = jnp.pad(small, ((0, -small.shape[0] % 8), (0, 0)))
    *cut, proj_cut, w_qkv, w_out, h, g, row, col, vec_0, bias_0, unit_0, vec_1, bias_1, unit_1 = run_start(
        0, lay, small, w_qkv[0], w_attn_out[0], w_fc[0], w_proj[0], jnp.swapaxes(inputs, 2, 3), jnp.swapaxes(cotangent, 2, 3)
    )
    qkv_cut, wo_cut, fc_cut = cut[0:2], cut[2:4], cut[4:6]
    smalls = [(vec_0, bias_0, unit_0), (vec_1, bias_1, unit_1)]
    outs, keeps, params = [], [], []
    for layer in range(lay.sections):
        last = layer == lay.sections - 1
        vec, bias, unit = smalls[layer]
        w_qkv = w_qkv.reshape(width, 3 * span)
        side = gather_side([fc_cut[layer], (proj_cut, layer)], {"qkv": 1, "q0": 1, "q3": 1}, (lay.zs - 1, lay.zs - 2))
        if last:
            side = both_sides(side, share_side(lay, g, ("qkv", "q3")))
        (full, qkv, attended, logs, mid, normed_two), (w_fc, w_proj, *shared) = run_attention_forward(
            1 + 2 * layer,
            lay.head,
            side,
            h,
            w_qkv,
            w_out,
            bias,
            col,
            row,
            vec,
        )
        if last:
            side = route_side(lay, outs[0], "start")
        else:
            side = gather_side([wo_cut[layer + 1], qkv_cut[layer + 1]], {"k3": 2, "sent": 1}, turn=span)
        (full_two, slope, activated, result, w_proj, w_fc), later = run_feed_forward(
            2 + 2 * layer, side, normed_two, mid, w_fc, w_proj, unit, vec
        )
        params.append((w_qkv, w_out, w_fc, w_proj.reshape(-1, width)))
        if last:
            (home,), (branch,) = later, shared
        else:
            w_out, w_qkv = later
        keeps.append((h, full, qkv, attended, logs, mid, full_two, slope, activated))
        h = result
        outs.append(h)

    rings = Rings(lay)
    plans = {
        ("feed", 1): [("proj", 1, 3)],
        ("attention", 1): [("fc", 1, 3)],
        ("feed", 0): [("q", 1, 3), ("k", 1, 3), ("v", 1, 3), ("proj", 0, 1)],
        ("attention", 0): [("fc", 0, 3), ("proj", 0, 2), ("out", 1, 3)],
    }
    paces = {
        ("feed", 1): {"proj": 1, "fc": 1},
        ("attention", 1): {"k2": 1, "grad": 1},
        ("feed", 0): {"k3": 3},
        ("attention", 0): {"k3": 3},
    }
    crossed = {}
    sums = [None] * lay.sections
    for layer in reversed(range(lay.sections)):
        w_qkv, w_out, w_fc, w_proj = params[layer]
        vec = smalls[layer][0]
        h, full, qkv, attended, logs, mid, full_two, slope, activated = keeps[layer]
        full, full_two = (a.reshape(lay.tokens, width) for a in (full, full_two))
        name = 1 + 4 * lay.sections - 2 * layer
        side = rings.side(plans["feed", layer], paces["feed", layer], {"proj": (lay.half, width)})
        late = layer == lay.sections - 1
        turn = SideWork() if late else turn_side(lay, grad_out)
        side = both_sides(side, turn, across_side(0 if late else 1, home), route_side(lay, outs[1] if late else g, "start"))
        (grad_mid, attn_rows, grad_proj, grad_fc, feed_sums, unit_sums), done = run_feed_backward(
            name, side, g, mid, w_fc, w_proj, slope, activated, full_two, vec, *([branch] if late else [])
        )
        rings.put("proj", layer, grad_proj)
        rings.put("fc", layer, grad_fc)
        rings.done(plans["feed", layer], done)
        if late:
            crossed["out", 0] = (home, done[-2])
        else:
            crossed["out", 1] = (home, done[-2])
            rings.put("out", 1, done[-3])
        home = done[-1]
        side = rings.side(plans["attention", layer], paces["attention", layer])
        if not late:
            side = both_sides(side, turn_side(lay), across_side(1, home))
        (g, *grad_parts, grad_out, attn_sums, head_sums), done = run_attention_backward(
            name + 1, lay.head, side, attn_rows, grad_mid, h, w_qkv, w_out, qkv, attended, logs, full, col, row, vec
        )
        rings.done(plans["attention", layer], done)
        if not late:
            rings.put("out", layer, done[-2])
            crossed["grad", 1] = (home, done[-1])
        for kind, part in zip("qkv", grad_parts):
            rings.put(kind, layer, part)
        sums[layer] = (feed_sums, attn_sums, head_sums, unit_sums)
    out_qkv, out_attn, out_fc, out_proj, rows, section_out, section_grad, *_ = run_end(
        3 + 4 * lay.sections,
        lay,
        [rings.state[kind, 0][0] for kind in ("q", "k", "v", "out")],
        [rings.state[kind, 1][1] for kind in ("q", "k", "v", "out")],
        [rings.state["fc", layer][1] for layer in range(2)],
        [rings.state["proj", layer][1] for layer in range(2)],
        [a for layer in range(2) for a in sums[layer]],
        g,
        [*crossed["out", 0], *crossed["out", 1], *crossed["grad", 1]],
    )
    cols = rows[:8, :block].T
    return (
        jnp.swapaxes(section_out, 1, 2)[None, :, None],
        jnp.swapaxes(section_grad, 1, 2)[None, :, None],
        jnp.swapaxes(out_qkv, 0, 1),
        jnp.swapaxes(out_attn, 0, 1),
        jnp.swapaxes(out_fc, 0, 1),
        out_proj.astype(F32)[None],
        cols[None, :, :2],
        cols[None, :, 2:],
        rows[8 : 8 + lay.unit_block // block, :block].reshape(1, lay.unit_block),
    )


def solution(mesh):
    sections, cores, contexts = (mesh.shape[a] for a in ("section", "dp", "ctx"))
    zs = sections * cores
    shape = (sections, cores, zs, contexts // zs)
    inner = Mesh(mesh.devices.reshape(shape), ALL)
    tokens = P(None, "dp", ("z", "r"), None)
    rows = P("section", ("dp", "z", "r"), None)
    units = P("section", ("dp", "z", "r"))
    out_tokens = P("section", None, "dp", ("z", "r"), None)
    return jax.shard_map(
        on_device,
        mesh=inner,
        in_specs=(tokens, tokens, P(None, ("z", "r"))) + (rows,) * 6 + (units,),
        out_specs=(out_tokens, out_tokens) + (rows,) * 6 + (units,),
        check_vma=False,
    )
```
